32 devices in a mesh: dp: 16 (over z, x, core), tensor: 2 (over y).
Axes of the slice: x: 2, y: 2, z: 4, core: 2. Of those that a mesh axis runs over, the one named last changes fastest.
Arguments:
- inputs: bfloat16 [16, 1024, 1536], P('dp', 'tensor'), may hold values from -6 to 6
- encoder_text_states: bfloat16 [16, 64, 1536], P('dp'), may hold values from -6 to 6
- cotangent: bfloat16 [16, 1024, 1536], P('dp', 'tensor'), may hold values from -1.5 to 1.5
- clip_adapter_index: int32 [16, 10], P('dp'), may hold values from 0 to 7
- self_norm_gain: float32 [1536], replicated, may hold values from 0.25 to 1.75
- cross_norm_gain: float32 [1536], replicated, may hold values from 0.25 to 1.75
- feed_norm_gain: float32 [1536], replicated, may hold values from 0.25 to 1.75
- self_query_key_value_weight: bfloat16 [3, 1536, 1536], P(None, None, 'tensor'), may hold values from -0.15625 to 0.15625
- self_output_weight: bfloat16 [1536, 1536], P('tensor'), may hold values from -0.625 to 0.625
- cross_query_weight: bfloat16 [1536, 1536], P(None, 'tensor'), may hold values from -0.15625 to 0.15625
- cross_key_value_weight: bfloat16 [2, 1536, 1536], P(None, None, 'tensor'), may hold values from -0.15625 to 0.15625
- cross_output_weight: bfloat16 [1536, 1536], P('tensor'), may hold values from -0.4375 to 0.4375
- up_weight: bfloat16 [1536, 6144], P(None, 'tensor'), may hold values from -0.15625 to 0.15625
- down_weight: bfloat16 [6144, 1536], P('tensor'), may hold values from -0.078125 to 0.078125
- self_first_factors: bfloat16 [3, 8, 16, 1536], replicated, may hold values from -0.15625 to 0.15625
- self_second_factors: bfloat16 [3, 8, 16, 1536], P(None, None, None, 'tensor'), may hold values from -0.375 to 0.375
- cross_first_factors: bfloat16 [3, 8, 16, 1536], replicated, may hold values from -0.15625 to 0.15625
- cross_second_factors: bfloat16 [3, 8, 16, 1536], P(None, None, None, 'tensor'), may hold values from -0.375 to 0.375
- attention_first_factors: bfloat16 [2, 8, 16, 1536], P(None, None, None, 'tensor'), may hold values from -0.15625 to 0.15625
- attention_second_factors: bfloat16 [2, 8, 16, 1536], replicated, may hold values from -0.75 to 0.75
- input_first_factors: bfloat16 [8, 16, 1536], replicated, may hold values from -0.15625 to 0.15625
- input_second_factors: bfloat16 [8, 16, 6144], P(None, None, 'tensor'), may hold values from -0.375 to 0.375
- output_first_factors: bfloat16 [8, 16, 6144], P(None, None, 'tensor'), may hold values from -0.078125 to 0.078125
- output_second_factors: bfloat16 [8, 16, 1536], replicated, may hold values from -0.375 to 0.375
Outputs:
- output: bfloat16 [16, 1024, 1536], P('dp', 'tensor')
- input_grad: float32 [16, 1024, 1536], P('dp', 'tensor')
- text_grad: float32 [16, 64, 1536], P('dp', None, 'tensor')
- grad_lora_self_a: float32 [3, 8, 16, 1536], P(None, None, None, 'tensor')
- grad_lora_self_b: float32 [3, 8, 16, 1536], P(None, None, None, 'tensor')
- grad_lora_cross_a: float32 [3, 8, 16, 1536], P(None, None, None, 'tensor')
- grad_lora_cross_b: float32 [3, 8, 16, 1536], P(None, None, None, 'tensor')
- grad_lora_out_a: float32 [2, 8, 16, 1536], P(None, None, None, 'tensor')
- grad_lora_out_b: float32 [2, 8, 16, 1536], P(None, None, None, 'tensor')
- grad_lora_up_a: float32 [8, 16, 1536], P(None, None, 'tensor')
- grad_lora_up_b: float32 [8, 16, 6144], P(None, None, 'tensor')
- grad_lora_down_a: float32 [8, 16, 6144], P(None, None, 'tensor')
- grad_lora_down_b: float32 [8, 16, 1536], P(None, None, 'tensor')
The draws below stay inside these ranges and needn't reach their ends.
Inputs may be any that keep to these rules, and one draw needn't show every extreme that they name: `clip_adapter_index`: the adapter, of 8, that clip c uses for projection j.
All inputs are finite; a program needn't handle non-finite values.
Results may differ from the reference program's by a relative error of at most 0.035.
Values may be sent and summed in bfloat16 or wider, within the bound.
No kernel may reach another device: no remote copies, remote signals or barrier semaphores. Data moves between devices by JAX's collectives and lax.ppermute only.
A program may use at most 384 MiB of HBM per device.

```python
import jax
import jax.numpy as jnp
from jax import lax

MODEL_WIDTH = 1536
HEADS = 24
HEAD_DIM = 64
HIDDEN_UNITS = 6144
ADAPTER_RANK = 16
ADAPTER_COUNT = 8
TEXT = 64
FRAMES = 1024
CLIPS = 16


def plant(entries, stream_key, least, high):
    longest = entries.shape.index(max(entries.shape))
    spots = []
    for shift in (0, 1):
        where = [jax.random.randint(jax.random.fold_in(stream_key, axis), (), 0, length) for axis, length in enumerate(entries.shape)]
        where[longest] = (where[longest] + shift) % entries.shape[longest]
        spots.append(tuple(where))
    return entries.at[spots[0]].set(least).at[spots[1]].set(high)


def level_of(key, dims, shards, smallest, high):
    factor_of = 1.0
    for position, blocks in shards:
        steps = jax.random.uniform(jax.random.fold_in(jax.random.fold_in(key, 6), position), (blocks,), jnp.float32, smallest / len(shards), high / len(shards))
        factor_of = factor_of * jnp.repeat(jnp.exp(steps), dims[position] // blocks).reshape((-1,) + (1,) * (len(dims) - 1 - position))
    return factor_of


def bell_draw(own_key, shape, deviation, bound, shards=(), kind=jnp.bfloat16):
    array = jax.random.normal(own_key, shape, jnp.float32) * deviation
    if len(shards) > 0:
        array = level_of(own_key, shape, shards, -0.22, 0.18) * array
    return jnp.clip(array, min=-bound, max=bound).astype(kind)


def setup_inputs(seed: int = 0) -> dict:
    splits = jax.random.split(jax.random.key(seed), 25)
    return {
        "inputs": bell_draw(splits[0], (CLIPS, FRAMES, MODEL_WIDTH), 1.0, 6.0, ((0, 16), (1, 2))),
        "encoder_text_states": bell_draw(splits[1], (CLIPS, TEXT, MODEL_WIDTH), 1.0, 6.0, ((0, 16),)),
        "cotangent": bell_draw(splits[2], (CLIPS, FRAMES, MODEL_WIDTH), 0.25, 1.5, ((0, 16), (1, 2))),
        "clip_adapter_index": plant(jax.random.randint(splits[3], (CLIPS, 10), 0, ADAPTER_COUNT), jax.random.fold_in(splits[3], 1), 0, ADAPTER_COUNT - 1).astype(jnp.int32),
        "self_norm_gain": jnp.clip(1.0 + 0.15 * jax.random.normal(splits[4], (MODEL_WIDTH,), jnp.float32), 0.25, 1.75),
        "cross_norm_gain": jnp.clip(1.0 + 0.15 * jax.random.normal(splits[5], (MODEL_WIDTH,), jnp.float32), 0.25, 1.75),
        "feed_norm_gain": jnp.clip(1.0 + 0.15 * jax.random.normal(splits[6], (MODEL_WIDTH,), jnp.float32), 0.25, 1.75),
        "self_query_key_value_weight": bell_draw(splits[7], (3, MODEL_WIDTH, MODEL_WIDTH), MODEL_WIDTH ** -0.5, 0.15625, ((2, 2),)),
        "self_output_weight": bell_draw(splits[8], (MODEL_WIDTH, MODEL_WIDTH), (MODEL_WIDTH // 16) ** -0.5, 0.625, ((0, 2),)),
        "cross_query_weight": bell_draw(splits[9], (MODEL_WIDTH, MODEL_WIDTH), MODEL_WIDTH ** -0.5, 0.15625, ((1, 2),)),
        "cross_key_value_weight": bell_draw(splits[10], (2, MODEL_WIDTH, MODEL_WIDTH), MODEL_WIDTH ** -0.5, 0.15625, ((2, 2),)),
        "cross_output_weight": bell_draw(splits[11], (MODEL_WIDTH, MODEL_WIDTH), (MODEL_WIDTH // 8) ** -0.5, 0.4375, ((0, 2),)),
        "up_weight": bell_draw(splits[12], (MODEL_WIDTH, HIDDEN_UNITS), MODEL_WIDTH ** -0.5, 0.15625, ((1, 2),)),
        "down_weight": bell_draw(splits[13], (HIDDEN_UNITS, MODEL_WIDTH), HIDDEN_UNITS ** -0.5, 0.078125, ((0, 2),)),
        "self_first_factors": bell_draw(splits[14], (3, ADAPTER_COUNT, ADAPTER_RANK, MODEL_WIDTH), MODEL_WIDTH ** -0.5, 0.15625),
        "self_second_factors": bell_draw(splits[15], (3, ADAPTER_COUNT, ADAPTER_RANK, MODEL_WIDTH), (16 * ADAPTER_RANK) ** -0.5, 0.375, ((3, 2),)),
        "cross_first_factors": bell_draw(splits[16], (3, ADAPTER_COUNT, ADAPTER_RANK, MODEL_WIDTH), MODEL_WIDTH ** -0.5, 0.15625),
        "cross_second_factors": bell_draw(splits[17], (3, ADAPTER_COUNT, ADAPTER_RANK, MODEL_WIDTH), (16 * ADAPTER_RANK) ** -0.5, 0.375, ((3, 2),)),
        "attention_first_factors": bell_draw(splits[18], (2, ADAPTER_COUNT, ADAPTER_RANK, MODEL_WIDTH), MODEL_WIDTH ** -0.5, 0.15625, ((3, 2),)),
        "attention_second_factors": bell_draw(splits[19], (2, ADAPTER_COUNT, ADAPTER_RANK, MODEL_WIDTH), (4 * ADAPTER_RANK) ** -0.5, 0.75),
        "input_first_factors": bell_draw(splits[20], (ADAPTER_COUNT, ADAPTER_RANK, MODEL_WIDTH), MODEL_WIDTH ** -0.5, 0.15625),
        "input_second_factors": bell_draw(splits[21], (ADAPTER_COUNT, ADAPTER_RANK, HIDDEN_UNITS), (16 * ADAPTER_RANK) ** -0.5, 0.375, ((2, 2),)),
        "output_first_factors": bell_draw(splits[22], (ADAPTER_COUNT, ADAPTER_RANK, HIDDEN_UNITS), HIDDEN_UNITS ** -0.5, 0.078125, ((2, 2),)),
        "output_second_factors": bell_draw(splits[23], (ADAPTER_COUNT, ADAPTER_RANK, MODEL_WIDTH), (16 * ADAPTER_RANK) ** -0.5, 0.375),
    }


highest = lax.Precision.HIGHEST
epsilon = 1e-05

@jax.custom_vjp
def low(v):
    return lax.optimization_barrier(v.astype(jnp.bfloat16)).astype(jnp.float32)

@jax.custom_vjp
def low_back(v):
    return v

def low_keep(v):
    return (low(v), None)

def low_pass(kept, grad):
    return (grad,)

def back_keep(v):
    return (v, None)

def back_low(kept, grad):
    return (low(grad),)
low.defvjp(low_keep, low_pass)
low_back.defvjp(back_keep, back_low)

def product(left, right):
    return jnp.dot(left, right, precision=highest, preferred_element_type=jnp.float32)

def layer_norm(stream, gain_vec):
    centred = stream - lax.optimization_barrier(jnp.mean(stream, axis=-1, keepdims=True))
    variance = lax.optimization_barrier(jnp.mean(centred * centred, axis=-1, keepdims=True))
    return centred * lax.rsqrt(variance + epsilon) * gain_vec

def project(act_rows, weight, down_map, up_map):
    return product(act_rows, weight) + product(product(act_rows, down_map.T), up_map)

def attend(queries, key_rows, value_rows, causal):
    frames = queries.shape[0]
    key_count = key_rows.shape[0]
    block_rows = min(512, frames)
    score_scale = HEAD_DIM ** (-0.5)
    query_blocks = queries.reshape(frames // block_rows, block_rows, HEADS, HEAD_DIM)
    starts = jnp.arange(frames // block_rows, dtype=jnp.int32) * block_rows

    def one_block(paired):
        query_block, start_row = paired
        scores = jnp.einsum('bhe,khe->hbk', query_block, key_rows, precision=highest) * score_scale
        scores = low_back(scores)
        if causal:
            query_at = start_row + jnp.arange(block_rows, dtype=jnp.int32)[:, None]
            key_at = jnp.arange(key_count, dtype=jnp.int32)[None, :]
            scores = jnp.where(key_at <= query_at, scores, -1e+30)
        weights_low = low(jax.nn.softmax(scores, axis=-1))
        return jnp.einsum('hbk,khe->bhe', weights_low, value_rows, precision=highest)
    blocks_out = lax.map(jax.checkpoint(one_block), (query_blocks, starts))
    return blocks_out.reshape(frames, HEADS * HEAD_DIM)

def split_heads(stacked):
    return stacked.reshape(stacked.shape[0], HEADS, HEAD_DIM)

def clip_layer(stream, text_rows, gain_set, weight_set, picked_slots, adapter_group):
    self_norm_gain, cross_norm_gain, feed_norm_gain = gain_set
    self_query_key_value_weight, self_output_weight, cross_query_weight, cross_key_value_weight, cross_output_weight, up_weight, down_weight = weight_set
    self_a, self_b, cross_a, cross_b, out_a, out_b, up_a, up_b, down_a, down_b = adapter_group
    normed = low(layer_norm(stream, self_norm_gain))
    head_rows = []
    for slot_number in range(3):
        projected = project(normed, self_query_key_value_weight[slot_number], self_a[slot_number, picked_slots[slot_number]], self_b[slot_number, picked_slots[slot_number]])
        head_rows.append(split_heads(low(low_back(projected))))
    mixed_heads = low(low_back(attend(head_rows[0], head_rows[1], head_rows[2], True)))
    branch = low_back(project(mixed_heads, self_output_weight, out_a[0, picked_slots[3]], out_b[0, picked_slots[3]]))
    stream_one = stream + branch
    normed = low(layer_norm(stream_one, cross_norm_gain))
    query_two = low(low_back(project(normed, cross_query_weight, cross_a[0, picked_slots[4]], cross_b[0, picked_slots[4]])))
    key_two = low(low_back(project(text_rows, cross_key_value_weight[0], cross_a[1, picked_slots[5]], cross_b[1, picked_slots[5]])))
    value_two = low(low_back(project(text_rows, cross_key_value_weight[1], cross_a[2, picked_slots[6]], cross_b[2, picked_slots[6]])))
    mixed_heads = low(low_back(attend(split_heads(query_two), split_heads(key_two), split_heads(value_two), False)))
    branch = low_back(project(mixed_heads, cross_output_weight, out_a[1, picked_slots[7]], out_b[1, picked_slots[7]]))
    stream_two = stream_one + branch
    normed = low(layer_norm(stream_two, feed_norm_gain))
    before = low_back(project(normed, up_weight, up_a[picked_slots[8]], up_b[picked_slots[8]]))
    hidden = low(jax.nn.gelu(before, approximate=False))
    branch = low_back(project(hidden, down_weight, down_a[picked_slots[9]], down_b[picked_slots[9]]))
    return stream_two + branch

def reference(inputs, encoder_text_states, cotangent, clip_adapter_index, self_norm_gain, cross_norm_gain, feed_norm_gain, self_query_key_value_weight, self_output_weight, cross_query_weight, cross_key_value_weight, cross_output_weight, up_weight, down_weight, self_first_factors, self_second_factors, cross_first_factors, cross_second_factors, attention_first_factors, attention_second_factors, input_first_factors, input_second_factors, output_first_factors, output_second_factors):
    gain_set = (self_norm_gain.astype(jnp.float32), cross_norm_gain.astype(jnp.float32), feed_norm_gain.astype(jnp.float32))
    weight_set = tuple((matrix.astype(jnp.float32) for matrix in (self_query_key_value_weight, self_output_weight, cross_query_weight, cross_key_value_weight, cross_output_weight, up_weight, down_weight)))
    adapter_group = tuple((adapter_slot_table.astype(jnp.float32) for adapter_slot_table in (self_first_factors, self_second_factors, cross_first_factors, cross_second_factors, attention_first_factors, attention_second_factors, input_first_factors, input_second_factors, output_first_factors, output_second_factors)))

    def clip_step(running, clip_data):
        stream, text_rows, grad_out, picked_slots = clip_data

        def forward(stream_in, text_in, *tables):
            return clip_layer(stream_in, text_in, gain_set, weight_set, picked_slots, tables)
        result, pullback = jax.vjp(forward, stream.astype(jnp.float32), text_rows.astype(jnp.float32), *adapter_group)
        gradients = pullback(grad_out.astype(jnp.float32))
        running = tuple((earlier + fresh for earlier, fresh in zip(running, gradients[2:])))
        return (running, (result.astype(jnp.bfloat16), gradients[0], gradients[1]))
    initial = tuple((jnp.zeros(adapter_slot_table.shape, jnp.float32) for adapter_slot_table in adapter_group))
    totals, (output, input_grad, text_grad) = lax.scan(clip_step, initial, (inputs, encoder_text_states, cotangent, clip_adapter_index))
    return (output, input_grad, text_grad, totals[0], totals[1], totals[2], totals[3], totals[4], totals[5], totals[6], totals[7], totals[8], totals[9])
```

```python
import jax
import jax.numpy as jnp
from jax import lax
from jax.experimental import pallas as pl
from jax.experimental.pallas import tpu as pltpu
from jax.sharding import PartitionSpec as P

HEAD_DIM = 64


epsilon = 1e-05


def split_dot(form, wide_part, narrow_part):
    high_part = wide_part.astype(jnp.bfloat16)
    rest_part = (wide_part - high_part.astype(jnp.float32)).astype(jnp.bfloat16)
    first = jnp.einsum(form, high_part, narrow_part, preferred_element_type=jnp.float32)
    return first + jnp.einsum(form, rest_part, narrow_part, preferred_element_type=jnp.float32)


def layer_norm(stream, gain_vec):
    centred = stream - jnp.mean(stream, axis=-1, keepdims=True)
    inverse = lax.rsqrt(jnp.mean(centred * centred, axis=-1, keepdims=True) + epsilon)
    normed = centred * inverse
    return (normed * gain_vec, normed, inverse)


def norm_back(grad_out, gain_vec, normed, inverse):
    grad_norm = grad_out * gain_vec
    mean_grad = jnp.mean(grad_norm, axis=-1, keepdims=True)
    mean_cross = jnp.mean(grad_norm * normed, axis=-1, keepdims=True)
    return inverse * (grad_norm - mean_grad - normed * mean_cross)


def spread_rows(local_rows):
    return lax.all_gather(local_rows.astype(jnp.bfloat16), "tensor", axis=1, tiled=True)


def reduce_grads(partial_sum):
    return lax.psum_scatter(
        partial_sum.astype(jnp.bfloat16), "tensor", scatter_dimension=1, tiled=True
    ).astype(jnp.float32)


def project_rows(act_rows, weight, output_choice, input_choice):
    low_rank = jnp.einsum(
        "ctd,crd->ctr", act_rows, output_choice, preferred_element_type=jnp.float32
    )
    result = jnp.einsum("ctd,de->cte", act_rows, weight, preferred_element_type=jnp.float32)
    result = result + split_dot("ctr,cre->cte", low_rank, input_choice)
    return (result, low_rank)


def project_back(grad_low, act_rows, weight, output_choice, input_choice, low_rank):
    grad_rank = jnp.einsum(
        "cte,cre->ctr", grad_low, input_choice, preferred_element_type=jnp.float32
    )
    grad_rows = jnp.einsum("cte,de->ctd", grad_low, weight, preferred_element_type=jnp.float32)
    grad_rows = grad_rows + split_dot("ctr,crd->ctd", grad_rank, output_choice)
    grad_down = split_dot("ctr,ctd->crd", grad_rank, act_rows)
    grad_up = split_dot("ctr,cte->cre", low_rank, grad_low)
    return (grad_rows, grad_down, grad_up)


def causal_keep(first_row, block_rows, key_count):
    query_at = first_row + jnp.arange(block_rows, dtype=jnp.int32)[:, None]
    key_at = jnp.arange(key_count, dtype=jnp.int32)[None, :]
    return key_at <= query_at


def attention_forward(queries, key_rows, value_rows, causal):
    frames = queries.shape[1]
    key_count = key_rows.shape[1]
    block_rows = min(512, frames)
    score_scale = HEAD_DIM ** (-0.5)
    outputs = []
    log_totals = []
    for first_row in range(0, frames, block_rows):
        key_end = first_row + block_rows if causal else key_count
        query_block = queries[:, first_row : first_row + block_rows]
        scores = (
            jnp.einsum(
                "cbhe,ckhe->chbk",
                query_block,
                key_rows[:, :key_end],
                preferred_element_type=jnp.float32,
            )
            * score_scale
        )
        if causal:
            scores = jnp.where(causal_keep(first_row, block_rows, key_end), scores, -1e30)
        largest = jnp.max(scores, axis=-1, keepdims=True)
        exponent = jnp.exp(scores - largest)
        summed = jnp.sum(exponent, axis=-1, keepdims=True)
        prob_low = (exponent / summed).astype(jnp.bfloat16)
        outputs.append(
            jnp.einsum(
                "chbk,ckhe->cbhe",
                prob_low,
                value_rows[:, :key_end],
                preferred_element_type=jnp.float32,
            )
        )
        log_totals.append(largest + jnp.log(summed))
    return (jnp.concatenate(outputs, axis=1), jnp.concatenate(log_totals, axis=2))


def attention_back(queries, key_rows, value_rows, log_totals, grad_mixed, causal):
    frames = queries.shape[1]
    key_count = key_rows.shape[1]
    block_rows = min(512, frames)
    score_scale = HEAD_DIM ** (-0.5)
    grad_keys = jnp.zeros(key_rows.shape, jnp.float32)
    grad_values = jnp.zeros(value_rows.shape, jnp.float32)
    grad_queries = []
    for first_row in range(0, frames, block_rows):
        key_end = first_row + block_rows if causal else key_count
        key_part = key_rows[:, :key_end]
        value_part = value_rows[:, :key_end]
        query_block = queries[:, first_row : first_row + block_rows]
        grad_block = grad_mixed[:, first_row : first_row + block_rows]
        scores = (
            jnp.einsum("cbhe,ckhe->chbk", query_block, key_part, preferred_element_type=jnp.float32)
            * score_scale
        )
        if causal:
            scores = jnp.where(causal_keep(first_row, block_rows, key_end), scores, -1e30)
        probs = jnp.exp(scores - log_totals[:, :, first_row : first_row + block_rows])
        grad_values = grad_values.at[:, :key_end].add(
            jnp.einsum(
                "chbk,cbhe->ckhe",
                probs.astype(jnp.bfloat16),
                grad_block,
                preferred_element_type=jnp.float32,
            )
        )
        grad_probs = jnp.einsum(
            "cbhe,ckhe->chbk", grad_block, value_part, preferred_element_type=jnp.float32
        )
        inner_sum = jnp.sum(probs * grad_probs, axis=-1, keepdims=True)
        grad_scores = (probs * (grad_probs - inner_sum)).astype(jnp.bfloat16)
        grad_queries.append(
            jnp.einsum("chbk,ckhe->cbhe", grad_scores, key_part, preferred_element_type=jnp.float32)
            * score_scale
        )
        grad_keys = grad_keys.at[:, :key_end].add(
            jnp.einsum(
                "chbk,cbhe->ckhe", grad_scores, query_block, preferred_element_type=jnp.float32
            )
            * score_scale
        )
    return (jnp.concatenate(grad_queries, axis=1), grad_keys, grad_values)


def gelu_exact(pre_act):
    return jax.nn.gelu(pre_act, approximate=False)


def on_device(
    inputs,
    encoder_text_states,
    cotangent,
    clip_adapter_index,
    self_norm_gain,
    cross_norm_gain,
    feed_norm_gain,
    self_query_key_value_weight,
    self_output_weight,
    cross_query_weight,
    cross_key_value_weight,
    cross_output_weight,
    up_weight,
    down_weight,
    self_first_factors,
    self_second_factors,
    cross_first_factors,
    cross_second_factors,
    attention_first_factors,
    attention_second_factors,
    input_first_factors,
    input_second_factors,
    output_first_factors,
    output_second_factors,
):
    adapter_slot_count = input_first_factors.shape[0]
    chooser = (
        clip_adapter_index[:, :, None]
        == jnp.arange(adapter_slot_count, dtype=jnp.int32)[None, None, :]
    ).astype(jnp.bfloat16)
    local_heads = self_output_weight.shape[0] // HEAD_DIM

    def choose_adapter_slot(adapter_slot_table, column_index):
        return jnp.einsum(
            "cn,npq->cpq",
            chooser[:, column_index],
            adapter_slot_table,
            preferred_element_type=jnp.float32,
        ).astype(jnp.bfloat16)

    def slot_grads(grad_pick, column_index):
        return split_dot("cpq,cn->npq", grad_pick, chooser[:, column_index])

    def split_heads(stacked):
        return stacked.reshape(stacked.shape[0], stacked.shape[1], local_heads, HEAD_DIM)

    def join_heads(stacked):
        return stacked.reshape(stacked.shape[0], stacked.shape[1], local_heads * HEAD_DIM)

    def out_forward(mixed_in, inner_layer):
        column_index = 3 + 4 * inner_layer
        input_choice = choose_adapter_slot(attention_second_factors[inner_layer], column_index)
        weight = self_output_weight if inner_layer == 0 else cross_output_weight
        output_choice = choose_adapter_slot(attention_first_factors[inner_layer], column_index)
        partial_out, low_rank = project_rows(mixed_in, weight, output_choice, input_choice)
        branch = lax.psum_scatter(
            partial_out.astype(jnp.bfloat16), "tensor", scatter_dimension=1, tiled=True
        ).astype(jnp.float32)
        kept_data = (mixed_in, weight, output_choice, input_choice, low_rank)
        return (branch, kept_data)

    def out_back(grad_stream, kept_data):
        mixed_in, weight, output_choice, input_choice, low_rank = kept_data
        grad_low = grad_stream.astype(jnp.bfloat16)
        grad_full = lax.all_gather(grad_low, "tensor", axis=1, tiled=True)
        grad_rows, grad_down, grad_up = project_back(
            grad_full, mixed_in, weight, output_choice, input_choice, low_rank
        )
        grad_mixed = grad_rows.astype(jnp.bfloat16)
        return (grad_mixed, grad_down, grad_up)

    stream = inputs.astype(jnp.float32)
    normed_value, normed_one, inverse_one = layer_norm(stream, self_norm_gain)
    rows_one = spread_rows(normed_value)
    self_down_factor = [
        choose_adapter_slot(self_first_factors[slot_number], slot_number)
        for slot_number in range(3)
    ]
    self_up_factor = [
        choose_adapter_slot(self_second_factors[slot_number], slot_number)
        for slot_number in range(3)
    ]
    self_parts = [
        project_rows(
            rows_one,
            self_query_key_value_weight[slot_number],
            self_down_factor[slot_number],
            self_up_factor[slot_number],
        )
        for slot_number in range(3)
    ]
    self_heads = [
        split_heads(self_parts[slot_number][0].astype(jnp.bfloat16)) for slot_number in range(3)
    ]
    mixed_one, totals_one = attention_forward(self_heads[0], self_heads[1], self_heads[2], True)
    mixed_one = join_heads(mixed_one).astype(jnp.bfloat16)
    branch_one, kept_one = out_forward(mixed_one, 0)
    stream_one = stream + branch_one
    normed_value, normed_two, inverse_two = layer_norm(stream_one, cross_norm_gain)
    rows_two = spread_rows(normed_value)
    cross_down_factor = [
        choose_adapter_slot(cross_first_factors[slot_number], 4 + slot_number)
        for slot_number in range(3)
    ]
    cross_up_factor = [
        choose_adapter_slot(cross_second_factors[slot_number], 4 + slot_number)
        for slot_number in range(3)
    ]
    query_full, query_rank = project_rows(
        rows_two, cross_query_weight, cross_down_factor[0], cross_up_factor[0]
    )
    key_full, key_rank = project_rows(
        encoder_text_states, cross_key_value_weight[0], cross_down_factor[1], cross_up_factor[1]
    )
    value_full, value_rank = project_rows(
        encoder_text_states, cross_key_value_weight[1], cross_down_factor[2], cross_up_factor[2]
    )
    query_two = split_heads(query_full.astype(jnp.bfloat16))
    key_two = split_heads(key_full.astype(jnp.bfloat16))
    value_two = split_heads(value_full.astype(jnp.bfloat16))
    mixed_two, totals_two = attention_forward(query_two, key_two, value_two, False)
    mixed_two = join_heads(mixed_two).astype(jnp.bfloat16)
    branch_two, kept_two = out_forward(mixed_two, 1)
    stream_two = stream_one + branch_two
    normed_value, normed_three, inverse_three = layer_norm(stream_two, feed_norm_gain)
    rows_three = spread_rows(normed_value)
    input_second_choice = choose_adapter_slot(input_first_factors, 8)
    input_first_choice = choose_adapter_slot(input_second_factors, 8)
    before, up_rank = project_rows(rows_three, up_weight, input_second_choice, input_first_choice)
    gelu_value, gelu_pull = jax.vjp(gelu_exact, before)
    hidden = gelu_value.astype(jnp.bfloat16)
    output_second_choice = choose_adapter_slot(output_first_factors, 9)
    output_first_choice = choose_adapter_slot(output_second_factors, 9)
    partial_out, down_rank = project_rows(
        hidden, down_weight, output_second_choice, output_first_choice
    )
    branch_three = lax.psum_scatter(
        partial_out.astype(jnp.bfloat16), "tensor", scatter_dimension=1, tiled=True
    ).astype(jnp.float32)
    output = (stream_two + branch_three).astype(jnp.bfloat16)
    grad_full = lax.all_gather(cotangent, "tensor", axis=1, tiled=True)
    grad_hidden, grad_down_a, grad_down_b = project_back(
        grad_full, hidden, down_weight, output_second_choice, output_first_choice, down_rank
    )
    grad_before = gelu_pull(grad_hidden)[0].astype(jnp.bfloat16)
    grad_rows, grad_up_a, grad_up_b = project_back(
        grad_before, rows_three, up_weight, input_second_choice, input_first_choice, up_rank
    )
    grad_stream = cotangent.astype(jnp.float32) + norm_back(
        reduce_grads(grad_rows), feed_norm_gain, normed_three, inverse_three
    )
    grad_mixed, grad_out_a_two, grad_out_b_two = out_back(grad_stream, kept_two)
    grad_query, grad_key, grad_value = attention_back(
        query_two, key_two, value_two, totals_two, split_heads(grad_mixed), False
    )
    grad_query = join_heads(grad_query).astype(jnp.bfloat16)
    grad_key = join_heads(grad_key).astype(jnp.bfloat16)
    grad_value = join_heads(grad_value).astype(jnp.bfloat16)
    grad_rows_query, cross_grad_a_zero, cross_grad_b_zero = project_back(
        grad_query,
        rows_two,
        cross_query_weight,
        cross_down_factor[0],
        cross_up_factor[0],
        query_rank,
    )
    grad_text_key, cross_grad_a_one, cross_grad_b_one = project_back(
        grad_key,
        encoder_text_states,
        cross_key_value_weight[0],
        cross_down_factor[1],
        cross_up_factor[1],
        key_rank,
    )
    grad_text_value, cross_grad_a_two, cross_grad_b_two = project_back(
        grad_value,
        encoder_text_states,
        cross_key_value_weight[1],
        cross_down_factor[2],
        cross_up_factor[2],
        value_rank,
    )
    normed_grad, text_grad = (
        lax.psum_scatter(
            grad_rows_query.astype(jnp.bfloat16), "tensor", scatter_dimension=1, tiled=True
        ).astype(jnp.float32),
        lax.psum_scatter(
            (grad_text_key + grad_text_value).astype(jnp.bfloat16),
            "tensor",
            scatter_dimension=2,
            tiled=True,
        ).astype(jnp.float32),
    )
    grad_stream = grad_stream + norm_back(normed_grad, cross_norm_gain, normed_two, inverse_two)
    grad_mixed, grad_out_a_one, grad_out_b_one = out_back(grad_stream, kept_one)
    grad_query, grad_key, grad_value = attention_back(
        self_heads[0], self_heads[1], self_heads[2], totals_one, split_heads(grad_mixed), True
    )
    self_grads = [
        join_heads(grad_query).astype(jnp.bfloat16),
        join_heads(grad_key).astype(jnp.bfloat16),
        join_heads(grad_value).astype(jnp.bfloat16),
    ]
    self_rows_total = jnp.zeros(rows_one.shape, jnp.float32)
    self_grad_a = []
    self_grad_b = []
    for slot_number in range(3):
        grad_rows, grad_a_part, grad_b_part = project_back(
            self_grads[slot_number],
            rows_one,
            self_query_key_value_weight[slot_number],
            self_down_factor[slot_number],
            self_up_factor[slot_number],
            self_parts[slot_number][1],
        )
        self_rows_total = self_rows_total + grad_rows
        self_grad_a.append(slot_grads(grad_a_part, slot_number))
        self_grad_b.append(slot_grads(grad_b_part, slot_number))
    input_grad = grad_stream + norm_back(
        reduce_grads(self_rows_total), self_norm_gain, normed_one, inverse_one
    )
    sum_self_a = jnp.stack(self_grad_a)
    sum_self_b = jnp.stack(self_grad_b)
    sum_cross_a = jnp.stack(
        [
            slot_grads(cross_grad_a_zero, 4),
            slot_grads(cross_grad_a_one, 5),
            slot_grads(cross_grad_a_two, 6),
        ]
    )
    sum_cross_b = jnp.stack(
        [
            slot_grads(cross_grad_b_zero, 4),
            slot_grads(cross_grad_b_one, 5),
            slot_grads(cross_grad_b_two, 6),
        ]
    )
    sum_out_a = jnp.stack([slot_grads(grad_out_a_one, 3), slot_grads(grad_out_a_two, 7)])
    sum_out_b = jnp.stack([slot_grads(grad_out_b_one, 3), slot_grads(grad_out_b_two, 7)])
    sum_up_a = slot_grads(grad_up_a, 8)
    sum_up_b = slot_grads(grad_up_b, 8)
    sum_down_a = slot_grads(grad_down_a, 9)
    sum_down_b = slot_grads(grad_down_b, 9)
    sum_self_a, sum_cross_a, sum_out_b, sum_up_a, sum_down_b = (
        lax.psum_scatter(
            sum_self_a.astype(jnp.bfloat16), "tensor", scatter_dimension=3, tiled=True
        ).astype(jnp.float32),
        lax.psum_scatter(
            sum_cross_a.astype(jnp.bfloat16), "tensor", scatter_dimension=3, tiled=True
        ).astype(jnp.float32),
        lax.psum_scatter(
            sum_out_b.astype(jnp.bfloat16), "tensor", scatter_dimension=3, tiled=True
        ).astype(jnp.float32),
        lax.psum_scatter(
            sum_up_a.astype(jnp.bfloat16), "tensor", scatter_dimension=2, tiled=True
        ).astype(jnp.float32),
        lax.psum_scatter(
            sum_down_b.astype(jnp.bfloat16), "tensor", scatter_dimension=2, tiled=True
        ).astype(jnp.float32),
    )
    totals = (
        lax.psum(sum_self_a.astype(jnp.bfloat16), "dp").astype(jnp.float32),
        lax.psum(sum_self_b.astype(jnp.bfloat16), "dp").astype(jnp.float32),
        lax.psum(sum_cross_a.astype(jnp.bfloat16), "dp").astype(jnp.float32),
        lax.psum(sum_cross_b.astype(jnp.bfloat16), "dp").astype(jnp.float32),
        lax.psum(sum_out_a.astype(jnp.bfloat16), "dp").astype(jnp.float32),
        lax.psum(sum_out_b.astype(jnp.bfloat16), "dp").astype(jnp.float32),
        lax.psum(sum_up_a.astype(jnp.bfloat16), "dp").astype(jnp.float32),
        lax.psum(sum_up_b.astype(jnp.bfloat16), "dp").astype(jnp.float32),
        lax.psum(sum_down_a.astype(jnp.bfloat16), "dp").astype(jnp.float32),
        lax.psum(sum_down_b.astype(jnp.bfloat16), "dp").astype(jnp.float32),
    )
    return (
        output,
        input_grad,
        text_grad,
        totals[0],
        totals[1],
        totals[2],
        totals[3],
        totals[4],
        totals[5],
        totals[6],
        totals[7],
        totals[8],
        totals[9],
    )


LOW = jnp.bfloat16
WIDE = jnp.float32
VMEM_BYTES = 58 * 1024 * 1024
RANK_UNIT = 16


def mm(left, right, left_dim=1, right_dim=0):
    return lax.dot_general(
        left, right, (((left_dim,), (right_dim,)), ((), ())), preferred_element_type=WIDE
    )


def mm_nt(left, right):
    return mm(left, right, 1, 1)


def mm_tn(left, right):
    return mm(left, right, 0, 0)


def norm_rows(rows, gain):
    centred = rows - jnp.mean(rows, axis=-1, keepdims=True)
    inverse = lax.rsqrt(jnp.mean(centred * centred, axis=-1, keepdims=True) + epsilon)
    normed = centred * inverse
    return normed * gain, normed, inverse


def lane_halves():
    lane = lax.broadcasted_iota(jnp.int32, (1, 2 * HEAD_DIM), 1)
    return lane < HEAD_DIM


def half_masks():
    left = lane_halves()
    first = jnp.where(left, 1.0, 0.0)
    return first.astype(LOW), (1.0 - first).astype(LOW)


def gelu_parts(pre):
    bell = jnp.exp(-0.5 * pre * pre)
    step = 1.0 / (1.0 + (0.3275911 * 0.7071067811865476) * jnp.abs(pre))
    tail = step * (
        0.5 * 0.254829592
        + step
        * (
            0.5 * -0.284496736
            + step
            * (0.5 * 1.421413741 + step * (0.5 * -1.453152027 + step * (0.5 * 1.061405429)))
        )
    )
    tail = tail * bell
    phi = jnp.where(pre >= 0.0, 1.0 - tail, tail)
    return pre * phi, phi + pre * bell * 0.3989422804014327


def whole(shape, where=None):
    place = (0,) * len(shape) if where is None else where
    return pl.BlockSpec(shape, lambda *_: place, pipeline_mode=pl.Buffered(1))


def call(body, grid, in_specs, out_specs, out_shape, scratch, flops, moved, name, args):
    return pl.pallas_call(
        body,
        grid_spec=pltpu.PrefetchScalarGridSpec(
            num_scalar_prefetch=1,
            grid=grid,
            in_specs=in_specs,
            out_specs=out_specs,
            scratch_shapes=scratch,
        ),
        out_shape=out_shape,
        compiler_params=pltpu.CompilerParams(
            dimension_semantics=("arbitrary",) * len(grid), vmem_limit_bytes=VMEM_BYTES
        ),
        cost_estimate=pl.CostEstimate(flops=flops, bytes_accessed=moved, transcendentals=0),
        name=name,
    )(*args)


def shaped(shape, dtype):
    return jax.ShapeDtypeStruct(shape, dtype)


def first_norm_body(_, x_ref, gain_ref, out_ref):
    rows, _, _ = norm_rows(x_ref[...].astype(WIDE), gain_ref[...])
    out_ref[...] = rows.astype(LOW)


def first_norm(meta, x, gain):
    frames, width = x.shape
    block = min(256, frames)
    rows = pl.BlockSpec((block, width), lambda t, _: (t, 0))
    return call(
        first_norm_body,
        (frames // block,),
        [rows, whole((1, width))],
        rows,
        shaped(x.shape, LOW),
        [],
        10 * x.size,
        4 * x.size,
        "first_norm",
        (meta, x, gain),
    )


def project_body(_, act_ref, weight_ref, down_ref, up_ref, out_ref):
    act = act_ref[...]
    rank = mm_nt(act, down_ref[0, 0]).astype(LOW)
    out_ref[0] = (mm(act, weight_ref[0]) + mm(rank, up_ref[0, 0])).astype(LOW)


def project_heads(meta, act, weights, down, up, slots, skip, name):
    rows, width = act.shape
    count, _, local = weights.shape
    first_slot = slots
    return call(
        project_body,
        (count,),
        [
            whole((rows, width)),
            pl.BlockSpec((1, width, local), lambda j, m: (j, 0, 0)),
            pl.BlockSpec((1, 1, RANK_UNIT, width), lambda j, m: (j + skip, m[first_slot + j], 0, 0)),
            pl.BlockSpec((1, 1, RANK_UNIT, local), lambda j, m: (j + skip, m[first_slot + j], 0, 0)),
        ],
        pl.BlockSpec((1, rows, local), lambda j, m: (j, 0, 0)),
        shaped((count, rows, local), LOW),
        [],
        2 * rows * width * local * count,
        2 * (weights.size + act.size + count * rows * local),
        name,
        (meta, act, weights, down, up),
    )


def project_back_body(
    _, last, act_ref, grad_ref, weight_ref, down_ref, up_ref, out_ref, ga_ref, gb_ref, total_ref
):
    step = pl.program_id(0)
    act = act_ref[...]
    grad = grad_ref[0]
    down = down_ref[0, 0]
    rank = mm_nt(act, down).astype(LOW)
    grad_rank = mm_nt(grad, up_ref[0, 0]).astype(LOW)
    ga_ref[0] = mm_tn(grad_rank, act)
    gb_ref[0] = mm_tn(rank, grad)
    part = mm_nt(grad, weight_ref[0]) + mm(grad_rank, down)

    @pl.when(step == 0)
    def _():
        total_ref[...] = part

    @pl.when(step > 0)
    def _():
        total_ref[...] += part

    @pl.when(step == last)
    def _():
        out_ref[...] = total_ref[...].astype(out_ref.dtype)


def project_back_heads(meta, act, grads, weights, down, up, slots, skip, kind, name):
    rows, width = act.shape
    count, _, local = weights.shape
    first_slot = slots
    return call(
        lambda m, *refs: project_back_body(m, count - 1, *refs),
        (count,),
        [
            whole((rows, width)),
            pl.BlockSpec((1, rows, local), lambda j, m: (j, 0, 0)),
            pl.BlockSpec((1, width, local), lambda j, m: (j, 0, 0)),
            pl.BlockSpec((1, 1, RANK_UNIT, width), lambda j, m: (j + skip, m[first_slot + j], 0, 0)),
            pl.BlockSpec((1, 1, RANK_UNIT, local), lambda j, m: (j + skip, m[first_slot + j], 0, 0)),
        ],
        (
            whole((rows, width)),
            pl.BlockSpec((1, RANK_UNIT, width), lambda j, m: (j, 0, 0)),
            pl.BlockSpec((1, RANK_UNIT, local), lambda j, m: (j, 0, 0)),
        ),
        (
            shaped((rows, width), kind),
            shaped((count, RANK_UNIT, width), WIDE),
            shaped((count, RANK_UNIT, local), WIDE),
        ),
        [pltpu.VMEM((rows, width), WIDE)],
        2 * rows * width * local * count,
        2 * (weights.size + act.size + count * rows * local) + 4 * rows * width,
        name,
        (meta, act, grads, weights, down, up),
    )


ROW_BLOCK = 256


def order_frames(is_first, own, other, low_part, high_part):
    @pl.when(is_first)
    def _():
        low_part[...] = own[...]
        high_part[...] = other[...]

    @pl.when(jnp.logical_not(is_first))
    def _():
        low_part[...] = other[...]
        high_part[...] = own[...]


def self_forward_body(meta, own_ref, other_ref, out_own_ref, out_other_ref, held, result):
    half = own_ref.shape[1]
    is_first = meta[10] == 0
    order_frames(is_first, own_ref, other_ref, held.at[:, :half], held.at[:, half:])
    left = lane_halves()
    masks = half_masks()
    scale = HEAD_DIM**-0.5
    query_at = lax.broadcasted_iota(jnp.int32, (ROW_BLOCK, ROW_BLOCK), 0)
    key_at = lax.broadcasted_iota(jnp.int32, (ROW_BLOCK, ROW_BLOCK), 1)
    keep = key_at <= query_at
    for first in range(0, 2 * half, ROW_BLOCK):
        end = first + ROW_BLOCK
        query = held[0, first:end] * jnp.asarray(scale, LOW)
        keys = held[1, :end]
        values = held[2, :end]
        parts = []
        for which in (0, 1):
            one_query = query * masks[which]
            near = jnp.where(keep, mm_nt(one_query, keys[first:]), -1e30)
            largest = jnp.max(near, axis=-1, keepdims=True)
            spread = values * masks[which] + masks[1 - which]
            if first > 0:
                far = mm_nt(one_query, keys[:first])
                largest = jnp.maximum(largest, jnp.max(far, axis=-1, keepdims=True))
                mixed = mm(jnp.exp(far - largest).astype(LOW), spread[:first])
                mixed = mixed + mm(jnp.exp(near - largest).astype(LOW), spread[first:])
            else:
                mixed = mm(jnp.exp(near - largest).astype(LOW), spread)
            parts.append(mixed)
        mixed = jnp.where(left, parts[0], parts[1])
        summed = pltpu.roll(jnp.where(left, parts[1], parts[0]), HEAD_DIM, 1)
        result[first:end] = (mixed / summed).astype(LOW)

    @pl.when(is_first)
    def _():
        out_own_ref[...] = result[:half]
        out_other_ref[...] = result[half:]

    @pl.when(jnp.logical_not(is_first))
    def _():
        out_own_ref[...] = result[half:]
        out_other_ref[...] = result[:half]


def self_forward(meta, own, other):
    _, half, local = own.shape
    pair = 2 * HEAD_DIM
    three = pl.BlockSpec((3, half, pair), lambda p, m: (0, 0, p))
    one = pl.BlockSpec((half, pair), lambda p, m: (0, p))
    return call(
        self_forward_body,
        (local // pair,),
        [three, three],
        (one, one),
        (shaped((half, local), LOW), shaped((half, local), LOW)),
        [pltpu.VMEM((3, 2 * half, pair), LOW), pltpu.VMEM((2 * half, pair), LOW)],
        20 * half * half * local,
        16 * half * local,
        "self_forward",
        (meta, own, other),
    )


def self_back_body(
    meta,
    own_ref,
    other_ref,
    grad_own_ref,
    grad_other_ref,
    out_own_ref,
    out_other_ref,
    held,
    grads,
    key_total,
    value_total,
    result,
):
    half = own_ref.shape[1]
    is_first = meta[10] == 0
    order_frames(is_first, own_ref, other_ref, held.at[:, :half], held.at[:, half:])
    order_frames(is_first, grad_own_ref, grad_other_ref, grads.at[:half], grads.at[half:])
    masks = half_masks()
    scale = HEAD_DIM**-0.5
    query_at = lax.broadcasted_iota(jnp.int32, (ROW_BLOCK, ROW_BLOCK), 1)
    key_at = lax.broadcasted_iota(jnp.int32, (ROW_BLOCK, ROW_BLOCK), 0)
    keep = key_at <= query_at
    key_total[...] = jnp.zeros_like(key_total)
    value_total[...] = jnp.zeros_like(value_total)
    for first in range(0, 2 * half, ROW_BLOCK):
        end = first + ROW_BLOCK
        query = held[0, first:end] * jnp.asarray(scale, LOW)
        grad = grads[first:end]
        spans = [(first, end)] + ([(0, first)] if first > 0 else [])
        query_grad = None
        for which in (0, 1):
            mask = masks[which]
            one_query = query * mask
            one_grad = grad * mask
            scores = []
            for low_key, high_key in spans:
                score = mm_nt(held[1, low_key:high_key], one_query)
                if low_key == first:
                    score = jnp.where(keep, score, -1e30)
                scores.append(score)
            largest = jnp.max(scores[0], axis=0, keepdims=True)
            for score in scores[1:]:
                largest = jnp.maximum(largest, jnp.max(score, axis=0, keepdims=True))
            probs = [jnp.exp(score - largest) for score in scores]
            summed = jnp.sum(probs[0], axis=0, keepdims=True)
            for prob in probs[1:]:
                summed = summed + jnp.sum(prob, axis=0, keepdims=True)
            inverse = 1.0 / summed
            probs = [prob * inverse for prob in probs]
            prob_grads = [
                mm_nt(held[2, low_key:high_key], one_grad) for low_key, high_key in spans
            ]
            inner = jnp.sum(probs[0] * prob_grads[0], axis=0, keepdims=True)
            for prob, prob_grad in zip(probs[1:], prob_grads[1:]):
                inner = inner + jnp.sum(prob * prob_grad, axis=0, keepdims=True)
            for (low_key, high_key), prob, prob_grad in zip(spans, probs, prob_grads):
                score_grad = (prob * (prob_grad - inner)).astype(LOW)
                value_total[low_key:high_key] += mm(prob.astype(LOW), one_grad)
                key_total[low_key:high_key] += mm(score_grad, one_query)
                part = mm_tn(score_grad, held[1, low_key:high_key] * mask)
                query_grad = part if query_grad is None else query_grad + part
        result[0, first:end] = (query_grad * scale).astype(LOW)
    result[1] = key_total[...].astype(LOW)
    result[2] = value_total[...].astype(LOW)

    @pl.when(is_first)
    def _():
        out_own_ref[...] = result[:, :half]
        out_other_ref[...] = result[:, half:]

    @pl.when(jnp.logical_not(is_first))
    def _():
        out_own_ref[...] = result[:, half:]
        out_other_ref[...] = result[:, :half]


def self_back(meta, own, other, grad_own, grad_other):
    _, half, local = own.shape
    pair = 2 * HEAD_DIM
    three = pl.BlockSpec((3, half, pair), lambda p, m: (0, 0, p))
    one = pl.BlockSpec((half, pair), lambda p, m: (0, p))
    return call(
        self_back_body,
        (local // pair,),
        [three, three, one, one],
        (three, three),
        (shaped(own.shape, LOW), shaped(own.shape, LOW)),
        [
            pltpu.VMEM((3, 2 * half, pair), LOW),
            pltpu.VMEM((2 * half, pair), LOW),
            pltpu.VMEM((2 * half, pair), WIDE),
            pltpu.VMEM((2 * half, pair), WIDE),
            pltpu.VMEM((3, 2 * half, pair), LOW),
        ],
        50 * half * half * local,
        30 * half * local,
        "self_back",
        (meta, own, other, grad_own, grad_other),
    )


def halves_of(ref, local):
    step = ref.shape[2] // 2
    return (
        ref[:, 0, :step, :].reshape(local, ref.shape[3]),
        ref[:, 0, step:, :].reshape(local, ref.shape[3]),
    )


def full_of(ref):
    return ref[:, 0].reshape(ref.shape[0] * ref.shape[2], ref.shape[3])


def pair_tiles(keys, values, pair, masks):
    span = slice(2 * HEAD_DIM * pair, 2 * HEAD_DIM * (pair + 1))
    key_part = keys[:, span]
    value_part = values[:, span]
    key_tile = jnp.concatenate([key_part * masks[0], key_part * masks[1]], axis=0)
    value_tile = jnp.concatenate([value_part * masks[0], value_part * masks[1]], axis=0)
    return key_tile, value_tile


def both_halves(left, values, reduce, empty):
    first = reduce(jnp.where(left, values, empty), axis=-1, keepdims=True)
    second = reduce(jnp.where(left, empty, values), axis=-1, keepdims=True)
    return jnp.where(left, first, second)


def text_weights(left, query, key_tile):
    scores = mm_nt(query, key_tile)
    return jnp.exp(scores - both_halves(left, scores, jnp.max, -1e30))


def mix_text(query, keys, values, left, masks):
    mixed = []
    ones = jnp.concatenate(
        [jnp.broadcast_to(masks[0], (HEAD_DIM, 2 * HEAD_DIM)), jnp.broadcast_to(masks[1], (HEAD_DIM, 2 * HEAD_DIM))],
        axis=0,
    )
    for pair in range(query.shape[1] // (2 * HEAD_DIM)):
        key_tile, value_tile = pair_tiles(keys, values, pair, masks)
        one_query = query[:, 2 * HEAD_DIM * pair : 2 * HEAD_DIM * (pair + 1)]
        weights = text_weights(left, one_query * jnp.asarray(HEAD_DIM**-0.5, LOW), key_tile)
        weights = weights.astype(LOW)
        mixed.append((mm(weights, value_tile) / mm(weights, ones)).astype(LOW))
    return jnp.concatenate(mixed, axis=1)


def middle_forward_body(
    _,
    x_ref,
    z_own_ref,
    z_other_ref,
    out_own_ref,
    out_other_ref,
    query_own_ref,
    query_other_ref,
    cross_own_ref,
    cross_other_ref,
    down3_ref,
    down3_other_ref,
    up3_ref,
    down4_ref,
    up4_ref,
    up4_other_ref,
    down7_ref,
    down7_other_ref,
    up7_ref,
    text_own_ref,
    text_other_ref,
    gain_two_ref,
    gain_three_ref,
    stream_one_ref,
    stream_two_ref,
    rows_three_ref,
    query_out_own_ref,
    query_out_other_ref,
    z2_own_ref,
    z2_other_ref,
):
    local = z_own_ref.shape[1]
    left = lane_halves()
    masks = half_masks()

    def out_product(own, other, weight_own, weight_other_ref, down, down_other, up):
        rank = (mm_nt(own, down) + mm_nt(other, down_other)).astype(LOW)
        first, second = halves_of(weight_other_ref, local)
        product = mm(own, weight_own[...]) + mm(rank, up)
        return product + jnp.concatenate([mm(other, first), mm(other, second)], axis=1)

    stream = x_ref[...].astype(WIDE) + out_product(
        z_own_ref[...],
        z_other_ref[...],
        out_own_ref,
        out_other_ref,
        down3_ref[0, 0],
        down3_other_ref[...],
        up3_ref[0, 0],
    )
    stream_one_ref[...] = stream
    rows_two = norm_rows(stream, gain_two_ref[...])[0].astype(LOW)
    rank = mm_nt(rows_two, down4_ref[0, 0]).astype(LOW)
    query_own = (mm(rows_two, query_own_ref[...]) + mm(rank, up4_ref[0, 0])).astype(LOW)
    query_other = (
        mm(rows_two, full_of(query_other_ref)) + mm(rank, up4_other_ref[...])
    ).astype(LOW)
    query_out_own_ref[...] = query_own
    query_out_other_ref[...] = query_other
    z2_own = mix_text(query_own, text_own_ref[0], text_own_ref[1], left, masks)
    z2_other = mix_text(query_other, text_other_ref[0], text_other_ref[1], left, masks)
    z2_own_ref[...] = z2_own
    z2_other_ref[...] = z2_other
    stream = stream + out_product(
        z2_own,
        z2_other,
        cross_own_ref,
        cross_other_ref,
        down7_ref[0, 0],
        down7_other_ref[...],
        up7_ref[0, 0],
    )
    stream_two_ref[...] = stream
    rows_three_ref[...] = norm_rows(stream, gain_three_ref[...])[0].astype(LOW)


def chosen(table, entry, slot):
    shape = (1, 1) + table.shape[2:]
    return pl.BlockSpec(
        shape, lambda t, m: (entry, m[slot], 0, 0), pipeline_mode=pl.Buffered(1)
    )


def middle_specs(weights, gathered, tables, packed):
    out_weight, query_weight, cross_weight = weights
    attention_down, attention_up, cross_down, cross_up = tables
    shards, _, depth, local = gathered.shape
    one = (shards, 1, depth, local)
    rank = (RANK_UNIT, local)
    specs = [
        whole(out_weight.shape),
        whole(one, (0, 0, 0, 0)),
        whole(query_weight.shape),
        whole(one, (0, 1, 0, 0)),
        whole(cross_weight.shape),
        whole(one, (0, 2, 0, 0)),
        chosen(attention_down, 0, 3),
        whole(rank, (0, 0)),
        chosen(attention_up, 0, 3),
        chosen(cross_down, 0, 4),
        chosen(cross_up, 0, 4),
        whole(rank, (0, 2)),
        chosen(attention_down, 1, 7),
        whole(rank, (0, 1)),
        chosen(attention_up, 1, 7),
    ]
    args = (
        out_weight,
        gathered,
        query_weight,
        gathered,
        cross_weight,
        gathered,
        attention_down,
        packed,
        attention_up,
        cross_down,
        cross_up,
        packed,
        attention_down,
        packed,
        attention_up,
    )
    return specs, args


def middle_forward(meta, x, z_own, z_other, weights, gathered, tables, packed, text_own, text_other, gains):
    frames, width = x.shape
    local = z_own.shape[1]
    block = min(256, frames)
    wide = pl.BlockSpec((block, width), lambda t, m: (t, 0))
    narrow = pl.BlockSpec((block, local), lambda t, m: (t, 0))
    specs, args = middle_specs(weights, gathered, tables, packed)
    return call(
        middle_forward_body,
        (frames // block,),
        [wide, narrow, narrow]
        + specs
        + [whole(text_own.shape), whole(text_other.shape), whole((1, width)), whole((1, width))],
        (wide, wide, wide, narrow, narrow, narrow, narrow),
        (
            shaped((frames, width), WIDE),
            shaped((frames, width), WIDE),
            shaped((frames, width), LOW),
            shaped((frames, local), LOW),
            shaped((frames, local), LOW),
            shaped((frames, local), LOW),
            shaped((frames, local), LOW),
        ),
        [],
        6 * frames * width * width,
        6 * width * width + 20 * frames * width,
        "middle_forward",
        (meta, x, z_own, z_other) + args + (text_own, text_other) + gains,
    )


def middle_back_body(
    _,
    last,
    grad_ref,
    stream_one_ref,
    z_own_ref,
    z_other_ref,
    query_in_own_ref,
    query_in_other_ref,
    z2_own_ref,
    z2_other_ref,
    out_own_ref,
    out_other_ref,
    query_own_ref,
    query_other_ref,
    cross_own_ref,
    cross_other_ref,
    down3_ref,
    down3_other_ref,
    up3_ref,
    down4_ref,
    up4_ref,
    up4_other_ref,
    down7_ref,
    down7_other_ref,
    up7_ref,
    text_own_ref,
    text_other_ref,
    gain_two_ref,
    grad_one_ref,
    dz_own_ref,
    dz_other_ref,
    text_grad_own_ref,
    text_grad_other_ref,
    ga3_ref,
    gb3_ref,
    ga4_ref,
    gb4_ref,
    ga7_ref,
    gb7_ref,
    key_total,
    value_total,
):
    step = pl.program_id(0)
    local = z_own_ref.shape[1]
    pairs = local // (2 * HEAD_DIM)
    left = lane_halves()
    masks = half_masks()
    scale = jnp.asarray(HEAD_DIM**-0.5, LOW)

    @pl.when(step == 0)
    def _():
        key_total[...] = jnp.zeros_like(key_total)
        value_total[...] = jnp.zeros_like(value_total)
        for ref in (ga3_ref, gb3_ref, ga4_ref, gb4_ref, ga7_ref, gb7_ref):
            ref[...] = jnp.zeros_like(ref)

    def out_back(grad, own, other, weight_own, weight_other_ref, down, down_other, up, ga_ref, gb_ref):
        rank = (mm_nt(own, down) + mm_nt(other, down_other)).astype(LOW)
        grad_rank = mm_nt(grad, up).astype(LOW)
        ga_ref[:, :local] += mm_tn(grad_rank, own)
        ga_ref[:, local:] += mm_tn(grad_rank, other)
        gb_ref[...] += mm_tn(rank, grad)
        first, second = halves_of(weight_other_ref, local)
        middle = grad.shape[1] // 2
        grad_own = mm_nt(grad, weight_own[...]) + mm(grad_rank, down)
        grad_other = (
            mm_nt(grad[:, :middle], first)
            + mm_nt(grad[:, middle:], second)
            + mm(grad_rank, down_other)
        )
        return grad_own.astype(LOW), grad_other.astype(LOW)

    grad = grad_ref[...]
    dz2_own, dz2_other = out_back(
        grad.astype(LOW),
        z2_own_ref[...],
        z2_other_ref[...],
        cross_own_ref,
        cross_other_ref,
        down7_ref[0, 0],
        down7_other_ref[...],
        up7_ref[0, 0],
        ga7_ref,
        gb7_ref,
    )

    ones = jnp.concatenate(
        [jnp.broadcast_to(masks[0], (HEAD_DIM, 2 * HEAD_DIM)), jnp.broadcast_to(masks[1], (HEAD_DIM, 2 * HEAD_DIM))],
        axis=0,
    )

    def text_back(query, dz2, keys, values, part):
        query_grads = []
        for pair in range(pairs):
            span = slice(2 * HEAD_DIM * pair, 2 * HEAD_DIM * (pair + 1))
            key_tile, value_tile = pair_tiles(keys, values, pair, masks)
            one_query = query[:, span] * scale
            one_grad = dz2[:, span]
            weights = text_weights(left, one_query, key_tile)
            probs = weights / mm(weights.astype(LOW), ones)
            prob_grads = mm_nt(one_grad, value_tile)
            inner = both_halves(left, probs * prob_grads, jnp.sum, 0.0)
            score_grads = (probs * (prob_grads - inner)).astype(LOW)
            query_grads.append(
                (mm(score_grads, key_tile) * HEAD_DIM**-0.5).astype(LOW)
            )
            key_total[part, pair] += mm_tn(score_grads, one_query)
            value_total[part, pair] += mm_tn(probs.astype(LOW), one_grad)
        return jnp.concatenate(query_grads, axis=1)

    dq_own = text_back(query_in_own_ref[...], dz2_own, text_own_ref[0], text_own_ref[1], 0)
    dq_other = text_back(query_in_other_ref[...], dz2_other, text_other_ref[0], text_other_ref[1], 1)

    rows_two, normed, inverse = norm_rows(stream_one_ref[...], gain_two_ref[...])
    rows_two = rows_two.astype(LOW)
    rank = mm_nt(rows_two, down4_ref[0, 0]).astype(LOW)
    grad_rank = (mm_nt(dq_own, up4_ref[0, 0]) + mm_nt(dq_other, up4_other_ref[...])).astype(LOW)
    ga4_ref[...] += mm_tn(grad_rank, rows_two)
    gb4_ref[:, :local] += mm_tn(rank, dq_own)
    gb4_ref[:, local:] += mm_tn(rank, dq_other)
    grad_rows = (
        mm_nt(dq_own, query_own_ref[...])
        + mm_nt(dq_other, full_of(query_other_ref))
        + mm(grad_rank, down4_ref[0, 0])
    )
    grad = grad + norm_back(grad_rows, gain_two_ref[...], normed, inverse)
    grad_one_ref[...] = grad
    dz_own, dz_other = out_back(
        grad.astype(LOW),
        z_own_ref[...],
        z_other_ref[...],
        out_own_ref,
        out_other_ref,
        down3_ref[0, 0],
        down3_other_ref[...],
        up3_ref[0, 0],
        ga3_ref,
        gb3_ref,
    )
    dz_own_ref[...] = dz_own
    dz_other_ref[...] = dz_other

    @pl.when(step == last)
    def _():
        for total, slot in ((key_total, 0), (value_total, 1)):
            for part, ref in ((0, text_grad_own_ref), (1, text_grad_other_ref)):
                for pair in range(pairs):
                    span = slice(2 * HEAD_DIM * pair, 2 * HEAD_DIM * (pair + 1))
                    tile = total[part, pair]
                    ref[slot, :, span] = jnp.where(left, tile[:HEAD_DIM], tile[HEAD_DIM:])


def middle_back(
    meta, grad, stream_one, z_own, z_other, q_own, q_other, z2_own, z2_other,
    weights, gathered, tables, packed, text_own, text_other, gain,
):
    frames, width = grad.shape
    local = z_own.shape[1]
    pairs = local // (2 * HEAD_DIM)
    block = min(256, frames)
    wide = pl.BlockSpec((block, width), lambda t, m: (t, 0))
    narrow = pl.BlockSpec((block, local), lambda t, m: (t, 0))
    specs, args = middle_specs(weights, gathered, tables, packed)
    rank = (RANK_UNIT, width)
    steps = frames // block
    return call(
        lambda m, *refs: middle_back_body(m, steps - 1, *refs),
        (steps,),
        [wide, wide] + [narrow] * 6 + specs + [whole(text_own.shape), whole(text_other.shape), whole((1, width))],
        (wide, narrow, narrow, whole(text_own.shape), whole(text_own.shape)) + (whole(rank),) * 6,
        (
            shaped((frames, width), WIDE),
            shaped((frames, local), LOW),
            shaped((frames, local), LOW),
            shaped(text_own.shape, WIDE),
            shaped(text_own.shape, WIDE),
        )
        + (shaped(rank, WIDE),) * 6,
        [
            pltpu.VMEM((2, pairs, 2 * HEAD_DIM, 2 * HEAD_DIM), WIDE),
            pltpu.VMEM((2, pairs, 2 * HEAD_DIM, 2 * HEAD_DIM), WIDE),
        ],
        6 * frames * width * width,
        6 * width * width + 24 * frames * width,
        "middle_back",
        (meta, grad, stream_one, z_own, z_other, q_own, q_other, z2_own, z2_other)
        + args
        + (text_own, text_other, gain),
    )


def feed_tile(
    rows_ref, cot_ref, up_weight, down_weight, up_rank, down_rank,
    ga9_ref, gb8_ref, branch, grad_rows, rank9, grad_rank8, rank8, grad_rank9,
):
    frames = rows_ref.shape[0]
    block = min(256, frames)
    ga9 = None
    gb8 = None
    for first in range(0, frames, block):
        span = slice(first, first + block)
        rows = rows_ref[span]
        cot = cot_ref[span]
        pre = mm(rows, up_weight) + mm(rank8[span], up_rank)
        grad_hidden = mm_nt(cot, down_weight) + mm(grad_rank9[span], down_rank)
        hidden, slope = gelu_parts(pre)
        hidden = hidden.astype(LOW)
        grad_pre = (grad_hidden * slope).astype(LOW)
        branch[span] += mm(hidden, down_weight)
        rank9[span] += mm_nt(hidden, down_rank)
        grad_rows[span] += mm_nt(grad_pre, up_weight)
        grad_rank8[span] += mm_nt(grad_pre, up_rank)
        one = mm_tn(grad_rank9[span], hidden)
        two = mm_tn(rank8[span], grad_pre)
        ga9 = one if ga9 is None else ga9 + one
        gb8 = two if gb8 is None else gb8 + two
    ga9_ref[...] = ga9
    gb8_ref[...] = gb8


def feed_own_body(
    _, rows_ref, cot_ref, up_weight_ref, down_weight_ref, up_rank_ref, down_rank_ref,
    down8_ref, up9_ref,
    branch_ref, grad_rows_ref, rank9_ref, grad_rank8_ref, ga9_ref, gb8_ref,
    rank8, grad_rank9,
):
    @pl.when(pl.program_id(0) == 0)
    def _():
        rank8[...] = mm_nt(rows_ref[...], down8_ref[0]).astype(LOW)
        grad_rank9[...] = mm_nt(cot_ref[...], up9_ref[0]).astype(LOW)
        for ref in (branch_ref, grad_rows_ref, rank9_ref, grad_rank8_ref):
            ref[...] = jnp.zeros_like(ref)

    feed_tile(
        rows_ref, cot_ref, up_weight_ref[...], down_weight_ref[...], up_rank_ref[0], down_rank_ref[0],
        ga9_ref, gb8_ref, branch_ref, grad_rows_ref, rank9_ref, grad_rank8_ref, rank8, grad_rank9,
    )


def table_tile(tile, slot):
    return pl.BlockSpec((1, RANK_UNIT, tile), lambda t, m: (m[slot], 0, t))


def feed_own(meta, rows, cot, up_weight, down_weight, input_down, input_up, output_down, output_up, tile):
    frames, width = rows.shape
    hidden = up_weight.shape[1]
    grads = pl.BlockSpec((RANK_UNIT, tile), lambda t, m: (0, t))
    picked = pl.BlockSpec((1, RANK_UNIT, width), lambda t, m: (m[8], 0, 0))
    picked_out = pl.BlockSpec((1, RANK_UNIT, width), lambda t, m: (m[9], 0, 0))
    rank = (frames, RANK_UNIT)
    return call(
        feed_own_body,
        (hidden // tile,),
        [
            whole((frames, width)),
            whole((frames, width)),
            pl.BlockSpec((width, tile), lambda t, m: (0, t)),
            pl.BlockSpec((tile, width), lambda t, m: (t, 0)),
            table_tile(tile, 8),
            table_tile(tile, 9),
            picked,
            picked_out,
        ],
        (whole((frames, width)), whole((frames, width)), whole(rank), whole(rank), grads, grads),
        (
            shaped((frames, width), WIDE),
            shaped((frames, width), WIDE),
            shaped(rank, WIDE),
            shaped(rank, WIDE),
            shaped((RANK_UNIT, hidden), WIDE),
            shaped((RANK_UNIT, hidden), WIDE),
        ),
        [pltpu.VMEM(rank, LOW), pltpu.VMEM(rank, LOW)],
        8 * frames * width * hidden,
        4 * width * hidden + 12 * frames * width,
        "feed_own",
        (meta, rows, cot, up_weight, down_weight, input_up, output_down, input_down, output_up),
    )


def feed_other_body(
    _, last, rows_ref, cot_ref, up_weight_ref, down_weight_ref, up_rank_ref, down_rank_ref,
    down8_ref, up9_ref, branch_in_ref, grad_rows_in_ref, rank9_in_ref, grad_rank8_in_ref,
    stream_ref, gain_ref,
    out_ref, grad_ref, ga9_ref, gb8_ref, ga8_ref, gb9_ref,
    branch, grad_rows, rank9, grad_rank8, rank8, grad_rank9,
):
    step = pl.program_id(0)

    @pl.when(step == 0)
    def _():
        rank8[...] = mm_nt(rows_ref[...], down8_ref[0]).astype(LOW)
        grad_rank9[...] = mm_nt(cot_ref[...], up9_ref[0]).astype(LOW)
        branch[...] = branch_in_ref[...]
        grad_rows[...] = grad_rows_in_ref[...]
        rank9[...] = rank9_in_ref[...]
        grad_rank8[...] = grad_rank8_in_ref[...]

    shards, _, depth, tile = up_weight_ref.shape
    up_weight = up_weight_ref[...].reshape(shards * depth, tile)
    down_weight = down_weight_ref[...].reshape(tile, down_weight_ref.shape[3])
    feed_tile(
        rows_ref, cot_ref, up_weight, down_weight, up_rank_ref[...], down_rank_ref[...],
        ga9_ref, gb8_ref, branch, grad_rows, rank9, grad_rank8, rank8, grad_rank9,
    )

    @pl.when(step == last)
    def _():
        frames = rows_ref.shape[0]
        block = min(128, frames)
        last8 = grad_rank8[...].astype(LOW)
        last9 = rank9[...].astype(LOW)
        ga8_ref[...] = mm_tn(last8, rows_ref[...])
        gb9_ref[...] = mm_tn(last9, cot_ref[...])
        for first in range(0, frames, block):
            span = slice(first, first + block)
            stream = stream_ref[span]
            out = stream + branch[span] + mm(last9[span], up9_ref[0])
            out_ref[span] = out.astype(LOW)
            _, normed, inverse = norm_rows(stream, gain_ref[...])
            grad = grad_rows[span] + mm(last8[span], down8_ref[0])
            grad_ref[span] = cot_ref[span].astype(WIDE) + norm_back(
                grad, gain_ref[...], normed, inverse
            )


def feed_other(
    meta, rows, cot, gathered, packed, first_pack, input_down, output_up, carried, stream, gain, tile
):
    frames, width = rows.shape
    shards, quarters, depth, _ = gathered.shape
    hidden = quarters // 2 * width
    per_half = width // tile
    own_shards = tile // (quarters // 2 * depth)
    down_first = quarters // 2
    grads = pl.BlockSpec((RANK_UNIT, tile), lambda t, m: (0, t))
    picked = pl.BlockSpec((1, RANK_UNIT, width), lambda t, m: (m[8], 0, 0))
    picked_out = pl.BlockSpec((1, RANK_UNIT, width), lambda t, m: (m[9], 0, 0))
    rank = (frames, RANK_UNIT)
    steps = hidden // tile
    full = whole((frames, width))
    return call(
        lambda m, *refs: feed_other_body(m, steps - 1, *refs),
        (steps,),
        [
            full,
            full,
            pl.BlockSpec(
                (shards, 1, depth, tile),
                lambda t, m: (0, down_first + t // per_half, 0, t % per_half),
            ),
            pl.BlockSpec((own_shards, down_first, depth, width), lambda t, m: (t, 0, 0, 0)),
            pl.BlockSpec((RANK_UNIT, tile), lambda t, m: (0, first_pack // tile + t)),
            pl.BlockSpec((RANK_UNIT, tile), lambda t, m: (0, (first_pack + hidden) // tile + t)),
            picked,
            picked_out,
            full,
            full,
            whole(rank),
            whole(rank),
            full,
            whole((1, width)),
        ],
        (full, full, grads, grads, whole((RANK_UNIT, width)), whole((RANK_UNIT, width))),
        (
            shaped((frames, width), LOW),
            shaped((frames, width), WIDE),
            shaped((RANK_UNIT, hidden), WIDE),
            shaped((RANK_UNIT, hidden), WIDE),
            shaped((RANK_UNIT, width), WIDE),
            shaped((RANK_UNIT, width), WIDE),
        ),
        [
            pltpu.VMEM((frames, width), WIDE),
            pltpu.VMEM((frames, width), WIDE),
            pltpu.VMEM(rank, WIDE),
            pltpu.VMEM(rank, WIDE),
            pltpu.VMEM(rank, LOW),
            pltpu.VMEM(rank, LOW),
        ],
        8 * frames * width * hidden,
        4 * width * hidden + 24 * frames * width,
        "feed_other",
        (meta, rows, cot, gathered, gathered, packed, packed, input_down, output_up)
        + tuple(carried)
        + (stream, gain),
    )


def last_norm_body(_, x_ref, own_ref, other_ref, grad_ref, gain_ref, out_ref):
    _, normed, inverse = norm_rows(x_ref[...].astype(WIDE), gain_ref[...])
    total = own_ref[...] + other_ref[...].astype(WIDE)
    out_ref[...] = grad_ref[...] + norm_back(total, gain_ref[...], normed, inverse)


def last_norm(meta, x, own, other, grad, gain):
    frames, width = x.shape
    block = min(256, frames)
    rows = pl.BlockSpec((block, width), lambda t, _: (t, 0))
    return call(
        last_norm_body,
        (frames // block,),
        [rows, rows, rows, rows, whole((1, width))],
        rows,
        shaped(x.shape, WIDE),
        [],
        20 * x.size,
        16 * x.size,
        "last_norm",
        (meta, x, own, other, grad, gain),
    )


def on_pair(
    inputs,
    encoder_text_states,
    cotangent,
    clip_adapter_index,
    self_norm_gain,
    cross_norm_gain,
    feed_norm_gain,
    self_query_key_value_weight,
    self_output_weight,
    cross_query_weight,
    cross_key_value_weight,
    cross_output_weight,
    up_weight,
    down_weight,
    self_first_factors,
    self_second_factors,
    cross_first_factors,
    cross_second_factors,
    attention_first_factors,
    attention_second_factors,
    input_first_factors,
    input_second_factors,
    output_first_factors,
    output_second_factors,
):
    x = inputs[0]
    text = encoder_text_states[0]
    cot = cotangent[0]
    width = x.shape[1]
    local = self_output_weight.shape[0]
    hidden = up_weight.shape[1]
    slots = input_first_factors.shape[0]
    group_count = lax.axis_size("dp")
    place = lax.axis_index("dp")
    side = lax.axis_index("tensor")
    picks = clip_adapter_index[0]
    meta = jnp.concatenate([picks, side[None].astype(jnp.int32)])
    gain_one, gain_two, gain_three = (
        vec.reshape(1, width) for vec in (self_norm_gain, cross_norm_gain, feed_norm_gain)
    )

    def swap(array):
        return lax.ppermute(array, "tensor", [(0, 1), (1, 0)])

    depth = width // group_count
    step = local // group_count

    def share(weight, size):
        return lax.dynamic_slice_in_dim(weight, place * size, size, axis=0)

    def side_by_side(rows, count):
        return rows.reshape(rows.shape[0], count, -1).transpose(1, 0, 2)

    out_share = side_by_side(share(self_output_weight, step), 2).reshape(depth, local)
    query_share = share(cross_query_weight, depth)
    cross_share = side_by_side(share(cross_output_weight, step), 2).reshape(depth, local)
    share_one = swap(jnp.stack([out_share, query_share, cross_share]))
    gathered_one = lax.all_gather(share_one, "dp", axis=0)

    rows_one = first_norm(meta, x, gain_one)
    rows_one_other = swap(rows_one)

    def pick(table, slot):
        return lax.dynamic_index_in_dim(table, picks[slot], axis=0, keepdims=False)

    packed = swap(
        jnp.concatenate(
            [
                pick(attention_first_factors[0], 3),
                pick(attention_first_factors[1], 7),
                pick(cross_second_factors[0], 4),
                jnp.zeros((RANK_UNIT, local), LOW),
                pick(input_second_factors, 8),
                pick(output_first_factors, 9),
            ],
            axis=1,
        )
    )
    first_pack = 4 * local

    parts = hidden // width
    down_share = share(down_weight, parts * depth).reshape(parts, depth, width)
    up_share = side_by_side(share(up_weight, depth), parts)
    share_two = swap(jnp.concatenate([down_share, up_share], axis=0))
    gathered_two = lax.all_gather(share_two, "dp", axis=0)

    text_own = project_heads(
        meta, text, cross_key_value_weight, cross_first_factors, cross_second_factors, 5, 1, "text_heads"
    )
    text_other = swap(text_own)
    heads_own = project_heads(
        meta, rows_one, self_query_key_value_weight, self_first_factors, self_second_factors, 0, 0, "own_heads"
    )
    heads_other = project_heads(
        meta, rows_one_other, self_query_key_value_weight, self_first_factors, self_second_factors, 0, 0, "other_heads"
    )
    z_own_frames, z_other_frames = self_forward(meta, heads_own, heads_other)
    z_other_heads = swap(z_other_frames)
    weights = (self_output_weight, cross_query_weight, cross_output_weight)
    tables = (attention_first_factors, attention_second_factors, cross_first_factors, cross_second_factors)
    stream_one, stream_two, rows_three, q_own, q_other, z2_own, z2_other = middle_forward(
        meta, x, z_own_frames, z_other_heads, weights, gathered_one, tables, packed,
        text_own, text_other, (gain_two, gain_three),
    )
    tile = local
    branch, grad_rows, rank9, grad_rank8, ga9_own, gb8_own = feed_own(
        meta, rows_three, cot, up_weight, down_weight, input_first_factors, input_second_factors,
        output_first_factors, output_second_factors, tile,
    )
    output, grad_two, ga9_other, gb8_other, ga8, gb9 = feed_other(
        meta, rows_three, cot, gathered_two, packed, first_pack, input_first_factors,
        output_second_factors, (branch, grad_rows, rank9, grad_rank8), stream_two, gain_three, tile,
    )

    (
        grad_one, dz_own_heads, dz_other_heads, text_grad_own, text_grad_other,
        ga3, gb3, ga4, gb4, ga7, gb7,
    ) = middle_back(
        meta, grad_two, stream_one, z_own_frames, z_other_heads, q_own, q_other, z2_own, z2_other,
        weights, gathered_one, tables, packed, text_own, text_other, gain_two,
    )
    dz_other_frames = swap(dz_other_heads)
    text_heads_grad = (text_grad_own + swap(text_grad_other.astype(LOW)).astype(WIDE)).astype(LOW)
    text_rows, ga56, gb56 = project_back_heads(
        meta, text, text_heads_grad, cross_key_value_weight, cross_first_factors, cross_second_factors,
        5, 1, WIDE, "text_back",
    )
    grads_own, grads_other = self_back(meta, heads_own, heads_other, dz_own_heads, dz_other_frames)
    partial_other, ga012_other, gb012_other = project_back_heads(
        meta, rows_one_other, grads_other, self_query_key_value_weight, self_first_factors,
        self_second_factors, 0, 0, LOW, "other_back",
    )
    received = swap(partial_other)
    partial_own, ga012_own, gb012_own = project_back_heads(
        meta, rows_one, grads_own, self_query_key_value_weight, self_first_factors,
        self_second_factors, 0, 0, WIDE, "own_back",
    )
    input_grad = last_norm(meta, x, partial_own, received, grad_one, gain_one)

    def my_half(array):
        return lax.dynamic_slice_in_dim(array, side * (array.shape[1] // 2), array.shape[1] // 2, axis=1)

    def other_half(array):
        return lax.dynamic_slice_in_dim(
            array, (1 - side) * (array.shape[1] // 2), array.shape[1] // 2, axis=1
        )

    def over_clips(mine, theirs, ready, columns):
        received_part = swap(jnp.concatenate(theirs, axis=1).astype(LOW)).astype(WIDE)
        both = jnp.concatenate(mine, axis=1) + received_part
        labels = jnp.zeros((RANK_UNIT, 2 * HEAD_DIM), WIDE).at[0, : picks.shape[0]].set(picks.astype(WIDE))
        payload = jnp.concatenate([both] + ready + [labels], axis=1).astype(LOW)
        everyone = lax.all_gather(payload, "dp", axis=0)
        names = everyone[:, 0, -2 * HEAD_DIM :][:, : picks.shape[0]].astype(jnp.int32)
        results = []
        first = 0
        for column, size in columns:
            choose = (names[:, column, None] == jnp.arange(slots, dtype=jnp.int32)[None]).astype(LOW)
            results.append(
                jnp.einsum(
                    "cn,cpq->npq", choose, everyone[:, :, first : first + size],
                    preferred_element_type=WIDE,
                )
            )
            first += size
        return results

    def text_half(which):
        return text_rows[:, : width // 2] if which == 0 else text_rows[:, width // 2 :]

    text_mine = jnp.where(side == 0, text_half(0), text_half(1))
    text_theirs = jnp.where(side == 0, text_half(1), text_half(0))
    text_grad = text_mine + swap(text_theirs.astype(LOW)).astype(WIDE)

    half_width = width // 2
    early = over_clips(
        [my_half(ga8), my_half(gb9), my_half(gb3), my_half(gb7), my_half(ga4), my_half(ga56[0]), my_half(ga56[1])]
        + [ga9_own, gb8_own, ga3[:, :local], ga7[:, :local], gb4[:, :local]],
        [other_half(ga8), other_half(gb9), other_half(gb3), other_half(gb7), other_half(ga4), other_half(ga56[0]), other_half(ga56[1])]
        + [ga9_other, gb8_other, ga3[:, local:], ga7[:, local:], gb4[:, local:]],
        [gb56[0], gb56[1]],
        [
            (8, half_width), (9, half_width), (3, half_width), (7, half_width), (4, half_width),
            (5, half_width), (6, half_width), (9, hidden), (8, hidden), (3, local), (7, local), (4, local),
            (5, local), (6, local),
        ],
    )
    ga8_sum, gb9_sum, gb3_sum, gb7_sum, ga4_sum, ga5_sum, ga6_sum = early[:7]
    ga9_sum, gb8_sum, ga3_sum, ga7_sum, gb4_sum, gb5_sum, gb6_sum = early[7:]
    ga012 = ga012_own + ga012_other
    gb012 = gb012_own + gb012_other
    late = over_clips(
        [my_half(ga012[j]) for j in range(3)],
        [other_half(ga012[j]) for j in range(3)],
        [gb012[j] for j in range(3)],
        [(j, half_width) for j in range(3)] + [(j, local) for j in range(3)],
    )
    return (
        output[None],
        input_grad[None],
        text_grad[None],
        jnp.stack(late[:3]),
        jnp.stack(late[3:]),
        jnp.stack([ga4_sum, ga5_sum, ga6_sum]),
        jnp.stack([gb4_sum, gb5_sum, gb6_sum]),
        jnp.stack([ga3_sum, ga7_sum]),
        jnp.stack([gb3_sum, gb7_sum]),
        ga8_sum,
        gb8_sum,
        ga9_sum,
        gb9_sum,
    )


def solution(mesh):
    in_specs = (
        P("dp", "tensor", None),
        P("dp", None, None),
        P("dp", "tensor", None),
        P("dp", None),
        P(),
        P(),
        P(),
        P(None, None, "tensor"),
        P("tensor", None),
        P(None, "tensor"),
        P(None, None, "tensor"),
        P("tensor", None),
        P(None, "tensor"),
        P("tensor", None),
        P(),
        P(None, None, None, "tensor"),
        P(),
        P(None, None, None, "tensor"),
        P(None, None, None, "tensor"),
        P(),
        P(),
        P(None, None, "tensor"),
        P(None, None, "tensor"),
        P(),
    )
    out_specs = (
        P("dp", "tensor", None),
        P("dp", "tensor", None),
        P("dp", None, "tensor"),
        P(None, None, None, "tensor"),
        P(None, None, None, "tensor"),
        P(None, None, None, "tensor"),
        P(None, None, None, "tensor"),
        P(None, None, None, "tensor"),
        P(None, None, None, "tensor"),
        P(None, None, "tensor"),
        P(None, None, "tensor"),
        P(None, None, "tensor"),
        P(None, None, "tensor"),
    )
    layer = on_pair if mesh.shape["tensor"] == 2 else on_device
    return jax.shard_map(
        layer, mesh=mesh, in_specs=in_specs, out_specs=out_specs, check_vma=False
    )
```

```python
import jax
import jax.numpy as jnp
from jax import lax
from jax.experimental import pallas as pl
from jax.experimental.pallas import tpu as pltpu
from jax.sharding import PartitionSpec as P

HEAD_DIM = 64


epsilon = 1e-05


def split_dot(form, wide_part, narrow_part):
    high_part = wide_part.astype(jnp.bfloat16)
    rest_part = (wide_part - high_part.astype(jnp.float32)).astype(jnp.bfloat16)
    first = jnp.einsum(form, high_part, narrow_part, preferred_element_type=jnp.float32)
    return first + jnp.einsum(form, rest_part, narrow_part, preferred_element_type=jnp.float32)


def layer_norm(stream, gain_vec):
    centred = stream - jnp.mean(stream, axis=-1, keepdims=True)
    inverse = lax.rsqrt(jnp.mean(centred * centred, axis=-1, keepdims=True) + epsilon)
    normed = centred * inverse
    return (normed * gain_vec, normed, inverse)


def norm_back(grad_out, gain_vec, normed, inverse):
    grad_norm = grad_out * gain_vec
    mean_grad = jnp.mean(grad_norm, axis=-1, keepdims=True)
    mean_cross = jnp.mean(grad_norm * normed, axis=-1, keepdims=True)
    return inverse * (grad_norm - mean_grad - normed * mean_cross)


def spread_rows(local_rows):
    return lax.all_gather(local_rows.astype(jnp.bfloat16), "tensor", axis=1, tiled=True)


def reduce_grads(partial_sum):
    return lax.psum_scatter(
        partial_sum.astype(jnp.bfloat16), "tensor", scatter_dimension=1, tiled=True
    ).astype(jnp.float32)


def project_rows(act_rows, weight, output_choice, input_choice):
    low_rank = jnp.einsum(
        "ctd,crd->ctr", act_rows, output_choice, preferred_element_type=jnp.float32
    )
    result = jnp.einsum("ctd,de->cte", act_rows, weight, preferred_element_type=jnp.float32)
    result = result + split_dot("ctr,cre->cte", low_rank, input_choice)
    return (result, low_rank)


def project_back(grad_low, act_rows, weight, output_choice, input_choice, low_rank):
    grad_rank = jnp.einsum(
        "cte,cre->ctr", grad_low, input_choice, preferred_element_type=jnp.float32
    )
    grad_rows = jnp.einsum("cte,de->ctd", grad_low, weight, preferred_element_type=jnp.float32)
    grad_rows = grad_rows + split_dot("ctr,crd->ctd", grad_rank, output_choice)
    grad_down = split_dot("ctr,ctd->crd", grad_rank, act_rows)
    grad_up = split_dot("ctr,cte->cre", low_rank, grad_low)
    return (grad_rows, grad_down, grad_up)


def causal_frames(first_row, block_rows, key_count):
    query_at = first_row + jnp.arange(block_rows, dtype=jnp.int32)[:, None]
    key_at = jnp.arange(key_count, dtype=jnp.int32)[None, :]
    return key_at <= query_at


def attention_forward(queries, key_rows, value_rows, causal):
    frames = queries.shape[1]
    key_count = key_rows.shape[1]
    block_rows = min(512, frames)
    score_scale = HEAD_DIM ** (-0.5)
    outputs = []
    log_totals = []
    for first_row in range(0, frames, block_rows):
        key_end = first_row + block_rows if causal else key_count
        query_block = queries[:, first_row : first_row + block_rows]
        scores = (
            jnp.einsum(
                "cbhe,ckhe->chbk",
                query_block,
                key_rows[:, :key_end],
                preferred_element_type=jnp.float32,
            )
            * score_scale
        )
        if causal:
            scores = jnp.where(causal_frames(first_row, block_rows, key_end), scores, -1e30)
        largest = jnp.max(scores, axis=-1, keepdims=True)
        exponent = jnp.exp(scores - largest)
        summed = jnp.sum(exponent, axis=-1, keepdims=True)
        prob_low = (exponent / summed).astype(jnp.bfloat16)
        outputs.append(
            jnp.einsum(
                "chbk,ckhe->cbhe",
                prob_low,
                value_rows[:, :key_end],
                preferred_element_type=jnp.float32,
            )
        )
        log_totals.append(largest + jnp.log(summed))
    return (jnp.concatenate(outputs, axis=1), jnp.concatenate(log_totals, axis=2))


def attention_back(queries, key_rows, value_rows, log_totals, grad_mixed, causal):
    frames = queries.shape[1]
    key_count = key_rows.shape[1]
    block_rows = min(512, frames)
    score_scale = HEAD_DIM ** (-0.5)
    grad_keys = jnp.zeros(key_rows.shape, jnp.float32)
    grad_values = jnp.zeros(value_rows.shape, jnp.float32)
    grad_queries = []
    for first_row in range(0, frames, block_rows):
        key_end = first_row + block_rows if causal else key_count
        key_part = key_rows[:, :key_end]
        value_part = value_rows[:, :key_end]
        query_block = queries[:, first_row : first_row + block_rows]
        grad_block = grad_mixed[:, first_row : first_row + block_rows]
        scores = (
            jnp.einsum("cbhe,ckhe->chbk", query_block, key_part, preferred_element_type=jnp.float32)
            * score_scale
        )
        if causal:
            scores = jnp.where(causal_frames(first_row, block_rows, key_end), scores, -1e30)
        probs = jnp.exp(scores - log_totals[:, :, first_row : first_row + block_rows])
        grad_values = grad_values.at[:, :key_end].add(
            jnp.einsum(
                "chbk,cbhe->ckhe",
                probs.astype(jnp.bfloat16),
                grad_block,
                preferred_element_type=jnp.float32,
            )
        )
        grad_probs = jnp.einsum(
            "cbhe,ckhe->chbk", grad_block, value_part, preferred_element_type=jnp.float32
        )
        inner_sum = jnp.sum(probs * grad_probs, axis=-1, keepdims=True)
        grad_scores = (probs * (grad_probs - inner_sum)).astype(jnp.bfloat16)
        grad_queries.append(
            jnp.einsum("chbk,ckhe->cbhe", grad_scores, key_part, preferred_element_type=jnp.float32)
            * score_scale
        )
        grad_keys = grad_keys.at[:, :key_end].add(
            jnp.einsum(
                "chbk,cbhe->ckhe", grad_scores, query_block, preferred_element_type=jnp.float32
            )
            * score_scale
        )
    return (jnp.concatenate(grad_queries, axis=1), grad_keys, grad_values)


def gelu_exact(pre_act):
    return jax.nn.gelu(pre_act, approximate=False)


def on_device(
    inputs,
    encoder_text_states,
    cotangent,
    clip_adapter_index,
    self_norm_gain,
    cross_norm_gain,
    feed_norm_gain,
    self_query_key_value_weight,
    self_output_weight,
    cross_query_weight,
    cross_key_value_weight,
    cross_output_weight,
    up_weight,
    down_weight,
    self_first_factors,
    self_second_factors,
    cross_first_factors,
    cross_second_factors,
    attention_first_factors,
    attention_second_factors,
    input_first_factors,
    input_second_factors,
    output_first_factors,
    output_second_factors,
):
    adapter_slot_count = input_first_factors.shape[0]
    chooser = (
        clip_adapter_index[:, :, None]
        == jnp.arange(adapter_slot_count, dtype=jnp.int32)[None, None, :]
    ).astype(jnp.bfloat16)
    local_heads = self_output_weight.shape[0] // HEAD_DIM

    def choose_adapter_slot(adapter_slot_table, column_index):
        return jnp.einsum(
            "cn,npq->cpq",
            chooser[:, column_index],
            adapter_slot_table,
            preferred_element_type=jnp.float32,
        ).astype(jnp.bfloat16)

    def slot_grads(grad_pick, column_index):
        return split_dot("cpq,cn->npq", grad_pick, chooser[:, column_index])

    def split_heads(stacked):
        return stacked.reshape(stacked.shape[0], stacked.shape[1], local_heads, HEAD_DIM)

    def join_heads(stacked):
        return stacked.reshape(stacked.shape[0], stacked.shape[1], local_heads * HEAD_DIM)

    def out_forward(mixed_in, inner_layer):
        column_index = 3 + 4 * inner_layer
        input_choice = choose_adapter_slot(attention_second_factors[inner_layer], column_index)
        weight = self_output_weight if inner_layer == 0 else cross_output_weight
        output_choice = choose_adapter_slot(attention_first_factors[inner_layer], column_index)
        partial_out, low_rank = project_rows(mixed_in, weight, output_choice, input_choice)
        branch = lax.psum_scatter(
            partial_out.astype(jnp.bfloat16), "tensor", scatter_dimension=1, tiled=True
        ).astype(jnp.float32)
        kept_data = (mixed_in, weight, output_choice, input_choice, low_rank)
        return (branch, kept_data)

    def out_back(grad_stream, kept_data):
        mixed_in, weight, output_choice, input_choice, low_rank = kept_data
        grad_low = grad_stream.astype(jnp.bfloat16)
        grad_full = lax.all_gather(grad_low, "tensor", axis=1, tiled=True)
        grad_rows, grad_down, grad_up = project_back(
            grad_full, mixed_in, weight, output_choice, input_choice, low_rank
        )
        grad_mixed = grad_rows.astype(jnp.bfloat16)
        return (grad_mixed, grad_down, grad_up)

    stream = inputs.astype(jnp.float32)
    normed_value, normed_one, inverse_one = layer_norm(stream, self_norm_gain)
    rows_one = spread_rows(normed_value)
    self_down_factor = [
        choose_adapter_slot(self_first_factors[slot_number], slot_number)
        for slot_number in range(3)
    ]
    self_up_factor = [
        choose_adapter_slot(self_second_factors[slot_number], slot_number)
        for slot_number in range(3)
    ]
    self_parts = [
        project_rows(
            rows_one,
            self_query_key_value_weight[slot_number],
            self_down_factor[slot_number],
            self_up_factor[slot_number],
        )
        for slot_number in range(3)
    ]
    self_heads = [
        split_heads(self_parts[slot_number][0].astype(jnp.bfloat16)) for slot_number in range(3)
    ]
    mixed_one, totals_one = attention_forward(self_heads[0], self_heads[1], self_heads[2], True)
    mixed_one = join_heads(mixed_one).astype(jnp.bfloat16)
    branch_one, kept_one = out_forward(mixed_one, 0)
    stream_one = stream + branch_one
    normed_value, normed_two, inverse_two = layer_norm(stream_one, cross_norm_gain)
    rows_two = spread_rows(normed_value)
    cross_down_factor = [
        choose_adapter_slot(cross_first_factors[slot_number], 4 + slot_number)
        for slot_number in range(3)
    ]
    cross_up_factor = [
        choose_adapter_slot(cross_second_factors[slot_number], 4 + slot_number)
        for slot_number in range(3)
    ]
    query_full, query_rank = project_rows(
        rows_two, cross_query_weight, cross_down_factor[0], cross_up_factor[0]
    )
    key_full, key_rank = project_rows(
        encoder_text_states, cross_key_value_weight[0], cross_down_factor[1], cross_up_factor[1]
    )
    value_full, value_rank = project_rows(
        encoder_text_states, cross_key_value_weight[1], cross_down_factor[2], cross_up_factor[2]
    )
    query_two = split_heads(query_full.astype(jnp.bfloat16))
    key_two = split_heads(key_full.astype(jnp.bfloat16))
    value_two = split_heads(value_full.astype(jnp.bfloat16))
    mixed_two, totals_two = attention_forward(query_two, key_two, value_two, False)
    mixed_two = join_heads(mixed_two).astype(jnp.bfloat16)
    branch_two, kept_two = out_forward(mixed_two, 1)
    stream_two = stream_one + branch_two
    normed_value, normed_three, inverse_three = layer_norm(stream_two, feed_norm_gain)
    rows_three = spread_rows(normed_value)
    input_second_choice = choose_adapter_slot(input_first_factors, 8)
    input_first_choice = choose_adapter_slot(input_second_factors, 8)
    before, up_rank = project_rows(rows_three, up_weight, input_second_choice, input_first_choice)
    gelu_value, gelu_pull = jax.vjp(gelu_exact, before)
    hidden = gelu_value.astype(jnp.bfloat16)
    output_second_choice = choose_adapter_slot(output_first_factors, 9)
    output_first_choice = choose_adapter_slot(output_second_factors, 9)
    partial_out, down_rank = project_rows(
        hidden, down_weight, output_second_choice, output_first_choice
    )
    branch_three = lax.psum_scatter(
        partial_out.astype(jnp.bfloat16), "tensor", scatter_dimension=1, tiled=True
    ).astype(jnp.float32)
    output = (stream_two + branch_three).astype(jnp.bfloat16)
    grad_full = lax.all_gather(cotangent, "tensor", axis=1, tiled=True)
    grad_hidden, grad_down_a, grad_down_b = project_back(
        grad_full, hidden, down_weight, output_second_choice, output_first_choice, down_rank
    )
    grad_before = gelu_pull(grad_hidden)[0].astype(jnp.bfloat16)
    grad_rows, grad_up_a, grad_up_b = project_back(
        grad_before, rows_three, up_weight, input_second_choice, input_first_choice, up_rank
    )
    grad_stream = cotangent.astype(jnp.float32) + norm_back(
        reduce_grads(grad_rows), feed_norm_gain, normed_three, inverse_three
    )
    grad_mixed, grad_out_a_two, grad_out_b_two = out_back(grad_stream, kept_two)
    grad_query, grad_key, grad_value = attention_back(
        query_two, key_two, value_two, totals_two, split_heads(grad_mixed), False
    )
    grad_query = join_heads(grad_query).astype(jnp.bfloat16)
    grad_key = join_heads(grad_key).astype(jnp.bfloat16)
    grad_value = join_heads(grad_value).astype(jnp.bfloat16)
    grad_rows_query, cross_grad_a_zero, cross_grad_b_zero = project_back(
        grad_query,
        rows_two,
        cross_query_weight,
        cross_down_factor[0],
        cross_up_factor[0],
        query_rank,
    )
    grad_text_key, cross_grad_a_one, cross_grad_b_one = project_back(
        grad_key,
        encoder_text_states,
        cross_key_value_weight[0],
        cross_down_factor[1],
        cross_up_factor[1],
        key_rank,
    )
    grad_text_value, cross_grad_a_two, cross_grad_b_two = project_back(
        grad_value,
        encoder_text_states,
        cross_key_value_weight[1],
        cross_down_factor[2],
        cross_up_factor[2],
        value_rank,
    )
    normed_grad, text_grad = (
        lax.psum_scatter(
            grad_rows_query.astype(jnp.bfloat16), "tensor", scatter_dimension=1, tiled=True
        ).astype(jnp.float32),
        lax.psum_scatter(
            (grad_text_key + grad_text_value).astype(jnp.bfloat16),
            "tensor",
            scatter_dimension=2,
            tiled=True,
        ).astype(jnp.float32),
    )
    grad_stream = grad_stream + norm_back(normed_grad, cross_norm_gain, normed_two, inverse_two)
    grad_mixed, grad_out_a_one, grad_out_b_one = out_back(grad_stream, kept_one)
    grad_query, grad_key, grad_value = attention_back(
        self_heads[0], self_heads[1], self_heads[2], totals_one, split_heads(grad_mixed), True
    )
    self_grads = [
        join_heads(grad_query).astype(jnp.bfloat16),
        join_heads(grad_key).astype(jnp.bfloat16),
        join_heads(grad_value).astype(jnp.bfloat16),
    ]
    self_rows_total = jnp.zeros(rows_one.shape, jnp.float32)
    self_grad_a = []
    self_grad_b = []
    for slot_number in range(3):
        grad_rows, grad_a_part, grad_b_part = project_back(
            self_grads[slot_number],
            rows_one,
            self_query_key_value_weight[slot_number],
            self_down_factor[slot_number],
            self_up_factor[slot_number],
            self_parts[slot_number][1],
        )
        self_rows_total = self_rows_total + grad_rows
        self_grad_a.append(slot_grads(grad_a_part, slot_number))
        self_grad_b.append(slot_grads(grad_b_part, slot_number))
    input_grad = grad_stream + norm_back(
        reduce_grads(self_rows_total), self_norm_gain, normed_one, inverse_one
    )
    sum_self_a = jnp.stack(self_grad_a)
    sum_self_b = jnp.stack(self_grad_b)
    sum_cross_a = jnp.stack(
        [
            slot_grads(cross_grad_a_zero, 4),
            slot_grads(cross_grad_a_one, 5),
            slot_grads(cross_grad_a_two, 6),
        ]
    )
    sum_cross_b = jnp.stack(
        [
            slot_grads(cross_grad_b_zero, 4),
            slot_grads(cross_grad_b_one, 5),
            slot_grads(cross_grad_b_two, 6),
        ]
    )
    sum_out_a = jnp.stack([slot_grads(grad_out_a_one, 3), slot_grads(grad_out_a_two, 7)])
    sum_out_b = jnp.stack([slot_grads(grad_out_b_one, 3), slot_grads(grad_out_b_two, 7)])
    sum_up_a = slot_grads(grad_up_a, 8)
    sum_up_b = slot_grads(grad_up_b, 8)
    sum_down_a = slot_grads(grad_down_a, 9)
    sum_down_b = slot_grads(grad_down_b, 9)
    sum_self_a, sum_cross_a, sum_out_b, sum_up_a, sum_down_b = (
        lax.psum_scatter(
            sum_self_a.astype(jnp.bfloat16), "tensor", scatter_dimension=3, tiled=True
        ).astype(jnp.float32),
        lax.psum_scatter(
            sum_cross_a.astype(jnp.bfloat16), "tensor", scatter_dimension=3, tiled=True
        ).astype(jnp.float32),
        lax.psum_scatter(
            sum_out_b.astype(jnp.bfloat16), "tensor", scatter_dimension=3, tiled=True
        ).astype(jnp.float32),
        lax.psum_scatter(
            sum_up_a.astype(jnp.bfloat16), "tensor", scatter_dimension=2, tiled=True
        ).astype(jnp.float32),
        lax.psum_scatter(
            sum_down_b.astype(jnp.bfloat16), "tensor", scatter_dimension=2, tiled=True
        ).astype(jnp.float32),
    )
    totals = (
        lax.psum(sum_self_a.astype(jnp.bfloat16), "dp").astype(jnp.float32),
        lax.psum(sum_self_b.astype(jnp.bfloat16), "dp").astype(jnp.float32),
        lax.psum(sum_cross_a.astype(jnp.bfloat16), "dp").astype(jnp.float32),
        lax.psum(sum_cross_b.astype(jnp.bfloat16), "dp").astype(jnp.float32),
        lax.psum(sum_out_a.astype(jnp.bfloat16), "dp").astype(jnp.float32),
        lax.psum(sum_out_b.astype(jnp.bfloat16), "dp").astype(jnp.float32),
        lax.psum(sum_up_a.astype(jnp.bfloat16), "dp").astype(jnp.float32),
        lax.psum(sum_up_b.astype(jnp.bfloat16), "dp").astype(jnp.float32),
        lax.psum(sum_down_a.astype(jnp.bfloat16), "dp").astype(jnp.float32),
        lax.psum(sum_down_b.astype(jnp.bfloat16), "dp").astype(jnp.float32),
    )
    return (
        output,
        input_grad,
        text_grad,
        totals[0],
        totals[1],
        totals[2],
        totals[3],
        totals[4],
        totals[5],
        totals[6],
        totals[7],
        totals[8],
        totals[9],
    )


LOW = jnp.bfloat16
WIDE = jnp.float32
VMEM_BYTES = 58 * 1024 * 1024
RANK_UNIT = 16
COST_SCALE = 1


def mm(left, right, left_dim=1, right_dim=0):
    return lax.dot_general(
        left, right, (((left_dim,), (right_dim,)), ((), ())), preferred_element_type=WIDE
    )


def mm_nt(left, right):
    return mm(left, right, 1, 1)


def mm_tn(left, right):
    return mm(left, right, 0, 0)


def low_rank(factor, rows):
    return mm_nt(factor, rows).astype(LOW)


def norm_rows(rows, gain):
    centred = rows - jnp.mean(rows, axis=-1, keepdims=True)
    inverse = lax.rsqrt(jnp.mean(centred * centred, axis=-1, keepdims=True) + epsilon)
    normed = centred * inverse
    return normed * gain, normed, inverse


def lane_halves():
    lane = lax.broadcasted_iota(jnp.int32, (1, 2 * HEAD_DIM), 1)
    return lane < HEAD_DIM


def half_masks():
    left = lane_halves()
    first = jnp.where(left, 1.0, 0.0)
    return first.astype(LOW), (1.0 - first).astype(LOW)


def gelu_parts(pre):
    bell = jnp.exp(-0.5 * pre * pre)
    step = 1.0 / (1.0 + (0.3275911 * 0.7071067811865476) * jnp.abs(pre))
    tail = step * (
        0.5 * 0.254829592
        + step
        * (
            0.5 * -0.284496736
            + step
            * (0.5 * 1.421413741 + step * (0.5 * -1.453152027 + step * (0.5 * 1.061405429)))
        )
    )
    tail = tail * bell
    phi = jnp.where(pre >= 0.0, 1.0 - tail, tail)
    return pre * phi, phi + pre * bell * 0.3989422804014327


def whole(shape, where=None):
    place = (0,) * len(shape) if where is None else where
    return pl.BlockSpec(shape, lambda *_: place, pipeline_mode=pl.Buffered(1))


def call(body, grid, in_specs, out_specs, out_shape, scratch, flops, moved, name, args, vmem=VMEM_BYTES):
    return pl.pallas_call(
        body,
        grid_spec=pltpu.PrefetchScalarGridSpec(
            num_scalar_prefetch=1,
            grid=grid,
            in_specs=in_specs,
            out_specs=out_specs,
            scratch_shapes=scratch,
        ),
        out_shape=out_shape,
        compiler_params=pltpu.CompilerParams(
            dimension_semantics=("arbitrary",) * len(grid), vmem_limit_bytes=vmem
        ),
        cost_estimate=pl.CostEstimate(
            flops=flops // COST_SCALE, bytes_accessed=moved // COST_SCALE, transcendentals=0
        ),
        name=name,
    )(*args)


def shaped(shape, dtype):
    return jax.ShapeDtypeStruct(shape, dtype)


IN_PLACE = pl.BlockSpec(memory_space=pl.ANY)


def factors_body(_, *refs):
    out_ref = refs[-1]
    first = 0
    for ref in refs[:-1]:
        size = ref.shape[-1]
        out_ref[:, first : first + size] = ref[...]
        first += size


def picked_factors(meta, sources):
    specs = []
    total = 0
    for table, entry, slot in sources:
        if entry is None:
            spec = pl.BlockSpec((None,) + table.shape[1:], lambda t, m, slot=slot: (m[slot], 0, 0))
        else:
            spec = pl.BlockSpec(
                (None, None) + table.shape[2:], lambda t, m, entry=entry, slot=slot: (entry, m[slot], 0, 0)
            )
        specs.append(spec)
        total += table.shape[-1]
    shape = (RANK_UNIT, total)
    return call(
        factors_body, (1,), specs, whole(shape), shaped(shape, LOW), [], 0, 4 * RANK_UNIT * total,
        "picked_factors", (meta,) + tuple(table for table, _, _ in sources),
    )


def share_body(_, parts, down_ref, up_ref, *refs):
    out_ref = refs[-1]
    step = pl.program_id(0)

    @pl.when(step < parts)
    def _():
        out_ref[0] = down_ref[...]

    @pl.when(step >= parts)
    def _():
        out_ref[0] = up_ref[...]


def feed_share(meta, down_weight, up_weight, depth, after):
    hidden, width = down_weight.shape
    parts = hidden // width
    return call(
        lambda m, *refs: share_body(m, parts, *refs),
        (2 * parts,),
        [
            pl.BlockSpec(
                (depth, width), lambda t, m: (m[11] * parts + jnp.minimum(t, parts - 1), 0)
            ),
            pl.BlockSpec((depth, width), lambda t, m: (m[11], jnp.maximum(t - parts, 0))),
        ]
        + [IN_PLACE] * len(after),
        pl.BlockSpec((1, depth, width), lambda t, m: (t, 0, 0)),
        shaped((2 * parts, depth, width), LOW),
        [],
        0,
        8 * parts * depth * width,
        "feed_share",
        (meta, down_weight, up_weight, *after),
    )


def first_norm_body(_, x_ref, gain_ref, out_ref):
    rows, _, _ = norm_rows(x_ref[...].astype(WIDE), gain_ref[...])
    out_ref[...] = rows.astype(LOW)


def first_norm(meta, x, gain):
    frames, width = x.shape
    block = min(256, frames)
    rows = pl.BlockSpec((block, width), lambda t, _: (t, 0))
    return call(
        first_norm_body,
        (frames // block,),
        [rows, whole((1, width))],
        rows,
        shaped(x.shape, LOW),
        [],
        10 * x.size,
        4 * x.size,
        "first_norm",
        (meta, x, gain),
    )


def project_body(_, act_ref, weight_ref, down_ref, up_ref, *refs):
    out_ref = refs[-1]
    act = act_ref[...]
    rank = low_rank(down_ref[0, 0], act)
    out_ref[0] = (mm(act, weight_ref[0]) + mm_tn(rank, up_ref[0, 0])).astype(LOW)


def project_heads(meta, act, weights, down, up, slots, skip, name, after=()):
    rows, width = act.shape
    count, _, local = weights.shape
    first_slot = slots
    return call(
        project_body,
        (count,),
        [
            whole((rows, width)),
            pl.BlockSpec((1, width, local), lambda j, m: (j, 0, 0)),
            pl.BlockSpec((1, 1, RANK_UNIT, width), lambda j, m: (j + skip, m[first_slot + j], 0, 0)),
            pl.BlockSpec((1, 1, RANK_UNIT, local), lambda j, m: (j + skip, m[first_slot + j], 0, 0)),
        ]
        + [IN_PLACE] * len(after),
        pl.BlockSpec((1, rows, local), lambda j, m: (j, 0, 0)),
        shaped((count, rows, local), LOW),
        [],
        2 * rows * width * local * count,
        2 * (weights.size + act.size + count * rows * local),
        name,
        (meta, act, weights, down, up, *after),
    )


def project_back_body(_, last, grad_ref, weight_ref, down_ref, up_ref, after_ref, out_ref, total_ref):
    step = pl.program_id(0)
    grad = grad_ref[0]
    grad_rank = low_rank(up_ref[0, 0], grad)
    part = mm_nt(grad, weight_ref[0]) + mm_tn(grad_rank, down_ref[0, 0])

    @pl.when(step == 0)
    def _():
        total_ref[...] = part

    @pl.when(step > 0)
    def _():
        total_ref[...] += part

    @pl.when(step == last)
    def _():
        out_ref[...] = total_ref[...].astype(out_ref.dtype)


def project_back_heads(meta, grads, weights, down, up, slots, skip, kind, name, after):
    count, width, local = weights.shape
    rows = grads.shape[1]
    return call(
        lambda m, *refs: project_back_body(m, count - 1, *refs),
        (count,),
        [
            pl.BlockSpec((1, rows, local), lambda j, m: (j, 0, 0)),
            pl.BlockSpec((1, width, local), lambda j, m: (j, 0, 0)),
            pl.BlockSpec((1, 1, RANK_UNIT, width), lambda j, m: (j + skip, m[slots + j], 0, 0)),
            pl.BlockSpec((1, 1, RANK_UNIT, local), lambda j, m: (j + skip, m[slots + j], 0, 0)),
            IN_PLACE,
        ],
        whole((rows, width)),
        shaped((rows, width), kind),
        [pltpu.VMEM((rows, width), WIDE)],
        2 * rows * width * local * count,
        2 * (weights.size + count * rows * local) + 4 * rows * width,
        name,
        (meta, grads, weights, down, up, after),
    )


def rank_grads_body(meta, count, parts, *refs):
    acts = refs[:parts]
    grads = refs[parts : 2 * parts]
    downs = refs[2 * parts : 2 * parts + count]
    ups = refs[2 * parts + count : 2 * parts + 2 * count]
    mine_ref, theirs_ref, ga = refs[2 * parts + 2 * count :]
    half = ga.shape[1] // 2
    local = ups[0].shape[3]
    down = jnp.concatenate([ref[0, 0] for ref in downs], axis=0)
    for part in range(parts):
        act = acts[part][...]
        rank = low_rank(down, act)
        grad_rank = jnp.concatenate(
            [low_rank(ups[j][0, 0], grads[part][j]) for j in range(count)], axis=0
        )
        if part == 0:
            ga[...] = mm(grad_rank, act)
        else:
            ga[...] += mm(grad_rank, act)
        for j in range(count):
            gb = mm(rank[RANK_UNIT * j : RANK_UNIT * (j + 1)], grads[part][j])
            span = slice(count * half + j * local, count * half + (j + 1) * local)
            if part == 0:
                mine_ref[:, span] = gb
            else:
                mine_ref[:, span] += gb
    side = meta[10]
    for j in range(count):
        rows = slice(RANK_UNIT * j, RANK_UNIT * (j + 1))
        span = slice(j * half, (j + 1) * half)
        mine_ref[:, span] = ga[rows, pl.ds(pl.multiple_of(side * half, 128), half)]
        theirs = ga[rows, pl.ds(pl.multiple_of((1 - side) * half, 128), half)]
        theirs_ref[:, span] = theirs.astype(LOW)


def rank_grads(meta, acts, grads, down, up, slots, skip, name):
    rows, width = acts[0].shape
    count, _, local = grads[0].shape
    parts = len(acts)

    def table(size, j):
        return pl.BlockSpec(
            (1, 1, RANK_UNIT, size),
            lambda t, m: (j + skip, m[slots + j], 0, 0),
            pipeline_mode=pl.Buffered(1),
        )

    shared = count * width // 2
    total = shared + count * local
    return call(
        lambda m, *refs: rank_grads_body(m, count, parts, *refs),
        (1,),
        [whole((rows, width))] * parts
        + [whole((count, rows, local))] * parts
        + [table(width, j) for j in range(count)]
        + [table(local, j) for j in range(count)],
        (whole((RANK_UNIT, total)), whole((RANK_UNIT, shared))),
        (shaped((RANK_UNIT, total), WIDE), shaped((RANK_UNIT, shared), LOW)),
        [pltpu.VMEM((RANK_UNIT * count, width), WIDE)],
        8 * parts * rows * (width + local) * RANK_UNIT * count,
        2 * parts * rows * (width + count * local),
        name,
        (meta, *acts, *grads, *([down] * count), *([up] * count)),
    )


def split_columns(meta, mine_ref, theirs_ref, first, array):
    half = array.shape[-1] // 2
    span = slice(first, first + half)
    side = meta[10]
    mine_ref[:, span] = array[:, pl.ds(pl.multiple_of(side * half, 128), half)]
    theirs = array[:, pl.ds(pl.multiple_of((1 - side) * half, 128), half)]
    theirs_ref[:, span] = theirs.astype(LOW)


def own_columns(mine_ref, theirs_ref, first, array):
    half = array.shape[-1] // 2
    span = slice(first, first + half)
    mine_ref[:, span] = array[:, :half]
    theirs_ref[:, span] = array[:, half:].astype(LOW)


def join(mine, received):
    both = jnp.concatenate(received, axis=1).astype(WIDE)
    width = both.shape[1]
    return (mine + jnp.pad(both, ((0, 0), (0, mine.shape[1] - width)))).astype(LOW)


def clip_names(label_ref):
    clips, rank, width = label_ref.shape
    return label_ref[...].reshape(clips * rank, width).astype(WIDE).T


def slot_take(names, slots, rank):
    source = lax.broadcasted_iota(jnp.int32, names.shape, 1)
    target = (source & (rank - 1)) + rank * names.astype(jnp.int32)
    place = lax.broadcasted_iota(jnp.int32, (slots * rank, names.shape[1]), 0)
    return jnp.where(place == target, 1.0, 0.0).astype(LOW)


def slot_sum_body(_, plan, slots, everyone_ref, label_ref, *refs):
    names = refs[-1]
    out_refs = refs[-1 - len({which for _, which, _ in plan}) : -1]
    step = pl.program_id(0)
    clips, rank, unit = everyone_ref.shape

    @pl.when(step == 0)
    def _():
        names[...] = clip_names(label_ref)

    column = jnp.int32(0)
    chosen_out = jnp.int32(0)
    for number, (place, which, _) in enumerate(plan):
        column = jnp.where(step == number, place, column)
        chosen_out = jnp.where(step == number, which, chosen_out)
    take = slot_take(names[pl.ds(column, 1)], slots, rank)
    total = mm(take, everyone_ref[...].reshape(clips * rank, unit))
    for which, ref in enumerate(out_refs):

        @pl.when(chosen_out == which)
        def _():
            ref[...] = total.reshape(ref.shape)


def late_sum_body(_, plan, slots, carried, everyone_ref, label_ref, *refs):
    count = len({which for _, which, _ in plan})
    earlier = refs[: len(carried)]
    out_refs = refs[-5 - count : -5]
    names, arrived, totals, in_sems, out_sems = refs[-5:]
    clips, rank, unit = arrived.shape[1:]
    incoming = [
        pltpu.make_async_copy(
            everyone_ref.at[:, :, pl.ds(unit * number, unit)], arrived.at[number], in_sems.at[number]
        )
        for number in range(len(plan))
    ]
    for copy in incoming:
        copy.start()
    names[...] = clip_names(label_ref)
    outgoing = []
    for number, (which, ref) in enumerate(zip(carried, earlier)):
        copy = pltpu.make_async_copy(ref.at[0], out_refs[which].at[0], out_sems.at[len(plan) + number])
        copy.start()
        outgoing.append(copy)
    for number, (column, which, place) in enumerate(plan):
        incoming[number].wait()
        take = slot_take(names[column : column + 1], slots, rank)
        total = mm(take, arrived[number].reshape(clips * rank, unit))
        totals[number] = total.reshape(slots, rank, unit)
        copy = pltpu.make_async_copy(totals.at[number], out_refs[which].at[place], out_sems.at[number])
        copy.start()
        outgoing.append(copy)
    for copy in outgoing:
        copy.wait()


def late_sums(meta, everyone, plan, outs, slots, unit, carried, name, after):
    clips, rank, total = everyone.shape
    label_width = 2 * HEAD_DIM
    units = len(plan)
    return call(
        lambda m, *refs: late_sum_body(m, plan, slots, tuple(carried), *refs),
        (1,),
        [IN_PLACE, whole((clips, rank, label_width), (0, 0, total // label_width - 1))]
        + [whole(array.shape) for array in carried.values()]
        + [IN_PLACE] * len(after),
        (IN_PLACE,) * len(outs),
        tuple(shaped((stack, slots, rank, width), WIDE) for stack, width in outs),
        [
            pltpu.VMEM((label_width, clips * rank), WIDE),
            pltpu.VMEM((units, clips, rank, unit), LOW),
            pltpu.VMEM((units, slots, rank, unit), WIDE),
            pltpu.SemaphoreType.DMA((units,)),
            pltpu.SemaphoreType.DMA((units + len(carried),)),
        ],
        0,
        2 * everyone.size + 4 * slots * rank * total,
        name,
        (meta, everyone, everyone, *carried.values(), *after),
    )


def slot_sums(meta, everyone, plan, outs, slots, unit, name, after):
    clips, rank, total = everyone.shape
    steps = len(plan)

    def place_of(which):
        def place(t, m):
            places = [(step, place) for step, (_, target, place) in enumerate(plan) if target == which]
            value = jnp.int32(places[0][1])
            for step, place in places:
                value = jnp.where(t >= step, place, value)
            return value

        return place

    out_specs = []
    out_shapes = []
    for which, (stack, width) in enumerate(outs):
        place = place_of(which)
        if stack is None:
            out_specs.append(
                pl.BlockSpec((slots, rank, unit), lambda t, m, place=place: (0, 0, place(t, m)))
            )
            out_shapes.append(shaped((slots, rank, width), WIDE))
        else:
            out_specs.append(
                pl.BlockSpec((1, slots, rank, unit), lambda t, m, place=place: (place(t, m), 0, 0, 0))
            )
            out_shapes.append(shaped((stack, slots, rank, width), WIDE))
    label_width = 2 * HEAD_DIM
    return call(
        lambda m, *refs: slot_sum_body(m, plan, slots, *refs),
        (steps,),
        [
            pl.BlockSpec((clips, rank, unit), lambda t, m: (0, 0, t)),
            whole((clips, rank, label_width), (0, 0, total // label_width - 1)),
        ]
        + [IN_PLACE] * len(after),
        tuple(out_specs),
        tuple(out_shapes),
        [pltpu.VMEM((label_width, clips * rank), WIDE)],
        0,
        2 * everyone.size + 4 * slots * rank * total,
        name,
        (meta, everyone, everyone, *after),
    )


ROW_BLOCK = 512


def order_frames(is_first, own, other, low_part, high_part):
    @pl.when(is_first)
    def _():
        low_part[...] = own[...]
        high_part[...] = other[...]

    @pl.when(jnp.logical_not(is_first))
    def _():
        low_part[...] = other[...]
        high_part[...] = own[...]


def causal_spans(first):
    return [(first, first + ROW_BLOCK)] + [(key, key + ROW_BLOCK) for key in range(0, first, ROW_BLOCK)]


def causal_keep(rows):
    key_at = lax.broadcasted_iota(jnp.int32, (rows, rows), 0)
    return key_at <= lax.broadcasted_iota(jnp.int32, (rows, rows), 1)


def turned(rows):
    return rows.astype(WIDE).T.astype(LOW)


def self_forward_body(
    meta,
    own_ref,
    other_ref,
    out_own_ref,
    out_other_ref,
    log_own_ref,
    log_other_ref,
    held,
    value_turned,
    result,
    logs,
):
    half = own_ref.shape[1]
    is_first = meta[10] == 0
    order_frames(is_first, own_ref, other_ref, held.at[:, :half], held.at[:, half:])
    masks = half_masks()
    keep = causal_keep(ROW_BLOCK)
    for first in range(0, 2 * half, ROW_BLOCK):
        span = slice(first, first + ROW_BLOCK)
        values = turned(held[2, span])
        for which in (0, 1):
            value_turned[which, :HEAD_DIM, span] = values[HEAD_DIM * which : HEAD_DIM * (which + 1)]
            value_turned[which, HEAD_DIM:, span] = jnp.ones((RANK_UNIT, ROW_BLOCK), LOW)
    for first in range(0, 2 * half, ROW_BLOCK):
        span = slice(first, first + ROW_BLOCK)
        query = held[0, span] * jnp.asarray(HEAD_DIM**-0.5, LOW)
        mixes = []
        totals = []
        for which in (0, 1):
            one_query = query * masks[which]
            largest = None
            scores = []
            for begin, end in causal_spans(first):
                score = mm_nt(held[1, begin:end], one_query)
                if begin == first:
                    score = jnp.where(keep, score, -1e30)
                top = jnp.max(score, axis=0, keepdims=True)
                largest = top if largest is None else jnp.maximum(largest, top)
                scores.append(score)
            mixed = None
            for (begin, end), score in zip(causal_spans(first), scores):
                weights = jnp.exp(score - largest).astype(LOW)
                part = mm(value_turned[which, :, begin:end], weights)
                mixed = part if mixed is None else mixed + part
            summed = mixed[HEAD_DIM : HEAD_DIM + 1]
            mixes.append(mixed[:HEAD_DIM] * (1.0 / summed))
            totals.append(jnp.broadcast_to(jnp.log(summed) + largest, (HEAD_DIM, ROW_BLOCK)))
        result[span] = jnp.concatenate(mixes, axis=0).T.astype(LOW)
        logs[span] = jnp.concatenate(totals, axis=0).T

    @pl.when(is_first)
    def _():
        out_own_ref[...] = result[:half]
        out_other_ref[...] = result[half:]
        log_own_ref[...] = logs[:half]
        log_other_ref[...] = logs[half:]

    @pl.when(jnp.logical_not(is_first))
    def _():
        out_own_ref[...] = result[half:]
        out_other_ref[...] = result[:half]
        log_own_ref[...] = logs[half:]
        log_other_ref[...] = logs[:half]


def self_forward(meta, own, other):
    _, half, local = own.shape
    pair = 2 * HEAD_DIM
    three = pl.BlockSpec((3, half, pair), lambda p, m: (0, 0, p))
    one = pl.BlockSpec((half, pair), lambda p, m: (0, p))
    rows = shaped((half, local), LOW)
    logs = shaped((half, local), WIDE)
    return call(
        self_forward_body,
        (local // pair,),
        [three, three],
        (one, one, one, one),
        (rows, rows, logs, logs),
        [
            pltpu.VMEM((3, 2 * half, pair), LOW),
            pltpu.VMEM((2, HEAD_DIM + RANK_UNIT, 2 * half), LOW),
            pltpu.VMEM((2 * half, pair), LOW),
            pltpu.VMEM((2 * half, pair), WIDE),
        ],
        20 * half * half * local,
        16 * half * local,
        "self_forward",
        (meta, own, other),
    )


def three_parts(column):
    high = column.astype(LOW)
    rest = column - high.astype(WIDE)
    middle = rest.astype(LOW)
    return high, middle, (rest - middle.astype(WIDE)).astype(LOW)


def self_back_body(
    meta,
    own_ref,
    other_ref,
    z_own_ref,
    z_other_ref,
    log_own_ref,
    log_other_ref,
    grad_own_ref,
    grad_other_ref,
    _early,
    out_own_ref,
    out_other_ref,
    held,
    mixed,
    logs,
    grads,
    key_turned,
    query_turned,
    grad_turned,
    query_wide,
    key_wide,
    grad_wide,
    value_wide,
    key_total,
    value_total,
    result,
):
    half = own_ref.shape[1]
    is_first = meta[10] == 0
    order_frames(is_first, own_ref, other_ref, held.at[:, :half], held.at[:, half:])
    order_frames(is_first, grad_own_ref, grad_other_ref, grads.at[:half], grads.at[half:])
    order_frames(is_first, z_own_ref, z_other_ref, mixed.at[:half], mixed.at[half:])
    order_frames(is_first, log_own_ref, log_other_ref, logs.at[:half], logs.at[half:])
    masks = half_masks()
    scale = HEAD_DIM**-0.5
    lane = lax.broadcasted_iota(jnp.int32, (1, 2 * HEAD_DIM), 1)
    keep = causal_keep(ROW_BLOCK)
    for first in range(0, 2 * half, ROW_BLOCK):
        span = slice(first, first + ROW_BLOCK)
        grad = grads[span]
        product = grad.astype(WIDE) * mixed[span].astype(WIDE)
        query = held[0, span] * jnp.asarray(scale, LOW)
        key_turned[:, span] = turned(held[1, span])
        query_turned[:, span] = turned(query)
        grad_turned[:, span] = turned(grad)
        for which in (0, 1):
            spare = HEAD_DIM * (1 - which)
            marks = [jnp.where(lane == spare + i, 1.0, 0.0).astype(LOW) for i in range(3)]
            marked = marks[0] + marks[1] + marks[2]
            others = 1 - marked
            inner = jnp.sum(product * masks[which].astype(WIDE), axis=-1, keepdims=True)
            log_column = logs[span][:, HEAD_DIM * which : HEAD_DIM * which + 1]
            query_rows = query * masks[which]
            for part, mark in zip(three_parts(log_column), marks):
                query_rows = query_rows - part * mark
            query_wide[which, span] = query_rows
            grad_rows = grad * masks[which]
            for part, mark in zip(three_parts(inner), marks):
                grad_rows = grad_rows - part * mark
            grad_wide[which, span] = grad_rows
            key_wide[which, span] = held[1, span] * others + marked
            value_wide[which, span] = held[2, span] * others + marked
    key_total[...] = jnp.zeros_like(key_total)
    value_total[...] = jnp.zeros_like(value_total)
    for first in range(0, 2 * half, ROW_BLOCK):
        span = slice(first, first + ROW_BLOCK)
        query_grads = [None, None]
        for begin, end in causal_spans(first):
            for which in (0, 1):
                head = slice(HEAD_DIM * which, HEAD_DIM * (which + 1))
                score = mm_nt(key_wide[which, begin:end], query_wide[which, span])
                if begin == first:
                    score = jnp.where(keep, score, -1e30)
                prob = jnp.exp(score)
                prob_grad = mm_nt(value_wide[which, begin:end], grad_wide[which, span])
                score_grad = (prob * prob_grad).astype(LOW)
                value_total[head, begin:end] += mm_nt(grad_turned[head, span], prob.astype(LOW))
                key_total[head, begin:end] += mm_nt(query_turned[head, span], score_grad)
                part = mm(key_turned[head, begin:end], score_grad)
                query_grads[which] = part if query_grads[which] is None else query_grads[which] + part
        result[0, span] = (jnp.concatenate(query_grads, axis=0).T * scale).astype(LOW)
    for first in range(0, 2 * half, ROW_BLOCK):
        span = slice(first, first + ROW_BLOCK)
        result[1, span] = key_total[:, span].T.astype(LOW)
        result[2, span] = value_total[:, span].T.astype(LOW)

    @pl.when(is_first)
    def _():
        out_own_ref[...] = result[:, :half]
        out_other_ref[...] = result[:, half:]

    @pl.when(jnp.logical_not(is_first))
    def _():
        out_own_ref[...] = result[:, half:]
        out_other_ref[...] = result[:, :half]


def self_back(meta, own, other, z_own, z_other, log_own, log_other, grad_own, grad_other, after):
    _, half, local = own.shape
    pair = 2 * HEAD_DIM
    full = 2 * half
    three = pl.BlockSpec((3, half, pair), lambda p, m: (0, 0, p))
    one = pl.BlockSpec((half, pair), lambda p, m: (0, p))
    return call(
        self_back_body,
        (local // pair,),
        [three, three] + [one] * 6 + [IN_PLACE] * len(after),
        (three, three),
        (shaped(own.shape, LOW), shaped(own.shape, LOW)),
        [
            pltpu.VMEM((3, full, pair), LOW),
            pltpu.VMEM((full, pair), LOW),
            pltpu.VMEM((full, pair), WIDE),
            pltpu.VMEM((full, pair), LOW),
        ]
        + [pltpu.VMEM((pair, full), LOW)] * 3
        + [pltpu.VMEM((2, full, pair), LOW)] * 4
        + [pltpu.VMEM((pair, full), WIDE)] * 2
        + [pltpu.VMEM((3, full, pair), LOW)],
        500 * half * half * local,
        30 * half * local,
        "self_back",
        (meta, own, other, z_own, z_other, log_own, log_other, grad_own, grad_other, *after),
    )


def halves_of(ref, local):
    step = ref.shape[1] // 2
    return (
        ref[:, :step, :].reshape(local, ref.shape[2]),
        ref[:, step:, :].reshape(local, ref.shape[2]),
    )


def full_of(ref):
    return ref[...].reshape(ref.shape[0] * ref.shape[1], ref.shape[2])


def fetch_weights(step, order, sources, gathered, held, sems):
    copies = {}
    for which in order:
        copies[which] = (
            pltpu.make_async_copy(sources[which], held[2 * which], sems.at[2 * which]),
            pltpu.make_async_copy(gathered.at[:, which], held[2 * which + 1], sems.at[2 * which + 1]),
        )

    @pl.when(step == 0)
    def _():
        for which in order:
            for copy in copies[which]:
                copy.start()

    def ready(which):
        @pl.when(step == 0)
        def _():
            for copy in copies[which]:
                copy.wait()

        return held[2 * which], held[2 * which + 1]

    return ready


def pair_tiles(keys, values, pair, masks):
    span = slice(2 * HEAD_DIM * pair, 2 * HEAD_DIM * (pair + 1))
    key_part = keys[:, span]
    value_part = values[:, span]
    key_tile = jnp.concatenate([key_part * masks[0], key_part * masks[1]], axis=0)
    value_tile = jnp.concatenate([value_part * masks[0], value_part * masks[1]], axis=0)
    return key_tile, value_tile


def by_head(values, reduce):
    keys, rows = values.shape
    reduced = reduce(values.reshape(2, keys // 2, rows), axis=1, keepdims=True)
    return jnp.broadcast_to(reduced, (2, keys // 2, rows)).reshape(keys, rows)


def text_weights(key_tile, query):
    scores = mm_nt(key_tile, query)
    weights = jnp.exp(scores - by_head(scores, jnp.max))
    return weights * (1.0 / by_head(weights, jnp.sum))


def mix_text(query, keys, values, masks):
    mixed = []
    for pair in range(query.shape[1] // (2 * HEAD_DIM)):
        key_tile, value_tile = pair_tiles(keys, values, pair, masks)
        one_query = query[:, 2 * HEAD_DIM * pair : 2 * HEAD_DIM * (pair + 1)]
        weights = text_weights(key_tile, one_query * jnp.asarray(HEAD_DIM**-0.5, LOW))
        mixed.append(mm_tn(weights.astype(LOW), value_tile).astype(LOW))
    return jnp.concatenate(mixed, axis=1)


def middle_forward_body(
    _,
    x_ref,
    z_own_ref,
    z_other_ref,
    out_weight_ref,
    query_weight_ref,
    cross_weight_ref,
    gathered_ref,
    down3_ref,
    down3_other_ref,
    up3_ref,
    down4_ref,
    up4_ref,
    up4_other_ref,
    down7_ref,
    down7_other_ref,
    up7_ref,
    text_own_ref,
    text_other_ref,
    gain_two_ref,
    gain_three_ref,
    stream_one_ref,
    stream_two_ref,
    rows_three_ref,
    query_out_own_ref,
    query_out_other_ref,
    z2_own_ref,
    z2_other_ref,
    *scratch,
):
    local = z_own_ref.shape[1]
    masks = half_masks()
    ready = fetch_weights(
        pl.program_id(0),
        (0, 1, 2),
        (out_weight_ref, query_weight_ref, cross_weight_ref),
        gathered_ref,
        scratch[:6],
        scratch[6],
    )

    def out_product(own, other, which, down, down_other, up):
        rank = (mm_nt(down, own) + mm_nt(down_other, other)).astype(LOW)
        weight_own, weight_other_ref = ready(which)
        first, second = halves_of(weight_other_ref, local)
        product = mm(own, weight_own[...]) + mm_tn(rank, up)
        return product + jnp.concatenate([mm(other, first), mm(other, second)], axis=1)

    stream = x_ref[...].astype(WIDE) + out_product(
        z_own_ref[...],
        z_other_ref[...],
        0,
        down3_ref[0, 0],
        down3_other_ref[...],
        up3_ref[0, 0],
    )
    stream_one_ref[...] = stream
    rows_two = norm_rows(stream, gain_two_ref[...])[0].astype(LOW)
    rank = low_rank(down4_ref[0, 0], rows_two)
    query_own_ref, query_other_ref = ready(1)
    query_own = (mm(rows_two, query_own_ref[...]) + mm_tn(rank, up4_ref[0, 0])).astype(LOW)
    query_other = (
        mm(rows_two, full_of(query_other_ref)) + mm_tn(rank, up4_other_ref[...])
    ).astype(LOW)
    query_out_own_ref[...] = query_own
    query_out_other_ref[...] = query_other
    z2_own = mix_text(query_own, text_own_ref[0], text_own_ref[1], masks)
    z2_other = mix_text(query_other, text_other_ref[0], text_other_ref[1], masks)
    z2_own_ref[...] = z2_own
    z2_other_ref[...] = z2_other
    stream = stream + out_product(
        z2_own,
        z2_other,
        2,
        down7_ref[0, 0],
        down7_other_ref[...],
        up7_ref[0, 0],
    )
    stream_two_ref[...] = stream
    rows_three_ref[...] = norm_rows(stream, gain_three_ref[...])[0].astype(LOW)


def chosen(table, entry, slot):
    shape = (1, 1) + table.shape[2:]
    return pl.BlockSpec(
        shape, lambda t, m: (entry, m[slot], 0, 0), pipeline_mode=pl.Buffered(1)
    )


def middle_specs(weights, gathered, tables, packed):
    attention_down, attention_up, cross_down, cross_up = tables
    rank = (RANK_UNIT, gathered.shape[3])
    specs = [
        IN_PLACE,
        IN_PLACE,
        IN_PLACE,
        IN_PLACE,
        chosen(attention_down, 0, 3),
        whole(rank, (0, 0)),
        chosen(attention_up, 0, 3),
        chosen(cross_down, 0, 4),
        chosen(cross_up, 0, 4),
        whole(rank, (0, 2)),
        chosen(attention_down, 1, 7),
        whole(rank, (0, 1)),
        chosen(attention_up, 1, 7),
    ]
    args = weights + (
        gathered,
        attention_down,
        packed,
        attention_up,
        cross_down,
        cross_up,
        packed,
        attention_down,
        packed,
        attention_up,
    )
    return specs, args


def middle_scratch(weights, gathered):
    shards, _, depth, local = gathered.shape
    held = []
    for weight in weights:
        held += [pltpu.VMEM(weight.shape, LOW), pltpu.VMEM((shards, depth, local), LOW)]
    return held + [pltpu.SemaphoreType.DMA((2 * len(weights),))]


def middle_forward(meta, x, z_own, z_other, weights, gathered, tables, packed, text_own, text_other, gains):
    frames, width = x.shape
    local = z_own.shape[1]
    block = min(256, frames)
    wide = pl.BlockSpec((block, width), lambda t, m: (t, 0))
    narrow = pl.BlockSpec((block, local), lambda t, m: (t, 0))
    specs, args = middle_specs(weights, gathered, tables, packed)
    return call(
        middle_forward_body,
        (frames // block,),
        [wide, narrow, narrow]
        + specs
        + [whole(text_own.shape), whole(text_other.shape), whole((1, width)), whole((1, width))],
        (wide, wide, wide, narrow, narrow, narrow, narrow),
        (
            shaped((frames, width), WIDE),
            shaped((frames, width), WIDE),
            shaped((frames, width), LOW),
            shaped((frames, local), LOW),
            shaped((frames, local), LOW),
            shaped((frames, local), LOW),
            shaped((frames, local), LOW),
        ),
        middle_scratch(weights, gathered),
        6 * frames * width * width,
        6 * width * width + 20 * frames * width,
        "middle_forward",
        (meta, x, z_own, z_other) + args + (text_own, text_other) + gains,
    )


def middle_back_body(
    meta,
    last,
    grad_ref,
    stream_one_ref,
    z_own_ref,
    z_other_ref,
    query_in_own_ref,
    query_in_other_ref,
    z2_own_ref,
    z2_other_ref,
    out_weight_ref,
    query_weight_ref,
    cross_weight_ref,
    gathered_ref,
    down3_ref,
    down3_other_ref,
    up3_ref,
    down4_ref,
    up4_ref,
    up4_other_ref,
    down7_ref,
    down7_other_ref,
    up7_ref,
    text_own_ref,
    text_other_ref,
    gain_two_ref,
    grad_one_ref,
    dz_own_ref,
    dz_other_ref,
    text_grad_own_ref,
    text_grad_other_ref,
    mine_ref,
    theirs_ref,
    key_total,
    value_total,
    ga3_ref,
    gb3_ref,
    ga4_ref,
    gb4_ref,
    ga7_ref,
    gb7_ref,
    *scratch,
):
    step = pl.program_id(0)
    ready = fetch_weights(
        step,
        (2, 1, 0),
        (out_weight_ref, query_weight_ref, cross_weight_ref),
        gathered_ref,
        scratch[:6],
        scratch[6],
    )
    local = z_own_ref.shape[1]
    pairs = local // (2 * HEAD_DIM)
    left = lane_halves()
    masks = half_masks()
    scale = jnp.asarray(HEAD_DIM**-0.5, LOW)

    @pl.when(step == 0)
    def _():
        key_total[...] = jnp.zeros_like(key_total)
        value_total[...] = jnp.zeros_like(value_total)
        for ref in (ga3_ref, gb3_ref, ga4_ref, gb4_ref, ga7_ref, gb7_ref):
            ref[...] = jnp.zeros_like(ref)

    def out_back(grad, own, other, which, down, down_other, up, ga_ref, gb_ref):
        rank = (mm_nt(down, own) + mm_nt(down_other, other)).astype(LOW)
        grad_rank = low_rank(up, grad)
        ga_ref[:, :local] += mm(grad_rank, own)
        ga_ref[:, local:] += mm(grad_rank, other)
        gb_ref[...] += mm(rank, grad)
        weight_own, weight_other_ref = ready(which)
        first, second = halves_of(weight_other_ref, local)
        middle = grad.shape[1] // 2
        grad_own = mm_nt(grad, weight_own[...]) + mm_tn(grad_rank, down)
        grad_other = (
            mm_nt(grad[:, :middle], first)
            + mm_nt(grad[:, middle:], second)
            + mm_tn(grad_rank, down_other)
        )
        return grad_own.astype(LOW), grad_other.astype(LOW)

    grad = grad_ref[...]
    dz2_own, dz2_other = out_back(
        grad.astype(LOW),
        z2_own_ref[...],
        z2_other_ref[...],
        2,
        down7_ref[0, 0],
        down7_other_ref[...],
        up7_ref[0, 0],
        ga7_ref,
        gb7_ref,
    )

    def text_back(query, dz2, keys, values, part):
        query_grads = []
        for pair in range(pairs):
            span = slice(2 * HEAD_DIM * pair, 2 * HEAD_DIM * (pair + 1))
            key_tile, value_tile = pair_tiles(keys, values, pair, masks)
            one_query = query[:, span] * scale
            one_grad = dz2[:, span]
            probs = text_weights(key_tile, one_query)
            prob_grads = mm_nt(value_tile, one_grad)
            inner = by_head(probs * prob_grads, jnp.sum)
            score_grads = (probs * (prob_grads - inner)).astype(LOW)
            query_grads.append((mm_tn(score_grads, key_tile) * HEAD_DIM**-0.5).astype(LOW))
            key_total[part, pair] += mm(score_grads, one_query)
            value_total[part, pair] += mm(probs.astype(LOW), one_grad)
        return jnp.concatenate(query_grads, axis=1)

    dq_own = text_back(query_in_own_ref[...], dz2_own, text_own_ref[0], text_own_ref[1], 0)
    dq_other = text_back(query_in_other_ref[...], dz2_other, text_other_ref[0], text_other_ref[1], 1)

    rows_two, normed, inverse = norm_rows(stream_one_ref[...], gain_two_ref[...])
    rows_two = rows_two.astype(LOW)
    rank = low_rank(down4_ref[0, 0], rows_two)
    grad_rank = (mm_nt(up4_ref[0, 0], dq_own) + mm_nt(up4_other_ref[...], dq_other)).astype(LOW)
    ga4_ref[...] += mm(grad_rank, rows_two)
    gb4_ref[:, :local] += mm(rank, dq_own)
    gb4_ref[:, local:] += mm(rank, dq_other)
    query_own_ref, query_other_ref = ready(1)
    grad_rows = (
        mm_nt(dq_own, query_own_ref[...])
        + mm_nt(dq_other, full_of(query_other_ref))
        + mm_tn(grad_rank, down4_ref[0, 0])
    )
    grad = grad + norm_back(grad_rows, gain_two_ref[...], normed, inverse)
    grad_one_ref[...] = grad
    dz_own, dz_other = out_back(
        grad.astype(LOW),
        z_own_ref[...],
        z_other_ref[...],
        0,
        down3_ref[0, 0],
        down3_other_ref[...],
        up3_ref[0, 0],
        ga3_ref,
        gb3_ref,
    )
    dz_own_ref[...] = dz_own
    dz_other_ref[...] = dz_other

    @pl.when(step == last)
    def _():
        split_columns(meta, mine_ref, theirs_ref, 0, ga4_ref)
        own_columns(mine_ref, theirs_ref, local, gb4_ref)
        own_columns(mine_ref, theirs_ref, 2 * local, ga3_ref)
        own_columns(mine_ref, theirs_ref, 3 * local, ga7_ref)
        split_columns(meta, mine_ref, theirs_ref, 4 * local, gb3_ref)
        split_columns(meta, mine_ref, theirs_ref, 5 * local, gb7_ref)
        for total, slot in ((key_total, 0), (value_total, 1)):
            for part, ref in ((0, text_grad_own_ref), (1, text_grad_other_ref)):
                for pair in range(pairs):
                    span = slice(2 * HEAD_DIM * pair, 2 * HEAD_DIM * (pair + 1))
                    tile = total[part, pair]
                    ref[slot, :, span] = jnp.where(left, tile[:HEAD_DIM], tile[HEAD_DIM:]).astype(ref.dtype)


def middle_back(
    meta, grad, stream_one, z_own, z_other, q_own, q_other, z2_own, z2_other,
    weights, gathered, tables, packed, text_own, text_other, gain,
):
    frames, width = grad.shape
    local = z_own.shape[1]
    pairs = local // (2 * HEAD_DIM)
    block = min(256, frames)
    wide = pl.BlockSpec((block, width), lambda t, m: (t, 0))
    narrow = pl.BlockSpec((block, local), lambda t, m: (t, 0))
    specs, args = middle_specs(weights, gathered, tables, packed)
    rank = (RANK_UNIT, width)
    packs = (RANK_UNIT, 6 * local)
    steps = frames // block
    return call(
        lambda m, *refs: middle_back_body(m, steps - 1, *refs),
        (steps,),
        [wide, wide] + [narrow] * 6 + specs + [whole(text_own.shape), whole(text_other.shape), whole((1, width))],
        (wide, narrow, narrow, whole(text_own.shape), whole(text_own.shape), whole(packs), whole(packs)),
        (
            shaped((frames, width), WIDE),
            shaped((frames, local), LOW),
            shaped((frames, local), LOW),
            shaped(text_own.shape, WIDE),
            shaped(text_own.shape, LOW),
            shaped(packs, WIDE),
            shaped(packs, LOW),
        ),
        [
            pltpu.VMEM((2, pairs, 2 * HEAD_DIM, 2 * HEAD_DIM), WIDE),
            pltpu.VMEM((2, pairs, 2 * HEAD_DIM, 2 * HEAD_DIM), WIDE),
        ]
        + [pltpu.VMEM(rank, WIDE)] * 6
        + middle_scratch(weights, gathered),
        6 * frames * width * width,
        6 * width * width + 24 * frames * width,
        "middle_back",
        (meta, grad, stream_one, z_own, z_other, q_own, q_other, z2_own, z2_other)
        + args
        + (text_own, text_other, gain),
    )


def feed_tile(
    rows_ref, cot_ref, up_weight, down_weight, up_rank, down_rank,
    ga9_ref, gb8_ref, branch, grad_rows, rank9, grad_rank8, rank8, grad_rank9,
):
    frames = rows_ref.shape[0]
    block = min(256, frames)
    ga9 = None
    gb8 = None
    for first in range(0, frames, block):
        span = slice(first, first + block)
        rows = rows_ref[span]
        cot = cot_ref[span]
        pre = mm(rows, up_weight) + mm_tn(rank8[:, span], up_rank)
        grad_hidden = mm_nt(cot, down_weight) + mm_tn(grad_rank9[:, span], down_rank)
        hidden, slope = gelu_parts(pre)
        hidden = hidden.astype(LOW)
        grad_pre = (grad_hidden * slope).astype(LOW)
        branch[span] += mm(hidden, down_weight)
        rank9[:, span] += mm_nt(down_rank, hidden)
        grad_rows[span] += mm_nt(grad_pre, up_weight)
        grad_rank8[:, span] += mm_nt(up_rank, grad_pre)
        one = mm(grad_rank9[:, span], hidden)
        two = mm(rank8[:, span], grad_pre)
        ga9 = one if ga9 is None else ga9 + one
        gb8 = two if gb8 is None else gb8 + two
    ga9_ref[...] = ga9.astype(ga9_ref.dtype)
    gb8_ref[...] = gb8.astype(gb8_ref.dtype)


def feed_own_body(
    _, rows_ref, cot_ref, up_weight_ref, down_weight_ref, up_rank_ref, down_rank_ref,
    down8_ref, up9_ref,
    branch_ref, grad_rows_ref, rank9_ref, grad_rank8_ref, ga9_ref, gb8_ref,
    rank8, grad_rank9,
):
    @pl.when(pl.program_id(0) == 0)
    def _():
        rank8[...] = low_rank(down8_ref[0], rows_ref[...])
        grad_rank9[...] = low_rank(up9_ref[0], cot_ref[...])
        for ref in (branch_ref, grad_rows_ref, rank9_ref, grad_rank8_ref):
            ref[...] = jnp.zeros_like(ref)

    feed_tile(
        rows_ref, cot_ref, up_weight_ref[...], down_weight_ref[...], up_rank_ref[0], down_rank_ref[0],
        ga9_ref, gb8_ref, branch_ref, grad_rows_ref, rank9_ref, grad_rank8_ref, rank8, grad_rank9,
    )


def table_tile(tile, slot):
    return pl.BlockSpec((1, RANK_UNIT, tile), lambda t, m: (m[slot], 0, t))


def feed_own(meta, rows, cot, up_weight, down_weight, input_down, input_up, output_down, output_up, tile):
    frames, width = rows.shape
    hidden = up_weight.shape[1]
    grads = pl.BlockSpec((RANK_UNIT, tile), lambda t, m: (0, t))
    picked = pl.BlockSpec((1, RANK_UNIT, width), lambda t, m: (m[8], 0, 0))
    picked_out = pl.BlockSpec((1, RANK_UNIT, width), lambda t, m: (m[9], 0, 0))
    rank = (RANK_UNIT, frames)
    return call(
        feed_own_body,
        (hidden // tile,),
        [
            whole((frames, width)),
            whole((frames, width)),
            pl.BlockSpec((width, tile), lambda t, m: (0, t)),
            pl.BlockSpec((tile, width), lambda t, m: (t, 0)),
            table_tile(tile, 8),
            table_tile(tile, 9),
            picked,
            picked_out,
        ],
        (whole((frames, width)), whole((frames, width)), whole(rank), whole(rank), grads, grads),
        (
            shaped((frames, width), WIDE),
            shaped((frames, width), WIDE),
            shaped(rank, WIDE),
            shaped(rank, WIDE),
            shaped((RANK_UNIT, hidden), WIDE),
            shaped((RANK_UNIT, hidden), WIDE),
        ),
        [pltpu.VMEM(rank, LOW), pltpu.VMEM(rank, LOW)],
        8 * frames * width * hidden,
        4 * width * hidden + 12 * frames * width,
        "feed_own",
        (meta, rows, cot, up_weight, down_weight, input_up, output_down, input_down, output_up),
    )


def feed_other_body(
    meta, last, rows_ref, cot_ref, up_weight_ref, down_weight_ref, up_rank_ref, down_rank_ref,
    down8_ref, up9_ref, branch_in_ref, grad_rows_in_ref, rank9_in_ref, grad_rank8_in_ref,
    stream_ref, gain_ref,
    out_ref, grad_ref, ga9_ref, gb8_ref, mine_ref, theirs_ref,
    branch, grad_rows, rank9, grad_rank8, rank8, grad_rank9, ga8_ref, gb9_ref, branch_in, grad_rows_in, stream_in, sems,
):
    step = pl.program_id(0)
    copies = [
        pltpu.make_async_copy(source, target, sems.at[i])
        for i, (source, target) in enumerate(
            ((branch_in_ref, branch_in), (grad_rows_in_ref, grad_rows_in), (stream_ref, stream_in))
        )
    ]

    @pl.when(step == 0)
    def _():
        for copy in copies:
            copy.start()
        rank8[...] = low_rank(down8_ref[0], rows_ref[...])
        grad_rank9[...] = low_rank(up9_ref[0], cot_ref[...])
        branch[...] = jnp.zeros_like(branch)
        grad_rows[...] = jnp.zeros_like(grad_rows)
        rank9[...] = rank9_in_ref[...]
        grad_rank8[...] = grad_rank8_in_ref[...]

    shards, _, depth, tile = up_weight_ref.shape
    up_weight = up_weight_ref[...].reshape(shards * depth, tile)
    down_weight = down_weight_ref[...].reshape(tile, down_weight_ref.shape[3])
    feed_tile(
        rows_ref, cot_ref, up_weight, down_weight, up_rank_ref[...], down_rank_ref[...],
        ga9_ref, gb8_ref, branch, grad_rows, rank9, grad_rank8, rank8, grad_rank9,
    )

    @pl.when(step == last)
    def _():
        for copy in copies:
            copy.wait()
        frames = rows_ref.shape[0]
        block = min(128, frames)
        last8 = grad_rank8[...].astype(LOW)
        last9 = rank9[...].astype(LOW)
        ga8_ref[...] = mm(last8, rows_ref[...])
        gb9_ref[...] = mm(last9, cot_ref[...])
        split_columns(meta, mine_ref, theirs_ref, 0, ga8_ref)
        split_columns(meta, mine_ref, theirs_ref, ga8_ref.shape[1] // 2, gb9_ref)
        for first in range(0, frames, block):
            span = slice(first, first + block)
            stream = stream_in[span]
            out = stream + (branch[span] + branch_in[span]) + mm_tn(last9[:, span], up9_ref[0])
            out_ref[span] = out.astype(LOW)
            _, normed, inverse = norm_rows(stream, gain_ref[...])
            grad = grad_rows[span] + grad_rows_in[span] + mm_tn(last8[:, span], down8_ref[0])
            grad_ref[span] = cot_ref[span].astype(WIDE) + norm_back(
                grad, gain_ref[...], normed, inverse
            )


def feed_other(
    meta, rows, cot, gathered, packed, first_pack, input_down, output_up, carried, stream, gain, tile
):
    frames, width = rows.shape
    shards, quarters, depth, _ = gathered.shape
    hidden = quarters // 2 * width
    per_half = width // tile
    own_shards = tile // (quarters // 2 * depth)
    down_first = quarters // 2
    grads = pl.BlockSpec((RANK_UNIT, tile), lambda t, m: (0, t))
    picked = pl.BlockSpec((1, RANK_UNIT, width), lambda t, m: (m[8], 0, 0))
    picked_out = pl.BlockSpec((1, RANK_UNIT, width), lambda t, m: (m[9], 0, 0))
    rank = (RANK_UNIT, frames)
    steps = hidden // tile
    full = whole((frames, width))
    wide = pltpu.VMEM((frames, width), WIDE)
    return call(
        lambda m, *refs: feed_other_body(m, steps - 1, *refs),
        (steps,),
        [
            full,
            full,
            pl.BlockSpec(
                (shards, 1, depth, tile),
                lambda t, m: (0, down_first + t // per_half, 0, t % per_half),
            ),
            pl.BlockSpec((own_shards, down_first, depth, width), lambda t, m: (t, 0, 0, 0)),
            pl.BlockSpec((RANK_UNIT, tile), lambda t, m: (0, first_pack // tile + t)),
            pl.BlockSpec((RANK_UNIT, tile), lambda t, m: (0, (first_pack + hidden) // tile + t)),
            picked,
            picked_out,
            IN_PLACE,
            IN_PLACE,
            whole(rank),
            whole(rank),
            IN_PLACE,
            whole((1, width)),
        ],
        (full, full, grads, grads, whole((RANK_UNIT, width)), whole((RANK_UNIT, width))),
        (
            shaped((frames, width), LOW),
            shaped((frames, width), WIDE),
            shaped((RANK_UNIT, hidden), LOW),
            shaped((RANK_UNIT, hidden), LOW),
            shaped((RANK_UNIT, width), WIDE),
            shaped((RANK_UNIT, width), LOW),
        ),
        [
            wide,
            wide,
            pltpu.VMEM(rank, WIDE),
            pltpu.VMEM(rank, WIDE),
            pltpu.VMEM(rank, LOW),
            pltpu.VMEM(rank, LOW),
            pltpu.VMEM((RANK_UNIT, width), WIDE),
            pltpu.VMEM((RANK_UNIT, width), WIDE),
            wide,
            wide,
            wide,
            pltpu.SemaphoreType.DMA((3,)),
        ],
        8 * frames * width * hidden,
        4 * width * hidden + 24 * frames * width,
        "feed_other",
        (meta, rows, cot, gathered, gathered, packed, packed, input_down, output_up)
        + tuple(carried)
        + (stream, gain),
    )


def last_norm_body(_, x_ref, own_ref, other_ref, grad_ref, gain_ref, after_ref, out_ref):
    _, normed, inverse = norm_rows(x_ref[...].astype(WIDE), gain_ref[...])
    total = own_ref[...] + other_ref[...].astype(WIDE)
    out_ref[...] = grad_ref[...] + norm_back(total, gain_ref[...], normed, inverse)


def last_norm(meta, x, own, other, grad, gain, after):
    frames, width = x.shape
    block = min(256, frames)
    rows = pl.BlockSpec((block, width), lambda t, _: (t, 0))
    return call(
        last_norm_body,
        (frames // block,),
        [rows, rows, rows, rows, whole((1, width)), IN_PLACE],
        rows,
        shaped(x.shape, WIDE),
        [],
        20 * x.size,
        16 * x.size,
        "last_norm",
        (meta, x, own, other, grad, gain, after),
        vmem=VMEM_BYTES // 2,
    )


def on_pair(
    inputs,
    encoder_text_states,
    cotangent,
    clip_adapter_index,
    self_norm_gain,
    cross_norm_gain,
    feed_norm_gain,
    self_query_key_value_weight,
    self_output_weight,
    cross_query_weight,
    cross_key_value_weight,
    cross_output_weight,
    up_weight,
    down_weight,
    self_first_factors,
    self_second_factors,
    cross_first_factors,
    cross_second_factors,
    attention_first_factors,
    attention_second_factors,
    input_first_factors,
    input_second_factors,
    output_first_factors,
    output_second_factors,
):
    x = inputs[0]
    text = encoder_text_states[0]
    cot = cotangent[0]
    width = x.shape[1]
    local = self_output_weight.shape[0]
    hidden = up_weight.shape[1]
    slots = input_first_factors.shape[0]
    group_count = lax.axis_size("dp")
    place = lax.axis_index("dp")
    side = lax.axis_index("tensor")
    picks = clip_adapter_index[0]
    meta = jnp.concatenate([picks, jnp.stack([side, place]).astype(jnp.int32)])
    gain_one, gain_two, gain_three = (
        vec.reshape(1, width) for vec in (self_norm_gain, cross_norm_gain, feed_norm_gain)
    )

    def swap(array):
        return lax.ppermute(array, "tensor", [(0, 1), (1, 0)])

    depth = width // group_count
    step = local // group_count

    def share(weight, size):
        return lax.dynamic_slice_in_dim(weight, place * size, size, axis=0)

    def side_by_side(rows, count):
        return rows.reshape(rows.shape[0], count, -1).transpose(1, 0, 2)

    out_share = side_by_side(share(self_output_weight, step), 2).reshape(depth, local)
    query_share = share(cross_query_weight, depth)
    cross_share = side_by_side(share(cross_output_weight, step), 2).reshape(depth, local)
    share_one = swap(jnp.stack([out_share, query_share, cross_share]))
    gathered_one = lax.all_gather(share_one, "dp", axis=0)

    rows_one = first_norm(meta, x, gain_one)
    rows_one_other = swap(rows_one)
    factors = picked_factors(
        meta,
        [
            (attention_first_factors, 0, 3),
            (attention_first_factors, 1, 7),
            (cross_second_factors, 0, 4),
            (cross_second_factors, 0, 4),
            (input_second_factors, None, 8),
            (output_first_factors, None, 9),
        ],
    )
    packed = swap(factors)
    first_pack = 4 * local

    heads_own = project_heads(
        meta, rows_one, self_query_key_value_weight, self_first_factors, self_second_factors, 0, 0, "own_heads"
    )
    text_own = project_heads(
        meta, text, cross_key_value_weight, cross_first_factors, cross_second_factors, 5, 1, "text_heads"
    )
    text_other = swap(text_own)
    share_two = feed_share(
        meta, down_weight, up_weight, depth, (heads_own, text_own, rows_one_other, factors)
    )
    heads_other = project_heads(
        meta, rows_one_other, self_query_key_value_weight, self_first_factors, self_second_factors,
        0, 0, "other_heads", (share_two,),
    )
    z_own_frames, z_other_frames, log_own, log_other = self_forward(meta, heads_own, heads_other)
    share_two, z_other_frames = lax.optimization_barrier((swap(share_two), z_other_frames))
    gathered_two = lax.all_gather(share_two, "dp", axis=0)
    z_other_heads = swap(z_other_frames)
    weights = (self_output_weight, cross_query_weight, cross_output_weight)
    tables = (attention_first_factors, attention_second_factors, cross_first_factors, cross_second_factors)
    stream_one, stream_two, rows_three, q_own, q_other, z2_own, z2_other = middle_forward(
        meta, x, z_own_frames, z_other_heads, weights, gathered_one, tables, packed,
        text_own, text_other, (gain_two, gain_three),
    )
    tile = local
    branch, grad_rows, rank9, grad_rank8, ga9_own, gb8_own = feed_own(
        meta, rows_three, cot, up_weight, down_weight, input_first_factors, input_second_factors,
        output_first_factors, output_second_factors, tile,
    )
    output, grad_two, ga9_other, gb8_other, feed_mine, feed_theirs = feed_other(
        meta, rows_three, cot, gathered_two, packed, first_pack, input_first_factors,
        output_second_factors, (branch, grad_rows, rank9, grad_rank8), stream_two, gain_three, tile,
    )

    gb8_received = swap(gb8_other)
    ga9_received = swap(ga9_other)
    feed_received = swap(feed_theirs)

    (
        grad_one, dz_own_heads, dz_other_heads, text_grad_own, text_grad_other, mine, theirs,
    ) = middle_back(
        meta, grad_two, stream_one, z_own_frames, z_other_heads, q_own, q_other, z2_own, z2_other,
        weights, gathered_one, tables, packed, text_own, text_other, gain_two,
    )
    gb8_received, ga9_received, feed_received, dz_other_heads, theirs, text_grad_other = lax.optimization_barrier(
        (gb8_received, ga9_received, feed_received, dz_other_heads, theirs, text_grad_other)
    )
    dz_other_frames = swap(dz_other_heads)

    unit = local
    hidden_units = hidden // unit
    labels = jnp.zeros((RANK_UNIT, 2 * HEAD_DIM), LOW).at[:, : picks.shape[0]].set(picks.astype(LOW)[None])
    early = jnp.concatenate(
        [
            join(mine, [swap(theirs)]),
            join(feed_mine, [feed_received]),
            join(jnp.concatenate([gb8_own, ga9_own], axis=1), [gb8_received, ga9_received]),
            labels,
        ],
        axis=1,
    )
    early_all = lax.all_gather(early, "dp", axis=0)
    grads_own, grads_other = self_back(
        meta, heads_own, heads_other, z_own_frames, z_other_frames, log_own, log_other,
        dz_own_heads, dz_other_frames, (early,),
    )
    text_grad_other, grads_own = lax.optimization_barrier((swap(text_grad_other), grads_own))
    text_heads_grad = (text_grad_own + text_grad_other.astype(WIDE)).astype(LOW)
    text_mine_rank, text_theirs_rank = rank_grads(
        meta, [text], [text_heads_grad], cross_first_factors, cross_second_factors, 5, 1, "text_ranks"
    )
    text_theirs_rank = swap(text_theirs_rank)
    mine, theirs = rank_grads(
        meta, [rows_one, rows_one_other], [grads_own, grads_other], self_first_factors,
        self_second_factors, 0, 0, "self_ranks",
    )
    partial_other = project_back_heads(
        meta, grads_other, self_query_key_value_weight, self_first_factors, self_second_factors,
        0, 0, LOW, "other_back", theirs,
    )
    labels = lax.dynamic_index_in_dim(early_all[:, :, -2 * HEAD_DIM :], place, axis=0, keepdims=False)
    late = jnp.concatenate(
        [join(mine, [swap(theirs)]), join(text_mine_rank, [text_theirs_rank]), labels], axis=1
    )
    late_all = lax.all_gather(late, "dp", axis=0)
    received = swap(partial_other)
    text_rows = project_back_heads(
        meta, text_heads_grad, cross_key_value_weight, cross_first_factors, cross_second_factors,
        5, 1, WIDE, "text_back", partial_other,
    )
    text_halves = (text_rows[:, : width // 2], text_rows[:, width // 2 :])
    text_mine = jnp.where(side == 0, text_halves[0], text_halves[1])
    text_theirs = jnp.where(side == 0, text_halves[1], text_halves[0])
    text_received = swap(text_theirs.astype(LOW))
    partial_own = project_back_heads(
        meta, grads_own, self_query_key_value_weight, self_first_factors, self_second_factors,
        0, 0, WIDE, "own_back", late,
    )
    sums = slot_sums(
        meta,
        early_all,
        [(4, 0, 0), (4, 1, 0), (3, 2, 0), (7, 2, 1), (3, 3, 0), (7, 3, 1), (8, 4, 0), (9, 5, 0)]
        + [(8, 6, i) for i in range(hidden_units)]
        + [(9, 7, i) for i in range(hidden_units)],
        [(1, unit), (1, unit), (2, unit), (2, unit), (None, unit), (None, unit), (None, hidden), (None, hidden)],
        slots, unit, "early_slots", (partial_own,),
    )
    sum_cross_a, sum_cross_b, sum_out_a, sum_out_b, sum_up_a, sum_down_b, sum_up_b, sum_down_a = sums
    received, text_received, sum_cross_a = lax.optimization_barrier((received, text_received, sum_cross_a))
    text_grad = text_mine + text_received.astype(WIDE)
    input_grad = last_norm(meta, x, partial_own, received, grad_one, gain_one, sum_cross_a)
    sum_self_a, sum_self_b, sum_cross_a, sum_cross_b = late_sums(
        meta, late_all,
        [(0, 0, 0), (1, 0, 1), (2, 0, 2), (0, 1, 0), (1, 1, 1), (2, 1, 2)]
        + [(5, 2, 1), (6, 2, 2), (5, 3, 1), (6, 3, 2)],
        [(3, unit), (3, unit), (3, unit), (3, unit)], slots, unit,
        {2: sum_cross_a, 3: sum_cross_b}, "late_slots", (input_grad,),
    )
    return (
        output[None],
        input_grad[None],
        text_grad[None],
        sum_self_a,
        sum_self_b,
        sum_cross_a,
        sum_cross_b,
        sum_out_a,
        sum_out_b,
        sum_up_a,
        sum_up_b,
        sum_down_a,
        sum_down_b,
    )


def solution(mesh):
    in_specs = (
        P("dp", "tensor", None),
        P("dp", None, None),
        P("dp", "tensor", None),
        P("dp", None),
        P(),
        P(),
        P(),
        P(None, None, "tensor"),
        P("tensor", None),
        P(None, "tensor"),
        P(None, None, "tensor"),
        P("tensor", None),
        P(None, "tensor"),
        P("tensor", None),
        P(),
        P(None, None, None, "tensor"),
        P(),
        P(None, None, None, "tensor"),
        P(None, None, None, "tensor"),
        P(),
        P(),
        P(None, None, "tensor"),
        P(None, None, "tensor"),
        P(),
    )
    out_specs = (
        P("dp", "tensor", None),
        P("dp", "tensor", None),
        P("dp", None, "tensor"),
        P(None, None, None, "tensor"),
        P(None, None, None, "tensor"),
        P(None, None, None, "tensor"),
        P(None, None, None, "tensor"),
        P(None, None, None, "tensor"),
        P(None, None, None, "tensor"),
        P(None, None, "tensor"),
        P(None, None, "tensor"),
        P(None, None, "tensor"),
        P(None, None, "tensor"),
    )
    layer = on_pair if mesh.shape["tensor"] == 2 else on_device
    return jax.shard_map(
        layer, mesh=mesh, in_specs=in_specs, out_specs=out_specs, check_vma=False
    )
```

```python
import jax
import jax.numpy as jnp
from jax import lax
from jax.experimental import pallas as pl
from jax.experimental.pallas import tpu as pltpu
from jax.sharding import PartitionSpec as P

HEAD_DIM = 64


epsilon = 1e-05


def split_dot(form, wide_part, narrow_part):
    high_part = wide_part.astype(jnp.bfloat16)
    rest_part = (wide_part - high_part.astype(jnp.float32)).astype(jnp.bfloat16)
    first = jnp.einsum(form, high_part, narrow_part, preferred_element_type=jnp.float32)
    return first + jnp.einsum(form, rest_part, narrow_part, preferred_element_type=jnp.float32)


def layer_norm(stream, gain_vec):
    centred = stream - jnp.mean(stream, axis=-1, keepdims=True)
    inverse = lax.rsqrt(jnp.mean(centred * centred, axis=-1, keepdims=True) + epsilon)
    normed = centred * inverse
    return (normed * gain_vec, normed, inverse)


def norm_back(grad_out, gain_vec, normed, inverse):
    grad_norm = grad_out * gain_vec
    mean_grad = jnp.mean(grad_norm, axis=-1, keepdims=True)
    mean_cross = jnp.mean(grad_norm * normed, axis=-1, keepdims=True)
    return inverse * (grad_norm - mean_grad - normed * mean_cross)


def spread_rows(local_rows):
    return lax.all_gather(local_rows.astype(jnp.bfloat16), "tensor", axis=1, tiled=True)


def reduce_grads(partial_sum):
    return lax.psum_scatter(
        partial_sum.astype(jnp.bfloat16), "tensor", scatter_dimension=1, tiled=True
    ).astype(jnp.float32)


def project_rows(act_rows, weight, output_choice, input_choice):
    low_rank = jnp.einsum(
        "ctd,crd->ctr", act_rows, output_choice, preferred_element_type=jnp.float32
    )
    result = jnp.einsum("ctd,de->cte", act_rows, weight, preferred_element_type=jnp.float32)
    result = result + split_dot("ctr,cre->cte", low_rank, input_choice)
    return (result, low_rank)


def project_back(grad_low, act_rows, weight, output_choice, input_choice, low_rank):
    grad_rank = jnp.einsum(
        "cte,cre->ctr", grad_low, input_choice, preferred_element_type=jnp.float32
    )
    grad_rows = jnp.einsum("cte,de->ctd", grad_low, weight, preferred_element_type=jnp.float32)
    grad_rows = grad_rows + split_dot("ctr,crd->ctd", grad_rank, output_choice)
    grad_down = split_dot("ctr,ctd->crd", grad_rank, act_rows)
    grad_up = split_dot("ctr,cte->cre", low_rank, grad_low)
    return (grad_rows, grad_down, grad_up)


def causal_frames(first_row, block_rows, key_count):
    query_at = first_row + jnp.arange(block_rows, dtype=jnp.int32)[:, None]
    key_at = jnp.arange(key_count, dtype=jnp.int32)[None, :]
    return key_at <= query_at


def attention_forward(queries, key_rows, value_rows, causal):
    frames = queries.shape[1]
    key_count = key_rows.shape[1]
    block_rows = min(512, frames)
    score_scale = HEAD_DIM ** (-0.5)
    outputs = []
    log_totals = []
    for first_row in range(0, frames, block_rows):
        key_end = first_row + block_rows if causal else key_count
        query_block = queries[:, first_row : first_row + block_rows]
        scores = (
            jnp.einsum(
                "cbhe,ckhe->chbk",
                query_block,
                key_rows[:, :key_end],
                preferred_element_type=jnp.float32,
            )
            * score_scale
        )
        if causal:
            scores = jnp.where(causal_frames(first_row, block_rows, key_end), scores, -1e30)
        largest = jnp.max(scores, axis=-1, keepdims=True)
        exponent = jnp.exp(scores - largest)
        summed = jnp.sum(exponent, axis=-1, keepdims=True)
        prob_low = (exponent / summed).astype(jnp.bfloat16)
        outputs.append(
            jnp.einsum(
                "chbk,ckhe->cbhe",
                prob_low,
                value_rows[:, :key_end],
                preferred_element_type=jnp.float32,
            )
        )
        log_totals.append(largest + jnp.log(summed))
    return (jnp.concatenate(outputs, axis=1), jnp.concatenate(log_totals, axis=2))


def attention_back(queries, key_rows, value_rows, log_totals, grad_mixed, causal):
    frames = queries.shape[1]
    key_count = key_rows.shape[1]
    block_rows = min(512, frames)
    score_scale = HEAD_DIM ** (-0.5)
    grad_keys = jnp.zeros(key_rows.shape, jnp.float32)
    grad_values = jnp.zeros(value_rows.shape, jnp.float32)
    grad_queries = []
    for first_row in range(0, frames, block_rows):
        key_end = first_row + block_rows if causal else key_count
        key_part = key_rows[:, :key_end]
        value_part = value_rows[:, :key_end]
        query_block = queries[:, first_row : first_row + block_rows]
        grad_block = grad_mixed[:, first_row : first_row + block_rows]
        scores = (
            jnp.einsum("cbhe,ckhe->chbk", query_block, key_part, preferred_element_type=jnp.float32)
            * score_scale
        )
        if causal:
            scores = jnp.where(causal_frames(first_row, block_rows, key_end), scores, -1e30)
        probs = jnp.exp(scores - log_totals[:, :, first_row : first_row + block_rows])
        grad_values = grad_values.at[:, :key_end].add(
            jnp.einsum(
                "chbk,cbhe->ckhe",
                probs.astype(jnp.bfloat16),
                grad_block,
                preferred_element_type=jnp.float32,
            )
        )
        grad_probs = jnp.einsum(
            "cbhe,ckhe->chbk", grad_block, value_part, preferred_element_type=jnp.float32
        )
        inner_sum = jnp.sum(probs * grad_probs, axis=-1, keepdims=True)
        grad_scores = (probs * (grad_probs - inner_sum)).astype(jnp.bfloat16)
        grad_queries.append(
            jnp.einsum("chbk,ckhe->cbhe", grad_scores, key_part, preferred_element_type=jnp.float32)
            * score_scale
        )
        grad_keys = grad_keys.at[:, :key_end].add(
            jnp.einsum(
                "chbk,cbhe->ckhe", grad_scores, query_block, preferred_element_type=jnp.float32
            )
            * score_scale
        )
    return (jnp.concatenate(grad_queries, axis=1), grad_keys, grad_values)


def gelu_exact(pre_act):
    return jax.nn.gelu(pre_act, approximate=False)


def on_device(
    inputs,
    encoder_text_states,
    cotangent,
    clip_adapter_index,
    self_norm_gain,
    cross_norm_gain,
    feed_norm_gain,
    self_query_key_value_weight,
    self_output_weight,
    cross_query_weight,
    cross_key_value_weight,
    cross_output_weight,
    up_weight,
    down_weight,
    self_first_factors,
    self_second_factors,
    cross_first_factors,
    cross_second_factors,
    attention_first_factors,
    attention_second_factors,
    input_first_factors,
    input_second_factors,
    output_first_factors,
    output_second_factors,
):
    adapter_slot_count = input_first_factors.shape[0]
    chooser = (
        clip_adapter_index[:, :, None]
        == jnp.arange(adapter_slot_count, dtype=jnp.int32)[None, None, :]
    ).astype(jnp.bfloat16)
    local_heads = self_output_weight.shape[0] // HEAD_DIM

    def choose_adapter_slot(adapter_slot_table, column_index):
        return jnp.einsum(
            "cn,npq->cpq",
            chooser[:, column_index],
            adapter_slot_table,
            preferred_element_type=jnp.float32,
        ).astype(jnp.bfloat16)

    def slot_grads(grad_pick, column_index):
        return split_dot("cpq,cn->npq", grad_pick, chooser[:, column_index])

    def split_heads(stacked):
        return stacked.reshape(stacked.shape[0], stacked.shape[1], local_heads, HEAD_DIM)

    def join_heads(stacked):
        return stacked.reshape(stacked.shape[0], stacked.shape[1], local_heads * HEAD_DIM)

    def out_forward(mixed_in, inner_layer):
        column_index = 3 + 4 * inner_layer
        input_choice = choose_adapter_slot(attention_second_factors[inner_layer], column_index)
        weight = self_output_weight if inner_layer == 0 else cross_output_weight
        output_choice = choose_adapter_slot(attention_first_factors[inner_layer], column_index)
        partial_out, low_rank = project_rows(mixed_in, weight, output_choice, input_choice)
        branch = lax.psum_scatter(
            partial_out.astype(jnp.bfloat16), "tensor", scatter_dimension=1, tiled=True
        ).astype(jnp.float32)
        kept_data = (mixed_in, weight, output_choice, input_choice, low_rank)
        return (branch, kept_data)

    def out_back(grad_stream, kept_data):
        mixed_in, weight, output_choice, input_choice, low_rank = kept_data
        grad_low = grad_stream.astype(jnp.bfloat16)
        grad_full = lax.all_gather(grad_low, "tensor", axis=1, tiled=True)
        grad_rows, grad_down, grad_up = project_back(
            grad_full, mixed_in, weight, output_choice, input_choice, low_rank
        )
        grad_mixed = grad_rows.astype(jnp.bfloat16)
        return (grad_mixed, grad_down, grad_up)

    stream = inputs.astype(jnp.float32)
    normed_value, normed_one, inverse_one = layer_norm(stream, self_norm_gain)
    rows_one = spread_rows(normed_value)
    self_down_factor = [
        choose_adapter_slot(self_first_factors[slot_number], slot_number)
        for slot_number in range(3)
    ]
    self_up_factor = [
        choose_adapter_slot(self_second_factors[slot_number], slot_number)
        for slot_number in range(3)
    ]
    self_parts = [
        project_rows(
            rows_one,
            self_query_key_value_weight[slot_number],
            self_down_factor[slot_number],
            self_up_factor[slot_number],
        )
        for slot_number in range(3)
    ]
    self_heads = [
        split_heads(self_parts[slot_number][0].astype(jnp.bfloat16)) for slot_number in range(3)
    ]
    mixed_one, totals_one = attention_forward(self_heads[0], self_heads[1], self_heads[2], True)
    mixed_one = join_heads(mixed_one).astype(jnp.bfloat16)
    branch_one, kept_one = out_forward(mixed_one, 0)
    stream_one = stream + branch_one
    normed_value, normed_two, inverse_two = layer_norm(stream_one, cross_norm_gain)
    rows_two = spread_rows(normed_value)
    cross_down_factor = [
        choose_adapter_slot(cross_first_factors[slot_number], 4 + slot_number)
        for slot_number in range(3)
    ]
    cross_up_factor = [
        choose_adapter_slot(cross_second_factors[slot_number], 4 + slot_number)
        for slot_number in range(3)
    ]
    query_full, query_rank = project_rows(
        rows_two, cross_query_weight, cross_down_factor[0], cross_up_factor[0]
    )
    key_full, key_rank = project_rows(
        encoder_text_states, cross_key_value_weight[0], cross_down_factor[1], cross_up_factor[1]
    )
    value_full, value_rank = project_rows(
        encoder_text_states, cross_key_value_weight[1], cross_down_factor[2], cross_up_factor[2]
    )
    query_two = split_heads(query_full.astype(jnp.bfloat16))
    key_two = split_heads(key_full.astype(jnp.bfloat16))
    value_two = split_heads(value_full.astype(jnp.bfloat16))
    mixed_two, totals_two = attention_forward(query_two, key_two, value_two, False)
    mixed_two = join_heads(mixed_two).astype(jnp.bfloat16)
    branch_two, kept_two = out_forward(mixed_two, 1)
    stream_two = stream_one + branch_two
    normed_value, normed_three, inverse_three = layer_norm(stream_two, feed_norm_gain)
    rows_three = spread_rows(normed_value)
    input_second_choice = choose_adapter_slot(input_first_factors, 8)
    input_first_choice = choose_adapter_slot(input_second_factors, 8)
    before, up_rank = project_rows(rows_three, up_weight, input_second_choice, input_first_choice)
    gelu_value, gelu_pull = jax.vjp(gelu_exact, before)
    hidden = gelu_value.astype(jnp.bfloat16)
    output_second_choice = choose_adapter_slot(output_first_factors, 9)
    output_first_choice = choose_adapter_slot(output_second_factors, 9)
    partial_out, down_rank = project_rows(
        hidden, down_weight, output_second_choice, output_first_choice
    )
    branch_three = lax.psum_scatter(
        partial_out.astype(jnp.bfloat16), "tensor", scatter_dimension=1, tiled=True
    ).astype(jnp.float32)
    output = (stream_two + branch_three).astype(jnp.bfloat16)
    grad_full = lax.all_gather(cotangent, "tensor", axis=1, tiled=True)
    grad_hidden, grad_down_a, grad_down_b = project_back(
        grad_full, hidden, down_weight, output_second_choice, output_first_choice, down_rank
    )
    grad_before = gelu_pull(grad_hidden)[0].astype(jnp.bfloat16)
    grad_rows, grad_up_a, grad_up_b = project_back(
        grad_before, rows_three, up_weight, input_second_choice, input_first_choice, up_rank
    )
    grad_stream = cotangent.astype(jnp.float32) + norm_back(
        reduce_grads(grad_rows), feed_norm_gain, normed_three, inverse_three
    )
    grad_mixed, grad_out_a_two, grad_out_b_two = out_back(grad_stream, kept_two)
    grad_query, grad_key, grad_value = attention_back(
        query_two, key_two, value_two, totals_two, split_heads(grad_mixed), False
    )
    grad_query = join_heads(grad_query).astype(jnp.bfloat16)
    grad_key = join_heads(grad_key).astype(jnp.bfloat16)
    grad_value = join_heads(grad_value).astype(jnp.bfloat16)
    grad_rows_query, cross_grad_a_zero, cross_grad_b_zero = project_back(
        grad_query,
        rows_two,
        cross_query_weight,
        cross_down_factor[0],
        cross_up_factor[0],
        query_rank,
    )
    grad_text_key, cross_grad_a_one, cross_grad_b_one = project_back(
        grad_key,
        encoder_text_states,
        cross_key_value_weight[0],
        cross_down_factor[1],
        cross_up_factor[1],
        key_rank,
    )
    grad_text_value, cross_grad_a_two, cross_grad_b_two = project_back(
        grad_value,
        encoder_text_states,
        cross_key_value_weight[1],
        cross_down_factor[2],
        cross_up_factor[2],
        value_rank,
    )
    normed_grad, text_grad = (
        lax.psum_scatter(
            grad_rows_query.astype(jnp.bfloat16), "tensor", scatter_dimension=1, tiled=True
        ).astype(jnp.float32),
        lax.psum_scatter(
            (grad_text_key + grad_text_value).astype(jnp.bfloat16),
            "tensor",
            scatter_dimension=2,
            tiled=True,
        ).astype(jnp.float32),
    )
    grad_stream = grad_stream + norm_back(normed_grad, cross_norm_gain, normed_two, inverse_two)
    grad_mixed, grad_out_a_one, grad_out_b_one = out_back(grad_stream, kept_one)
    grad_query, grad_key, grad_value = attention_back(
        self_heads[0], self_heads[1], self_heads[2], totals_one, split_heads(grad_mixed), True
    )
    self_grads = [
        join_heads(grad_query).astype(jnp.bfloat16),
        join_heads(grad_key).astype(jnp.bfloat16),
        join_heads(grad_value).astype(jnp.bfloat16),
    ]
    self_rows_total = jnp.zeros(rows_one.shape, jnp.float32)
    self_grad_a = []
    self_grad_b = []
    for slot_number in range(3):
        grad_rows, grad_a_part, grad_b_part = project_back(
            self_grads[slot_number],
            rows_one,
            self_query_key_value_weight[slot_number],
            self_down_factor[slot_number],
            self_up_factor[slot_number],
            self_parts[slot_number][1],
        )
        self_rows_total = self_rows_total + grad_rows
        self_grad_a.append(slot_grads(grad_a_part, slot_number))
        self_grad_b.append(slot_grads(grad_b_part, slot_number))
    input_grad = grad_stream + norm_back(
        reduce_grads(self_rows_total), self_norm_gain, normed_one, inverse_one
    )
    sum_self_a = jnp.stack(self_grad_a)
    sum_self_b = jnp.stack(self_grad_b)
    sum_cross_a = jnp.stack(
        [
            slot_grads(cross_grad_a_zero, 4),
            slot_grads(cross_grad_a_one, 5),
            slot_grads(cross_grad_a_two, 6),
        ]
    )
    sum_cross_b = jnp.stack(
        [
            slot_grads(cross_grad_b_zero, 4),
            slot_grads(cross_grad_b_one, 5),
            slot_grads(cross_grad_b_two, 6),
        ]
    )
    sum_out_a = jnp.stack([slot_grads(grad_out_a_one, 3), slot_grads(grad_out_a_two, 7)])
    sum_out_b = jnp.stack([slot_grads(grad_out_b_one, 3), slot_grads(grad_out_b_two, 7)])
    sum_up_a = slot_grads(grad_up_a, 8)
    sum_up_b = slot_grads(grad_up_b, 8)
    sum_down_a = slot_grads(grad_down_a, 9)
    sum_down_b = slot_grads(grad_down_b, 9)
    sum_self_a, sum_cross_a, sum_out_b, sum_up_a, sum_down_b = (
        lax.psum_scatter(
            sum_self_a.astype(jnp.bfloat16), "tensor", scatter_dimension=3, tiled=True
        ).astype(jnp.float32),
        lax.psum_scatter(
            sum_cross_a.astype(jnp.bfloat16), "tensor", scatter_dimension=3, tiled=True
        ).astype(jnp.float32),
        lax.psum_scatter(
            sum_out_b.astype(jnp.bfloat16), "tensor", scatter_dimension=3, tiled=True
        ).astype(jnp.float32),
        lax.psum_scatter(
            sum_up_a.astype(jnp.bfloat16), "tensor", scatter_dimension=2, tiled=True
        ).astype(jnp.float32),
        lax.psum_scatter(
            sum_down_b.astype(jnp.bfloat16), "tensor", scatter_dimension=2, tiled=True
        ).astype(jnp.float32),
    )
    totals = (
        lax.psum(sum_self_a.astype(jnp.bfloat16), "dp").astype(jnp.float32),
        lax.psum(sum_self_b.astype(jnp.bfloat16), "dp").astype(jnp.float32),
        lax.psum(sum_cross_a.astype(jnp.bfloat16), "dp").astype(jnp.float32),
        lax.psum(sum_cross_b.astype(jnp.bfloat16), "dp").astype(jnp.float32),
        lax.psum(sum_out_a.astype(jnp.bfloat16), "dp").astype(jnp.float32),
        lax.psum(sum_out_b.astype(jnp.bfloat16), "dp").astype(jnp.float32),
        lax.psum(sum_up_a.astype(jnp.bfloat16), "dp").astype(jnp.float32),
        lax.psum(sum_up_b.astype(jnp.bfloat16), "dp").astype(jnp.float32),
        lax.psum(sum_down_a.astype(jnp.bfloat16), "dp").astype(jnp.float32),
        lax.psum(sum_down_b.astype(jnp.bfloat16), "dp").astype(jnp.float32),
    )
    return (
        output,
        input_grad,
        text_grad,
        totals[0],
        totals[1],
        totals[2],
        totals[3],
        totals[4],
        totals[5],
        totals[6],
        totals[7],
        totals[8],
        totals[9],
    )


LOW = jnp.bfloat16
WIDE = jnp.float32
VMEM_BYTES = 58 * 1024 * 1024
RANK_UNIT = 16
COST_SCALE = 1


def mm(left, right, left_dim=1, right_dim=0):
    return lax.dot_general(
        left, right, (((left_dim,), (right_dim,)), ((), ())), preferred_element_type=WIDE
    )


def mm_nt(left, right):
    return mm(left, right, 1, 1)


def mm_tn(left, right):
    return mm(left, right, 0, 0)


def low_rank(factor, rows):
    return mm_nt(factor, rows).astype(LOW)


def norm_rows(rows, gain):
    centred = rows - jnp.mean(rows, axis=-1, keepdims=True)
    inverse = lax.rsqrt(jnp.mean(centred * centred, axis=-1, keepdims=True) + epsilon)
    normed = centred * inverse
    return normed * gain, normed, inverse


def lane_halves():
    lane = lax.broadcasted_iota(jnp.int32, (1, 2 * HEAD_DIM), 1)
    return lane < HEAD_DIM


def half_masks():
    left = lane_halves()
    first = jnp.where(left, 1.0, 0.0)
    return first.astype(LOW), (1.0 - first).astype(LOW)


def gelu_parts(pre):
    bell = jnp.exp(-0.5 * pre * pre)
    step = 1.0 / (1.0 + (0.3275911 * 0.7071067811865476) * jnp.abs(pre))
    tail = step * (
        0.5 * 0.254829592
        + step
        * (
            0.5 * -0.284496736
            + step
            * (0.5 * 1.421413741 + step * (0.5 * -1.453152027 + step * (0.5 * 1.061405429)))
        )
    )
    tail = tail * bell
    phi = jnp.where(pre >= 0.0, 1.0 - tail, tail)
    return pre * phi, phi + pre * bell * 0.3989422804014327


def whole(shape, where=None):
    place = (0,) * len(shape) if where is None else where
    return pl.BlockSpec(shape, lambda *_: place, pipeline_mode=pl.Buffered(1))


def call(body, grid, in_specs, out_specs, out_shape, scratch, flops, moved, name, args):
    return pl.pallas_call(
        body,
        grid_spec=pltpu.PrefetchScalarGridSpec(
            num_scalar_prefetch=1,
            grid=grid,
            in_specs=in_specs,
            out_specs=out_specs,
            scratch_shapes=scratch,
        ),
        out_shape=out_shape,
        compiler_params=pltpu.CompilerParams(
            dimension_semantics=("arbitrary",) * len(grid), vmem_limit_bytes=VMEM_BYTES
        ),
        cost_estimate=pl.CostEstimate(
            flops=flops // COST_SCALE, bytes_accessed=moved // COST_SCALE, transcendentals=0
        ),
        name=name,
    )(*args)


def shaped(shape, dtype):
    return jax.ShapeDtypeStruct(shape, dtype)


IN_PLACE = pl.BlockSpec(memory_space=pl.ANY)


def factors_body(_, *refs):
    out_ref = refs[-1]
    first = 0
    for ref in refs[:-1]:
        size = ref.shape[-1]
        out_ref[:, first : first + size] = ref[...]
        first += size


def picked_factors(meta, sources):
    specs = []
    total = 0
    for table, entry, slot in sources:
        if entry is None:
            spec = pl.BlockSpec((None,) + table.shape[1:], lambda t, m, slot=slot: (m[slot], 0, 0))
        else:
            spec = pl.BlockSpec(
                (None, None) + table.shape[2:], lambda t, m, entry=entry, slot=slot: (entry, m[slot], 0, 0)
            )
        specs.append(spec)
        total += table.shape[-1]
    shape = (RANK_UNIT, total)
    return call(
        factors_body, (1,), specs, whole(shape), shaped(shape, LOW), [], 0, 4 * RANK_UNIT * total,
        "picked_factors", (meta,) + tuple(table for table, _, _ in sources),
    )


def share_body(_, parts, down_ref, up_ref, *refs):
    out_ref = refs[-1]
    step = pl.program_id(0)

    @pl.when(step < parts)
    def _():
        out_ref[0] = down_ref[...]

    @pl.when(step >= parts)
    def _():
        out_ref[0] = up_ref[...]


def feed_share(meta, down_weight, up_weight, depth, after):
    hidden, width = down_weight.shape
    parts = hidden // width
    return call(
        lambda m, *refs: share_body(m, parts, *refs),
        (2 * parts,),
        [
            pl.BlockSpec(
                (depth, width), lambda t, m: (m[11] * parts + jnp.minimum(t, parts - 1), 0)
            ),
            pl.BlockSpec((depth, width), lambda t, m: (m[11], jnp.maximum(t - parts, 0))),
        ]
        + [IN_PLACE] * len(after),
        pl.BlockSpec((1, depth, width), lambda t, m: (t, 0, 0)),
        shaped((2 * parts, depth, width), LOW),
        [],
        0,
        8 * parts * depth * width,
        "feed_share",
        (meta, down_weight, up_weight, *after),
    )


def first_norm_body(_, x_ref, gain_ref, out_ref):
    rows, _, _ = norm_rows(x_ref[...].astype(WIDE), gain_ref[...])
    out_ref[...] = rows.astype(LOW)


def first_norm(meta, x, gain):
    frames, width = x.shape
    block = min(256, frames)
    rows = pl.BlockSpec((block, width), lambda t, _: (t, 0))
    return call(
        first_norm_body,
        (frames // block,),
        [rows, whole((1, width))],
        rows,
        shaped(x.shape, LOW),
        [],
        10 * x.size,
        4 * x.size,
        "first_norm",
        (meta, x, gain),
    )


def project_body(_, act_ref, weight_ref, down_ref, up_ref, *refs):
    out_ref = refs[-1]
    act = act_ref[...]
    rank = low_rank(down_ref[0, 0], act)
    out_ref[0] = (mm(act, weight_ref[0]) + mm_tn(rank, up_ref[0, 0])).astype(LOW)


def project_heads(meta, act, weights, down, up, slots, skip, name, after=()):
    rows, width = act.shape
    count, _, local = weights.shape
    first_slot = slots
    return call(
        project_body,
        (count,),
        [
            whole((rows, width)),
            pl.BlockSpec((1, width, local), lambda j, m: (j, 0, 0)),
            pl.BlockSpec((1, 1, RANK_UNIT, width), lambda j, m: (j + skip, m[first_slot + j], 0, 0)),
            pl.BlockSpec((1, 1, RANK_UNIT, local), lambda j, m: (j + skip, m[first_slot + j], 0, 0)),
        ]
        + [IN_PLACE] * len(after),
        pl.BlockSpec((1, rows, local), lambda j, m: (j, 0, 0)),
        shaped((count, rows, local), LOW),
        [],
        2 * rows * width * local * count,
        2 * (weights.size + act.size + count * rows * local),
        name,
        (meta, act, weights, down, up, *after),
    )


def project_back_body(_, last, grad_ref, weight_ref, down_ref, up_ref, after_ref, out_ref, total_ref):
    step = pl.program_id(0)
    grad = grad_ref[0]
    grad_rank = low_rank(up_ref[0, 0], grad)
    part = mm_nt(grad, weight_ref[0]) + mm_tn(grad_rank, down_ref[0, 0])

    @pl.when(step == 0)
    def _():
        total_ref[...] = part

    @pl.when(step > 0)
    def _():
        total_ref[...] += part

    @pl.when(step == last)
    def _():
        out_ref[...] = total_ref[...].astype(out_ref.dtype)


def project_back_heads(meta, grads, weights, down, up, slots, skip, kind, name, after):
    count, width, local = weights.shape
    rows = grads.shape[1]
    return call(
        lambda m, *refs: project_back_body(m, count - 1, *refs),
        (count,),
        [
            pl.BlockSpec((1, rows, local), lambda j, m: (j, 0, 0)),
            pl.BlockSpec((1, width, local), lambda j, m: (j, 0, 0)),
            pl.BlockSpec((1, 1, RANK_UNIT, width), lambda j, m: (j + skip, m[slots + j], 0, 0)),
            pl.BlockSpec((1, 1, RANK_UNIT, local), lambda j, m: (j + skip, m[slots + j], 0, 0)),
            IN_PLACE,
        ],
        whole((rows, width)),
        shaped((rows, width), kind),
        [pltpu.VMEM((rows, width), WIDE)],
        2 * rows * width * local * count,
        2 * (weights.size + count * rows * local) + 4 * rows * width,
        name,
        (meta, grads, weights, down, up, after),
    )


def rank_grads_body(meta, count, parts, *refs):
    acts = []
    grads = []
    act_scratch, grad_scratch, sems = refs[-3:]
    copies = []
    for part in range(parts):
        pairs = ((refs[part], act_scratch.at[part]), (refs[parts + part], grad_scratch.at[part]))
        copies.append(
            [pltpu.make_async_copy(*pair, sems.at[2 * part + number]) for number, pair in enumerate(pairs)]
        )
        for copy in copies[-1]:
            copy.start()
        acts.append(act_scratch.at[part])
        grads.append(grad_scratch.at[part])
    downs = refs[2 * parts : 2 * parts + count]
    ups = refs[2 * parts + count : 2 * parts + 2 * count]
    mine_ref, theirs_ref, ga = refs[-6:-3]
    half = ga.shape[1] // 2
    local = ups[0].shape[3]
    down = jnp.concatenate([ref[0, 0] for ref in downs], axis=0)
    for part in range(parts):
        for copy in copies[part]:
            copy.wait()
        act = acts[part][...]
        rank = low_rank(down, act)
        grad_rank = jnp.concatenate(
            [low_rank(ups[j][0, 0], grads[part][j]) for j in range(count)], axis=0
        )
        if part == 0:
            ga[...] = mm(grad_rank, act)
        else:
            ga[...] += mm(grad_rank, act)
        for j in range(count):
            gb = mm(rank[RANK_UNIT * j : RANK_UNIT * (j + 1)], grads[part][j])
            span = slice(count * half + j * local, count * half + (j + 1) * local)
            if part == 0:
                mine_ref[:, span] = gb
            else:
                mine_ref[:, span] += gb
    side = meta[10]
    for j in range(count):
        rows = slice(RANK_UNIT * j, RANK_UNIT * (j + 1))
        span = slice(j * half, (j + 1) * half)
        mine_ref[:, span] = ga[rows, pl.ds(pl.multiple_of(side * half, 128), half)]
        theirs = ga[rows, pl.ds(pl.multiple_of((1 - side) * half, 128), half)]
        theirs_ref[:, span] = theirs.astype(LOW)


def rank_grads(meta, acts, grads, down, up, slots, skip, name):
    rows, width = acts[0].shape
    count, _, local = grads[0].shape
    parts = len(acts)

    def table(size, j):
        return pl.BlockSpec(
            (1, 1, RANK_UNIT, size),
            lambda t, m: (j + skip, m[slots + j], 0, 0),
            pipeline_mode=pl.Buffered(1),
        )

    shared = count * width // 2
    total = shared + count * local
    return call(
        lambda m, *refs: rank_grads_body(m, count, parts, *refs),
        (1,),
        [IN_PLACE] * (2 * parts)
        + [table(width, j) for j in range(count)]
        + [table(local, j) for j in range(count)],
        (whole((RANK_UNIT, total)), whole((RANK_UNIT, shared))),
        (shaped((RANK_UNIT, total), WIDE), shaped((RANK_UNIT, shared), LOW)),
        [
            pltpu.VMEM((RANK_UNIT * count, width), WIDE),
            pltpu.VMEM((parts, rows, width), LOW),
            pltpu.VMEM((parts, count, rows, local), LOW),
            pltpu.SemaphoreType.DMA((2 * parts,)),
        ],
        8 * parts * rows * (width + local) * RANK_UNIT * count,
        2 * parts * rows * (width + count * local),
        name,
        (meta, *acts, *grads, *([down] * count), *([up] * count)),
    )


def split_columns(meta, mine_ref, theirs_ref, first, array):
    half = array.shape[-1] // 2
    span = slice(first, first + half)
    side = meta[10]
    mine_ref[:, span] = array[:, pl.ds(pl.multiple_of(side * half, 128), half)]
    theirs = array[:, pl.ds(pl.multiple_of((1 - side) * half, 128), half)]
    theirs_ref[:, span] = theirs.astype(LOW)


def own_columns(mine_ref, theirs_ref, first, array):
    half = array.shape[-1] // 2
    span = slice(first, first + half)
    mine_ref[:, span] = array[:, :half]
    theirs_ref[:, span] = array[:, half:].astype(LOW)


def join(mine, received):
    both = jnp.concatenate(received, axis=1).astype(WIDE)
    width = both.shape[1]
    return (mine + jnp.pad(both, ((0, 0), (0, mine.shape[1] - width)))).astype(LOW)


def clip_names(label_ref):
    clips, rank, width = label_ref.shape
    return label_ref[...].reshape(clips * rank, width).astype(WIDE).T


def slot_take(names, slots, rank):
    source = lax.broadcasted_iota(jnp.int32, names.shape, 1)
    target = (source & (rank - 1)) + rank * names.astype(jnp.int32)
    place = lax.broadcasted_iota(jnp.int32, (slots * rank, names.shape[1]), 0)
    return jnp.where(place == target, 1.0, 0.0).astype(LOW)


def slot_sum_body(_, plan, slots, carried, everyone_ref, label_ref, *refs):
    count = len({which for _, which, _ in plan})
    earlier = refs[: len(carried)]
    out_refs = refs[-5 - count : -5]
    names, arrived, totals, in_sems, out_sems = refs[-5:]
    clips, rank, unit = arrived.shape[1:]
    incoming = [
        pltpu.make_async_copy(
            everyone_ref.at[:, :, pl.ds(unit * number, unit)], arrived.at[number], in_sems.at[number]
        )
        for number in range(len(plan))
    ]
    for copy in incoming:
        copy.start()
    names[...] = clip_names(label_ref)
    outgoing = []
    for number, (which, ref) in enumerate(zip(carried, earlier)):
        copy = pltpu.make_async_copy(ref.at[0], out_refs[which].at[0], out_sems.at[len(plan) + number])
        copy.start()
        outgoing.append(copy)
    for number, (column, which, place) in enumerate(plan):
        incoming[number].wait()
        take = slot_take(names[column : column + 1], slots, rank)
        total = mm(take, arrived[number].reshape(clips * rank, unit))
        totals[number] = total.reshape(slots, rank, unit)
        out_ref = out_refs[which]
        target = out_ref.at[place] if len(out_ref.shape) == 4 else out_ref.at[:, :, pl.ds(unit * place, unit)]
        copy = pltpu.make_async_copy(totals.at[number], target, out_sems.at[number])
        copy.start()
        outgoing.append(copy)
    for copy in outgoing:
        copy.wait()


def slot_sums(meta, everyone, plan, outs, slots, unit, carried, name, after):
    clips, rank, total = everyone.shape
    label_width = 2 * HEAD_DIM
    units = len(plan)
    return call(
        lambda m, *refs: slot_sum_body(m, plan, slots, tuple(carried), *refs),
        (1,),
        [IN_PLACE, whole((clips, rank, label_width), (0, 0, total // label_width - 1))]
        + [whole(array.shape) for array in carried.values()]
        + [IN_PLACE] * len(after),
        (IN_PLACE,) * len(outs),
        tuple(
            shaped((slots, rank, width) if stack is None else (stack, slots, rank, width), WIDE)
            for stack, width in outs
        ),
        [
            pltpu.VMEM((label_width, clips * rank), WIDE),
            pltpu.VMEM((units, clips, rank, unit), LOW),
            pltpu.VMEM((units, slots, rank, unit), WIDE),
            pltpu.SemaphoreType.DMA((units,)),
            pltpu.SemaphoreType.DMA((units + len(carried),)),
        ],
        0,
        2 * everyone.size + 4 * slots * rank * total,
        name,
        (meta, everyone, everyone, *carried.values(), *after),
    )


def causal_keep(rows):
    key_at = lax.broadcasted_iota(jnp.int32, (rows, rows), 0)
    return key_at <= lax.broadcasted_iota(jnp.int32, (rows, rows), 1)


def turned(rows):
    return rows.astype(WIDE).T.astype(LOW)


def forward_block(query, keys, value_turned, diagonal, earlier=None):
    score = mm_nt(keys, query)
    if diagonal:
        score = jnp.where(causal_keep(score.shape[0]), score, -1e30)
    largest = jnp.max(score, axis=0, keepdims=True)
    if earlier is not None:
        largest = jnp.maximum(largest, earlier[0])
    mixed = mm(value_turned, jnp.exp(score - largest).astype(LOW))
    if earlier is not None:
        mixed = mixed + earlier[1] * jnp.exp(earlier[0] - largest)
    return largest, mixed


def values_of(rows_ref):
    values = turned(rows_ref[2])
    ones = jnp.ones((RANK_UNIT, values.shape[1]), LOW)
    return [
        jnp.concatenate([values[HEAD_DIM * which : HEAD_DIM * (which + 1)], ones], axis=0)
        for which in (0, 1)
    ]


def forward_finish(blocks, out_ref, log_ref):
    mixes = []
    totals = []
    for largest, mixed in blocks:
        summed = mixed[HEAD_DIM : HEAD_DIM + 1]
        mixes.append(mixed[:HEAD_DIM] * (1.0 / summed))
        totals.append(jnp.broadcast_to(jnp.log(summed) + largest, (HEAD_DIM, summed.shape[1])))
    out_ref[...] = jnp.concatenate(mixes, axis=0).T.astype(LOW)
    log_ref[...] = jnp.concatenate(totals, axis=0).T


MIXED_ROWS = HEAD_DIM + RANK_UNIT
PART_ROWS = MIXED_ROWS + 8


def self_forward_own_body(_, own_ref, part_ref):
    masks = half_masks()
    query = own_ref[0] * jnp.asarray(HEAD_DIM**-0.5, LOW)
    values = values_of(own_ref)
    for which in (0, 1):
        largest, mixed = forward_block(query * masks[which], own_ref[1], values[which], True)
        part_ref[0, which, :MIXED_ROWS] = mixed
        part_ref[0, which, MIXED_ROWS:] = jnp.broadcast_to(largest, (8, largest.shape[1]))


def self_forward_own(meta, own, after):
    _, half, local = own.shape
    pair = 2 * HEAD_DIM
    shape = (local // pair, 2, PART_ROWS, half)
    return call(
        lambda m, own_ref, after_ref, part_ref: self_forward_own_body(m, own_ref, part_ref),
        (local // pair,),
        [pl.BlockSpec((3, half, pair), lambda p, m: (0, 0, p)), IN_PLACE],
        pl.BlockSpec((1,) + shape[1:], lambda p, m: (p, 0, 0, 0)),
        shaped(shape, WIDE),
        [],
        4 * half * half * local,
        10 * half * local,
        "self_forward_own",
        (meta, own, after),
    )


def self_forward_body(
    meta, part_ref, own_ref, other_ref, out_own_ref, out_other_ref, log_own_ref, log_other_ref, keys, values, queries
):
    side = meta[10]
    masks = half_masks()
    for slot, ref in ((0, own_ref), (1, other_ref)):
        keys[slot] = ref[1]
        queries[slot] = ref[0] * jnp.asarray(HEAD_DIM**-0.5, LOW)
        for which, value in enumerate(values_of(ref)):
            values[slot, which] = value
    blocks = []
    for which in (0, 1):
        own = (part_ref[0, which, MIXED_ROWS : MIXED_ROWS + 1], part_ref[0, which, :MIXED_ROWS])
        other = forward_block(queries[1] * masks[which], keys[1], values[1, which], True)
        earlier = (jnp.where(side == 0, other[0], own[0]), jnp.where(side == 0, other[1], own[1]))
        later = forward_block(
            queries[1 - side] * masks[which], keys[side], values[side, which], False, earlier
        )
        blocks.append(
            (
                (jnp.where(side == 0, own[0], later[0]), jnp.where(side == 0, own[1], later[1])),
                (jnp.where(side == 0, later[0], other[0]), jnp.where(side == 0, later[1], other[1])),
            )
        )
    forward_finish([blocks[0][0], blocks[1][0]], out_own_ref, log_own_ref)
    forward_finish([blocks[0][1], blocks[1][1]], out_other_ref, log_other_ref)


def self_forward(meta, part, own, other):
    _, half, local = own.shape
    pair = 2 * HEAD_DIM
    three = pl.BlockSpec((3, half, pair), lambda p, m: (0, 0, p))
    one = pl.BlockSpec((half, pair), lambda p, m: (0, p))
    rows = shaped((half, local), LOW)
    logs = shaped((half, local), WIDE)
    return call(
        self_forward_body,
        (local // pair,),
        [pl.BlockSpec((1,) + part.shape[1:], lambda p, m: (p, 0, 0, 0)), three, three],
        (one, one, one, one),
        (rows, rows, logs, logs),
        [
            pltpu.VMEM((2, half, pair), LOW),
            pltpu.VMEM((2, 2, MIXED_ROWS, half), LOW),
            pltpu.VMEM((2, half, pair), LOW),
        ],
        12 * half * half * local,
        20 * half * local,
        "self_forward",
        (meta, part, own, other),
    )


def three_parts(column):
    high = column.astype(LOW)
    rest = column - high.astype(WIDE)
    middle = rest.astype(LOW)
    return high, middle, (rest - middle.astype(WIDE)).astype(LOW)


def back_scratch(slots, half):
    pair = 2 * HEAD_DIM
    return [pltpu.VMEM((slots, pair, half), LOW)] * 3 + [pltpu.VMEM((slots, 2, half, pair), LOW)] * 4


def back_prepare_keys(slot, rows_ref, scratch):
    key_turned, _, _, _, key_wide, _, value_wide = scratch
    lane = lax.broadcasted_iota(jnp.int32, (1, 2 * HEAD_DIM), 1)
    key_turned[slot] = turned(rows_ref[1])
    for which in (0, 1):
        spare = HEAD_DIM * (1 - which)
        marked = jnp.where((lane >= spare) & (lane < spare + 3), 1.0, 0.0).astype(LOW)
        key_wide[slot, which] = rows_ref[1] * (1 - marked) + marked
        value_wide[slot, which] = rows_ref[2] * (1 - marked) + marked


def back_prepare_queries(slot, rows_ref, mixed_ref, logs_ref, grad_ref, scratch):
    _, query_turned, grad_turned, query_wide, _, grad_wide, _ = scratch
    masks = half_masks()
    lane = lax.broadcasted_iota(jnp.int32, (1, 2 * HEAD_DIM), 1)
    grad = grad_ref[...]
    product = grad.astype(WIDE) * mixed_ref[...].astype(WIDE)
    query = rows_ref[0] * jnp.asarray(HEAD_DIM**-0.5, LOW)
    logs = logs_ref[...]
    query_turned[slot] = turned(query)
    grad_turned[slot] = turned(grad)
    for which in (0, 1):
        spare = HEAD_DIM * (1 - which)
        marks = [jnp.where(lane == spare + i, 1.0, 0.0).astype(LOW) for i in range(3)]
        inner = jnp.sum(product * masks[which].astype(WIDE), axis=-1, keepdims=True)
        query_rows = query * masks[which]
        for part, mark in zip(three_parts(logs[:, HEAD_DIM * which : HEAD_DIM * which + 1]), marks):
            query_rows = query_rows - part * mark
        query_wide[slot, which] = query_rows
        grad_rows = grad * masks[which]
        for part, mark in zip(three_parts(inner), marks):
            grad_rows = grad_rows - part * mark
        grad_wide[slot, which] = grad_rows


def back_block(query_slot, key_slot, diagonal, scratch, totals):
    key_turned, query_turned, grad_turned, query_wide, key_wide, grad_wide, value_wide = scratch
    half = key_turned.shape[2]
    for which in (0, 1):
        head = slice(HEAD_DIM * which, HEAD_DIM * (which + 1))
        score = mm_nt(key_wide[key_slot, which], query_wide[query_slot, which])
        if diagonal:
            score = jnp.where(causal_keep(half), score, -1e30)
        prob = jnp.exp(score)
        prob_grad = mm_nt(value_wide[key_slot, which], grad_wide[query_slot, which])
        score_grad = (prob * prob_grad).astype(LOW)
        totals[2, key_slot, head] += mm_nt(grad_turned[query_slot, head], prob.astype(LOW))
        totals[1, key_slot, head] += mm_nt(query_turned[query_slot, head], score_grad)
        totals[0, query_slot, head] += mm(key_turned[key_slot, head], score_grad)


def self_back_own_body(_, own_ref, z_ref, log_ref, grad_ref, out_ref, *scratch):
    totals = scratch[-1]
    totals[...] = jnp.zeros_like(totals)
    back_prepare_keys(0, own_ref, scratch[:-1])
    back_prepare_queries(0, own_ref, z_ref, log_ref, grad_ref, scratch[:-1])
    back_block(0, 0, True, scratch[:-1], totals)
    out_ref[...] = totals[:, 0]


def self_back_own(meta, own, z_own, log_own, grad_own):
    _, half, local = own.shape
    pair = 2 * HEAD_DIM
    three = pl.BlockSpec((3, half, pair), lambda p, m: (0, 0, p))
    one = pl.BlockSpec((half, pair), lambda p, m: (0, p))
    return call(
        self_back_own_body,
        (local // pair,),
        [three, one, one, one],
        pl.BlockSpec((3, pair, half), lambda p, m: (0, p, 0)),
        shaped((3, local, half), WIDE),
        back_scratch(1, half) + [pltpu.VMEM((3, 1, pair, half), WIDE)],
        100 * half * half * local,
        24 * half * local,
        "self_back_own",
        (meta, own, z_own, log_own, grad_own),
    )


def self_back_body(
    meta,
    part_ref,
    own_ref,
    other_ref,
    z_own_ref,
    z_other_ref,
    log_own_ref,
    log_other_ref,
    grad_own_ref,
    grad_other_ref,
    _early,
    out_own_ref,
    out_other_ref,
    *scratch,
):
    totals = scratch[-1]
    scratch = scratch[:-1]
    side = meta[10]
    totals[:, 0] = part_ref[...]
    totals[:, 1] = jnp.zeros_like(totals[:, 1])

    @pl.when(side == 0)
    def _():
        back_prepare_keys(0, own_ref, scratch)

    @pl.when(side != 0)
    def _():
        back_prepare_queries(0, own_ref, z_own_ref, log_own_ref, grad_own_ref, scratch)

    back_prepare_keys(1, other_ref, scratch)
    back_prepare_queries(1, other_ref, z_other_ref, log_other_ref, grad_other_ref, scratch)
    back_block(1, 1, True, scratch, totals)
    back_block(1 - side, side, False, scratch, totals)
    for slot, ref in ((0, out_own_ref), (1, out_other_ref)):
        ref[0] = (totals[0, slot].T * HEAD_DIM**-0.5).astype(LOW)
        ref[1] = totals[1, slot].T.astype(LOW)
        ref[2] = totals[2, slot].T.astype(LOW)


def self_back(meta, part, own, other, z_own, z_other, log_own, log_other, grad_own, grad_other, after):
    _, half, local = own.shape
    pair = 2 * HEAD_DIM
    three = pl.BlockSpec((3, half, pair), lambda p, m: (0, 0, p))
    one = pl.BlockSpec((half, pair), lambda p, m: (0, p))
    return call(
        self_back_body,
        (local // pair,),
        [pl.BlockSpec((3, pair, half), lambda p, m: (0, p, 0)), three, three]
        + [one] * 6
        + [IN_PLACE] * len(after),
        (three, three),
        (shaped(own.shape, LOW), shaped(own.shape, LOW)),
        back_scratch(2, half) + [pltpu.VMEM((3, 2, pair, half), WIDE)],
        200 * half * half * local,
        40 * half * local,
        "self_back",
        (meta, part, own, other, z_own, z_other, log_own, log_other, grad_own, grad_other, *after),
    )


def halves_of(ref, local):
    step = ref.shape[1] // 2
    return (
        ref[:, :step, :].reshape(local, ref.shape[2]),
        ref[:, step:, :].reshape(local, ref.shape[2]),
    )


def full_of(ref):
    return ref[...].reshape(ref.shape[0] * ref.shape[1], ref.shape[2])


def fetch_weights(step, order, sources, gathered, held, sems, between=()):
    copies = {}
    for which in order:
        copies[which] = (
            pltpu.make_async_copy(sources[which], held[2 * which], sems.at[2 * which]),
            pltpu.make_async_copy(gathered.at[:, which], held[2 * which + 1], sems.at[2 * which + 1]),
        )

    @pl.when(step == 0)
    def _():
        for place, which in enumerate(order):
            for copy in copies[which]:
                copy.start()
            for copy in between[place] if between else ():
                copy.start()

    def ready(which):
        @pl.when(step == 0)
        def _():
            for copy in copies[which]:
                copy.wait()

        return held[2 * which], held[2 * which + 1]

    return ready


TILE_HEADS = 4


def tile_span(tile):
    return slice(TILE_HEADS * HEAD_DIM * tile, TILE_HEADS * HEAD_DIM * (tile + 1))


def tile_masks():
    lane = lax.broadcasted_iota(jnp.int32, (1, TILE_HEADS * HEAD_DIM), 1)
    return [jnp.where(lane // HEAD_DIM == head, 1.0, 0.0).astype(LOW) for head in range(TILE_HEADS)]


def text_tile(rows, tile, masks):
    part = rows[:, tile_span(tile)]
    return jnp.concatenate([part * mask for mask in masks], axis=0)


def by_head(values, reduce):
    keys, rows = values.shape
    apart = values.reshape(TILE_HEADS, keys // TILE_HEADS, rows)
    reduced = reduce(apart, axis=1, keepdims=True)
    return jnp.broadcast_to(reduced, apart.shape).reshape(keys, rows)


def text_weights(key_tile, query):
    scores = mm_nt(key_tile, query)
    weights = jnp.exp(scores - by_head(scores, jnp.max))
    return weights * (1.0 / by_head(weights, jnp.sum))


def mix_text(query, keys, values):
    masks = tile_masks()
    mixed = []
    for tile in range(query.shape[1] // (TILE_HEADS * HEAD_DIM)):
        one_query = query[:, tile_span(tile)] * jnp.asarray(HEAD_DIM**-0.5, LOW)
        weights = text_weights(text_tile(keys, tile, masks), one_query)
        mixed.append(mm_tn(weights.astype(LOW), text_tile(values, tile, masks)).astype(LOW))
    return jnp.concatenate(mixed, axis=1)


def middle_forward_body(
    _,
    x_ref,
    z_own_ref,
    z_other_ref,
    out_weight_ref,
    query_weight_ref,
    cross_weight_ref,
    gathered_ref,
    down3_ref,
    down3_other_ref,
    up3_ref,
    down4_ref,
    up4_ref,
    up4_other_ref,
    down7_ref,
    down7_other_ref,
    up7_ref,
    text_own_ref,
    text_other_ref,
    gain_two_ref,
    gain_three_ref,
    stream_one_ref,
    stream_two_ref,
    rows_three_ref,
    query_out_own_ref,
    query_out_other_ref,
    z2_own_ref,
    z2_other_ref,
    *scratch,
):
    local = z_own_ref.shape[1]
    ready = fetch_weights(
        pl.program_id(0),
        (0, 1, 2),
        (out_weight_ref, query_weight_ref, cross_weight_ref),
        gathered_ref,
        scratch[:6],
        scratch[6],
    )

    def out_product(own, other, which, down, down_other, up):
        rank = (mm_nt(down, own) + mm_nt(down_other, other)).astype(LOW)
        weight_own, weight_other_ref = ready(which)
        first, second = halves_of(weight_other_ref, local)
        product = mm(own, weight_own[...]) + mm_tn(rank, up)
        return product + jnp.concatenate([mm(other, first), mm(other, second)], axis=1)

    stream = x_ref[...].astype(WIDE) + out_product(
        z_own_ref[...],
        z_other_ref[...],
        0,
        down3_ref[0, 0],
        down3_other_ref[...],
        up3_ref[0, 0],
    )
    stream_one_ref[...] = stream
    rows_two = norm_rows(stream, gain_two_ref[...])[0].astype(LOW)
    rank = low_rank(down4_ref[0, 0], rows_two)
    query_own_ref, query_other_ref = ready(1)
    query_own = (mm(rows_two, query_own_ref[...]) + mm_tn(rank, up4_ref[0, 0])).astype(LOW)
    query_other = (
        mm(rows_two, full_of(query_other_ref)) + mm_tn(rank, up4_other_ref[...])
    ).astype(LOW)
    query_out_own_ref[...] = query_own
    query_out_other_ref[...] = query_other
    z2_own = mix_text(query_own, text_own_ref[0], text_own_ref[1])
    z2_other = mix_text(query_other, text_other_ref[0], text_other_ref[1])
    z2_own_ref[...] = z2_own
    z2_other_ref[...] = z2_other
    stream = stream + out_product(
        z2_own,
        z2_other,
        2,
        down7_ref[0, 0],
        down7_other_ref[...],
        up7_ref[0, 0],
    )
    stream_two_ref[...] = stream
    rows_three_ref[...] = norm_rows(stream, gain_three_ref[...])[0].astype(LOW)


def chosen(table, entry, slot):
    shape = (1, 1) + table.shape[2:]
    return pl.BlockSpec(
        shape, lambda t, m: (entry, m[slot], 0, 0), pipeline_mode=pl.Buffered(1)
    )


def middle_specs(weights, gathered, tables, packed):
    attention_down, attention_up, cross_down, cross_up = tables
    rank = (RANK_UNIT, gathered.shape[3])
    specs = [
        IN_PLACE,
        IN_PLACE,
        IN_PLACE,
        IN_PLACE,
        chosen(attention_down, 0, 3),
        whole(rank, (0, 0)),
        chosen(attention_up, 0, 3),
        chosen(cross_down, 0, 4),
        chosen(cross_up, 0, 4),
        whole(rank, (0, 2)),
        chosen(attention_down, 1, 7),
        whole(rank, (0, 1)),
        chosen(attention_up, 1, 7),
    ]
    args = weights + (
        gathered,
        attention_down,
        packed,
        attention_up,
        cross_down,
        cross_up,
        packed,
        attention_down,
        packed,
        attention_up,
    )
    return specs, args


def middle_scratch(weights, gathered):
    shards, _, depth, local = gathered.shape
    held = []
    for weight in weights:
        held += [pltpu.VMEM(weight.shape, LOW), pltpu.VMEM((shards, depth, local), LOW)]
    return held + [pltpu.SemaphoreType.DMA((2 * len(weights),))]


def middle_forward(meta, x, z_own, z_other, weights, gathered, tables, packed, text_own, text_other, gains):
    frames, width = x.shape
    local = z_own.shape[1]
    block = min(512, frames)
    wide = pl.BlockSpec((block, width), lambda t, m: (t, 0))
    narrow = pl.BlockSpec((block, local), lambda t, m: (t, 0))
    specs, args = middle_specs(weights, gathered, tables, packed)
    return call(
        middle_forward_body,
        (frames // block,),
        [wide, narrow, narrow]
        + specs
        + [whole(text_own.shape), whole(text_other.shape), whole((1, width)), whole((1, width))],
        (wide, wide, wide, narrow, narrow, narrow, narrow),
        (
            shaped((frames, width), WIDE),
            shaped((frames, width), WIDE),
            shaped((frames, width), LOW),
            shaped((frames, local), LOW),
            shaped((frames, local), LOW),
            shaped((frames, local), LOW),
            shaped((frames, local), LOW),
        ),
        middle_scratch(weights, gathered),
        6 * frames * width * width,
        6 * width * width + 20 * frames * width,
        "middle_forward",
        (meta, x, z_own, z_other) + args + (text_own, text_other) + gains,
    )


def middle_back_body(
    meta,
    last,
    grad_ref,
    stream_one_ref,
    z_own_ref,
    z_other_ref,
    query_in_own_ref,
    query_in_other_ref,
    z2_own_ref,
    z2_other_ref,
    out_weight_ref,
    query_weight_ref,
    cross_weight_ref,
    gathered_ref,
    down3_ref,
    down3_other_ref,
    up3_ref,
    down4_ref,
    up4_ref,
    up4_other_ref,
    down7_ref,
    down7_other_ref,
    up7_ref,
    text_own_ref,
    text_other_ref,
    gain_two_ref,
    text_ref,
    down5_ref,
    down6_ref,
    up5_ref,
    up6_ref,
    up5_other_ref,
    up6_other_ref,
    grad_one_ref,
    dz_own_ref,
    dz_other_ref,
    text_grad_own_ref,
    text_grad_other_ref,
    mine_ref,
    theirs_ref,
    text_mine_ref,
    text_theirs_ref,
    key_total,
    value_total,
    ga3_ref,
    gb3_ref,
    ga4_ref,
    gb4_ref,
    ga7_ref,
    gb7_ref,
    *scratch,
):
    step = pl.program_id(0)
    late = scratch[7:12]
    late_sems = scratch[13]
    late_copies = [
        pltpu.make_async_copy(source, target, late_sems.at[number])
        for number, (source, target) in enumerate(
            zip((query_in_own_ref, query_in_other_ref, stream_one_ref, z_own_ref, z_other_ref), late)
        )
    ]
    query_in_own_ref, query_in_other_ref, stream_one_ref, z_own_ref, z_other_ref = late
    grad_one_copy = pltpu.make_async_copy(scratch[12], grad_one_ref, late_sems.at[5])
    ready = fetch_weights(
        step,
        (2, 1, 0),
        (out_weight_ref, query_weight_ref, cross_weight_ref),
        gathered_ref,
        scratch[:6],
        scratch[6],
        (late_copies[:2], late_copies[2:], ()),
    )
    local = z_own_ref.shape[1]
    tiles = local // (TILE_HEADS * HEAD_DIM)
    masks = tile_masks()
    scale = jnp.asarray(HEAD_DIM**-0.5, LOW)

    @pl.when(step == 0)
    def _():
        key_total[...] = jnp.zeros_like(key_total)
        value_total[...] = jnp.zeros_like(value_total)
        for ref in (ga3_ref, gb3_ref, ga4_ref, gb4_ref, ga7_ref, gb7_ref):
            ref[...] = jnp.zeros_like(ref)

    def out_back(grad, own, other, which, down, down_other, up, ga_ref, gb_ref):
        rank = (mm_nt(down, own) + mm_nt(down_other, other)).astype(LOW)
        grad_rank = low_rank(up, grad)
        ga_ref[:, :local] += mm(grad_rank, own)
        ga_ref[:, local:] += mm(grad_rank, other)
        gb_ref[...] += mm(rank, grad)
        weight_own, weight_other_ref = ready(which)
        first, second = halves_of(weight_other_ref, local)
        middle = grad.shape[1] // 2
        grad_own = mm_nt(grad, weight_own[...]) + mm_tn(grad_rank, down)
        grad_other = (
            mm_nt(grad[:, :middle], first)
            + mm_nt(grad[:, middle:], second)
            + mm_tn(grad_rank, down_other)
        )
        return grad_own.astype(LOW), grad_other.astype(LOW)

    grad = grad_ref[...]
    dz2_own, dz2_other = out_back(
        grad.astype(LOW),
        z2_own_ref[...],
        z2_other_ref[...],
        2,
        down7_ref[0, 0],
        down7_other_ref[...],
        up7_ref[0, 0],
        ga7_ref,
        gb7_ref,
    )

    def text_back(query, dz2, keys, values, part):
        query_grads = []
        for tile in range(tiles):
            key_tile = text_tile(keys, tile, masks)
            value_tile = text_tile(values, tile, masks)
            one_query = query[:, tile_span(tile)] * scale
            one_grad = dz2[:, tile_span(tile)]
            probs = text_weights(key_tile, one_query)
            prob_grads = mm_nt(value_tile, one_grad)
            inner = by_head(probs * prob_grads, jnp.sum)
            score_grads = (probs * (prob_grads - inner)).astype(LOW)
            query_grads.append((mm_tn(score_grads, key_tile) * HEAD_DIM**-0.5).astype(LOW))
            key_total[part, tile] += mm(score_grads, one_query)
            value_total[part, tile] += mm(probs.astype(LOW), one_grad)
        return jnp.concatenate(query_grads, axis=1)

    for copy in late_copies[:2]:
        copy.wait()
    dq_own = text_back(query_in_own_ref[...], dz2_own, text_own_ref[0], text_own_ref[1], 0)
    dq_other = text_back(query_in_other_ref[...], dz2_other, text_other_ref[0], text_other_ref[1], 1)

    for copy in late_copies[2:]:
        copy.wait()
    rows_two, normed, inverse = norm_rows(stream_one_ref[...], gain_two_ref[...])
    rows_two = rows_two.astype(LOW)
    rank = low_rank(down4_ref[0, 0], rows_two)
    grad_rank = (mm_nt(up4_ref[0, 0], dq_own) + mm_nt(up4_other_ref[...], dq_other)).astype(LOW)
    ga4_ref[...] += mm(grad_rank, rows_two)
    gb4_ref[:, :local] += mm(rank, dq_own)
    gb4_ref[:, local:] += mm(rank, dq_other)
    query_own_ref, query_other_ref = ready(1)
    grad_rows = (
        mm_nt(dq_own, query_own_ref[...])
        + mm_nt(dq_other, full_of(query_other_ref))
        + mm_tn(grad_rank, down4_ref[0, 0])
    )
    grad = grad + norm_back(grad_rows, gain_two_ref[...], normed, inverse)
    scratch[12][...] = grad
    grad_one_copy.start()
    dz_own, dz_other = out_back(
        grad.astype(LOW),
        z_own_ref[...],
        z_other_ref[...],
        0,
        down3_ref[0, 0],
        down3_other_ref[...],
        up3_ref[0, 0],
        ga3_ref,
        gb3_ref,
    )
    dz_own_ref[...] = dz_own
    dz_other_ref[...] = dz_other
    grad_one_copy.wait()

    @pl.when(step == last)
    def _():
        split_columns(meta, mine_ref, theirs_ref, 0, ga4_ref)
        own_columns(mine_ref, theirs_ref, local, gb4_ref)
        own_columns(mine_ref, theirs_ref, 2 * local, ga3_ref)
        own_columns(mine_ref, theirs_ref, 3 * local, ga7_ref)
        split_columns(meta, mine_ref, theirs_ref, 4 * local, gb3_ref)
        split_columns(meta, mine_ref, theirs_ref, 5 * local, gb7_ref)
        for total, slot in ((key_total, 0), (value_total, 1)):
            for part, ref in ((0, text_grad_own_ref), (1, text_grad_other_ref)):
                for tile in range(tiles):
                    stacked = total[part, tile]
                    rows = 0.0
                    for head, mask in enumerate(masks):
                        rows = rows + stacked[HEAD_DIM * head : HEAD_DIM * (head + 1)] * mask.astype(WIDE)
                    ref[slot, :, tile_span(tile)] = rows.astype(ref.dtype)
        text = text_ref[...]
        factors = ((down5_ref, up5_ref, up5_other_ref), (down6_ref, up6_ref, up6_other_ref))
        for slot, (down_ref, up_ref, up_other_ref) in enumerate(factors):
            grad_own = text_grad_own_ref[slot].astype(LOW)
            grad_other = text_grad_other_ref[slot]
            rank = low_rank(down_ref[0, 0], text)
            grad_rank = mm_nt(up_ref[0, 0], grad_own) + mm_nt(up_other_ref[...], grad_other)
            ga4_ref[...] = mm(grad_rank.astype(LOW), text)
            split_columns(meta, text_mine_ref, text_theirs_ref, slot * local, ga4_ref)
            span = slice((2 + slot) * local, (3 + slot) * local)
            text_mine_ref[:, span] = mm(rank, grad_own)
            text_theirs_ref[:, span] = mm(rank, grad_other).astype(LOW)


def middle_back(
    meta, grad, stream_one, z_own, z_other, q_own, q_other, z2_own, z2_other,
    weights, gathered, tables, packed, text_own, text_other, gain, text,
):
    frames, width = grad.shape
    local = z_own.shape[1]
    tiles = local // (TILE_HEADS * HEAD_DIM)
    wide = whole((frames, width))
    narrow = whole((frames, local))
    specs, args = middle_specs(weights, gathered, tables, packed)
    rank = (RANK_UNIT, width)
    packs = (RANK_UNIT, 6 * local)
    text_packs = (RANK_UNIT, 4 * local)
    _, _, cross_down, cross_up = tables
    return call(
        lambda m, *refs: middle_back_body(m, 0, *refs),
        (1,),
        [wide, IN_PLACE]
        + [IN_PLACE] * 4
        + [narrow] * 2
        + specs
        + [whole(text_own.shape), whole(text_other.shape), whole((1, width)), whole(text.shape)]
        + [chosen(cross_down, 1, 5), chosen(cross_down, 2, 6), chosen(cross_up, 1, 5), chosen(cross_up, 2, 6)]
        + [whole((RANK_UNIT, local), (0, 3)), whole((RANK_UNIT, local), (0, 4))],
        (IN_PLACE, narrow, narrow, whole(text_own.shape), whole(text_own.shape))
        + (whole(packs), whole(packs), whole(text_packs), whole(text_packs)),
        (
            shaped((frames, width), WIDE),
            shaped((frames, local), LOW),
            shaped((frames, local), LOW),
            shaped(text_own.shape, WIDE),
            shaped(text_own.shape, LOW),
            shaped(packs, WIDE),
            shaped(packs, LOW),
            shaped(text_packs, WIDE),
            shaped(text_packs, LOW),
        ),
        [
            pltpu.VMEM((2, tiles, TILE_HEADS * HEAD_DIM, TILE_HEADS * HEAD_DIM), WIDE),
            pltpu.VMEM((2, tiles, TILE_HEADS * HEAD_DIM, TILE_HEADS * HEAD_DIM), WIDE),
        ]
        + [pltpu.VMEM(rank, WIDE)] * 6
        + middle_scratch(weights, gathered)
        + [pltpu.VMEM((frames, local), LOW)] * 2
        + [pltpu.VMEM((frames, width), WIDE)]
        + [pltpu.VMEM((frames, local), LOW)] * 2
        + [pltpu.VMEM((frames, width), WIDE), pltpu.SemaphoreType.DMA((6,))],
        6 * frames * width * width,
        6 * width * width + 24 * frames * width,
        "middle_back",
        (meta, grad, stream_one, z_own, z_other, q_own, q_other, z2_own, z2_other)
        + args
        + (text_own, text_other, gain, text)
        + (cross_down, cross_down, cross_up, cross_up, packed, packed),
    )


def feed_tile(
    rows_ref, cot_ref, up_weight, down_weight, up_rank, down_rank,
    ga9_ref, gb8_ref, branch, grad_rows, rank9, grad_rank8, rank8, grad_rank9,
):
    frames = rows_ref.shape[0]
    block = min(256, frames)
    low_pre = mm_tn(rank8[...], up_rank)
    low_grad = mm_tn(grad_rank9[...], down_rank)
    hidden_blocks = []
    grad_blocks = []
    for first in range(0, frames, block):
        span = slice(first, first + block)
        pre = mm(rows_ref[span], up_weight) + low_pre[span]
        grad_hidden = mm_nt(cot_ref[span], down_weight) + low_grad[span]
        hidden, slope = gelu_parts(pre)
        hidden = hidden.astype(LOW)
        grad_pre = (grad_hidden * slope).astype(LOW)
        branch[span] += mm(hidden, down_weight)
        grad_rows[span] += mm_nt(grad_pre, up_weight)
        hidden_blocks.append(hidden)
        grad_blocks.append(grad_pre)
    hidden = jnp.concatenate(hidden_blocks, axis=0)
    grad_pre = jnp.concatenate(grad_blocks, axis=0)
    rank9[...] += mm_nt(down_rank, hidden)
    grad_rank8[...] += mm_nt(up_rank, grad_pre)
    ga9_ref[...] = mm(grad_rank9[...], hidden).astype(ga9_ref.dtype)
    gb8_ref[...] = mm(rank8[...], grad_pre).astype(gb8_ref.dtype)


def feed_own_body(
    _, rows_ref, cot_ref, up_weight_ref, down_weight_ref, up_rank_ref, down_rank_ref,
    down8_ref, up9_ref,
    branch_ref, grad_rows_ref, rank9_ref, grad_rank8_ref, ga9_ref, gb8_ref,
    rank8, grad_rank9,
):
    @pl.when(pl.program_id(0) == 0)
    def _():
        rank8[...] = low_rank(down8_ref[0], rows_ref[...])
        grad_rank9[...] = low_rank(up9_ref[0], cot_ref[...])
        for ref in (branch_ref, grad_rows_ref, rank9_ref, grad_rank8_ref):
            ref[...] = jnp.zeros_like(ref)

    feed_tile(
        rows_ref, cot_ref, up_weight_ref[...], down_weight_ref[...], up_rank_ref[0], down_rank_ref[0],
        ga9_ref, gb8_ref, branch_ref, grad_rows_ref, rank9_ref, grad_rank8_ref, rank8, grad_rank9,
    )


def table_tile(tile, slot):
    return pl.BlockSpec((1, RANK_UNIT, tile), lambda t, m: (m[slot], 0, t))


def feed_own(meta, rows, cot, up_weight, down_weight, input_down, input_up, output_down, output_up, tile):
    frames, width = rows.shape
    hidden = up_weight.shape[1]
    grads = pl.BlockSpec((RANK_UNIT, tile), lambda t, m: (0, t))
    picked = pl.BlockSpec((1, RANK_UNIT, width), lambda t, m: (m[8], 0, 0))
    picked_out = pl.BlockSpec((1, RANK_UNIT, width), lambda t, m: (m[9], 0, 0))
    rank = (RANK_UNIT, frames)
    return call(
        feed_own_body,
        (hidden // tile,),
        [
            whole((frames, width)),
            whole((frames, width)),
            pl.BlockSpec((width, tile), lambda t, m: (0, t)),
            pl.BlockSpec((tile, width), lambda t, m: (t, 0)),
            table_tile(tile, 8),
            table_tile(tile, 9),
            picked,
            picked_out,
        ],
        (whole((frames, width)), whole((frames, width)), whole(rank), whole(rank), grads, grads),
        (
            shaped((frames, width), WIDE),
            shaped((frames, width), WIDE),
            shaped(rank, WIDE),
            shaped(rank, WIDE),
            shaped((RANK_UNIT, hidden), WIDE),
            shaped((RANK_UNIT, hidden), WIDE),
        ),
        [pltpu.VMEM(rank, LOW), pltpu.VMEM(rank, LOW)],
        8 * frames * width * hidden,
        4 * width * hidden + 12 * frames * width,
        "feed_own",
        (meta, rows, cot, up_weight, down_weight, input_up, output_down, input_down, output_up),
    )


def feed_other_body(
    meta, last, rows_ref, cot_ref, up_weight_ref, down_weight_ref, up_rank_ref, down_rank_ref,
    down8_ref, up9_ref, branch_in_ref, grad_rows_in_ref, rank9_in_ref, grad_rank8_in_ref,
    stream_ref, gain_ref,
    out_ref, grad_ref, ga9_ref, gb8_ref, mine_ref, theirs_ref,
    branch, grad_rows, rank9, grad_rank8, rank8, grad_rank9, ga8_ref, gb9_ref, branch_in, grad_rows_in, stream_in, sems,
):
    step = pl.program_id(0)
    copies = [
        pltpu.make_async_copy(source, target, sems.at[i])
        for i, (source, target) in enumerate(
            ((branch_in_ref, branch_in), (grad_rows_in_ref, grad_rows_in), (stream_ref, stream_in))
        )
    ]

    @pl.when(step == 0)
    def _():
        for copy in copies:
            copy.start()
        rank8[...] = low_rank(down8_ref[0], rows_ref[...])
        grad_rank9[...] = low_rank(up9_ref[0], cot_ref[...])
        branch[...] = jnp.zeros_like(branch)
        grad_rows[...] = jnp.zeros_like(grad_rows)
        rank9[...] = rank9_in_ref[...]
        grad_rank8[...] = grad_rank8_in_ref[...]

    shards, _, depth, tile = up_weight_ref.shape
    up_weight = up_weight_ref[...].reshape(shards * depth, tile)
    down_weight = down_weight_ref[...].reshape(tile, down_weight_ref.shape[3])
    feed_tile(
        rows_ref, cot_ref, up_weight, down_weight, up_rank_ref[...], down_rank_ref[...],
        ga9_ref, gb8_ref, branch, grad_rows, rank9, grad_rank8, rank8, grad_rank9,
    )

    @pl.when(step == last)
    def _():
        for copy in copies:
            copy.wait()
        frames = rows_ref.shape[0]
        block = min(128, frames)
        last8 = grad_rank8[...].astype(LOW)
        last9 = rank9[...].astype(LOW)
        ga8_ref[...] = mm(last8, rows_ref[...])
        gb9_ref[...] = mm(last9, cot_ref[...])
        split_columns(meta, mine_ref, theirs_ref, 0, ga8_ref)
        split_columns(meta, mine_ref, theirs_ref, ga8_ref.shape[1] // 2, gb9_ref)
        for first in range(0, frames, block):
            span = slice(first, first + block)
            stream = stream_in[span]
            out = stream + (branch[span] + branch_in[span]) + mm_tn(last9[:, span], up9_ref[0])
            out_ref[span] = out.astype(LOW)
            _, normed, inverse = norm_rows(stream, gain_ref[...])
            grad = grad_rows[span] + grad_rows_in[span] + mm_tn(last8[:, span], down8_ref[0])
            grad_ref[span] = cot_ref[span].astype(WIDE) + norm_back(
                grad, gain_ref[...], normed, inverse
            )


def feed_other(
    meta, rows, cot, gathered, packed, first_pack, input_down, output_up, carried, stream, gain, tile
):
    frames, width = rows.shape
    shards, quarters, depth, _ = gathered.shape
    hidden = quarters // 2 * width
    per_half = width // tile
    own_shards = tile // (quarters // 2 * depth)
    down_first = quarters // 2
    grads = pl.BlockSpec((RANK_UNIT, tile), lambda t, m: (0, t))
    picked = pl.BlockSpec((1, RANK_UNIT, width), lambda t, m: (m[8], 0, 0))
    picked_out = pl.BlockSpec((1, RANK_UNIT, width), lambda t, m: (m[9], 0, 0))
    rank = (RANK_UNIT, frames)
    steps = hidden // tile
    full = whole((frames, width))
    wide = pltpu.VMEM((frames, width), WIDE)
    return call(
        lambda m, *refs: feed_other_body(m, steps - 1, *refs),
        (steps,),
        [
            full,
            full,
            pl.BlockSpec(
                (shards, 1, depth, tile),
                lambda t, m: (0, down_first + t // per_half, 0, t % per_half),
            ),
            pl.BlockSpec((own_shards, down_first, depth, width), lambda t, m: (t, 0, 0, 0)),
            pl.BlockSpec((RANK_UNIT, tile), lambda t, m: (0, first_pack // tile + t)),
            pl.BlockSpec((RANK_UNIT, tile), lambda t, m: (0, (first_pack + hidden) // tile + t)),
            picked,
            picked_out,
            IN_PLACE,
            IN_PLACE,
            whole(rank),
            whole(rank),
            IN_PLACE,
            whole((1, width)),
        ],
        (full, full, grads, grads, whole((RANK_UNIT, width)), whole((RANK_UNIT, width))),
        (
            shaped((frames, width), LOW),
            shaped((frames, width), WIDE),
            shaped((RANK_UNIT, hidden), LOW),
            shaped((RANK_UNIT, hidden), LOW),
            shaped((RANK_UNIT, width), WIDE),
            shaped((RANK_UNIT, width), LOW),
        ),
        [
            wide,
            wide,
            pltpu.VMEM(rank, WIDE),
            pltpu.VMEM(rank, WIDE),
            pltpu.VMEM(rank, LOW),
            pltpu.VMEM(rank, LOW),
            pltpu.VMEM((RANK_UNIT, width), WIDE),
            pltpu.VMEM((RANK_UNIT, width), WIDE),
            wide,
            wide,
            wide,
            pltpu.SemaphoreType.DMA((3,)),
        ],
        8 * frames * width * hidden,
        4 * width * hidden + 24 * frames * width,
        "feed_other",
        (meta, rows, cot, gathered, gathered, packed, packed, input_down, output_up)
        + tuple(carried)
        + (stream, gain),
    )


def last_norm_body(_, x_ref, own_ref, other_ref, grad_ref, gain_ref, after_ref, out_ref):
    _, normed, inverse = norm_rows(x_ref[...].astype(WIDE), gain_ref[...])
    total = own_ref[...] + other_ref[...].astype(WIDE)
    out_ref[...] = grad_ref[...] + norm_back(total, gain_ref[...], normed, inverse)


def last_norm(meta, x, own, other, grad, gain, after):
    frames, width = x.shape
    block = min(256, frames)
    rows = pl.BlockSpec((block, width), lambda t, _: (t, 0))
    return call(
        last_norm_body,
        (frames // block,),
        [rows, rows, rows, rows, whole((1, width)), IN_PLACE],
        rows,
        shaped(x.shape, WIDE),
        [],
        20 * x.size,
        16 * x.size,
        "last_norm",
        (meta, x, own, other, grad, gain, after),
    )


def on_pair(
    inputs,
    encoder_text_states,
    cotangent,
    clip_adapter_index,
    self_norm_gain,
    cross_norm_gain,
    feed_norm_gain,
    self_query_key_value_weight,
    self_output_weight,
    cross_query_weight,
    cross_key_value_weight,
    cross_output_weight,
    up_weight,
    down_weight,
    self_first_factors,
    self_second_factors,
    cross_first_factors,
    cross_second_factors,
    attention_first_factors,
    attention_second_factors,
    input_first_factors,
    input_second_factors,
    output_first_factors,
    output_second_factors,
):
    x = inputs[0]
    text = encoder_text_states[0]
    cot = cotangent[0]
    width = x.shape[1]
    local = self_output_weight.shape[0]
    hidden = up_weight.shape[1]
    slots = input_first_factors.shape[0]
    group_count = lax.axis_size("dp")
    place = lax.axis_index("dp")
    side = lax.axis_index("tensor")
    picks = clip_adapter_index[0]
    meta = jnp.concatenate([picks, jnp.stack([side, place]).astype(jnp.int32)])
    gain_one, gain_two, gain_three = (
        vec.reshape(1, width) for vec in (self_norm_gain, cross_norm_gain, feed_norm_gain)
    )

    def swap(array):
        return lax.ppermute(array, "tensor", [(0, 1), (1, 0)])

    depth = width // group_count
    step = local // group_count

    def share(weight, size):
        return lax.dynamic_slice_in_dim(weight, place * size, size, axis=0)

    def side_by_side(rows, count):
        return rows.reshape(rows.shape[0], count, -1).transpose(1, 0, 2)

    out_share = side_by_side(share(self_output_weight, step), 2).reshape(depth, local)
    query_share = share(cross_query_weight, depth)
    cross_share = side_by_side(share(cross_output_weight, step), 2).reshape(depth, local)
    share_one = swap(jnp.stack([out_share, query_share, cross_share]))
    rows_one = first_norm(meta, x, gain_one)
    share_one, rows_one = lax.optimization_barrier((share_one, rows_one))
    gathered_one = lax.all_gather(share_one, "dp", axis=0)
    rows_one_other = swap(rows_one)
    factors = picked_factors(
        meta,
        [
            (attention_first_factors, 0, 3),
            (attention_first_factors, 1, 7),
            (cross_second_factors, 0, 4),
            (cross_second_factors, 1, 5),
            (cross_second_factors, 2, 6),
            (input_second_factors, None, 8),
            (output_first_factors, None, 9),
        ],
    )
    packed = swap(factors)
    first_pack = 5 * local

    heads_own = project_heads(
        meta, rows_one, self_query_key_value_weight, self_first_factors, self_second_factors, 0, 0, "own_heads"
    )
    part_own = self_forward_own(meta, heads_own, factors)
    text_own = project_heads(
        meta, text, cross_key_value_weight, cross_first_factors, cross_second_factors, 5, 1, "text_heads"
    )
    text_other = swap(text_own)
    share_two = feed_share(
        meta, down_weight, up_weight, depth, (part_own, text_own, rows_one_other)
    )
    heads_other = project_heads(
        meta, rows_one_other, self_query_key_value_weight, self_first_factors, self_second_factors,
        0, 0, "other_heads", (share_two,),
    )
    z_own_frames, z_other_frames, log_own, log_other = self_forward(meta, part_own, heads_own, heads_other)
    share_two, z_other_frames = lax.optimization_barrier((swap(share_two), z_other_frames))
    gathered_two = lax.all_gather(share_two, "dp", axis=0)
    z_other_heads = swap(z_other_frames)
    weights = (self_output_weight, cross_query_weight, cross_output_weight)
    tables = (attention_first_factors, attention_second_factors, cross_first_factors, cross_second_factors)
    stream_one, stream_two, rows_three, q_own, q_other, z2_own, z2_other = middle_forward(
        meta, x, z_own_frames, z_other_heads, weights, gathered_one, tables, packed,
        text_own, text_other, (gain_two, gain_three),
    )
    tile = local
    branch, grad_rows, rank9, grad_rank8, ga9_own, gb8_own = feed_own(
        meta, rows_three, cot, up_weight, down_weight, input_first_factors, input_second_factors,
        output_first_factors, output_second_factors, tile,
    )
    output, grad_two, ga9_other, gb8_other, feed_mine, feed_theirs = feed_other(
        meta, rows_three, cot, gathered_two, packed, first_pack, input_first_factors,
        output_second_factors, (branch, grad_rows, rank9, grad_rank8), stream_two, gain_three, tile,
    )

    gb8_received = swap(gb8_other)
    ga9_received = swap(ga9_other)
    feed_received = swap(feed_theirs)

    (
        grad_one, dz_own_heads, dz_other_heads, text_grad_own, text_grad_other, middle_mine, middle_theirs,
        text_mine_rank, text_theirs_rank,
    ) = middle_back(
        meta, grad_two, stream_one, z_own_frames, z_other_heads, q_own, q_other, z2_own, z2_other,
        weights, gathered_one, tables, packed, text_own, text_other, gain_two, text,
    )
    gb8_received, ga9_received, feed_received, dz_other_heads = lax.optimization_barrier(
        (gb8_received, ga9_received, feed_received, dz_other_heads)
    )
    dz_other_frames, text_theirs_rank, text_grad_other = lax.optimization_barrier(
        (swap(dz_other_heads), text_theirs_rank, text_grad_other)
    )

    unit = local
    hidden_units = hidden // unit
    labels = jnp.zeros((RANK_UNIT, 2 * HEAD_DIM), LOW).at[:, : picks.shape[0]].set(picks.astype(LOW)[None])
    early = jnp.concatenate(
        [
            join(middle_mine, [swap(middle_theirs)]),
            join(feed_mine, [feed_received]),
            join(jnp.concatenate([gb8_own, ga9_own], axis=1), [gb8_received, ga9_received]),
            labels,
        ],
        axis=1,
    )
    early_all = lax.all_gather(early, "dp", axis=0)
    grads_part = self_back_own(meta, heads_own, z_own_frames, log_own, dz_own_heads)
    grads_own, grads_other = self_back(
        meta, grads_part, heads_own, heads_other, z_own_frames, z_other_frames, log_own, log_other,
        dz_own_heads, dz_other_frames, (early,),
    )
    text_grad_other, text_received_rank, grads_own = lax.optimization_barrier(
        (swap(text_grad_other), swap(text_theirs_rank), grads_own)
    )
    text_heads_grad = (text_grad_own + text_grad_other.astype(WIDE)).astype(LOW)
    mine, theirs = rank_grads(
        meta, [rows_one, rows_one_other], [grads_own, grads_other], self_first_factors,
        self_second_factors, 0, 0, "self_ranks",
    )
    partial_other = project_back_heads(
        meta, grads_other, self_query_key_value_weight, self_first_factors, self_second_factors,
        0, 0, LOW, "other_back", theirs,
    )
    received = swap(partial_other)
    labels = lax.dynamic_index_in_dim(early_all[:, :, -2 * HEAD_DIM :], place, axis=0, keepdims=False)
    late = jnp.concatenate(
        [join(mine, [swap(theirs)]), join(text_mine_rank, [text_received_rank]), labels], axis=1
    )
    late_all = lax.all_gather(late, "dp", axis=0)
    text_rows = project_back_heads(
        meta, text_heads_grad, cross_key_value_weight, cross_first_factors, cross_second_factors,
        5, 1, WIDE, "text_back", partial_other,
    )
    text_halves = (text_rows[:, : width // 2], text_rows[:, width // 2 :])
    text_mine = jnp.where(side == 0, text_halves[0], text_halves[1])
    text_theirs = jnp.where(side == 0, text_halves[1], text_halves[0])
    text_received = swap(text_theirs.astype(LOW))
    partial_own = project_back_heads(
        meta, grads_own, self_query_key_value_weight, self_first_factors, self_second_factors,
        0, 0, WIDE, "own_back", late,
    )
    sum_query_a, sum_query_b, sum_out_a, sum_out_b, sum_up_a, sum_down_b, sum_up_b, sum_down_a = slot_sums(
        meta,
        early_all,
        [(4, 0, 0), (4, 1, 0), (3, 2, 0), (7, 2, 1), (3, 3, 0), (7, 3, 1), (8, 4, 0), (9, 5, 0)]
        + [(8, 6, i) for i in range(hidden_units)]
        + [(9, 7, i) for i in range(hidden_units)],
        [(1, unit), (1, unit), (2, unit), (2, unit), (None, unit), (None, unit), (None, hidden), (None, hidden)],
        slots, unit, {}, "early_slots", (partial_own,),
    )
    received, text_received, sum_up_a = lax.optimization_barrier((received, text_received, sum_up_a))
    text_grad = text_mine + text_received.astype(WIDE)
    input_grad = last_norm(meta, x, partial_own, received, grad_one, gain_one, sum_up_a)
    sum_self_a, sum_self_b, sum_cross_a, sum_cross_b = slot_sums(
        meta,
        late_all,
        [(0, 0, 0), (1, 0, 1), (2, 0, 2), (0, 1, 0), (1, 1, 1), (2, 1, 2)]
        + [(5, 2, 1), (6, 2, 2), (5, 3, 1), (6, 3, 2)],
        [(3, unit), (3, unit), (3, unit), (3, unit)],
        slots, unit, {2: sum_query_a, 3: sum_query_b}, "late_slots", (input_grad,),
    )
    return (
        output[None],
        input_grad[None],
        text_grad[None],
        sum_self_a,
        sum_self_b,
        sum_cross_a,
        sum_cross_b,
        sum_out_a,
        sum_out_b,
        sum_up_a,
        sum_up_b,
        sum_down_a,
        sum_down_b,
    )


def solution(mesh):
    in_specs = (
        P("dp", "tensor", None),
        P("dp", None, None),
        P("dp", "tensor", None),
        P("dp", None),
        P(),
        P(),
        P(),
        P(None, None, "tensor"),
        P("tensor", None),
        P(None, "tensor"),
        P(None, None, "tensor"),
        P("tensor", None),
        P(None, "tensor"),
        P("tensor", None),
        P(),
        P(None, None, None, "tensor"),
        P(),
        P(None, None, None, "tensor"),
        P(None, None, None, "tensor"),
        P(),
        P(),
        P(None, None, "tensor"),
        P(None, None, "tensor"),
        P(),
    )
    out_specs = (
        P("dp", "tensor", None),
        P("dp", "tensor", None),
        P("dp", None, "tensor"),
        P(None, None, None, "tensor"),
        P(None, None, None, "tensor"),
        P(None, None, None, "tensor"),
        P(None, None, None, "tensor"),
        P(None, None, None, "tensor"),
        P(None, None, None, "tensor"),
        P(None, None, "tensor"),
        P(None, None, "tensor"),
        P(None, None, "tensor"),
        P(None, None, "tensor"),
    )
    layer = on_pair if mesh.shape["tensor"] == 2 else on_device
    return jax.shard_map(
        layer, mesh=mesh, in_specs=in_specs, out_specs=out_specs, check_vma=False
    )
```

```python
import jax
import jax.numpy as jnp
from jax import lax
from jax.experimental import pallas as pl
from jax.experimental.pallas import tpu as pltpu
from jax.sharding import PartitionSpec as P

HEAD_DIM = 64


epsilon = 1e-05


def split_dot(form, wide_part, narrow_part):
    high_part = wide_part.astype(jnp.bfloat16)
    rest_part = (wide_part - high_part.astype(jnp.float32)).astype(jnp.bfloat16)
    first = jnp.einsum(form, high_part, narrow_part, preferred_element_type=jnp.float32)
    return first + jnp.einsum(form, rest_part, narrow_part, preferred_element_type=jnp.float32)


def layer_norm(stream, gain_vec):
    centred = stream - jnp.mean(stream, axis=-1, keepdims=True)
    inverse = lax.rsqrt(jnp.mean(centred * centred, axis=-1, keepdims=True) + epsilon)
    normed = centred * inverse
    return (normed * gain_vec, normed, inverse)


def norm_back(grad_out, gain_vec, normed, inverse):
    grad_norm = grad_out * gain_vec
    mean_grad = jnp.mean(grad_norm, axis=-1, keepdims=True)
    mean_cross = jnp.mean(grad_norm * normed, axis=-1, keepdims=True)
    return inverse * (grad_norm - mean_grad - normed * mean_cross)


def spread_rows(local_rows):
    return lax.all_gather(local_rows.astype(jnp.bfloat16), "tensor", axis=1, tiled=True)


def reduce_grads(partial_sum):
    return lax.psum_scatter(
        partial_sum.astype(jnp.bfloat16), "tensor", scatter_dimension=1, tiled=True
    ).astype(jnp.float32)


def project_rows(act_rows, weight, output_choice, input_choice):
    low_rank = jnp.einsum(
        "ctd,crd->ctr", act_rows, output_choice, preferred_element_type=jnp.float32
    )
    result = jnp.einsum("ctd,de->cte", act_rows, weight, preferred_element_type=jnp.float32)
    result = result + split_dot("ctr,cre->cte", low_rank, input_choice)
    return (result, low_rank)


def project_back(grad_low, act_rows, weight, output_choice, input_choice, low_rank):
    grad_rank = jnp.einsum(
        "cte,cre->ctr", grad_low, input_choice, preferred_element_type=jnp.float32
    )
    grad_rows = jnp.einsum("cte,de->ctd", grad_low, weight, preferred_element_type=jnp.float32)
    grad_rows = grad_rows + split_dot("ctr,crd->ctd", grad_rank, output_choice)
    grad_down = split_dot("ctr,ctd->crd", grad_rank, act_rows)
    grad_up = split_dot("ctr,cte->cre", low_rank, grad_low)
    return (grad_rows, grad_down, grad_up)


def causal_frames(first_row, block_rows, key_count):
    query_at = first_row + jnp.arange(block_rows, dtype=jnp.int32)[:, None]
    key_at = jnp.arange(key_count, dtype=jnp.int32)[None, :]
    return key_at <= query_at


def attention_forward(queries, key_rows, value_rows, causal):
    frames = queries.shape[1]
    key_count = key_rows.shape[1]
    block_rows = min(512, frames)
    score_scale = HEAD_DIM ** (-0.5)
    outputs = []
    log_totals = []
    for first_row in range(0, frames, block_rows):
        key_end = first_row + block_rows if causal else key_count
        query_block = queries[:, first_row : first_row + block_rows]
        scores = (
            jnp.einsum(
                "cbhe,ckhe->chbk",
                query_block,
                key_rows[:, :key_end],
                preferred_element_type=jnp.float32,
            )
            * score_scale
        )
        if causal:
            scores = jnp.where(causal_frames(first_row, block_rows, key_end), scores, -1e30)
        largest = jnp.max(scores, axis=-1, keepdims=True)
        exponent = jnp.exp(scores - largest)
        summed = jnp.sum(exponent, axis=-1, keepdims=True)
        prob_low = (exponent / summed).astype(jnp.bfloat16)
        outputs.append(
            jnp.einsum(
                "chbk,ckhe->cbhe",
                prob_low,
                value_rows[:, :key_end],
                preferred_element_type=jnp.float32,
            )
        )
        log_totals.append(largest + jnp.log(summed))
    return (jnp.concatenate(outputs, axis=1), jnp.concatenate(log_totals, axis=2))


def attention_back(queries, key_rows, value_rows, log_totals, grad_mixed, causal):
    frames = queries.shape[1]
    key_count = key_rows.shape[1]
    block_rows = min(512, frames)
    score_scale = HEAD_DIM ** (-0.5)
    grad_keys = jnp.zeros(key_rows.shape, jnp.float32)
    grad_values = jnp.zeros(value_rows.shape, jnp.float32)
    grad_queries = []
    for first_row in range(0, frames, block_rows):
        key_end = first_row + block_rows if causal else key_count
        key_part = key_rows[:, :key_end]
        value_part = value_rows[:, :key_end]
        query_block = queries[:, first_row : first_row + block_rows]
        grad_block = grad_mixed[:, first_row : first_row + block_rows]
        scores = (
            jnp.einsum("cbhe,ckhe->chbk", query_block, key_part, preferred_element_type=jnp.float32)
            * score_scale
        )
        if causal:
            scores = jnp.where(causal_frames(first_row, block_rows, key_end), scores, -1e30)
        probs = jnp.exp(scores - log_totals[:, :, first_row : first_row + block_rows])
        grad_values = grad_values.at[:, :key_end].add(
            jnp.einsum(
                "chbk,cbhe->ckhe",
                probs.astype(jnp.bfloat16),
                grad_block,
                preferred_element_type=jnp.float32,
            )
        )
        grad_probs = jnp.einsum(
            "cbhe,ckhe->chbk", grad_block, value_part, preferred_element_type=jnp.float32
        )
        inner_sum = jnp.sum(probs * grad_probs, axis=-1, keepdims=True)
        grad_scores = (probs * (grad_probs - inner_sum)).astype(jnp.bfloat16)
        grad_queries.append(
            jnp.einsum("chbk,ckhe->cbhe", grad_scores, key_part, preferred_element_type=jnp.float32)
            * score_scale
        )
        grad_keys = grad_keys.at[:, :key_end].add(
            jnp.einsum(
                "chbk,cbhe->ckhe", grad_scores, query_block, preferred_element_type=jnp.float32
            )
            * score_scale
        )
    return (jnp.concatenate(grad_queries, axis=1), grad_keys, grad_values)


def gelu_exact(pre_act):
    return jax.nn.gelu(pre_act, approximate=False)


def on_device(
    inputs,
    encoder_text_states,
    cotangent,
    clip_adapter_index,
    self_norm_gain,
    cross_norm_gain,
    feed_norm_gain,
    self_query_key_value_weight,
    self_output_weight,
    cross_query_weight,
    cross_key_value_weight,
    cross_output_weight,
    up_weight,
    down_weight,
    self_first_factors,
    self_second_factors,
    cross_first_factors,
    cross_second_factors,
    attention_first_factors,
    attention_second_factors,
    input_first_factors,
    input_second_factors,
    output_first_factors,
    output_second_factors,
):
    adapter_slot_count = input_first_factors.shape[0]
    chooser = (
        clip_adapter_index[:, :, None]
        == jnp.arange(adapter_slot_count, dtype=jnp.int32)[None, None, :]
    ).astype(jnp.bfloat16)
    local_heads = self_output_weight.shape[0] // HEAD_DIM

    def choose_adapter_slot(adapter_slot_table, column_index):
        return jnp.einsum(
            "cn,npq->cpq",
            chooser[:, column_index],
            adapter_slot_table,
            preferred_element_type=jnp.float32,
        ).astype(jnp.bfloat16)

    def slot_grads(grad_pick, column_index):
        return split_dot("cpq,cn->npq", grad_pick, chooser[:, column_index])

    def split_heads(stacked):
        return stacked.reshape(stacked.shape[0], stacked.shape[1], local_heads, HEAD_DIM)

    def join_heads(stacked):
        return stacked.reshape(stacked.shape[0], stacked.shape[1], local_heads * HEAD_DIM)

    def out_forward(mixed_in, inner_layer):
        column_index = 3 + 4 * inner_layer
        input_choice = choose_adapter_slot(attention_second_factors[inner_layer], column_index)
        weight = self_output_weight if inner_layer == 0 else cross_output_weight
        output_choice = choose_adapter_slot(attention_first_factors[inner_layer], column_index)
        partial_out, low_rank = project_rows(mixed_in, weight, output_choice, input_choice)
        branch = lax.psum_scatter(
            partial_out.astype(jnp.bfloat16), "tensor", scatter_dimension=1, tiled=True
        ).astype(jnp.float32)
        kept_data = (mixed_in, weight, output_choice, input_choice, low_rank)
        return (branch, kept_data)

    def out_back(grad_stream, kept_data):
        mixed_in, weight, output_choice, input_choice, low_rank = kept_data
        grad_low = grad_stream.astype(jnp.bfloat16)
        grad_full = lax.all_gather(grad_low, "tensor", axis=1, tiled=True)
        grad_rows, grad_down, grad_up = project_back(
            grad_full, mixed_in, weight, output_choice, input_choice, low_rank
        )
        grad_mixed = grad_rows.astype(jnp.bfloat16)
        return (grad_mixed, grad_down, grad_up)

    stream = inputs.astype(jnp.float32)
    normed_value, normed_one, inverse_one = layer_norm(stream, self_norm_gain)
    rows_one = spread_rows(normed_value)
    self_down_factor = [
        choose_adapter_slot(self_first_factors[slot_number], slot_number)
        for slot_number in range(3)
    ]
    self_up_factor = [
        choose_adapter_slot(self_second_factors[slot_number], slot_number)
        for slot_number in range(3)
    ]
    self_parts = [
        project_rows(
            rows_one,
            self_query_key_value_weight[slot_number],
            self_down_factor[slot_number],
            self_up_factor[slot_number],
        )
        for slot_number in range(3)
    ]
    self_heads = [
        split_heads(self_parts[slot_number][0].astype(jnp.bfloat16)) for slot_number in range(3)
    ]
    mixed_one, totals_one = attention_forward(self_heads[0], self_heads[1], self_heads[2], True)
    mixed_one = join_heads(mixed_one).astype(jnp.bfloat16)
    branch_one, kept_one = out_forward(mixed_one, 0)
    stream_one = stream + branch_one
    normed_value, normed_two, inverse_two = layer_norm(stream_one, cross_norm_gain)
    rows_two = spread_rows(normed_value)
    cross_down_factor = [
        choose_adapter_slot(cross_first_factors[slot_number], 4 + slot_number)
        for slot_number in range(3)
    ]
    cross_up_factor = [
        choose_adapter_slot(cross_second_factors[slot_number], 4 + slot_number)
        for slot_number in range(3)
    ]
    query_full, query_rank = project_rows(
        rows_two, cross_query_weight, cross_down_factor[0], cross_up_factor[0]
    )
    key_full, key_rank = project_rows(
        encoder_text_states, cross_key_value_weight[0], cross_down_factor[1], cross_up_factor[1]
    )
    value_full, value_rank = project_rows(
        encoder_text_states, cross_key_value_weight[1], cross_down_factor[2], cross_up_factor[2]
    )
    query_two = split_heads(query_full.astype(jnp.bfloat16))
    key_two = split_heads(key_full.astype(jnp.bfloat16))
    value_two = split_heads(value_full.astype(jnp.bfloat16))
    mixed_two, totals_two = attention_forward(query_two, key_two, value_two, False)
    mixed_two = join_heads(mixed_two).astype(jnp.bfloat16)
    branch_two, kept_two = out_forward(mixed_two, 1)
    stream_two = stream_one + branch_two
    normed_value, normed_three, inverse_three = layer_norm(stream_two, feed_norm_gain)
    rows_three = spread_rows(normed_value)
    input_second_choice = choose_adapter_slot(input_first_factors, 8)
    input_first_choice = choose_adapter_slot(input_second_factors, 8)
    before, up_rank = project_rows(rows_three, up_weight, input_second_choice, input_first_choice)
    gelu_value, gelu_pull = jax.vjp(gelu_exact, before)
    hidden = gelu_value.astype(jnp.bfloat16)
    output_second_choice = choose_adapter_slot(output_first_factors, 9)
    output_first_choice = choose_adapter_slot(output_second_factors, 9)
    partial_out, down_rank = project_rows(
        hidden, down_weight, output_second_choice, output_first_choice
    )
    branch_three = lax.psum_scatter(
        partial_out.astype(jnp.bfloat16), "tensor", scatter_dimension=1, tiled=True
    ).astype(jnp.float32)
    output = (stream_two + branch_three).astype(jnp.bfloat16)
    grad_full = lax.all_gather(cotangent, "tensor", axis=1, tiled=True)
    grad_hidden, grad_down_a, grad_down_b = project_back(
        grad_full, hidden, down_weight, output_second_choice, output_first_choice, down_rank
    )
    grad_before = gelu_pull(grad_hidden)[0].astype(jnp.bfloat16)
    grad_rows, grad_up_a, grad_up_b = project_back(
        grad_before, rows_three, up_weight, input_second_choice, input_first_choice, up_rank
    )
    grad_stream = cotangent.astype(jnp.float32) + norm_back(
        reduce_grads(grad_rows), feed_norm_gain, normed_three, inverse_three
    )
    grad_mixed, grad_out_a_two, grad_out_b_two = out_back(grad_stream, kept_two)
    grad_query, grad_key, grad_value = attention_back(
        query_two, key_two, value_two, totals_two, split_heads(grad_mixed), False
    )
    grad_query = join_heads(grad_query).astype(jnp.bfloat16)
    grad_key = join_heads(grad_key).astype(jnp.bfloat16)
    grad_value = join_heads(grad_value).astype(jnp.bfloat16)
    grad_rows_query, cross_grad_a_zero, cross_grad_b_zero = project_back(
        grad_query,
        rows_two,
        cross_query_weight,
        cross_down_factor[0],
        cross_up_factor[0],
        query_rank,
    )
    grad_text_key, cross_grad_a_one, cross_grad_b_one = project_back(
        grad_key,
        encoder_text_states,
        cross_key_value_weight[0],
        cross_down_factor[1],
        cross_up_factor[1],
        key_rank,
    )
    grad_text_value, cross_grad_a_two, cross_grad_b_two = project_back(
        grad_value,
        encoder_text_states,
        cross_key_value_weight[1],
        cross_down_factor[2],
        cross_up_factor[2],
        value_rank,
    )
    normed_grad, text_grad = (
        lax.psum_scatter(
            grad_rows_query.astype(jnp.bfloat16), "tensor", scatter_dimension=1, tiled=True
        ).astype(jnp.float32),
        lax.psum_scatter(
            (grad_text_key + grad_text_value).astype(jnp.bfloat16),
            "tensor",
            scatter_dimension=2,
            tiled=True,
        ).astype(jnp.float32),
    )
    grad_stream = grad_stream + norm_back(normed_grad, cross_norm_gain, normed_two, inverse_two)
    grad_mixed, grad_out_a_one, grad_out_b_one = out_back(grad_stream, kept_one)
    grad_query, grad_key, grad_value = attention_back(
        self_heads[0], self_heads[1], self_heads[2], totals_one, split_heads(grad_mixed), True
    )
    self_grads = [
        join_heads(grad_query).astype(jnp.bfloat16),
        join_heads(grad_key).astype(jnp.bfloat16),
        join_heads(grad_value).astype(jnp.bfloat16),
    ]
    self_rows_total = jnp.zeros(rows_one.shape, jnp.float32)
    self_grad_a = []
    self_grad_b = []
    for slot_number in range(3):
        grad_rows, grad_a_part, grad_b_part = project_back(
            self_grads[slot_number],
            rows_one,
            self_query_key_value_weight[slot_number],
            self_down_factor[slot_number],
            self_up_factor[slot_number],
            self_parts[slot_number][1],
        )
        self_rows_total = self_rows_total + grad_rows
        self_grad_a.append(slot_grads(grad_a_part, slot_number))
        self_grad_b.append(slot_grads(grad_b_part, slot_number))
    input_grad = grad_stream + norm_back(
        reduce_grads(self_rows_total), self_norm_gain, normed_one, inverse_one
    )
    sum_self_a = jnp.stack(self_grad_a)
    sum_self_b = jnp.stack(self_grad_b)
    sum_cross_a = jnp.stack(
        [
            slot_grads(cross_grad_a_zero, 4),
            slot_grads(cross_grad_a_one, 5),
            slot_grads(cross_grad_a_two, 6),
        ]
    )
    sum_cross_b = jnp.stack(
        [
            slot_grads(cross_grad_b_zero, 4),
            slot_grads(cross_grad_b_one, 5),
            slot_grads(cross_grad_b_two, 6),
        ]
    )
    sum_out_a = jnp.stack([slot_grads(grad_out_a_one, 3), slot_grads(grad_out_a_two, 7)])
    sum_out_b = jnp.stack([slot_grads(grad_out_b_one, 3), slot_grads(grad_out_b_two, 7)])
    sum_up_a = slot_grads(grad_up_a, 8)
    sum_up_b = slot_grads(grad_up_b, 8)
    sum_down_a = slot_grads(grad_down_a, 9)
    sum_down_b = slot_grads(grad_down_b, 9)
    sum_self_a, sum_cross_a, sum_out_b, sum_up_a, sum_down_b = (
        lax.psum_scatter(
            sum_self_a.astype(jnp.bfloat16), "tensor", scatter_dimension=3, tiled=True
        ).astype(jnp.float32),
        lax.psum_scatter(
            sum_cross_a.astype(jnp.bfloat16), "tensor", scatter_dimension=3, tiled=True
        ).astype(jnp.float32),
        lax.psum_scatter(
            sum_out_b.astype(jnp.bfloat16), "tensor", scatter_dimension=3, tiled=True
        ).astype(jnp.float32),
        lax.psum_scatter(
            sum_up_a.astype(jnp.bfloat16), "tensor", scatter_dimension=2, tiled=True
        ).astype(jnp.float32),
        lax.psum_scatter(
            sum_down_b.astype(jnp.bfloat16), "tensor", scatter_dimension=2, tiled=True
        ).astype(jnp.float32),
    )
    totals = (
        lax.psum(sum_self_a.astype(jnp.bfloat16), "dp").astype(jnp.float32),
        lax.psum(sum_self_b.astype(jnp.bfloat16), "dp").astype(jnp.float32),
        lax.psum(sum_cross_a.astype(jnp.bfloat16), "dp").astype(jnp.float32),
        lax.psum(sum_cross_b.astype(jnp.bfloat16), "dp").astype(jnp.float32),
        lax.psum(sum_out_a.astype(jnp.bfloat16), "dp").astype(jnp.float32),
        lax.psum(sum_out_b.astype(jnp.bfloat16), "dp").astype(jnp.float32),
        lax.psum(sum_up_a.astype(jnp.bfloat16), "dp").astype(jnp.float32),
        lax.psum(sum_up_b.astype(jnp.bfloat16), "dp").astype(jnp.float32),
        lax.psum(sum_down_a.astype(jnp.bfloat16), "dp").astype(jnp.float32),
        lax.psum(sum_down_b.astype(jnp.bfloat16), "dp").astype(jnp.float32),
    )
    return (
        output,
        input_grad,
        text_grad,
        totals[0],
        totals[1],
        totals[2],
        totals[3],
        totals[4],
        totals[5],
        totals[6],
        totals[7],
        totals[8],
        totals[9],
    )


LOW = jnp.bfloat16
WIDE = jnp.float32
VMEM_BYTES = 58 * 1024 * 1024
RANK_UNIT = 16
COST_SCALE = 1


def mm(left, right, left_dim=1, right_dim=0):
    return lax.dot_general(
        left, right, (((left_dim,), (right_dim,)), ((), ())), preferred_element_type=WIDE
    )


def mm_nt(left, right):
    return mm(left, right, 1, 1)


def mm_tn(left, right):
    return mm(left, right, 0, 0)


def low_rank(factor, rows):
    return mm_nt(factor, rows).astype(LOW)


def norm_rows(rows, gain):
    centred = rows - jnp.mean(rows, axis=-1, keepdims=True)
    inverse = lax.rsqrt(jnp.mean(centred * centred, axis=-1, keepdims=True) + epsilon)
    normed = centred * inverse
    return normed * gain, normed, inverse


def lane_halves():
    lane = lax.broadcasted_iota(jnp.int32, (1, 2 * HEAD_DIM), 1)
    return lane < HEAD_DIM


def half_masks():
    left = lane_halves()
    first = jnp.where(left, 1.0, 0.0)
    return first.astype(LOW), (1.0 - first).astype(LOW)


def gelu_parts(pre):
    bell = jnp.exp(-0.5 * pre * pre)
    step = 1.0 / (1.0 + (0.3275911 * 0.7071067811865476) * jnp.abs(pre))
    tail = step * (
        0.5 * 0.254829592
        + step
        * (
            0.5 * -0.284496736
            + step
            * (0.5 * 1.421413741 + step * (0.5 * -1.453152027 + step * (0.5 * 1.061405429)))
        )
    )
    tail = tail * bell
    phi = jnp.where(pre >= 0.0, 1.0 - tail, tail)
    return pre * phi, phi + pre * bell * 0.3989422804014327


def whole(shape, where=None):
    place = (0,) * len(shape) if where is None else where
    return pl.BlockSpec(shape, lambda *_: place, pipeline_mode=pl.Buffered(1))


def call(body, grid, in_specs, out_specs, out_shape, scratch, flops, moved, name, args):
    return pl.pallas_call(
        body,
        grid_spec=pltpu.PrefetchScalarGridSpec(
            num_scalar_prefetch=1,
            grid=grid,
            in_specs=in_specs,
            out_specs=out_specs,
            scratch_shapes=scratch,
        ),
        out_shape=out_shape,
        compiler_params=pltpu.CompilerParams(
            dimension_semantics=("arbitrary",) * len(grid), vmem_limit_bytes=VMEM_BYTES
        ),
        cost_estimate=pl.CostEstimate(
            flops=flops // COST_SCALE, bytes_accessed=moved // COST_SCALE, transcendentals=0
        ),
        name=name,
    )(*args)


def shaped(shape, dtype):
    return jax.ShapeDtypeStruct(shape, dtype)


IN_PLACE = pl.BlockSpec(memory_space=pl.ANY)


def factors_body(_, *refs):
    out_ref = refs[-1]
    first = 0
    for ref in refs[:-1]:
        size = ref.shape[-1]
        out_ref[:, first : first + size] = ref[...]
        first += size


def picked_factors(meta, sources):
    specs = []
    total = 0
    for table, entry, slot in sources:
        if entry is None:
            spec = pl.BlockSpec((None,) + table.shape[1:], lambda t, m, slot=slot: (m[slot], 0, 0))
        else:
            spec = pl.BlockSpec(
                (None, None) + table.shape[2:], lambda t, m, entry=entry, slot=slot: (entry, m[slot], 0, 0)
            )
        specs.append(spec)
        total += table.shape[-1]
    shape = (RANK_UNIT, total)
    return call(
        factors_body, (1,), specs, whole(shape), shaped(shape, LOW), [], 0, 4 * RANK_UNIT * total,
        "picked_factors", (meta,) + tuple(table for table, _, _ in sources),
    )


def share_body(_, parts, down_ref, up_ref, *refs):
    out_ref = refs[-1]
    step = pl.program_id(0)

    @pl.when(step < parts)
    def _():
        out_ref[0] = down_ref[...]

    @pl.when(step >= parts)
    def _():
        out_ref[0] = up_ref[...]


def feed_share(meta, down_weight, up_weight, depth, after):
    hidden, width = down_weight.shape
    parts = hidden // width
    return call(
        lambda m, *refs: share_body(m, parts, *refs),
        (2 * parts,),
        [
            pl.BlockSpec(
                (depth, width), lambda t, m: (m[11] * parts + jnp.minimum(t, parts - 1), 0)
            ),
            pl.BlockSpec((depth, width), lambda t, m: (m[11], jnp.maximum(t - parts, 0))),
        ]
        + [IN_PLACE] * len(after),
        pl.BlockSpec((1, depth, width), lambda t, m: (t, 0, 0)),
        shaped((2 * parts, depth, width), LOW),
        [],
        0,
        8 * parts * depth * width,
        "feed_share",
        (meta, down_weight, up_weight, *after),
    )


def first_norm_body(_, x_ref, gain_ref, out_ref):
    rows, _, _ = norm_rows(x_ref[...].astype(WIDE), gain_ref[...])
    out_ref[...] = rows.astype(LOW)


def first_norm(meta, x, gain):
    frames, width = x.shape
    block = min(256, frames)
    rows = pl.BlockSpec((block, width), lambda t, _: (t, 0))
    return call(
        first_norm_body,
        (frames // block,),
        [rows, whole((1, width))],
        rows,
        shaped(x.shape, LOW),
        [],
        10 * x.size,
        4 * x.size,
        "first_norm",
        (meta, x, gain),
    )


def project_body(_, act_ref, weight_ref, down_ref, up_ref, *refs):
    out_ref, rank_ref = refs[-2:]
    act = act_ref[...]
    rank = low_rank(down_ref[0, 0], act)
    rank_ref[0] = rank
    out_ref[0] = (mm(act, weight_ref[0]) + mm_tn(rank, up_ref[0, 0])).astype(LOW)


def project_heads(meta, act, weights, down, up, slots, skip, name, after=()):
    rows, width = act.shape
    count, _, local = weights.shape
    first_slot = slots
    return call(
        project_body,
        (count,),
        [
            whole((rows, width)),
            pl.BlockSpec((1, width, local), lambda j, m: (j, 0, 0)),
            pl.BlockSpec((1, 1, RANK_UNIT, width), lambda j, m: (j + skip, m[first_slot + j], 0, 0)),
            pl.BlockSpec((1, 1, RANK_UNIT, local), lambda j, m: (j + skip, m[first_slot + j], 0, 0)),
        ]
        + [IN_PLACE] * len(after),
        (
            pl.BlockSpec((1, rows, local), lambda j, m: (j, 0, 0)),
            pl.BlockSpec((1, RANK_UNIT, rows), lambda j, m: (j, 0, 0)),
        ),
        (shaped((count, rows, local), LOW), shaped((count, RANK_UNIT, rows), LOW)),
        [],
        2 * rows * width * local * count,
        2 * (weights.size + act.size + count * rows * local),
        name,
        (meta, act, weights, down, up, *after),
    )


def project_back_body(_, last, grad_ref, weight_ref, down_ref, up_ref, after_ref, out_ref, total_ref):
    step = pl.program_id(0)
    grad = grad_ref[0]
    grad_rank = low_rank(up_ref[0, 0], grad)
    part = mm_nt(grad, weight_ref[0]) + mm_tn(grad_rank, down_ref[0, 0])

    @pl.when(step == 0)
    def _():
        total_ref[...] = part

    @pl.when(step > 0)
    def _():
        total_ref[...] += part

    @pl.when(step == last)
    def _():
        out_ref[...] = total_ref[...].astype(out_ref.dtype)


def project_back_heads(meta, grads, weights, down, up, slots, skip, kind, name, after, part=(0, 1)):
    count, width, local = weights.shape
    which, parts = part
    rows = grads.shape[1] // parts
    return call(
        lambda m, *refs: project_back_body(m, count - 1, *refs),
        (count,),
        [
            pl.BlockSpec((1, rows, local), lambda j, m: (j, which, 0)),
            pl.BlockSpec((1, width, local), lambda j, m: (j, 0, 0)),
            pl.BlockSpec((1, 1, RANK_UNIT, width), lambda j, m: (j + skip, m[slots + j], 0, 0)),
            pl.BlockSpec((1, 1, RANK_UNIT, local), lambda j, m: (j + skip, m[slots + j], 0, 0)),
            IN_PLACE,
        ],
        whole((rows, width)),
        shaped((rows, width), kind),
        [pltpu.VMEM((rows, width), WIDE)],
        2 * rows * width * local * count,
        2 * (weights.size + count * rows * local) + 4 * rows * width,
        name,
        (meta, grads, weights, down, up, after),
    )


def first_grads_body(meta, count, parts, *refs):
    ups = refs[2 * parts : 2 * parts + count]
    mine_ref, theirs_ref, ga, act_scratch, grad_scratch, sems = refs[-6:]
    half = ga.shape[1] // 2
    copies = []
    for part in range(parts):
        pairs = ((refs[parts + part], grad_scratch.at[part]), (refs[part], act_scratch.at[part]))
        copies.append(
            [pltpu.make_async_copy(*pair, sems.at[2 * part + number]) for number, pair in enumerate(pairs)]
        )
        for copy in copies[-1]:
            copy.start()
    for part in range(parts):
        copies[part][0].wait()
        grad_rank = jnp.concatenate(
            [low_rank(ups[j][0, 0], grad_scratch[part, j]) for j in range(count)], axis=0
        )
        copies[part][1].wait()
        product = mm(grad_rank, act_scratch[part])
        if part == 0:
            ga[...] = product
        else:
            ga[...] += product
    side = meta[10]
    for j in range(count):
        rows = slice(RANK_UNIT * j, RANK_UNIT * (j + 1))
        span = slice(j * half, (j + 1) * half)
        mine_ref[:, span] = ga[rows, pl.ds(pl.multiple_of(side * half, 128), half)]
        theirs = ga[rows, pl.ds(pl.multiple_of((1 - side) * half, 128), half)]
        theirs_ref[:, span] = theirs.astype(LOW)


def first_grads(meta, acts, grads, up, slots, name):
    rows, width = acts[0].shape
    count, _, local = grads[0].shape
    parts = len(acts)

    def table(j):
        return pl.BlockSpec(
            (1, 1, RANK_UNIT, local), lambda t, m: (j, m[slots + j], 0, 0), pipeline_mode=pl.Buffered(1)
        )

    shape = (RANK_UNIT, count * width // 2)
    return call(
        lambda m, *refs: first_grads_body(m, count, parts, *refs),
        (1,),
        [IN_PLACE] * (2 * parts) + [table(j) for j in range(count)],
        (whole(shape), whole(shape)),
        (shaped(shape, WIDE), shaped(shape, LOW)),
        [
            pltpu.VMEM((RANK_UNIT * count, width), WIDE),
            pltpu.VMEM((parts, rows, width), LOW),
            pltpu.VMEM((parts, count, rows, local), LOW),
            pltpu.SemaphoreType.DMA((2 * parts,)),
        ],
        4 * parts * rows * (width + local) * RANK_UNIT * count,
        2 * parts * rows * (width + count * local),
        name,
        (meta, *acts, *grads, *([up] * count)),
    )


def second_grads_body(_, parts, *refs):
    out_ref, grad_scratch, sems = refs[-3:]
    count, _, local = refs[parts].shape
    copies = [
        pltpu.make_async_copy(refs[parts + part].at[j], grad_scratch.at[part, j], sems.at[part * count + j])
        for part in range(parts)
        for j in range(count)
    ]
    for j in range(count):
        for part in range(parts):
            copies[part * count + j].start()
    for j in range(count):
        total = None
        for part in range(parts):
            copies[part * count + j].wait()
            product = mm(refs[part][j], grad_scratch[part, j])
            total = product if total is None else total + product
        out_ref[:, j * local : (j + 1) * local] = total.astype(LOW)


def second_grads(meta, ranks, grads, name, after):
    count, rows, local = grads[0].shape
    parts = len(ranks)
    shape = (RANK_UNIT, count * local)
    return call(
        lambda m, *refs: second_grads_body(m, parts, *refs),
        (1,),
        [whole(ranks[0].shape)] * parts + [IN_PLACE] * (parts + 1),
        whole(shape),
        shaped(shape, LOW),
        [pltpu.VMEM((parts, count, rows, local), LOW), pltpu.SemaphoreType.DMA((parts * count,))],
        2 * parts * rows * local * RANK_UNIT * count,
        2 * parts * rows * count * local,
        name,
        (meta, *ranks, *grads, after),
    )


def split_columns(meta, mine_ref, theirs_ref, first, array, skip=0):
    half = array.shape[-1] // 2
    side = meta[10]
    mine_ref[:, first : first + half] = array[:, pl.ds(pl.multiple_of(side * half, 128), half)]
    theirs = array[:, pl.ds(pl.multiple_of((1 - side) * half, 128), half)]
    theirs_ref[:, skip + first : skip + first + half] = theirs.astype(LOW)


def own_columns(mine_ref, theirs_ref, first, array):
    half = array.shape[-1] // 2
    span = slice(first, first + half)
    mine_ref[:, span] = array[:, :half]
    theirs_ref[:, span] = array[:, half:].astype(LOW)


def join(mine, received):
    both = jnp.concatenate(received, axis=1).astype(WIDE)
    width = both.shape[1]
    return (mine + jnp.pad(both, ((0, 0), (0, mine.shape[1] - width)))).astype(LOW)


def clip_names(label_ref):
    clips, rank, width = label_ref.shape
    return label_ref[...].reshape(clips * rank, width).astype(WIDE).T


def slot_take(names, slots, rank):
    source = lax.broadcasted_iota(jnp.int32, names.shape, 1)
    target = (source & (rank - 1)) + rank * names.astype(jnp.int32)
    place = lax.broadcasted_iota(jnp.int32, (slots * rank, names.shape[1]), 0)
    return jnp.where(place == target, 1.0, 0.0).astype(LOW)


def slot_copies(unit, count, everyone_ref, arrived, in_sems):
    return [
        pltpu.make_async_copy(
            everyone_ref.at[:, :, pl.ds(unit * number, unit)], arrived.at[number], in_sems.at[number]
        )
        for number in range(count)
    ]


def slot_work(plan, slots, carried, everyone_ref, label_ref, earlier, out_refs, scratch):
    names, arrived, totals, in_sems, out_sems = scratch
    clips, rank, unit = arrived.shape[1:]
    incoming = slot_copies(unit, len(plan), everyone_ref, arrived, in_sems)
    names[...] = clip_names(label_ref)
    outgoing = []
    for number, (which, ref) in enumerate(zip(carried, earlier)):
        copy = pltpu.make_async_copy(ref.at[0], out_refs[which].at[0], out_sems.at[len(plan) + number])
        copy.start()
        outgoing.append(copy)
    for number, (column, which, place) in enumerate(plan):
        incoming[number].wait()
        take = slot_take(names[column : column + 1], slots, rank)
        total = mm(take, arrived[number].reshape(clips * rank, unit))
        totals[number] = total.reshape(slots, rank, unit)
        out_ref = out_refs[which]
        target = out_ref.at[place] if len(out_ref.shape) == 4 else out_ref.at[:, :, pl.ds(unit * place, unit)]
        copy = pltpu.make_async_copy(totals.at[number], target, out_sems.at[number])
        copy.start()
        outgoing.append(copy)
    for copy in outgoing:
        copy.wait()


def slot_scratch(everyone, plan, slots, unit, carried):
    clips, rank, _ = everyone.shape
    units = len(plan)
    return [
        pltpu.VMEM((2 * HEAD_DIM, clips * rank), WIDE),
        pltpu.VMEM((units, clips, rank, unit), LOW),
        pltpu.VMEM((units, slots, rank, unit), WIDE),
        pltpu.SemaphoreType.DMA((units,)),
        pltpu.SemaphoreType.DMA((units + len(carried),)),
    ]


def slot_specs(everyone, carried):
    clips, rank, total = everyone.shape
    label_width = 2 * HEAD_DIM
    return [IN_PLACE, whole((clips, rank, label_width), (0, 0, total // label_width - 1))] + [
        whole(array.shape) for array in carried.values()
    ]


def slot_shapes(everyone, outs, slots):
    rank = everyone.shape[1]
    return tuple(
        shaped((slots, rank, width) if stack is None else (stack, slots, rank, width), WIDE)
        for stack, width in outs
    )


def slot_sum_body(_, plan, slots, carried, outs, everyone_ref, label_ref, *refs):
    scratch = refs[-5:]
    for copy in slot_copies(scratch[1].shape[3], len(plan), everyone_ref, scratch[1], scratch[3]):
        copy.start()
    slot_work(
        plan, slots, carried, everyone_ref, label_ref, refs[: len(carried)], refs[-5 - outs : -5], scratch
    )


def slot_sums(meta, everyone, plan, outs, slots, unit, carried, name, after):
    return call(
        lambda m, *refs: slot_sum_body(m, plan, slots, tuple(carried), len(outs), *refs),
        (1,),
        slot_specs(everyone, carried) + [IN_PLACE] * len(after),
        (IN_PLACE,) * len(outs),
        slot_shapes(everyone, outs, slots),
        slot_scratch(everyone, plan, slots, unit, carried),
        0,
        2 * everyone.size,
        name,
        (meta, everyone, everyone, *carried.values(), *after),
    )


def causal_keep(rows):
    key_at = lax.broadcasted_iota(jnp.int32, (rows, rows), 0)
    return key_at <= lax.broadcasted_iota(jnp.int32, (rows, rows), 1)


def turned(rows):
    return rows.astype(WIDE).T.astype(LOW)


def forward_block(query, keys, value_turned, diagonal, earlier=None):
    score = mm_nt(keys, query)
    if diagonal:
        score = jnp.where(causal_keep(score.shape[0]), score, -1e30)
    largest = jnp.max(score, axis=0, keepdims=True)
    if earlier is not None:
        largest = jnp.maximum(largest, earlier[0])
    mixed = mm(value_turned, jnp.exp(score - largest).astype(LOW))
    if earlier is not None:
        mixed = mixed + earlier[1] * jnp.exp(earlier[0] - largest)
    return largest, mixed


def values_of(rows_ref):
    values = turned(rows_ref[2])
    ones = jnp.ones((RANK_UNIT, values.shape[1]), LOW)
    return [
        jnp.concatenate([values[HEAD_DIM * which : HEAD_DIM * (which + 1)], ones], axis=0)
        for which in (0, 1)
    ]


def forward_finish(blocks, out_ref, log_ref):
    mixes = []
    totals = []
    for largest, mixed in blocks:
        summed = mixed[HEAD_DIM : HEAD_DIM + 1]
        mixes.append(mixed[:HEAD_DIM] * (1.0 / summed))
        totals.append(jnp.broadcast_to(jnp.log(summed) + largest, (HEAD_DIM, summed.shape[1])))
    out_ref[...] = jnp.concatenate(mixes, axis=0).T.astype(LOW)
    log_ref[...] = jnp.concatenate(totals, axis=0).T


MIXED_ROWS = HEAD_DIM + RANK_UNIT
PART_ROWS = MIXED_ROWS + 8


def self_forward_own_body(_, own_ref, part_ref):
    masks = half_masks()
    query = own_ref[0] * jnp.asarray(HEAD_DIM**-0.5, LOW)
    values = values_of(own_ref)
    for which in (0, 1):
        largest, mixed = forward_block(query * masks[which], own_ref[1], values[which], True)
        part_ref[0, which, :MIXED_ROWS] = mixed
        part_ref[0, which, MIXED_ROWS:] = jnp.broadcast_to(largest, (8, largest.shape[1]))


def self_forward_own(meta, own, after):
    _, half, local = own.shape
    pair = 2 * HEAD_DIM
    shape = (local // pair, 2, PART_ROWS, half)
    return call(
        lambda m, own_ref, after_ref, part_ref: self_forward_own_body(m, own_ref, part_ref),
        (local // pair,),
        [pl.BlockSpec((3, half, pair), lambda p, m: (0, 0, p)), IN_PLACE],
        pl.BlockSpec((1,) + shape[1:], lambda p, m: (p, 0, 0, 0)),
        shaped(shape, WIDE),
        [],
        4 * half * half * local,
        10 * half * local,
        "self_forward_own",
        (meta, own, after),
    )


def self_forward_body(
    meta, part_ref, own_ref, other_ref, out_own_ref, out_other_ref, log_own_ref, log_other_ref, keys, values, queries
):
    side = meta[10]
    masks = half_masks()
    for slot, ref in ((0, own_ref), (1, other_ref)):
        keys[slot] = ref[1]
        queries[slot] = ref[0] * jnp.asarray(HEAD_DIM**-0.5, LOW)
        for which, value in enumerate(values_of(ref)):
            values[slot, which] = value
    blocks = []
    for which in (0, 1):
        own = (part_ref[0, which, MIXED_ROWS : MIXED_ROWS + 1], part_ref[0, which, :MIXED_ROWS])
        other = forward_block(queries[1] * masks[which], keys[1], values[1, which], True)
        earlier = (jnp.where(side == 0, other[0], own[0]), jnp.where(side == 0, other[1], own[1]))
        later = forward_block(
            queries[1 - side] * masks[which], keys[side], values[side, which], False, earlier
        )
        blocks.append(
            (
                (jnp.where(side == 0, own[0], later[0]), jnp.where(side == 0, own[1], later[1])),
                (jnp.where(side == 0, later[0], other[0]), jnp.where(side == 0, later[1], other[1])),
            )
        )
    forward_finish([blocks[0][0], blocks[1][0]], out_own_ref, log_own_ref)
    forward_finish([blocks[0][1], blocks[1][1]], out_other_ref, log_other_ref)


def self_forward(meta, part, own, other):
    _, half, local = own.shape
    pair = 2 * HEAD_DIM
    three = pl.BlockSpec((3, half, pair), lambda p, m: (0, 0, p))
    one = pl.BlockSpec((half, pair), lambda p, m: (0, p))
    rows = shaped((half, local), LOW)
    logs = shaped((half, local), WIDE)
    return call(
        self_forward_body,
        (local // pair,),
        [pl.BlockSpec((1,) + part.shape[1:], lambda p, m: (p, 0, 0, 0)), three, three],
        (one, one, one, one),
        (rows, rows, logs, logs),
        [
            pltpu.VMEM((2, half, pair), LOW),
            pltpu.VMEM((2, 2, MIXED_ROWS, half), LOW),
            pltpu.VMEM((2, half, pair), LOW),
        ],
        12 * half * half * local,
        20 * half * local,
        "self_forward",
        (meta, part, own, other),
    )


def three_parts(column):
    high = column.astype(LOW)
    rest = column - high.astype(WIDE)
    middle = rest.astype(LOW)
    return high, middle, (rest - middle.astype(WIDE)).astype(LOW)


def back_scratch(slots, half):
    pair = 2 * HEAD_DIM
    return [pltpu.VMEM((slots, pair, half), LOW)] * 3 + [pltpu.VMEM((slots, 2, half, pair), LOW)] * 4


def back_prepare_keys(slot, rows_ref, scratch):
    key_turned, _, _, _, key_wide, _, value_wide = scratch
    lane = lax.broadcasted_iota(jnp.int32, (1, 2 * HEAD_DIM), 1)
    key_turned[slot] = turned(rows_ref[1])
    for which in (0, 1):
        spare = HEAD_DIM * (1 - which)
        marked = jnp.where((lane >= spare) & (lane < spare + 3), 1.0, 0.0).astype(LOW)
        key_wide[slot, which] = rows_ref[1] * (1 - marked) + marked
        value_wide[slot, which] = rows_ref[2] * (1 - marked) + marked


def back_prepare_queries(slot, rows_ref, mixed_ref, logs_ref, grad_refs, scratch):
    _, query_turned, grad_turned, query_wide, _, grad_wide, _ = scratch
    masks = half_masks()
    lane = lax.broadcasted_iota(jnp.int32, (1, 2 * HEAD_DIM), 1)
    grad = jnp.concatenate([ref[...] for ref in grad_refs], axis=0)
    product = grad.astype(WIDE) * mixed_ref[...].astype(WIDE)
    query = rows_ref[0] * jnp.asarray(HEAD_DIM**-0.5, LOW)
    logs = logs_ref[...]
    query_turned[slot] = turned(query)
    grad_turned[slot] = turned(grad)
    for which in (0, 1):
        spare = HEAD_DIM * (1 - which)
        marks = [jnp.where(lane == spare + i, 1.0, 0.0).astype(LOW) for i in range(3)]
        inner = jnp.sum(product * masks[which].astype(WIDE), axis=-1, keepdims=True)
        query_rows = query * masks[which]
        for part, mark in zip(three_parts(logs[:, HEAD_DIM * which : HEAD_DIM * which + 1]), marks):
            query_rows = query_rows - part * mark
        query_wide[slot, which] = query_rows
        grad_rows = grad * masks[which]
        for part, mark in zip(three_parts(inner), marks):
            grad_rows = grad_rows - part * mark
        grad_wide[slot, which] = grad_rows


def back_block(query_slot, key_slot, diagonal, scratch, totals):
    key_turned, query_turned, grad_turned, query_wide, key_wide, grad_wide, value_wide = scratch
    half = key_turned.shape[2]
    for which in (0, 1):
        head = slice(HEAD_DIM * which, HEAD_DIM * (which + 1))
        score = mm_nt(key_wide[key_slot, which], query_wide[query_slot, which])
        if diagonal:
            score = jnp.where(causal_keep(half), score, -1e30)
        prob = jnp.exp(score)
        prob_grad = mm_nt(value_wide[key_slot, which], grad_wide[query_slot, which])
        score_grad = (prob * prob_grad).astype(LOW)
        totals[2, key_slot, head] += mm_nt(grad_turned[query_slot, head], prob.astype(LOW))
        totals[1, key_slot, head] += mm_nt(query_turned[query_slot, head], score_grad)
        totals[0, query_slot, head] += mm(key_turned[key_slot, head], score_grad)


def self_back_own_body(_, own_ref, z_ref, log_ref, grad_ref, out_ref, *scratch):
    totals = scratch[-1]
    totals[...] = jnp.zeros_like(totals)
    back_prepare_keys(0, own_ref, scratch[:-1])
    back_prepare_queries(0, own_ref, z_ref, log_ref, (grad_ref,), scratch[:-1])
    back_block(0, 0, True, scratch[:-1], totals)
    out_ref[...] = totals[:, 0]


def self_back_own(meta, own, z_own, log_own, grad_own):
    _, half, local = own.shape
    pair = 2 * HEAD_DIM
    three = pl.BlockSpec((3, half, pair), lambda p, m: (0, 0, p))
    one = pl.BlockSpec((half, pair), lambda p, m: (0, p))
    return call(
        self_back_own_body,
        (local // pair,),
        [three, one, one, one],
        pl.BlockSpec((3, pair, half), lambda p, m: (0, p, 0)),
        shaped((3, local, half), WIDE),
        back_scratch(1, half) + [pltpu.VMEM((3, 1, pair, half), WIDE)],
        100 * half * half * local,
        24 * half * local,
        "self_back_own",
        (meta, own, z_own, log_own, grad_own),
    )


def self_back_body(
    meta,
    part_ref,
    own_ref,
    other_ref,
    z_own_ref,
    z_other_ref,
    log_own_ref,
    log_other_ref,
    grad_own_ref,
    grad_first_ref,
    grad_second_ref,
    _early,
    out_own_ref,
    out_other_ref,
    *scratch,
):
    totals = scratch[-1]
    scratch = scratch[:-1]
    side = meta[10]
    totals[:, 0] = part_ref[...]
    totals[:, 1] = jnp.zeros_like(totals[:, 1])

    @pl.when(side == 0)
    def _():
        back_prepare_keys(0, own_ref, scratch)

    @pl.when(side != 0)
    def _():
        back_prepare_queries(0, own_ref, z_own_ref, log_own_ref, (grad_own_ref,), scratch)

    back_prepare_keys(1, other_ref, scratch)
    back_prepare_queries(1, other_ref, z_other_ref, log_other_ref, (grad_first_ref, grad_second_ref), scratch)
    back_block(1, 1, True, scratch, totals)
    back_block(1 - side, side, False, scratch, totals)
    for slot, ref in ((0, out_own_ref), (1, out_other_ref)):
        ref[0] = (totals[0, slot].T * HEAD_DIM**-0.5).astype(LOW)
        ref[1] = totals[1, slot].T.astype(LOW)
        ref[2] = totals[2, slot].T.astype(LOW)


def self_back(meta, part, own, other, z_own, z_other, log_own, log_other, grad_own, grads_other, after):
    _, half, local = own.shape
    pair = 2 * HEAD_DIM
    three = pl.BlockSpec((3, half, pair), lambda p, m: (0, 0, p))
    one = pl.BlockSpec((half, pair), lambda p, m: (0, p))
    return call(
        self_back_body,
        (local // pair,),
        [pl.BlockSpec((3, pair, half), lambda p, m: (0, p, 0)), three, three]
        + [one] * 5
        + [pl.BlockSpec((half // 2, pair), lambda p, m: (0, p))] * 2
        + [IN_PLACE] * len(after),
        (three, three),
        (shaped(own.shape, LOW), shaped(own.shape, LOW)),
        back_scratch(2, half) + [pltpu.VMEM((3, 2, pair, half), WIDE)],
        200 * half * half * local,
        40 * half * local,
        "self_back",
        (meta, part, own, other, z_own, z_other, log_own, log_other, grad_own, *grads_other, *after),
    )


def halves_of(ref, local):
    step = ref.shape[1] // 2
    return (
        ref[:, :step, :].reshape(local, ref.shape[2]),
        ref[:, step:, :].reshape(local, ref.shape[2]),
    )


def full_of(ref):
    return ref[...].reshape(ref.shape[0] * ref.shape[1], ref.shape[2])


def fetch_weights(step, order, sources, gathered, held, sems, between=()):
    copies = {}
    for which in order:
        copies[which] = (
            pltpu.make_async_copy(sources[which], held[2 * which], sems.at[2 * which]),
            pltpu.make_async_copy(gathered.at[:, which], held[2 * which + 1], sems.at[2 * which + 1]),
        )

    @pl.when(step == 0)
    def _():
        for place, which in enumerate(order):
            for copy in copies[which]:
                copy.start()
            for copy in between[place] if between else ():
                copy.start()

    def ready(which):
        @pl.when(step == 0)
        def _():
            for copy in copies[which]:
                copy.wait()

        return held[2 * which], held[2 * which + 1]

    return ready


TILE_HEADS = 4


def tile_span(tile):
    return slice(TILE_HEADS * HEAD_DIM * tile, TILE_HEADS * HEAD_DIM * (tile + 1))


def tile_masks():
    lane = lax.broadcasted_iota(jnp.int32, (1, TILE_HEADS * HEAD_DIM), 1)
    return [jnp.where(lane // HEAD_DIM == head, 1.0, 0.0).astype(LOW) for head in range(TILE_HEADS)]


def text_tile(rows, tile, masks):
    part = rows[:, tile_span(tile)]
    return jnp.concatenate([part * mask for mask in masks], axis=0)


def by_head(values, reduce):
    keys, rows = values.shape
    apart = values.reshape(TILE_HEADS, keys // TILE_HEADS, rows)
    reduced = reduce(apart, axis=1, keepdims=True)
    return jnp.broadcast_to(reduced, apart.shape).reshape(keys, rows)


def text_weights(key_tile, query):
    scores = mm_nt(key_tile, query)
    weights = jnp.exp(scores - by_head(scores, jnp.max))
    return weights * (1.0 / by_head(weights, jnp.sum))


def mix_text(query, keys, values):
    masks = tile_masks()
    mixed = []
    for tile in range(query.shape[1] // (TILE_HEADS * HEAD_DIM)):
        one_query = query[:, tile_span(tile)] * jnp.asarray(HEAD_DIM**-0.5, LOW)
        weights = text_weights(text_tile(keys, tile, masks), one_query)
        mixed.append(mm_tn(weights.astype(LOW), text_tile(values, tile, masks)).astype(LOW))
    return jnp.concatenate(mixed, axis=1)


def middle_forward_body(
    _,
    x_ref,
    z_own_ref,
    z_other_ref,
    out_weight_ref,
    query_weight_ref,
    cross_weight_ref,
    gathered_ref,
    down3_ref,
    down3_other_ref,
    up3_ref,
    down4_ref,
    up4_ref,
    up4_other_ref,
    down7_ref,
    down7_other_ref,
    up7_ref,
    text_own_ref,
    text_other_ref,
    gain_two_ref,
    gain_three_ref,
    stream_one_ref,
    stream_two_ref,
    rows_three_ref,
    query_out_own_ref,
    query_out_other_ref,
    z2_own_ref,
    z2_other_ref,
    *scratch,
):
    local = z_own_ref.shape[1]
    ready = fetch_weights(
        pl.program_id(0),
        (0, 1, 2),
        (out_weight_ref, query_weight_ref, cross_weight_ref),
        gathered_ref,
        scratch[:6],
        scratch[6],
    )

    def out_product(own, other, which, down, down_other, up):
        rank = (mm_nt(down, own) + mm_nt(down_other, other)).astype(LOW)
        weight_own, weight_other_ref = ready(which)
        first, second = halves_of(weight_other_ref, local)
        product = mm(own, weight_own[...]) + mm_tn(rank, up)
        return product + jnp.concatenate([mm(other, first), mm(other, second)], axis=1)

    stream = x_ref[...].astype(WIDE) + out_product(
        z_own_ref[...],
        z_other_ref[...],
        0,
        down3_ref[0, 0],
        down3_other_ref[...],
        up3_ref[0, 0],
    )
    stream_one_ref[...] = stream
    rows_two = norm_rows(stream, gain_two_ref[...])[0].astype(LOW)
    rank = low_rank(down4_ref[0, 0], rows_two)
    query_own_ref, query_other_ref = ready(1)
    query_own = (mm(rows_two, query_own_ref[...]) + mm_tn(rank, up4_ref[0, 0])).astype(LOW)
    query_other = (
        mm(rows_two, full_of(query_other_ref)) + mm_tn(rank, up4_other_ref[...])
    ).astype(LOW)
    query_out_own_ref[...] = query_own
    query_out_other_ref[...] = query_other
    z2_own = mix_text(query_own, text_own_ref[0], text_own_ref[1])
    z2_other = mix_text(query_other, text_other_ref[0], text_other_ref[1])
    z2_own_ref[...] = z2_own
    z2_other_ref[...] = z2_other
    stream = stream + out_product(
        z2_own,
        z2_other,
        2,
        down7_ref[0, 0],
        down7_other_ref[...],
        up7_ref[0, 0],
    )
    stream_two_ref[...] = stream
    rows_three_ref[...] = norm_rows(stream, gain_three_ref[...])[0].astype(LOW)


def chosen(table, entry, slot):
    shape = (1, 1) + table.shape[2:]
    return pl.BlockSpec(
        shape, lambda t, m: (entry, m[slot], 0, 0), pipeline_mode=pl.Buffered(1)
    )


def middle_specs(weights, gathered, tables, packed):
    attention_down, attention_up, cross_down, cross_up = tables
    rank = (RANK_UNIT, gathered.shape[3])
    specs = [
        IN_PLACE,
        IN_PLACE,
        IN_PLACE,
        IN_PLACE,
        chosen(attention_down, 0, 3),
        whole(rank, (0, 0)),
        chosen(attention_up, 0, 3),
        chosen(cross_down, 0, 4),
        chosen(cross_up, 0, 4),
        whole(rank, (0, 2)),
        chosen(attention_down, 1, 7),
        whole(rank, (0, 1)),
        chosen(attention_up, 1, 7),
    ]
    args = weights + (
        gathered,
        attention_down,
        packed,
        attention_up,
        cross_down,
        cross_up,
        packed,
        attention_down,
        packed,
        attention_up,
    )
    return specs, args


def middle_scratch(weights, gathered):
    shards, _, depth, local = gathered.shape
    held = []
    for weight in weights:
        held += [pltpu.VMEM(weight.shape, LOW), pltpu.VMEM((shards, depth, local), LOW)]
    return held + [pltpu.SemaphoreType.DMA((2 * len(weights),))]


def middle_forward(meta, x, z_own, z_other, weights, gathered, tables, packed, text_own, text_other, gains):
    frames, width = x.shape
    local = z_own.shape[1]
    block = min(512, frames)
    wide = pl.BlockSpec((block, width), lambda t, m: (t, 0))
    narrow = pl.BlockSpec((block, local), lambda t, m: (t, 0))
    specs, args = middle_specs(weights, gathered, tables, packed)
    return call(
        middle_forward_body,
        (frames // block,),
        [wide, narrow, narrow]
        + specs
        + [whole(text_own.shape), whole(text_other.shape), whole((1, width)), whole((1, width))],
        (wide, wide, wide, narrow, narrow, narrow, narrow),
        (
            shaped((frames, width), WIDE),
            shaped((frames, width), WIDE),
            shaped((frames, width), LOW),
            shaped((frames, local), LOW),
            shaped((frames, local), LOW),
            shaped((frames, local), LOW),
            shaped((frames, local), LOW),
        ),
        middle_scratch(weights, gathered),
        6 * frames * width * width,
        6 * width * width + 20 * frames * width,
        "middle_forward",
        (meta, x, z_own, z_other) + args + (text_own, text_other) + gains,
    )


def middle_back_body(
    meta,
    last,
    grad_ref,
    stream_one_ref,
    z_own_ref,
    z_other_ref,
    query_in_own_ref,
    query_in_other_ref,
    z2_own_ref,
    z2_other_ref,
    out_weight_ref,
    query_weight_ref,
    cross_weight_ref,
    gathered_ref,
    down3_ref,
    down3_other_ref,
    up3_ref,
    down4_ref,
    up4_ref,
    up4_other_ref,
    down7_ref,
    down7_other_ref,
    up7_ref,
    text_own_ref,
    text_other_ref,
    gain_two_ref,
    text_ref,
    down5_ref,
    down6_ref,
    up5_ref,
    up6_ref,
    up5_other_ref,
    up6_other_ref,
    grad_one_ref,
    dz_own_ref,
    dz_first_ref,
    dz_second_ref,
    text_grad_own_ref,
    mine_ref,
    theirs_ref,
    text_mine_ref,
    text_theirs_ref,
    key_total,
    value_total,
    ga3_ref,
    gb3_ref,
    ga4_ref,
    gb4_ref,
    ga7_ref,
    gb7_ref,
    *scratch,
):
    step = pl.program_id(0)
    late = scratch[7:12]
    late_sems = scratch[13]
    late_copies = [
        pltpu.make_async_copy(source, target, late_sems.at[number])
        for number, (source, target) in enumerate(
            zip((query_in_own_ref, query_in_other_ref, stream_one_ref, z_own_ref, z_other_ref), late)
        )
    ]
    query_in_own_ref, query_in_other_ref, stream_one_ref, z_own_ref, z_other_ref = late
    grad_one_copy = pltpu.make_async_copy(scratch[12], grad_one_ref, late_sems.at[5])
    ready = fetch_weights(
        step,
        (2, 1, 0),
        (out_weight_ref, query_weight_ref, cross_weight_ref),
        gathered_ref,
        scratch[:6],
        scratch[6],
        (late_copies[:2], late_copies[2:], ()),
    )
    local = z_own_ref.shape[1]
    tiles = local // (TILE_HEADS * HEAD_DIM)
    masks = tile_masks()
    scale = jnp.asarray(HEAD_DIM**-0.5, LOW)

    @pl.when(step == 0)
    def _():
        key_total[...] = jnp.zeros_like(key_total)
        value_total[...] = jnp.zeros_like(value_total)
        for ref in (ga3_ref, gb3_ref, ga4_ref, gb4_ref, ga7_ref, gb7_ref):
            ref[...] = jnp.zeros_like(ref)

    def out_back(grad, own, other, which, down, down_other, up, ga_ref, gb_ref):
        rank = (mm_nt(down, own) + mm_nt(down_other, other)).astype(LOW)
        grad_rank = low_rank(up, grad)
        ga_ref[:, :local] += mm(grad_rank, own)
        ga_ref[:, local:] += mm(grad_rank, other)
        gb_ref[...] += mm(rank, grad)
        weight_own, weight_other_ref = ready(which)
        first, second = halves_of(weight_other_ref, local)
        middle = grad.shape[1] // 2
        grad_own = mm_nt(grad, weight_own[...]) + mm_tn(grad_rank, down)
        grad_other = (
            mm_nt(grad[:, :middle], first)
            + mm_nt(grad[:, middle:], second)
            + mm_tn(grad_rank, down_other)
        )
        return grad_own.astype(LOW), grad_other.astype(LOW)

    grad = grad_ref[...]
    dz2_own, dz2_other = out_back(
        grad.astype(LOW),
        z2_own_ref[...],
        z2_other_ref[...],
        2,
        down7_ref[0, 0],
        down7_other_ref[...],
        up7_ref[0, 0],
        ga7_ref,
        gb7_ref,
    )

    def text_back(query, dz2, keys, values, part):
        query_grads = []
        for tile in range(tiles):
            key_tile = text_tile(keys, tile, masks)
            value_tile = text_tile(values, tile, masks)
            one_query = query[:, tile_span(tile)] * scale
            one_grad = dz2[:, tile_span(tile)]
            probs = text_weights(key_tile, one_query)
            prob_grads = mm_nt(value_tile, one_grad)
            inner = by_head(probs * prob_grads, jnp.sum)
            score_grads = (probs * (prob_grads - inner)).astype(LOW)
            query_grads.append((mm_tn(score_grads, key_tile) * HEAD_DIM**-0.5).astype(LOW))
            key_total[part, tile] += mm(score_grads, one_query)
            value_total[part, tile] += mm(probs.astype(LOW), one_grad)
        return jnp.concatenate(query_grads, axis=1)

    for copy in late_copies[:2]:
        copy.wait()
    dq_own = text_back(query_in_own_ref[...], dz2_own, text_own_ref[0], text_own_ref[1], 0)
    dq_other = text_back(query_in_other_ref[...], dz2_other, text_other_ref[0], text_other_ref[1], 1)

    for copy in late_copies[2:]:
        copy.wait()
    rows_two, normed, inverse = norm_rows(stream_one_ref[...], gain_two_ref[...])
    rows_two = rows_two.astype(LOW)
    rank = low_rank(down4_ref[0, 0], rows_two)
    grad_rank = (mm_nt(up4_ref[0, 0], dq_own) + mm_nt(up4_other_ref[...], dq_other)).astype(LOW)
    ga4_ref[...] += mm(grad_rank, rows_two)
    gb4_ref[:, :local] += mm(rank, dq_own)
    gb4_ref[:, local:] += mm(rank, dq_other)
    query_own_ref, query_other_ref = ready(1)
    grad_rows = (
        mm_nt(dq_own, query_own_ref[...])
        + mm_nt(dq_other, full_of(query_other_ref))
        + mm_tn(grad_rank, down4_ref[0, 0])
    )
    grad = grad + norm_back(grad_rows, gain_two_ref[...], normed, inverse)
    scratch[12][...] = grad
    grad_one_copy.start()
    dz_own, dz_other = out_back(
        grad.astype(LOW),
        z_own_ref[...],
        z_other_ref[...],
        0,
        down3_ref[0, 0],
        down3_other_ref[...],
        up3_ref[0, 0],
        ga3_ref,
        gb3_ref,
    )
    dz_own_ref[...] = dz_own
    half = dz_first_ref.shape[0]
    dz_first_ref[...] = dz_other[:half]
    dz_second_ref[...] = dz_other[half:]
    grad_one_copy.wait()

    @pl.when(step == last)
    def _():
        split_columns(meta, mine_ref, theirs_ref, 0, ga4_ref)
        own_columns(mine_ref, theirs_ref, local, gb4_ref)
        own_columns(mine_ref, theirs_ref, 2 * local, ga3_ref)
        own_columns(mine_ref, theirs_ref, 3 * local, ga7_ref)
        split_columns(meta, mine_ref, theirs_ref, 4 * local, gb3_ref)
        split_columns(meta, mine_ref, theirs_ref, 5 * local, gb7_ref)
        texts = text_ref.shape[0]
        for slot, total in enumerate((key_total, value_total)):
            for part in (0, 1):
                for tile in range(tiles):
                    stacked = total[part, tile]
                    rows = 0.0
                    for head, mask in enumerate(masks):
                        rows = rows + stacked[HEAD_DIM * head : HEAD_DIM * (head + 1)] * mask.astype(WIDE)
                    if part == 0:
                        text_grad_own_ref[slot, :, tile_span(tile)] = rows
                    else:
                        text_theirs_ref[texts * slot : texts * (slot + 1), tile_span(tile)] = rows.astype(LOW)
        text = text_ref[...]
        factors = ((down5_ref, up5_ref, up5_other_ref), (down6_ref, up6_ref, up6_other_ref))
        for slot, (down_ref, up_ref, up_other_ref) in enumerate(factors):
            grad_own = text_grad_own_ref[slot].astype(LOW)
            grad_other = text_theirs_ref[texts * slot : texts * (slot + 1)]
            rank = low_rank(down_ref[0, 0], text)
            grad_rank = mm_nt(up_ref[0, 0], grad_own) + mm_nt(up_other_ref[...], grad_other)
            ga4_ref[...] = mm(grad_rank.astype(LOW), text)
            first = slice(2 * texts + RANK_UNIT * slot, 2 * texts + RANK_UNIT * (slot + 1))
            second = slice(2 * texts + RANK_UNIT * (2 + slot), 2 * texts + RANK_UNIT * (3 + slot))
            split_columns(meta, text_mine_ref.at[:, pl.ds(slot * local, local)], text_theirs_ref.at[first], 0, ga4_ref)
            text_mine_ref[:, (2 + slot) * local : (3 + slot) * local] = mm(rank, grad_own)
            text_theirs_ref[second] = mm(rank, grad_other).astype(LOW)


def middle_back(
    meta, grad, stream_one, z_own, z_other, q_own, q_other, z2_own, z2_other,
    weights, gathered, tables, packed, text_own, text_other, gain, text,
):
    frames, width = grad.shape
    local = z_own.shape[1]
    tiles = local // (TILE_HEADS * HEAD_DIM)
    wide = whole((frames, width))
    narrow = whole((frames, local))
    specs, args = middle_specs(weights, gathered, tables, packed)
    rank = (RANK_UNIT, width)
    packs = (RANK_UNIT, 6 * local)
    text_packs = (RANK_UNIT, 4 * local)
    text_rows = (2 * text.shape[0] + 4 * RANK_UNIT, local)
    _, _, cross_down, cross_up = tables
    return call(
        lambda m, *refs: middle_back_body(m, 0, *refs),
        (1,),
        [wide, IN_PLACE]
        + [IN_PLACE] * 4
        + [narrow] * 2
        + specs
        + [whole(text_own.shape), whole(text_other.shape), whole((1, width)), whole(text.shape)]
        + [chosen(cross_down, 1, 5), chosen(cross_down, 2, 6), chosen(cross_up, 1, 5), chosen(cross_up, 2, 6)]
        + [whole((RANK_UNIT, local), (0, 3)), whole((RANK_UNIT, local), (0, 4))],
        (IN_PLACE, narrow, whole((frames // 2, local)), whole((frames // 2, local)), whole(text_own.shape))
        + (whole(packs), whole(packs), whole(text_packs), whole(text_rows)),
        (
            shaped((frames, width), WIDE),
            shaped((frames, local), LOW),
            shaped((frames // 2, local), LOW),
            shaped((frames // 2, local), LOW),
            shaped(text_own.shape, WIDE),
            shaped(packs, WIDE),
            shaped(packs, LOW),
            shaped(text_packs, WIDE),
            shaped(text_rows, LOW),
        ),
        [
            pltpu.VMEM((2, tiles, TILE_HEADS * HEAD_DIM, TILE_HEADS * HEAD_DIM), WIDE),
            pltpu.VMEM((2, tiles, TILE_HEADS * HEAD_DIM, TILE_HEADS * HEAD_DIM), WIDE),
        ]
        + [pltpu.VMEM(rank, WIDE)] * 6
        + middle_scratch(weights, gathered)
        + [pltpu.VMEM((frames, local), LOW)] * 2
        + [pltpu.VMEM((frames, width), WIDE)]
        + [pltpu.VMEM((frames, local), LOW)] * 2
        + [pltpu.VMEM((frames, width), WIDE), pltpu.SemaphoreType.DMA((6,))],
        6 * frames * width * width,
        6 * width * width + 24 * frames * width,
        "middle_back",
        (meta, grad, stream_one, z_own, z_other, q_own, q_other, z2_own, z2_other)
        + args
        + (text_own, text_other, gain, text)
        + (cross_down, cross_down, cross_up, cross_up, packed, packed),
    )


def feed_tile(
    rows_ref, cot_ref, up_weight, down_weight, up_rank, down_rank,
    ga9_ref, gb8_ref, branch, grad_rows, rank9, grad_rank8, rank8, grad_rank9,
):
    frames = rows_ref.shape[0]
    block = min(256, frames)
    low_pre = mm_tn(rank8[...], up_rank)
    low_grad = mm_tn(grad_rank9[...], down_rank)
    hidden_blocks = []
    grad_blocks = []
    for first in range(0, frames, block):
        span = slice(first, first + block)
        pre = mm(rows_ref[span], up_weight) + low_pre[span]
        grad_hidden = mm_nt(cot_ref[span], down_weight) + low_grad[span]
        hidden, slope = gelu_parts(pre)
        hidden = hidden.astype(LOW)
        grad_pre = (grad_hidden * slope).astype(LOW)
        branch[span] += mm(hidden, down_weight)
        grad_rows[span] += mm_nt(grad_pre, up_weight)
        hidden_blocks.append(hidden)
        grad_blocks.append(grad_pre)
    hidden = jnp.concatenate(hidden_blocks, axis=0)
    grad_pre = jnp.concatenate(grad_blocks, axis=0)
    rank9[...] += mm_nt(down_rank, hidden)
    grad_rank8[...] += mm_nt(up_rank, grad_pre)
    ga9_ref[...] = mm(grad_rank9[...], hidden).astype(ga9_ref.dtype)
    gb8_ref[...] = mm(rank8[...], grad_pre).astype(gb8_ref.dtype)


def feed_own_body(
    _, rows_ref, cot_ref, up_weight_ref, down_weight_ref, up_rank_ref, down_rank_ref,
    down8_ref, up9_ref,
    branch_ref, grad_rows_ref, rank9_ref, grad_rank8_ref, rank8, grad_rank9, ga9_ref, gb8_ref,
):
    @pl.when(pl.program_id(0) == 0)
    def _():
        rank8[...] = low_rank(down8_ref[0], rows_ref[...])
        grad_rank9[...] = low_rank(up9_ref[0], cot_ref[...])
        for ref in (branch_ref, grad_rows_ref, rank9_ref, grad_rank8_ref):
            ref[...] = jnp.zeros_like(ref)

    feed_tile(
        rows_ref, cot_ref, up_weight_ref[...], down_weight_ref[...], up_rank_ref[0], down_rank_ref[0],
        ga9_ref, gb8_ref, branch_ref, grad_rows_ref, rank9_ref, grad_rank8_ref, rank8, grad_rank9,
    )


def table_tile(tile, slot):
    return pl.BlockSpec((1, RANK_UNIT, tile), lambda t, m: (m[slot], 0, t))


def feed_own(meta, rows, cot, up_weight, down_weight, input_down, input_up, output_down, output_up, tile):
    frames, width = rows.shape
    hidden = up_weight.shape[1]
    grads = pl.BlockSpec((RANK_UNIT, tile), lambda t, m: (0, t))
    picked = pl.BlockSpec((1, RANK_UNIT, width), lambda t, m: (m[8], 0, 0))
    picked_out = pl.BlockSpec((1, RANK_UNIT, width), lambda t, m: (m[9], 0, 0))
    rank = (RANK_UNIT, frames)
    return call(
        feed_own_body,
        (hidden // tile,),
        [
            whole((frames, width)),
            whole((frames, width)),
            pl.BlockSpec((width, tile), lambda t, m: (0, t)),
            pl.BlockSpec((tile, width), lambda t, m: (t, 0)),
            table_tile(tile, 8),
            table_tile(tile, 9),
            picked,
            picked_out,
        ],
        (whole((frames, width)), whole((frames, width))) + (whole(rank),) * 4 + (grads, grads),
        (
            shaped((frames, width), WIDE),
            shaped((frames, width), WIDE),
            shaped(rank, WIDE),
            shaped(rank, WIDE),
            shaped(rank, LOW),
            shaped(rank, LOW),
            shaped((RANK_UNIT, hidden), WIDE),
            shaped((RANK_UNIT, hidden), WIDE),
        ),
        [],
        8 * frames * width * hidden,
        4 * width * hidden + 12 * frames * width,
        "feed_own",
        (meta, rows, cot, up_weight, down_weight, input_up, output_down, input_down, output_up),
    )


def feed_other_body(
    meta, last, rows_ref, cot_ref, up_weight_ref, down_weight_ref, up_rank_ref, down_rank_ref,
    down8_ref, up9_ref, branch_in_ref, grad_rows_in_ref, rank9_in_ref, grad_rank8_in_ref, rank8, grad_rank9,
    stream_ref, gain_ref,
    out_ref, grad_ref, mine_ref, theirs_ref,
    branch, grad_rows, rank9, grad_rank8, ga8_ref, gb9_ref, branch_in, grad_rows_in, stream_in, sems,
):
    step = pl.program_id(0)
    copies = [
        pltpu.make_async_copy(source, target, sems.at[i])
        for i, (source, target) in enumerate(
            ((branch_in_ref, branch_in), (grad_rows_in_ref, grad_rows_in), (stream_ref, stream_in))
        )
    ]

    @pl.when(step == 0)
    def _():
        for copy in copies:
            copy.start()
        branch[...] = jnp.zeros_like(branch)
        grad_rows[...] = jnp.zeros_like(grad_rows)
        rank9[...] = rank9_in_ref[...]
        grad_rank8[...] = grad_rank8_in_ref[...]

    shards, _, depth, tile = up_weight_ref.shape
    hidden = (last + 1) * tile
    first = pl.multiple_of(step * tile, 128)
    gb8_ref = theirs_ref.at[:, pl.ds(first, tile)]
    ga9_ref = theirs_ref.at[:, pl.ds(pl.multiple_of(hidden + first, 128), tile)]
    up_weight = up_weight_ref[...].reshape(shards * depth, tile)
    down_weight = down_weight_ref[...].reshape(tile, down_weight_ref.shape[3])
    feed_tile(
        rows_ref, cot_ref, up_weight, down_weight, up_rank_ref[...], down_rank_ref[...],
        ga9_ref, gb8_ref, branch, grad_rows, rank9, grad_rank8, rank8, grad_rank9,
    )

    @pl.when(step == last)
    def _():
        for copy in copies:
            copy.wait()
        frames = rows_ref.shape[0]
        block = min(128, frames)
        last8 = grad_rank8[...].astype(LOW)
        last9 = rank9[...].astype(LOW)
        ga8_ref[...] = mm(last8, rows_ref[...])
        gb9_ref[...] = mm(last9, cot_ref[...])
        half = ga8_ref.shape[1] // 2
        split_columns(meta, mine_ref, theirs_ref, 0, ga8_ref, 2 * hidden)
        split_columns(meta, mine_ref, theirs_ref, half, gb9_ref, 2 * hidden)
        for first in range(0, frames, block):
            span = slice(first, first + block)
            stream = stream_in[span]
            out = stream + (branch[span] + branch_in[span]) + mm_tn(last9[:, span], up9_ref[0])
            out_ref[span] = out.astype(LOW)
            _, normed, inverse = norm_rows(stream, gain_ref[...])
            grad = grad_rows[span] + grad_rows_in[span] + mm_tn(last8[:, span], down8_ref[0])
            grad_ref[span] = cot_ref[span].astype(WIDE) + norm_back(
                grad, gain_ref[...], normed, inverse
            )


def feed_other(
    meta, rows, cot, gathered, packed, first_pack, input_down, output_up, carried, stream, gain, tile
):
    frames, width = rows.shape
    shards, quarters, depth, _ = gathered.shape
    hidden = quarters // 2 * width
    per_half = width // tile
    own_shards = tile // (quarters // 2 * depth)
    down_first = quarters // 2
    picked = pl.BlockSpec((1, RANK_UNIT, width), lambda t, m: (m[8], 0, 0))
    picked_out = pl.BlockSpec((1, RANK_UNIT, width), lambda t, m: (m[9], 0, 0))
    rank = (RANK_UNIT, frames)
    steps = hidden // tile
    full = whole((frames, width))
    wide = pltpu.VMEM((frames, width), WIDE)
    return call(
        lambda m, *refs: feed_other_body(m, steps - 1, *refs),
        (steps,),
        [
            full,
            full,
            pl.BlockSpec(
                (shards, 1, depth, tile),
                lambda t, m: (0, down_first + t // per_half, 0, t % per_half),
            ),
            pl.BlockSpec((own_shards, down_first, depth, width), lambda t, m: (t, 0, 0, 0)),
            pl.BlockSpec((RANK_UNIT, tile), lambda t, m: (0, first_pack // tile + t)),
            pl.BlockSpec((RANK_UNIT, tile), lambda t, m: (0, (first_pack + hidden) // tile + t)),
            picked,
            picked_out,
            IN_PLACE,
            IN_PLACE,
            whole(rank),
            whole(rank),
            whole(rank),
            whole(rank),
            IN_PLACE,
            whole((1, width)),
        ],
        (full, full, whole((RANK_UNIT, width)), whole((RANK_UNIT, 2 * hidden + width))),
        (
            shaped((frames, width), LOW),
            shaped((frames, width), WIDE),
            shaped((RANK_UNIT, width), WIDE),
            shaped((RANK_UNIT, 2 * hidden + width), LOW),
        ),
        [
            wide,
            wide,
            pltpu.VMEM(rank, WIDE),
            pltpu.VMEM(rank, WIDE),
            pltpu.VMEM((RANK_UNIT, width), WIDE),
            pltpu.VMEM((RANK_UNIT, width), WIDE),
            wide,
            wide,
            wide,
            pltpu.SemaphoreType.DMA((3,)),
        ],
        8 * frames * width * hidden,
        4 * width * hidden + 24 * frames * width,
        "feed_other",
        (meta, rows, cot, gathered, gathered, packed, packed, input_down, output_up)
        + tuple(carried)
        + (stream, gain),
    )


def last_norm_body(_, half, slot_part, x_ref, own_ref, first_ref, second_ref, grad_ref, gain_ref, *refs):
    plan, slots, carried, outs = slot_part
    step = pl.program_id(0)
    everyone_ref, label_ref = refs[:2]
    earlier = refs[2 : 2 + len(carried)]
    out_ref = refs[-6 - outs]
    scratch = refs[-5:]

    @pl.when(step == 0)
    def _():
        for copy in slot_copies(scratch[1].shape[3], len(plan), everyone_ref, scratch[1], scratch[3]):
            copy.start()

    _, normed, inverse = norm_rows(x_ref[...].astype(WIDE), gain_ref[...])
    other = jnp.where(step < half, first_ref[...].astype(WIDE), second_ref[...].astype(WIDE))
    total = own_ref[...] + other
    out_ref[...] = grad_ref[...] + norm_back(total, gain_ref[...], normed, inverse)

    @pl.when(step == 2 * half - 1)
    def _():
        slot_work(plan, slots, carried, everyone_ref, label_ref, earlier, refs[-5 - outs : -5], scratch)


def last_norm(meta, x, own, received, grad, gain, everyone, plan, outs, slots, unit, carried, after):
    frames, width = x.shape
    block = min(256, frames // 2)
    half = frames // 2 // block
    rows = pl.BlockSpec((block, width), lambda t, _: (t, 0))
    first = pl.BlockSpec((block, width), lambda t, _: (jnp.minimum(t, half - 1), 0))
    second = pl.BlockSpec((block, width), lambda t, _: (jnp.maximum(t - half, 0), 0))
    slot_part = (plan, slots, tuple(carried), len(outs))
    return call(
        lambda m, *refs: last_norm_body(m, half, slot_part, *refs),
        (2 * half,),
        [rows, rows, first, second, rows, whole((1, width))]
        + slot_specs(everyone, carried)
        + [IN_PLACE] * len(after),
        (rows,) + (IN_PLACE,) * len(outs),
        (shaped(x.shape, WIDE),) + slot_shapes(everyone, outs, slots),
        slot_scratch(everyone, plan, slots, unit, carried),
        20 * x.size,
        16 * x.size,
        "last_norm",
        (meta, x, own, *received, grad, gain, everyone, everyone, *carried.values(), *after),
    )


def on_pair(
    inputs,
    encoder_text_states,
    cotangent,
    clip_adapter_index,
    self_norm_gain,
    cross_norm_gain,
    feed_norm_gain,
    self_query_key_value_weight,
    self_output_weight,
    cross_query_weight,
    cross_key_value_weight,
    cross_output_weight,
    up_weight,
    down_weight,
    self_first_factors,
    self_second_factors,
    cross_first_factors,
    cross_second_factors,
    attention_first_factors,
    attention_second_factors,
    input_first_factors,
    input_second_factors,
    output_first_factors,
    output_second_factors,
):
    x = inputs[0]
    text = encoder_text_states[0]
    cot = cotangent[0]
    width = x.shape[1]
    local = self_output_weight.shape[0]
    hidden = up_weight.shape[1]
    slots = input_first_factors.shape[0]
    group_count = lax.axis_size("dp")
    place = lax.axis_index("dp")
    side = lax.axis_index("tensor")
    picks = clip_adapter_index[0]
    meta = jnp.concatenate([picks, jnp.stack([side, place]).astype(jnp.int32)])
    gain_one, gain_two, gain_three = (
        vec.reshape(1, width) for vec in (self_norm_gain, cross_norm_gain, feed_norm_gain)
    )

    def swap(array):
        return lax.ppermute(array, "tensor", [(0, 1), (1, 0)])

    depth = width // group_count
    step = local // group_count

    def share(weight, size):
        return lax.dynamic_slice_in_dim(weight, place * size, size, axis=0)

    def side_by_side(rows, count):
        return rows.reshape(rows.shape[0], count, -1).transpose(1, 0, 2)

    out_share = side_by_side(share(self_output_weight, step), 2).reshape(depth, local)
    query_share = share(cross_query_weight, depth)
    cross_share = side_by_side(share(cross_output_weight, step), 2).reshape(depth, local)
    share_one = jnp.stack([swap(out_share), swap(query_share), swap(cross_share)])
    rows_one = first_norm(meta, x, gain_one)
    share_one, rows_one = lax.optimization_barrier((share_one, rows_one))
    gathered_one = lax.all_gather(share_one, "dp", axis=0)
    rows_one_other = swap(rows_one)
    factors = picked_factors(
        meta,
        [
            (attention_first_factors, 0, 3),
            (attention_first_factors, 1, 7),
            (cross_second_factors, 0, 4),
            (cross_second_factors, 1, 5),
            (cross_second_factors, 2, 6),
            (input_second_factors, None, 8),
            (output_first_factors, None, 9),
        ],
    )
    packed = swap(factors)
    first_pack = 5 * local

    heads_own, ranks_own = project_heads(
        meta, rows_one, self_query_key_value_weight, self_first_factors, self_second_factors, 0, 0, "own_heads"
    )
    part_own = self_forward_own(meta, heads_own, factors)
    text_own, _ = project_heads(
        meta, text, cross_key_value_weight, cross_first_factors, cross_second_factors, 5, 1, "text_heads"
    )
    text_other = swap(text_own)
    share_two = feed_share(
        meta, down_weight, up_weight, depth, (part_own, text_own, rows_one_other)
    )
    heads_other, ranks_other = project_heads(
        meta, rows_one_other, self_query_key_value_weight, self_first_factors, self_second_factors,
        0, 0, "other_heads", (share_two,),
    )
    z_own_frames, z_other_frames, log_own, log_other = self_forward(meta, part_own, heads_own, heads_other)
    share_two, z_other_frames = lax.optimization_barrier((swap(share_two), z_other_frames))
    gathered_two = lax.all_gather(share_two, "dp", axis=0)
    z_other_heads = swap(z_other_frames)
    weights = (self_output_weight, cross_query_weight, cross_output_weight)
    tables = (attention_first_factors, attention_second_factors, cross_first_factors, cross_second_factors)
    stream_one, stream_two, rows_three, q_own, q_other, z2_own, z2_other = middle_forward(
        meta, x, z_own_frames, z_other_heads, weights, gathered_one, tables, packed,
        text_own, text_other, (gain_two, gain_three),
    )
    tile = local
    *carried, ga9_own, gb8_own = feed_own(
        meta, rows_three, cot, up_weight, down_weight, input_first_factors, input_second_factors,
        output_first_factors, output_second_factors, tile,
    )
    output, grad_two, feed_mine, feed_theirs = feed_other(
        meta, rows_three, cot, gathered_two, packed, first_pack, input_first_factors,
        output_second_factors, carried, stream_two, gain_three, tile,
    )

    feed_received = swap(feed_theirs)

    (
        grad_one, dz_own_heads, *dz_other_heads, text_grad_own, middle_mine, middle_theirs,
        text_mine_rank, text_theirs,
    ) = middle_back(
        meta, grad_two, stream_one, z_own_frames, z_other_heads, q_own, q_other, z2_own, z2_other,
        weights, gathered_one, tables, packed, text_own, text_other, gain_two, text,
    )
    feed_received, middle_theirs, *dz_other_heads = lax.optimization_barrier(
        (feed_received, middle_theirs, *dz_other_heads)
    )
    *dz_other_frames, text_theirs = lax.optimization_barrier(
        (*[swap(half) for half in dz_other_heads], text_theirs)
    )

    unit = local
    hidden_units = hidden // unit
    labels = jnp.zeros((RANK_UNIT, 2 * HEAD_DIM), LOW).at[:, : picks.shape[0]].set(picks.astype(LOW)[None])
    early = jnp.concatenate(
        [
            join(middle_mine, [swap(middle_theirs)]),
            join(feed_mine, [feed_received[:, 2 * hidden :]]),
            join(jnp.concatenate([gb8_own, ga9_own], axis=1), [feed_received[:, : 2 * hidden]]),
            labels,
        ],
        axis=1,
    )
    early_all = lax.all_gather(early, "dp", axis=0)
    grads_part = self_back_own(meta, heads_own, z_own_frames, log_own, dz_own_heads)
    grads_own, grads_other = self_back(
        meta, grads_part, heads_own, heads_other, z_own_frames, z_other_frames, log_own, log_other,
        dz_own_heads, dz_other_frames, (early,),
    )
    text_received, grads_own = lax.optimization_barrier((swap(text_theirs), grads_own))
    texts = text.shape[0]
    text_grad_other = text_received[: 2 * texts].reshape(text_grad_own.shape)
    text_received_rank = side_by_side(
        text_received[2 * texts :].reshape(4, RANK_UNIT, local).transpose(1, 0, 2).reshape(RANK_UNIT, -1), 1
    )[0]
    text_heads_grad = (text_grad_own + text_grad_other.astype(WIDE)).astype(LOW)
    mine, theirs = first_grads(
        meta, [rows_one, rows_one_other], [grads_own, grads_other], self_second_factors, 0, "self_first"
    )
    seconds = second_grads(meta, [ranks_own, ranks_other], [grads_own, grads_other], "self_second", theirs)
    theirs, seconds = lax.optimization_barrier((swap(theirs), seconds))
    partial_other = [
        project_back_heads(
            meta, grads_other, self_query_key_value_weight, self_first_factors, self_second_factors,
            0, 0, LOW, "other_back", seconds, (part, 2),
        )
        for part in range(2)
    ]
    received = [swap(part) for part in partial_other]
    labels = lax.dynamic_index_in_dim(early_all[:, :, -2 * HEAD_DIM :], place, axis=0, keepdims=False)
    late = jnp.concatenate(
        [join(mine, [theirs]), seconds, join(text_mine_rank, [text_received_rank]), labels], axis=1
    )
    late_all = lax.all_gather(late, "dp", axis=0)
    text_rows = project_back_heads(
        meta, text_heads_grad, cross_key_value_weight, cross_first_factors, cross_second_factors,
        5, 1, WIDE, "text_back", partial_other[1],
    )
    text_halves = (text_rows[:, : width // 2], text_rows[:, width // 2 :])
    text_mine = jnp.where(side == 0, text_halves[0], text_halves[1])
    text_theirs = jnp.where(side == 0, text_halves[1], text_halves[0])
    text_received = swap(text_theirs.astype(LOW))
    partial_own = project_back_heads(
        meta, grads_own, self_query_key_value_weight, self_first_factors, self_second_factors,
        0, 0, WIDE, "own_back", late,
    )
    sum_query_a, sum_query_b, sum_out_a, sum_out_b, sum_up_a, sum_down_b, sum_up_b, sum_down_a = slot_sums(
        meta,
        early_all,
        [(4, 0, 0), (4, 1, 0), (3, 2, 0), (7, 2, 1), (3, 3, 0), (7, 3, 1), (8, 4, 0), (9, 5, 0)]
        + [(8, 6, i) for i in range(hidden_units)]
        + [(9, 7, i) for i in range(hidden_units)],
        [(1, unit), (1, unit), (2, unit), (2, unit), (None, unit), (None, unit), (None, hidden), (None, hidden)],
        slots, unit, {}, "early_slots", (partial_own,),
    )
    *received, text_received, sum_up_a = lax.optimization_barrier((*received, text_received, sum_up_a))
    text_grad = text_mine + text_received.astype(WIDE)
    input_grad, sum_self_a, sum_self_b, sum_cross_a, sum_cross_b = last_norm(
        meta, x, partial_own, received, grad_one, gain_one,
        late_all,
        [(0, 0, 0), (1, 0, 1), (2, 0, 2), (0, 1, 0), (1, 1, 1), (2, 1, 2)]
        + [(5, 2, 1), (6, 2, 2), (5, 3, 1), (6, 3, 2)],
        [(3, unit), (3, unit), (3, unit), (3, unit)],
        slots, unit, {2: sum_query_a, 3: sum_query_b}, (sum_up_a,),
    )
    return (
        output[None],
        input_grad[None],
        text_grad[None],
        sum_self_a,
        sum_self_b,
        sum_cross_a,
        sum_cross_b,
        sum_out_a,
        sum_out_b,
        sum_up_a,
        sum_up_b,
        sum_down_a,
        sum_down_b,
    )


def solution(mesh):
    in_specs = (
        P("dp", "tensor", None),
        P("dp", None, None),
        P("dp", "tensor", None),
        P("dp", None),
        P(),
        P(),
        P(),
        P(None, None, "tensor"),
        P("tensor", None),
        P(None, "tensor"),
        P(None, None, "tensor"),
        P("tensor", None),
        P(None, "tensor"),
        P("tensor", None),
        P(),
        P(None, None, None, "tensor"),
        P(),
        P(None, None, None, "tensor"),
        P(None, None, None, "tensor"),
        P(),
        P(),
        P(None, None, "tensor"),
        P(None, None, "tensor"),
        P(),
    )
    out_specs = (
        P("dp", "tensor", None),
        P("dp", "tensor", None),
        P("dp", None, "tensor"),
        P(None, None, None, "tensor"),
        P(None, None, None, "tensor"),
        P(None, None, None, "tensor"),
        P(None, None, None, "tensor"),
        P(None, None, None, "tensor"),
        P(None, None, None, "tensor"),
        P(None, None, "tensor"),
        P(None, None, "tensor"),
        P(None, None, "tensor"),
        P(None, None, "tensor"),
    )
    layer = on_pair if mesh.shape["tensor"] == 2 else on_device
    return jax.shard_map(
        layer, mesh=mesh, in_specs=in_specs, out_specs=out_specs, check_vma=False
    )
```

```python
import jax
import jax.numpy as jnp
from jax import lax
from jax.experimental import pallas as pl
from jax.experimental.pallas import tpu as pltpu
from jax.sharding import PartitionSpec as P

HEAD_DIM = 64


epsilon = 1e-05


def split_dot(form, wide_part, narrow_part):
    high_part = wide_part.astype(jnp.bfloat16)
    rest_part = (wide_part - high_part.astype(jnp.float32)).astype(jnp.bfloat16)
    first = jnp.einsum(form, high_part, narrow_part, preferred_element_type=jnp.float32)
    return first + jnp.einsum(form, rest_part, narrow_part, preferred_element_type=jnp.float32)


def layer_norm(stream, gain_vec):
    centred = stream - jnp.mean(stream, axis=-1, keepdims=True)
    inverse = lax.rsqrt(jnp.mean(centred * centred, axis=-1, keepdims=True) + epsilon)
    normed = centred * inverse
    return (normed * gain_vec, normed, inverse)


def norm_back(grad_out, gain_vec, normed, inverse):
    grad_norm = grad_out * gain_vec
    mean_grad = jnp.mean(grad_norm, axis=-1, keepdims=True)
    mean_cross = jnp.mean(grad_norm * normed, axis=-1, keepdims=True)
    return inverse * (grad_norm - mean_grad - normed * mean_cross)


def spread_rows(local_rows):
    return lax.all_gather(local_rows.astype(jnp.bfloat16), "tensor", axis=1, tiled=True)


def reduce_grads(partial_sum):
    return lax.psum_scatter(
        partial_sum.astype(jnp.bfloat16), "tensor", scatter_dimension=1, tiled=True
    ).astype(jnp.float32)


def project_rows(act_rows, weight, output_choice, input_choice):
    low_rank = jnp.einsum(
        "ctd,crd->ctr", act_rows, output_choice, preferred_element_type=jnp.float32
    )
    result = jnp.einsum("ctd,de->cte", act_rows, weight, preferred_element_type=jnp.float32)
    result = result + split_dot("ctr,cre->cte", low_rank, input_choice)
    return (result, low_rank)


def project_back(grad_low, act_rows, weight, output_choice, input_choice, low_rank):
    grad_rank = jnp.einsum(
        "cte,cre->ctr", grad_low, input_choice, preferred_element_type=jnp.float32
    )
    grad_rows = jnp.einsum("cte,de->ctd", grad_low, weight, preferred_element_type=jnp.float32)
    grad_rows = grad_rows + split_dot("ctr,crd->ctd", grad_rank, output_choice)
    grad_down = split_dot("ctr,ctd->crd", grad_rank, act_rows)
    grad_up = split_dot("ctr,cte->cre", low_rank, grad_low)
    return (grad_rows, grad_down, grad_up)


def causal_frames(first_row, block_rows, key_count):
    query_at = first_row + jnp.arange(block_rows, dtype=jnp.int32)[:, None]
    key_at = jnp.arange(key_count, dtype=jnp.int32)[None, :]
    return key_at <= query_at


def attention_forward(queries, key_rows, value_rows, causal):
    frames = queries.shape[1]
    key_count = key_rows.shape[1]
    block_rows = min(512, frames)
    score_scale = HEAD_DIM ** (-0.5)
    outputs = []
    log_totals = []
    for first_row in range(0, frames, block_rows):
        key_end = first_row + block_rows if causal else key_count
        query_block = queries[:, first_row : first_row + block_rows]
        scores = (
            jnp.einsum(
                "cbhe,ckhe->chbk",
                query_block,
                key_rows[:, :key_end],
                preferred_element_type=jnp.float32,
            )
            * score_scale
        )
        if causal:
            scores = jnp.where(causal_frames(first_row, block_rows, key_end), scores, -1e30)
        largest = jnp.max(scores, axis=-1, keepdims=True)
        exponent = jnp.exp(scores - largest)
        summed = jnp.sum(exponent, axis=-1, keepdims=True)
        prob_low = (exponent / summed).astype(jnp.bfloat16)
        outputs.append(
            jnp.einsum(
                "chbk,ckhe->cbhe",
                prob_low,
                value_rows[:, :key_end],
                preferred_element_type=jnp.float32,
            )
        )
        log_totals.append(largest + jnp.log(summed))
    return (jnp.concatenate(outputs, axis=1), jnp.concatenate(log_totals, axis=2))


def attention_back(queries, key_rows, value_rows, log_totals, grad_mixed, causal):
    frames = queries.shape[1]
    key_count = key_rows.shape[1]
    block_rows = min(512, frames)
    score_scale = HEAD_DIM ** (-0.5)
    grad_keys = jnp.zeros(key_rows.shape, jnp.float32)
    grad_values = jnp.zeros(value_rows.shape, jnp.float32)
    grad_queries = []
    for first_row in range(0, frames, block_rows):
        key_end = first_row + block_rows if causal else key_count
        key_part = key_rows[:, :key_end]
        value_part = value_rows[:, :key_end]
        query_block = queries[:, first_row : first_row + block_rows]
        grad_block = grad_mixed[:, first_row : first_row + block_rows]
        scores = (
            jnp.einsum("cbhe,ckhe->chbk", query_block, key_part, preferred_element_type=jnp.float32)
            * score_scale
        )
        if causal:
            scores = jnp.where(causal_frames(first_row, block_rows, key_end), scores, -1e30)
        probs = jnp.exp(scores - log_totals[:, :, first_row : first_row + block_rows])
        grad_values = grad_values.at[:, :key_end].add(
            jnp.einsum(
                "chbk,cbhe->ckhe",
                probs.astype(jnp.bfloat16),
                grad_block,
                preferred_element_type=jnp.float32,
            )
        )
        grad_probs = jnp.einsum(
            "cbhe,ckhe->chbk", grad_block, value_part, preferred_element_type=jnp.float32
        )
        inner_sum = jnp.sum(probs * grad_probs, axis=-1, keepdims=True)
        grad_scores = (probs * (grad_probs - inner_sum)).astype(jnp.bfloat16)
        grad_queries.append(
            jnp.einsum("chbk,ckhe->cbhe", grad_scores, key_part, preferred_element_type=jnp.float32)
            * score_scale
        )
        grad_keys = grad_keys.at[:, :key_end].add(
            jnp.einsum(
                "chbk,cbhe->ckhe", grad_scores, query_block, preferred_element_type=jnp.float32
            )
            * score_scale
        )
    return (jnp.concatenate(grad_queries, axis=1), grad_keys, grad_values)


def gelu_exact(pre_act):
    return jax.nn.gelu(pre_act, approximate=False)


def on_device(
    inputs,
    encoder_text_states,
    cotangent,
    clip_adapter_index,
    self_norm_gain,
    cross_norm_gain,
    feed_norm_gain,
    self_query_key_value_weight,
    self_output_weight,
    cross_query_weight,
    cross_key_value_weight,
    cross_output_weight,
    up_weight,
    down_weight,
    self_first_factors,
    self_second_factors,
    cross_first_factors,
    cross_second_factors,
    attention_first_factors,
    attention_second_factors,
    input_first_factors,
    input_second_factors,
    output_first_factors,
    output_second_factors,
):
    adapter_slot_count = input_first_factors.shape[0]
    chooser = (
        clip_adapter_index[:, :, None]
        == jnp.arange(adapter_slot_count, dtype=jnp.int32)[None, None, :]
    ).astype(jnp.bfloat16)
    local_heads = self_output_weight.shape[0] // HEAD_DIM

    def choose_adapter_slot(adapter_slot_table, column_index):
        return jnp.einsum(
            "cn,npq->cpq",
            chooser[:, column_index],
            adapter_slot_table,
            preferred_element_type=jnp.float32,
        ).astype(jnp.bfloat16)

    def slot_grads(grad_pick, column_index):
        return split_dot("cpq,cn->npq", grad_pick, chooser[:, column_index])

    def split_heads(stacked):
        return stacked.reshape(stacked.shape[0], stacked.shape[1], local_heads, HEAD_DIM)

    def join_heads(stacked):
        return stacked.reshape(stacked.shape[0], stacked.shape[1], local_heads * HEAD_DIM)

    def out_forward(mixed_in, inner_layer):
        column_index = 3 + 4 * inner_layer
        input_choice = choose_adapter_slot(attention_second_factors[inner_layer], column_index)
        weight = self_output_weight if inner_layer == 0 else cross_output_weight
        output_choice = choose_adapter_slot(attention_first_factors[inner_layer], column_index)
        partial_out, low_rank = project_rows(mixed_in, weight, output_choice, input_choice)
        branch = lax.psum_scatter(
            partial_out.astype(jnp.bfloat16), "tensor", scatter_dimension=1, tiled=True
        ).astype(jnp.float32)
        kept_data = (mixed_in, weight, output_choice, input_choice, low_rank)
        return (branch, kept_data)

    def out_back(grad_stream, kept_data):
        mixed_in, weight, output_choice, input_choice, low_rank = kept_data
        grad_low = grad_stream.astype(jnp.bfloat16)
        grad_full = lax.all_gather(grad_low, "tensor", axis=1, tiled=True)
        grad_rows, grad_down, grad_up = project_back(
            grad_full, mixed_in, weight, output_choice, input_choice, low_rank
        )
        grad_mixed = grad_rows.astype(jnp.bfloat16)
        return (grad_mixed, grad_down, grad_up)

    stream = inputs.astype(jnp.float32)
    normed_value, normed_one, inverse_one = layer_norm(stream, self_norm_gain)
    rows_one = spread_rows(normed_value)
    self_down_factor = [
        choose_adapter_slot(self_first_factors[slot_number], slot_number)
        for slot_number in range(3)
    ]
    self_up_factor = [
        choose_adapter_slot(self_second_factors[slot_number], slot_number)
        for slot_number in range(3)
    ]
    self_parts = [
        project_rows(
            rows_one,
            self_query_key_value_weight[slot_number],
            self_down_factor[slot_number],
            self_up_factor[slot_number],
        )
        for slot_number in range(3)
    ]
    self_heads = [
        split_heads(self_parts[slot_number][0].astype(jnp.bfloat16)) for slot_number in range(3)
    ]
    mixed_one, totals_one = attention_forward(self_heads[0], self_heads[1], self_heads[2], True)
    mixed_one = join_heads(mixed_one).astype(jnp.bfloat16)
    branch_one, kept_one = out_forward(mixed_one, 0)
    stream_one = stream + branch_one
    normed_value, normed_two, inverse_two = layer_norm(stream_one, cross_norm_gain)
    rows_two = spread_rows(normed_value)
    cross_down_factor = [
        choose_adapter_slot(cross_first_factors[slot_number], 4 + slot_number)
        for slot_number in range(3)
    ]
    cross_up_factor = [
        choose_adapter_slot(cross_second_factors[slot_number], 4 + slot_number)
        for slot_number in range(3)
    ]
    query_full, query_rank = project_rows(
        rows_two, cross_query_weight, cross_down_factor[0], cross_up_factor[0]
    )
    key_full, key_rank = project_rows(
        encoder_text_states, cross_key_value_weight[0], cross_down_factor[1], cross_up_factor[1]
    )
    value_full, value_rank = project_rows(
        encoder_text_states, cross_key_value_weight[1], cross_down_factor[2], cross_up_factor[2]
    )
    query_two = split_heads(query_full.astype(jnp.bfloat16))
    key_two = split_heads(key_full.astype(jnp.bfloat16))
    value_two = split_heads(value_full.astype(jnp.bfloat16))
    mixed_two, totals_two = attention_forward(query_two, key_two, value_two, False)
    mixed_two = join_heads(mixed_two).astype(jnp.bfloat16)
    branch_two, kept_two = out_forward(mixed_two, 1)
    stream_two = stream_one + branch_two
    normed_value, normed_three, inverse_three = layer_norm(stream_two, feed_norm_gain)
    rows_three = spread_rows(normed_value)
    input_second_choice = choose_adapter_slot(input_first_factors, 8)
    input_first_choice = choose_adapter_slot(input_second_factors, 8)
    before, up_rank = project_rows(rows_three, up_weight, input_second_choice, input_first_choice)
    gelu_value, gelu_pull = jax.vjp(gelu_exact, before)
    hidden = gelu_value.astype(jnp.bfloat16)
    output_second_choice = choose_adapter_slot(output_first_factors, 9)
    output_first_choice = choose_adapter_slot(output_second_factors, 9)
    partial_out, down_rank = project_rows(
        hidden, down_weight, output_second_choice, output_first_choice
    )
    branch_three = lax.psum_scatter(
        partial_out.astype(jnp.bfloat16), "tensor", scatter_dimension=1, tiled=True
    ).astype(jnp.float32)
    output = (stream_two + branch_three).astype(jnp.bfloat16)
    grad_full = lax.all_gather(cotangent, "tensor", axis=1, tiled=True)
    grad_hidden, grad_down_a, grad_down_b = project_back(
        grad_full, hidden, down_weight, output_second_choice, output_first_choice, down_rank
    )
    grad_before = gelu_pull(grad_hidden)[0].astype(jnp.bfloat16)
    grad_rows, grad_up_a, grad_up_b = project_back(
        grad_before, rows_three, up_weight, input_second_choice, input_first_choice, up_rank
    )
    grad_stream = cotangent.astype(jnp.float32) + norm_back(
        reduce_grads(grad_rows), feed_norm_gain, normed_three, inverse_three
    )
    grad_mixed, grad_out_a_two, grad_out_b_two = out_back(grad_stream, kept_two)
    grad_query, grad_key, grad_value = attention_back(
        query_two, key_two, value_two, totals_two, split_heads(grad_mixed), False
    )
    grad_query = join_heads(grad_query).astype(jnp.bfloat16)
    grad_key = join_heads(grad_key).astype(jnp.bfloat16)
    grad_value = join_heads(grad_value).astype(jnp.bfloat16)
    grad_rows_query, cross_grad_a_zero, cross_grad_b_zero = project_back(
        grad_query,
        rows_two,
        cross_query_weight,
        cross_down_factor[0],
        cross_up_factor[0],
        query_rank,
    )
    grad_text_key, cross_grad_a_one, cross_grad_b_one = project_back(
        grad_key,
        encoder_text_states,
        cross_key_value_weight[0],
        cross_down_factor[1],
        cross_up_factor[1],
        key_rank,
    )
    grad_text_value, cross_grad_a_two, cross_grad_b_two = project_back(
        grad_value,
        encoder_text_states,
        cross_key_value_weight[1],
        cross_down_factor[2],
        cross_up_factor[2],
        value_rank,
    )
    normed_grad, text_grad = (
        lax.psum_scatter(
            grad_rows_query.astype(jnp.bfloat16), "tensor", scatter_dimension=1, tiled=True
        ).astype(jnp.float32),
        lax.psum_scatter(
            (grad_text_key + grad_text_value).astype(jnp.bfloat16),
            "tensor",
            scatter_dimension=2,
            tiled=True,
        ).astype(jnp.float32),
    )
    grad_stream = grad_stream + norm_back(normed_grad, cross_norm_gain, normed_two, inverse_two)
    grad_mixed, grad_out_a_one, grad_out_b_one = out_back(grad_stream, kept_one)
    grad_query, grad_key, grad_value = attention_back(
        self_heads[0], self_heads[1], self_heads[2], totals_one, split_heads(grad_mixed), True
    )
    self_grads = [
        join_heads(grad_query).astype(jnp.bfloat16),
        join_heads(grad_key).astype(jnp.bfloat16),
        join_heads(grad_value).astype(jnp.bfloat16),
    ]
    self_rows_total = jnp.zeros(rows_one.shape, jnp.float32)
    self_grad_a = []
    self_grad_b = []
    for slot_number in range(3):
        grad_rows, grad_a_part, grad_b_part = project_back(
            self_grads[slot_number],
            rows_one,
            self_query_key_value_weight[slot_number],
            self_down_factor[slot_number],
            self_up_factor[slot_number],
            self_parts[slot_number][1],
        )
        self_rows_total = self_rows_total + grad_rows
        self_grad_a.append(slot_grads(grad_a_part, slot_number))
        self_grad_b.append(slot_grads(grad_b_part, slot_number))
    input_grad = grad_stream + norm_back(
        reduce_grads(self_rows_total), self_norm_gain, normed_one, inverse_one
    )
    sum_self_a = jnp.stack(self_grad_a)
    sum_self_b = jnp.stack(self_grad_b)
    sum_cross_a = jnp.stack(
        [
            slot_grads(cross_grad_a_zero, 4),
            slot_grads(cross_grad_a_one, 5),
            slot_grads(cross_grad_a_two, 6),
        ]
    )
    sum_cross_b = jnp.stack(
        [
            slot_grads(cross_grad_b_zero, 4),
            slot_grads(cross_grad_b_one, 5),
            slot_grads(cross_grad_b_two, 6),
        ]
    )
    sum_out_a = jnp.stack([slot_grads(grad_out_a_one, 3), slot_grads(grad_out_a_two, 7)])
    sum_out_b = jnp.stack([slot_grads(grad_out_b_one, 3), slot_grads(grad_out_b_two, 7)])
    sum_up_a = slot_grads(grad_up_a, 8)
    sum_up_b = slot_grads(grad_up_b, 8)
    sum_down_a = slot_grads(grad_down_a, 9)
    sum_down_b = slot_grads(grad_down_b, 9)
    sum_self_a, sum_cross_a, sum_out_b, sum_up_a, sum_down_b = (
        lax.psum_scatter(
            sum_self_a.astype(jnp.bfloat16), "tensor", scatter_dimension=3, tiled=True
        ).astype(jnp.float32),
        lax.psum_scatter(
            sum_cross_a.astype(jnp.bfloat16), "tensor", scatter_dimension=3, tiled=True
        ).astype(jnp.float32),
        lax.psum_scatter(
            sum_out_b.astype(jnp.bfloat16), "tensor", scatter_dimension=3, tiled=True
        ).astype(jnp.float32),
        lax.psum_scatter(
            sum_up_a.astype(jnp.bfloat16), "tensor", scatter_dimension=2, tiled=True
        ).astype(jnp.float32),
        lax.psum_scatter(
            sum_down_b.astype(jnp.bfloat16), "tensor", scatter_dimension=2, tiled=True
        ).astype(jnp.float32),
    )
    totals = (
        lax.psum(sum_self_a.astype(jnp.bfloat16), "dp").astype(jnp.float32),
        lax.psum(sum_self_b.astype(jnp.bfloat16), "dp").astype(jnp.float32),
        lax.psum(sum_cross_a.astype(jnp.bfloat16), "dp").astype(jnp.float32),
        lax.psum(sum_cross_b.astype(jnp.bfloat16), "dp").astype(jnp.float32),
        lax.psum(sum_out_a.astype(jnp.bfloat16), "dp").astype(jnp.float32),
        lax.psum(sum_out_b.astype(jnp.bfloat16), "dp").astype(jnp.float32),
        lax.psum(sum_up_a.astype(jnp.bfloat16), "dp").astype(jnp.float32),
        lax.psum(sum_up_b.astype(jnp.bfloat16), "dp").astype(jnp.float32),
        lax.psum(sum_down_a.astype(jnp.bfloat16), "dp").astype(jnp.float32),
        lax.psum(sum_down_b.astype(jnp.bfloat16), "dp").astype(jnp.float32),
    )
    return (
        output,
        input_grad,
        text_grad,
        totals[0],
        totals[1],
        totals[2],
        totals[3],
        totals[4],
        totals[5],
        totals[6],
        totals[7],
        totals[8],
        totals[9],
    )


LOW = jnp.bfloat16
WIDE = jnp.float32
VMEM_BYTES = 58 * 1024 * 1024
RANK_UNIT = 16
COST_SCALE = 1


def mm(left, right, left_dim=1, right_dim=0):
    return lax.dot_general(
        left, right, (((left_dim,), (right_dim,)), ((), ())), preferred_element_type=WIDE
    )


def mm_nt(left, right):
    return mm(left, right, 1, 1)


def mm_tn(left, right):
    return mm(left, right, 0, 0)


def low_rank(factor, rows):
    return mm_nt(factor, rows).astype(LOW)


def norm_rows(rows, gain):
    centred = rows - jnp.mean(rows, axis=-1, keepdims=True)
    inverse = lax.rsqrt(jnp.mean(centred * centred, axis=-1, keepdims=True) + epsilon)
    normed = centred * inverse
    return normed * gain, normed, inverse


def lane_halves():
    lane = lax.broadcasted_iota(jnp.int32, (1, 2 * HEAD_DIM), 1)
    return lane < HEAD_DIM


def half_masks():
    left = lane_halves()
    first = jnp.where(left, 1.0, 0.0)
    return first.astype(LOW), (1.0 - first).astype(LOW)


def gelu_parts(pre):
    bell = jnp.exp(-0.5 * pre * pre)
    step = 1.0 / (1.0 + (0.3275911 * 0.7071067811865476) * jnp.abs(pre))
    tail = step * (
        0.5 * 0.254829592
        + step
        * (
            0.5 * -0.284496736
            + step
            * (0.5 * 1.421413741 + step * (0.5 * -1.453152027 + step * (0.5 * 1.061405429)))
        )
    )
    tail = tail * bell
    phi = jnp.where(pre >= 0.0, 1.0 - tail, tail)
    return pre * phi, phi + pre * bell * 0.3989422804014327


def whole(shape, where=None):
    place = (0,) * len(shape) if where is None else where
    return pl.BlockSpec(shape, lambda *_: place, pipeline_mode=pl.Buffered(1))


def call(body, grid, in_specs, out_specs, out_shape, scratch, flops, moved, name, args):
    return pl.pallas_call(
        body,
        grid_spec=pltpu.PrefetchScalarGridSpec(
            num_scalar_prefetch=1,
            grid=grid,
            in_specs=in_specs,
            out_specs=out_specs,
            scratch_shapes=scratch,
        ),
        out_shape=out_shape,
        compiler_params=pltpu.CompilerParams(
            dimension_semantics=("arbitrary",) * len(grid), vmem_limit_bytes=VMEM_BYTES
        ),
        cost_estimate=pl.CostEstimate(
            flops=flops // COST_SCALE, bytes_accessed=moved // COST_SCALE, transcendentals=0
        ),
        name=name,
    )(*args)


def shaped(shape, dtype):
    return jax.ShapeDtypeStruct(shape, dtype)


IN_PLACE = pl.BlockSpec(memory_space=pl.ANY)


def factors_body(_, *refs):
    out_ref = refs[-1]
    first = 0
    for ref in refs[:-1]:
        size = ref.shape[-1]
        out_ref[:, first : first + size] = ref[...]
        first += size


def picked_factors(meta, sources):
    specs = []
    total = 0
    for table, entry, slot in sources:
        if entry is None:
            spec = pl.BlockSpec((None,) + table.shape[1:], lambda t, m, slot=slot: (m[slot], 0, 0))
        else:
            spec = pl.BlockSpec(
                (None, None) + table.shape[2:], lambda t, m, entry=entry, slot=slot: (entry, m[slot], 0, 0)
            )
        specs.append(spec)
        total += table.shape[-1]
    shape = (RANK_UNIT, total)
    return call(
        factors_body, (1,), specs, whole(shape), shaped(shape, LOW), [], 0, 4 * RANK_UNIT * total,
        "picked_factors", (meta,) + tuple(table for table, _, _ in sources),
    )


def share_body(_, parts, down_ref, up_ref, *refs):
    out_ref = refs[-1]
    step = pl.program_id(0)

    @pl.when(step < parts)
    def _():
        out_ref[0] = down_ref[...]

    @pl.when(step >= parts)
    def _():
        out_ref[0] = up_ref[...]


def feed_share(meta, down_weight, up_weight, depth, after):
    hidden, width = down_weight.shape
    parts = hidden // width
    return call(
        lambda m, *refs: share_body(m, parts, *refs),
        (2 * parts,),
        [
            pl.BlockSpec(
                (depth, width), lambda t, m: (m[11] * parts + jnp.minimum(t, parts - 1), 0)
            ),
            pl.BlockSpec((depth, width), lambda t, m: (m[11], jnp.maximum(t - parts, 0))),
        ]
        + [IN_PLACE] * len(after),
        pl.BlockSpec((1, depth, width), lambda t, m: (t, 0, 0)),
        shaped((2 * parts, depth, width), LOW),
        [],
        0,
        8 * parts * depth * width,
        "feed_share",
        (meta, down_weight, up_weight, *after),
    )


def first_norm_body(_, x_ref, gain_ref, out_ref):
    rows, _, _ = norm_rows(x_ref[...].astype(WIDE), gain_ref[...])
    out_ref[...] = rows.astype(LOW)


def first_norm(meta, x, gain):
    frames, width = x.shape
    block = min(256, frames)
    rows = pl.BlockSpec((block, width), lambda t, _: (t, 0))
    return call(
        first_norm_body,
        (frames // block,),
        [rows, whole((1, width))],
        rows,
        shaped(x.shape, LOW),
        [],
        10 * x.size,
        4 * x.size,
        "first_norm",
        (meta, x, gain),
    )


def project_body(_, act_ref, weight_ref, down_ref, up_ref, *refs):
    out_ref, rank_ref = refs[-2:]
    act = act_ref[...]
    rank = low_rank(down_ref[0, 0], act)
    rank_ref[0] = rank
    out_ref[0] = (mm(act, weight_ref[0]) + mm_tn(rank, up_ref[0, 0])).astype(LOW)


def project_heads(meta, act, weights, down, up, slots, skip, name, after=()):
    rows, width = act.shape
    count, _, local = weights.shape
    first_slot = slots
    return call(
        project_body,
        (count,),
        [
            whole((rows, width)),
            pl.BlockSpec((1, width, local), lambda j, m: (j, 0, 0)),
            pl.BlockSpec((1, 1, RANK_UNIT, width), lambda j, m: (j + skip, m[first_slot + j], 0, 0)),
            pl.BlockSpec((1, 1, RANK_UNIT, local), lambda j, m: (j + skip, m[first_slot + j], 0, 0)),
        ]
        + [IN_PLACE] * len(after),
        (
            pl.BlockSpec((1, rows, local), lambda j, m: (j, 0, 0)),
            pl.BlockSpec((1, RANK_UNIT, rows), lambda j, m: (j, 0, 0)),
        ),
        (shaped((count, rows, local), LOW), shaped((count, RANK_UNIT, rows), LOW)),
        [],
        2 * rows * width * local * count,
        2 * (weights.size + act.size + count * rows * local),
        name,
        (meta, act, weights, down, up, *after),
    )


def project_back_body(_, last, grad_ref, weight_ref, down_ref, up_ref, after_ref, out_ref, total_ref):
    step = pl.program_id(0)
    grad = grad_ref[0]
    grad_rank = low_rank(up_ref[0, 0], grad)
    part = mm_nt(grad, weight_ref[0]) + mm_tn(grad_rank, down_ref[0, 0])

    @pl.when(step == 0)
    def _():
        total_ref[...] = part

    @pl.when(step > 0)
    def _():
        total_ref[...] += part

    @pl.when(step == last)
    def _():
        out_ref[...] = total_ref[...].astype(out_ref.dtype)


def project_back_heads(meta, grads, weights, down, up, slots, skip, kind, name, after, part=(0, 1)):
    count, width, local = weights.shape
    which, parts = part
    rows = grads.shape[1] // parts
    return call(
        lambda m, *refs: project_back_body(m, count - 1, *refs),
        (count,),
        [
            pl.BlockSpec((1, rows, local), lambda j, m: (j, which, 0)),
            pl.BlockSpec((1, width, local), lambda j, m: (j, 0, 0)),
            pl.BlockSpec((1, 1, RANK_UNIT, width), lambda j, m: (j + skip, m[slots + j], 0, 0)),
            pl.BlockSpec((1, 1, RANK_UNIT, local), lambda j, m: (j + skip, m[slots + j], 0, 0)),
            IN_PLACE,
        ],
        whole((rows, width)),
        shaped((rows, width), kind),
        [pltpu.VMEM((rows, width), WIDE)],
        2 * rows * width * local * count,
        2 * (weights.size + count * rows * local) + 4 * rows * width,
        name,
        (meta, grads, weights, down, up, after),
    )


def first_grads_body(meta, count, parts, *refs):
    ups = refs[2 * parts : 2 * parts + count]
    mine_ref, theirs_ref, ga, act_scratch, grad_scratch, sems = refs[-6:]
    half = ga.shape[1] // 2
    copies = []
    for part in range(parts):
        pairs = ((refs[parts + part], grad_scratch.at[part]), (refs[part], act_scratch.at[part]))
        copies.append(
            [pltpu.make_async_copy(*pair, sems.at[2 * part + number]) for number, pair in enumerate(pairs)]
        )
        for copy in copies[-1]:
            copy.start()
    for part in range(parts):
        copies[part][0].wait()
        grad_rank = jnp.concatenate(
            [low_rank(ups[j][0, 0], grad_scratch[part, j]) for j in range(count)], axis=0
        )
        copies[part][1].wait()
        product = mm(grad_rank, act_scratch[part])
        if part == 0:
            ga[...] = product
        else:
            ga[...] += product
    side = meta[10]
    for j in range(count):
        rows = slice(RANK_UNIT * j, RANK_UNIT * (j + 1))
        span = slice(j * half, (j + 1) * half)
        mine_ref[:, span] = ga[rows, pl.ds(pl.multiple_of(side * half, 128), half)]
        theirs = ga[rows, pl.ds(pl.multiple_of((1 - side) * half, 128), half)]
        theirs_ref[:, span] = theirs.astype(LOW)


def first_grads(meta, acts, grads, up, slots, name):
    rows, width = acts[0].shape
    count, _, local = grads[0].shape
    parts = len(acts)

    def table(j):
        return pl.BlockSpec(
            (1, 1, RANK_UNIT, local), lambda t, m: (j, m[slots + j], 0, 0), pipeline_mode=pl.Buffered(1)
        )

    shape = (RANK_UNIT, count * width // 2)
    return call(
        lambda m, *refs: first_grads_body(m, count, parts, *refs),
        (1,),
        [IN_PLACE] * (2 * parts) + [table(j) for j in range(count)],
        (whole(shape), whole(shape)),
        (shaped(shape, WIDE), shaped(shape, LOW)),
        [
            pltpu.VMEM((RANK_UNIT * count, width), WIDE),
            pltpu.VMEM((parts, rows, width), LOW),
            pltpu.VMEM((parts, count, rows, local), LOW),
            pltpu.SemaphoreType.DMA((2 * parts,)),
        ],
        4 * parts * rows * (width + local) * RANK_UNIT * count,
        2 * parts * rows * (width + count * local),
        name,
        (meta, *acts, *grads, *([up] * count)),
    )


def second_grads_body(_, parts, *refs):
    out_ref, grad_scratch, sems = refs[-3:]
    count, _, local = refs[parts].shape
    copies = [
        pltpu.make_async_copy(refs[parts + part].at[j], grad_scratch.at[part, j], sems.at[part * count + j])
        for part in range(parts)
        for j in range(count)
    ]
    for j in range(count):
        for part in range(parts):
            copies[part * count + j].start()
    for j in range(count):
        total = None
        for part in range(parts):
            copies[part * count + j].wait()
            product = mm(refs[part][j], grad_scratch[part, j])
            total = product if total is None else total + product
        out_ref[:, j * local : (j + 1) * local] = total.astype(LOW)


def second_grads(meta, ranks, grads, name, after):
    count, rows, local = grads[0].shape
    parts = len(ranks)
    shape = (RANK_UNIT, count * local)
    return call(
        lambda m, *refs: second_grads_body(m, parts, *refs),
        (1,),
        [whole(ranks[0].shape)] * parts + [IN_PLACE] * (parts + 1),
        whole(shape),
        shaped(shape, LOW),
        [pltpu.VMEM((parts, count, rows, local), LOW), pltpu.SemaphoreType.DMA((parts * count,))],
        2 * parts * rows * local * RANK_UNIT * count,
        2 * parts * rows * count * local,
        name,
        (meta, *ranks, *grads, after),
    )


def split_columns(meta, mine_ref, theirs_ref, first, array, skip=0):
    half = array.shape[-1] // 2
    side = meta[10]
    mine_ref[:, first : first + half] = array[:, pl.ds(pl.multiple_of(side * half, 128), half)]
    theirs = array[:, pl.ds(pl.multiple_of((1 - side) * half, 128), half)]
    theirs_ref[:, skip + first : skip + first + half] = theirs.astype(LOW)


def own_columns(mine_ref, theirs_ref, first, array):
    half = array.shape[-1] // 2
    span = slice(first, first + half)
    mine_ref[:, span] = array[:, :half]
    theirs_ref[:, span] = array[:, half:].astype(LOW)


def join(mine, received):
    both = jnp.concatenate(received, axis=1).astype(WIDE)
    width = both.shape[1]
    return (mine + jnp.pad(both, ((0, 0), (0, mine.shape[1] - width)))).astype(LOW)


def clip_names(label_ref):
    clips, rank, width = label_ref.shape
    return label_ref[...].reshape(clips * rank, width).astype(WIDE).T


def slot_take(names, slots, rank):
    source = lax.broadcasted_iota(jnp.int32, names.shape, 1)
    target = (source & (rank - 1)) + rank * names.astype(jnp.int32)
    place = lax.broadcasted_iota(jnp.int32, (slots * rank, names.shape[1]), 0)
    return jnp.where(place == target, 1.0, 0.0).astype(LOW)


def slot_copies(unit, count, everyone_ref, arrived, in_sems):
    return [
        pltpu.make_async_copy(
            everyone_ref.at[:, :, pl.ds(unit * number, unit)], arrived.at[number], in_sems.at[number]
        )
        for number in range(count)
    ]


def slot_work(plan, slots, carried, everyone_ref, label_ref, earlier, out_refs, scratch):
    names, arrived, totals, in_sems, out_sems = scratch
    clips, rank, unit = arrived.shape[1:]
    incoming = slot_copies(unit, len(plan), everyone_ref, arrived, in_sems)
    names[...] = clip_names(label_ref)
    outgoing = []
    for number, (which, ref) in enumerate(zip(carried, earlier)):
        copy = pltpu.make_async_copy(ref.at[0], out_refs[which].at[0], out_sems.at[len(plan) + number])
        copy.start()
        outgoing.append(copy)
    for number, (column, which, place) in enumerate(plan):
        incoming[number].wait()
        take = slot_take(names[column : column + 1], slots, rank)
        total = mm(take, arrived[number].reshape(clips * rank, unit))
        totals[number] = total.reshape(slots, rank, unit)
        out_ref = out_refs[which]
        target = out_ref.at[place] if len(out_ref.shape) == 4 else out_ref.at[:, :, pl.ds(unit * place, unit)]
        copy = pltpu.make_async_copy(totals.at[number], target, out_sems.at[number])
        copy.start()
        outgoing.append(copy)
    for copy in outgoing:
        copy.wait()


def slot_scratch(everyone, plan, slots, unit, carried):
    clips, rank, _ = everyone.shape
    units = len(plan)
    return [
        pltpu.VMEM((2 * HEAD_DIM, clips * rank), WIDE),
        pltpu.VMEM((units, clips, rank, unit), LOW),
        pltpu.VMEM((units, slots, rank, unit), WIDE),
        pltpu.SemaphoreType.DMA((units,)),
        pltpu.SemaphoreType.DMA((units + len(carried),)),
    ]


def slot_specs(everyone, carried):
    clips, rank, total = everyone.shape
    label_width = 2 * HEAD_DIM
    return [IN_PLACE, whole((clips, rank, label_width), (0, 0, total // label_width - 1))] + [
        whole(array.shape) for array in carried.values()
    ]


def slot_shapes(everyone, outs, slots):
    rank = everyone.shape[1]
    return tuple(
        shaped((slots, rank, width) if stack is None else (stack, slots, rank, width), WIDE)
        for stack, width in outs
    )


def slot_sum_body(_, plan, slots, carried, outs, everyone_ref, label_ref, *refs):
    scratch = refs[-5:]
    for copy in slot_copies(scratch[1].shape[3], len(plan), everyone_ref, scratch[1], scratch[3]):
        copy.start()
    slot_work(
        plan, slots, carried, everyone_ref, label_ref, refs[: len(carried)], refs[-5 - outs : -5], scratch
    )


def slot_sums(meta, everyone, plan, outs, slots, unit, carried, name, after):
    return call(
        lambda m, *refs: slot_sum_body(m, plan, slots, tuple(carried), len(outs), *refs),
        (1,),
        slot_specs(everyone, carried) + [IN_PLACE] * len(after),
        (IN_PLACE,) * len(outs),
        slot_shapes(everyone, outs, slots),
        slot_scratch(everyone, plan, slots, unit, carried),
        0,
        2 * everyone.size,
        name,
        (meta, everyone, everyone, *carried.values(), *after),
    )


def causal_keep(rows):
    key_at = lax.broadcasted_iota(jnp.int32, (rows, rows), 0)
    return key_at <= lax.broadcasted_iota(jnp.int32, (rows, rows), 1)


def turned(rows):
    return rows.astype(WIDE).T.astype(LOW)


def forward_block(query, keys, value_turned, diagonal, earlier=None):
    score = mm_nt(keys, query)
    if diagonal:
        score = jnp.where(causal_keep(score.shape[0]), score, -1e30)
    largest = jnp.max(score, axis=0, keepdims=True)
    if earlier is not None:
        largest = jnp.maximum(largest, earlier[0])
    mixed = mm(value_turned, jnp.exp(score - largest).astype(LOW))
    if earlier is not None:
        mixed = mixed + earlier[1] * jnp.exp(earlier[0] - largest)
    return largest, mixed


def values_of(rows_ref):
    values = turned(rows_ref[2])
    ones = jnp.ones((RANK_UNIT, values.shape[1]), LOW)
    return [
        jnp.concatenate([values[HEAD_DIM * which : HEAD_DIM * (which + 1)], ones], axis=0)
        for which in (0, 1)
    ]


def forward_finish(blocks, out_ref, log_ref):
    mixes = []
    totals = []
    for largest, mixed in blocks:
        summed = mixed[HEAD_DIM : HEAD_DIM + 1]
        mixes.append(mixed[:HEAD_DIM] * (1.0 / summed))
        totals.append(jnp.broadcast_to(jnp.log(summed) + largest, (HEAD_DIM, summed.shape[1])))
    out_ref[...] = jnp.concatenate(mixes, axis=0).T.astype(LOW)
    log_ref[...] = jnp.concatenate(totals, axis=0).T


MIXED_ROWS = HEAD_DIM + RANK_UNIT
PART_ROWS = MIXED_ROWS + 8


def self_forward_own_body(_, own_ref, part_ref):
    masks = half_masks()
    query = own_ref[0] * jnp.asarray(HEAD_DIM**-0.5, LOW)
    values = values_of(own_ref)
    for which in (0, 1):
        largest, mixed = forward_block(query * masks[which], own_ref[1], values[which], True)
        part_ref[0, which, :MIXED_ROWS] = mixed
        part_ref[0, which, MIXED_ROWS:] = jnp.broadcast_to(largest, (8, largest.shape[1]))


def self_forward_own(meta, own, after):
    _, half, local = own.shape
    pair = 2 * HEAD_DIM
    shape = (local // pair, 2, PART_ROWS, half)
    return call(
        lambda m, own_ref, after_ref, part_ref: self_forward_own_body(m, own_ref, part_ref),
        (local // pair,),
        [pl.BlockSpec((3, half, pair), lambda p, m: (0, 0, p)), IN_PLACE],
        pl.BlockSpec((1,) + shape[1:], lambda p, m: (p, 0, 0, 0)),
        shaped(shape, WIDE),
        [],
        4 * half * half * local,
        10 * half * local,
        "self_forward_own",
        (meta, own, after),
    )


def self_forward_body(
    meta, part_ref, own_ref, other_ref, out_own_ref, out_other_ref, log_own_ref, log_other_ref, keys, values, queries
):
    side = meta[10]
    masks = half_masks()
    for slot, ref in ((0, own_ref), (1, other_ref)):
        keys[slot] = ref[1]
        queries[slot] = ref[0] * jnp.asarray(HEAD_DIM**-0.5, LOW)
        for which, value in enumerate(values_of(ref)):
            values[slot, which] = value
    blocks = []
    for which in (0, 1):
        own = (part_ref[0, which, MIXED_ROWS : MIXED_ROWS + 1], part_ref[0, which, :MIXED_ROWS])
        other = forward_block(queries[1] * masks[which], keys[1], values[1, which], True)
        earlier = (jnp.where(side == 0, other[0], own[0]), jnp.where(side == 0, other[1], own[1]))
        later = forward_block(
            queries[1 - side] * masks[which], keys[side], values[side, which], False, earlier
        )
        blocks.append(
            (
                (jnp.where(side == 0, own[0], later[0]), jnp.where(side == 0, own[1], later[1])),
                (jnp.where(side == 0, later[0], other[0]), jnp.where(side == 0, later[1], other[1])),
            )
        )
    forward_finish([blocks[0][0], blocks[1][0]], out_own_ref, log_own_ref)
    forward_finish([blocks[0][1], blocks[1][1]], out_other_ref, log_other_ref)


def self_forward(meta, part, own, other):
    _, half, local = own.shape
    pair = 2 * HEAD_DIM
    three = pl.BlockSpec((3, half, pair), lambda p, m: (0, 0, p))
    one = pl.BlockSpec((half, pair), lambda p, m: (0, p))
    rows = shaped((half, local), LOW)
    logs = shaped((half, local), WIDE)
    return call(
        self_forward_body,
        (local // pair,),
        [pl.BlockSpec((1,) + part.shape[1:], lambda p, m: (p, 0, 0, 0)), three, three],
        (one, one, one, one),
        (rows, rows, logs, logs),
        [
            pltpu.VMEM((2, half, pair), LOW),
            pltpu.VMEM((2, 2, MIXED_ROWS, half), LOW),
            pltpu.VMEM((2, half, pair), LOW),
        ],
        12 * half * half * local,
        20 * half * local,
        "self_forward",
        (meta, part, own, other),
    )


def three_parts(column):
    high = column.astype(LOW)
    rest = column - high.astype(WIDE)
    middle = rest.astype(LOW)
    return high, middle, (rest - middle.astype(WIDE)).astype(LOW)


def back_prepare_keys(slot, rows_ref, scratch):
    key_turned, _, _, _, key_wide, _, value_wide = scratch
    lane = lax.broadcasted_iota(jnp.int32, (1, 2 * HEAD_DIM), 1)
    key_turned[slot] = turned(rows_ref[1])
    for which in (0, 1):
        spare = HEAD_DIM * (1 - which)
        marked = jnp.where((lane >= spare) & (lane < spare + 3), 1.0, 0.0).astype(LOW)
        key_wide[slot, which] = rows_ref[1] * (1 - marked) + marked
        value_wide[slot, which] = rows_ref[2] * (1 - marked) + marked


def back_prepare_queries(slot, rows_ref, mixed_ref, logs_ref, grad_refs, scratch):
    _, query_turned, grad_turned, query_wide, _, grad_wide, _ = scratch
    masks = half_masks()
    lane = lax.broadcasted_iota(jnp.int32, (1, 2 * HEAD_DIM), 1)
    grad = jnp.concatenate([ref[...] for ref in grad_refs], axis=0)
    product = grad.astype(WIDE) * mixed_ref[...].astype(WIDE)
    query = rows_ref[0] * jnp.asarray(HEAD_DIM**-0.5, LOW)
    logs = logs_ref[...]
    query_turned[slot] = turned(query)
    grad_turned[slot] = turned(grad)
    for which in (0, 1):
        spare = HEAD_DIM * (1 - which)
        marks = [jnp.where(lane == spare + i, 1.0, 0.0).astype(LOW) for i in range(3)]
        inner = jnp.sum(product * masks[which].astype(WIDE), axis=-1, keepdims=True)
        query_rows = query * masks[which]
        for part, mark in zip(three_parts(logs[:, HEAD_DIM * which : HEAD_DIM * which + 1]), marks):
            query_rows = query_rows - part * mark
        query_wide[slot, which] = query_rows
        grad_rows = grad * masks[which]
        for part, mark in zip(three_parts(inner), marks):
            grad_rows = grad_rows - part * mark
        grad_wide[slot, which] = grad_rows


def back_block(queries, query_slot, keys, key_slot, diagonal, totals):
    _, query_turned, grad_turned, query_wide, _, grad_wide, _ = queries
    key_turned, _, _, _, key_wide, _, value_wide = keys
    half = key_turned.shape[2]
    for which in (0, 1):
        head = slice(HEAD_DIM * which, HEAD_DIM * (which + 1))
        score = mm_nt(key_wide[0, which], query_wide[0, which])
        if diagonal:
            score = jnp.where(causal_keep(half), score, -1e30)
        prob = jnp.exp(score)
        prob_grad = mm_nt(value_wide[0, which], grad_wide[0, which])
        score_grad = (prob * prob_grad).astype(LOW)
        totals[2, key_slot, head] += mm_nt(grad_turned[0, head], prob.astype(LOW))
        totals[1, key_slot, head] += mm_nt(query_turned[0, head], score_grad)
        totals[0, query_slot, head] += mm(key_turned[0, head], score_grad)


def self_back_own_body(_, own_ref, z_ref, log_ref, grad_ref, out_ref, *refs):
    prepared = refs[:-1]
    totals = refs[-1]
    totals[...] = jnp.zeros_like(totals)
    back_prepare_keys(0, own_ref, prepared)
    back_prepare_queries(0, own_ref, z_ref, log_ref, (grad_ref,), prepared)
    back_block(prepared, 0, prepared, 0, True, totals)
    out_ref[...] = totals[:, 0]


def prepared_specs(half):
    pair = 2 * HEAD_DIM
    return (pl.BlockSpec((1, pair, half), lambda p, m: (0, p, 0)),) * 3 + (
        pl.BlockSpec((1, 2, half, pair), lambda p, m: (0, 0, 0, p)),
    ) * 4


def self_back_own(meta, own, z_own, log_own, grad_own):
    _, half, local = own.shape
    pair = 2 * HEAD_DIM
    three = pl.BlockSpec((3, half, pair), lambda p, m: (0, 0, p))
    one = pl.BlockSpec((half, pair), lambda p, m: (0, p))
    return call(
        self_back_own_body,
        (local // pair,),
        [three, one, one, one],
        (pl.BlockSpec((3, pair, half), lambda p, m: (0, p, 0)),) + prepared_specs(half),
        (shaped((3, local, half), WIDE),)
        + (shaped((1, local, half), LOW),) * 3
        + (shaped((1, 2, half, local), LOW),) * 4,
        [pltpu.VMEM((3, 1, pair, half), WIDE)],
        100 * half * half * local,
        50 * half * local,
        "self_back_own",
        (meta, own, z_own, log_own, grad_own),
    )


def self_back_body(
    meta,
    part_ref,
    *refs,
):
    own = refs[:7]
    other_ref, z_ref, log_ref, grad_first_ref, grad_second_ref, _, out_own_ref, out_other_ref = refs[7:15]
    other = refs[15:22]
    totals = refs[22]
    side = meta[10]
    totals[:, 0] = part_ref[...]
    totals[:, 1] = jnp.zeros_like(totals[:, 1])
    back_prepare_keys(0, other_ref, other)
    back_prepare_queries(0, other_ref, z_ref, log_ref, (grad_first_ref, grad_second_ref), other)
    back_block(other, 1, other, 1, True, totals)

    @pl.when(side == 0)
    def _():
        back_block(other, 1, own, 0, False, totals)

    @pl.when(side != 0)
    def _():
        back_block(own, 0, other, 1, False, totals)

    for slot, ref in ((0, out_own_ref), (1, out_other_ref)):
        ref[0] = (totals[0, slot].T * HEAD_DIM**-0.5).astype(LOW)
        ref[1] = totals[1, slot].T.astype(LOW)
        ref[2] = totals[2, slot].T.astype(LOW)


def self_back(meta, part, prepared, other, z_other, log_other, grads_other, after):
    _, half, local = other.shape
    pair = 2 * HEAD_DIM
    three = pl.BlockSpec((3, half, pair), lambda p, m: (0, 0, p))
    one = pl.BlockSpec((half, pair), lambda p, m: (0, p))
    return call(
        self_back_body,
        (local // pair,),
        [pl.BlockSpec((3, pair, half), lambda p, m: (0, p, 0)), *prepared_specs(half), three, one, one]
        + [pl.BlockSpec((half // 2, pair), lambda p, m: (0, p))] * 2
        + [IN_PLACE],
        (three, three),
        (shaped(other.shape, LOW), shaped(other.shape, LOW)),
        [pltpu.VMEM((1, pair, half), LOW)] * 3
        + [pltpu.VMEM((1, 2, half, pair), LOW)] * 4
        + [pltpu.VMEM((3, 2, pair, half), WIDE)],
        200 * half * half * local,
        60 * half * local,
        "self_back",
        (meta, part, *prepared, other, z_other, log_other, *grads_other, after),
    )


def halves_of(ref, local):
    step = ref.shape[1] // 2
    return (
        ref[:, :step, :].reshape(local, ref.shape[2]),
        ref[:, step:, :].reshape(local, ref.shape[2]),
    )


def full_of(ref):
    return ref[...].reshape(ref.shape[0] * ref.shape[1], ref.shape[2])


def fetch_weights(step, order, sources, gathered, held, sems, between=()):
    copies = {}
    for which in order:
        copies[which] = (
            pltpu.make_async_copy(sources[which], held[2 * which], sems.at[2 * which]),
            pltpu.make_async_copy(gathered.at[:, which], held[2 * which + 1], sems.at[2 * which + 1]),
        )

    @pl.when(step == 0)
    def _():
        for place, which in enumerate(order):
            for copy in copies[which]:
                copy.start()
            for copy in between[place] if between else ():
                copy.start()

    def ready(which):
        @pl.when(step == 0)
        def _():
            for copy in copies[which]:
                copy.wait()

        return held[2 * which], held[2 * which + 1]

    return ready


TILE_HEADS = 4


def tile_span(tile):
    return slice(TILE_HEADS * HEAD_DIM * tile, TILE_HEADS * HEAD_DIM * (tile + 1))


def tile_masks():
    lane = lax.broadcasted_iota(jnp.int32, (1, TILE_HEADS * HEAD_DIM), 1)
    return [jnp.where(lane // HEAD_DIM == head, 1.0, 0.0).astype(LOW) for head in range(TILE_HEADS)]


def text_tile(rows, tile, masks):
    part = rows[:, tile_span(tile)]
    return jnp.concatenate([part * mask for mask in masks], axis=0)


def by_head(values, reduce):
    keys, rows = values.shape
    apart = values.reshape(TILE_HEADS, keys // TILE_HEADS, rows)
    reduced = reduce(apart, axis=1, keepdims=True)
    return jnp.broadcast_to(reduced, apart.shape).reshape(keys, rows)


def text_weights(key_tile, query):
    scores = mm_nt(key_tile, query)
    weights = jnp.exp(scores - by_head(scores, jnp.max))
    return weights * (1.0 / by_head(weights, jnp.sum))


def mix_text(query, keys, values):
    masks = tile_masks()
    mixed = []
    for tile in range(query.shape[1] // (TILE_HEADS * HEAD_DIM)):
        one_query = query[:, tile_span(tile)] * jnp.asarray(HEAD_DIM**-0.5, LOW)
        weights = text_weights(text_tile(keys, tile, masks), one_query)
        mixed.append(mm_tn(weights.astype(LOW), text_tile(values, tile, masks)).astype(LOW))
    return jnp.concatenate(mixed, axis=1)


def middle_forward_body(
    _,
    x_ref,
    z_own_ref,
    z_other_ref,
    out_weight_ref,
    query_weight_ref,
    cross_weight_ref,
    gathered_ref,
    down3_ref,
    down3_other_ref,
    up3_ref,
    down4_ref,
    up4_ref,
    up4_other_ref,
    down7_ref,
    down7_other_ref,
    up7_ref,
    text_own_ref,
    text_other_ref,
    gain_two_ref,
    gain_three_ref,
    stream_one_ref,
    stream_two_ref,
    rows_three_ref,
    query_out_own_ref,
    query_out_other_ref,
    z2_own_ref,
    z2_other_ref,
    rank3_ref,
    rank4_ref,
    rank7_ref,
    *scratch,
):
    local = z_own_ref.shape[1]
    ready = fetch_weights(
        pl.program_id(0),
        (0, 1, 2),
        (out_weight_ref, query_weight_ref, cross_weight_ref),
        gathered_ref,
        scratch[:6],
        scratch[6],
    )

    def out_product(own, other, which, down, down_other, up, rank_ref):
        rank = (mm_nt(down, own) + mm_nt(down_other, other)).astype(LOW)
        rank_ref[...] = rank
        weight_own, weight_other_ref = ready(which)
        first, second = halves_of(weight_other_ref, local)
        product = mm(own, weight_own[...]) + mm_tn(rank, up)
        return product + jnp.concatenate([mm(other, first), mm(other, second)], axis=1)

    stream = x_ref[...].astype(WIDE) + out_product(
        z_own_ref[...],
        z_other_ref[...],
        0,
        down3_ref[0, 0],
        down3_other_ref[...],
        up3_ref[0, 0],
        rank3_ref,
    )
    stream_one_ref[...] = stream
    rows_two = norm_rows(stream, gain_two_ref[...])[0].astype(LOW)
    rank = low_rank(down4_ref[0, 0], rows_two)
    rank4_ref[...] = rank
    query_own_ref, query_other_ref = ready(1)
    query_own = (mm(rows_two, query_own_ref[...]) + mm_tn(rank, up4_ref[0, 0])).astype(LOW)
    query_other = (
        mm(rows_two, full_of(query_other_ref)) + mm_tn(rank, up4_other_ref[...])
    ).astype(LOW)
    query_out_own_ref[...] = query_own
    query_out_other_ref[...] = query_other
    z2_own = mix_text(query_own, text_own_ref[0], text_own_ref[1])
    z2_other = mix_text(query_other, text_other_ref[0], text_other_ref[1])
    z2_own_ref[...] = z2_own
    z2_other_ref[...] = z2_other
    stream = stream + out_product(
        z2_own,
        z2_other,
        2,
        down7_ref[0, 0],
        down7_other_ref[...],
        up7_ref[0, 0],
        rank7_ref,
    )
    stream_two_ref[...] = stream
    rows_three_ref[...] = norm_rows(stream, gain_three_ref[...])[0].astype(LOW)


def chosen(table, entry, slot):
    shape = (1, 1) + table.shape[2:]
    return pl.BlockSpec(
        shape, lambda t, m: (entry, m[slot], 0, 0), pipeline_mode=pl.Buffered(1)
    )


def middle_specs(weights, gathered, tables, packed):
    attention_down, attention_up, cross_down, cross_up = tables
    rank = (RANK_UNIT, gathered.shape[3])
    specs = [
        IN_PLACE,
        IN_PLACE,
        IN_PLACE,
        IN_PLACE,
        chosen(attention_down, 0, 3),
        whole(rank, (0, 0)),
        chosen(attention_up, 0, 3),
        chosen(cross_down, 0, 4),
        chosen(cross_up, 0, 4),
        whole(rank, (0, 2)),
        chosen(attention_down, 1, 7),
        whole(rank, (0, 1)),
        chosen(attention_up, 1, 7),
    ]
    args = weights + (
        gathered,
        attention_down,
        packed,
        attention_up,
        cross_down,
        cross_up,
        packed,
        attention_down,
        packed,
        attention_up,
    )
    return specs, args


def middle_scratch(weights, gathered):
    shards, _, depth, local = gathered.shape
    held = []
    for weight in weights:
        held += [pltpu.VMEM(weight.shape, LOW), pltpu.VMEM((shards, depth, local), LOW)]
    return held + [pltpu.SemaphoreType.DMA((2 * len(weights),))]


def middle_forward(meta, x, z_own, z_other, weights, gathered, tables, packed, text_own, text_other, gains):
    frames, width = x.shape
    local = z_own.shape[1]
    block = min(512, frames)
    wide = pl.BlockSpec((block, width), lambda t, m: (t, 0))
    narrow = pl.BlockSpec((block, local), lambda t, m: (t, 0))
    ranks = pl.BlockSpec((RANK_UNIT, block), lambda t, m: (0, t))
    specs, args = middle_specs(weights, gathered, tables, packed)
    return call(
        middle_forward_body,
        (frames // block,),
        [wide, narrow, narrow]
        + specs
        + [whole(text_own.shape), whole(text_other.shape), whole((1, width)), whole((1, width))],
        (wide, wide, wide, narrow, narrow, narrow, narrow) + (ranks,) * 3,
        (
            shaped((frames, width), WIDE),
            shaped((frames, width), WIDE),
            shaped((frames, width), LOW),
            shaped((frames, local), LOW),
            shaped((frames, local), LOW),
            shaped((frames, local), LOW),
            shaped((frames, local), LOW),
        )
        + (shaped((RANK_UNIT, frames), LOW),) * 3,
        middle_scratch(weights, gathered),
        6 * frames * width * width,
        6 * width * width + 20 * frames * width,
        "middle_forward",
        (meta, x, z_own, z_other) + args + (text_own, text_other) + gains,
    )


def middle_back_body(
    meta,
    last,
    grad_ref,
    stream_one_ref,
    z_own_ref,
    z_other_ref,
    query_in_own_ref,
    query_in_other_ref,
    z2_own_ref,
    z2_other_ref,
    out_weight_ref,
    query_weight_ref,
    cross_weight_ref,
    gathered_ref,
    down3_ref,
    down3_other_ref,
    up3_ref,
    down4_ref,
    up4_ref,
    up4_other_ref,
    down7_ref,
    down7_other_ref,
    up7_ref,
    text_own_ref,
    text_other_ref,
    gain_two_ref,
    text_ref,
    down5_ref,
    down6_ref,
    up5_ref,
    up6_ref,
    up5_other_ref,
    up6_other_ref,
    rank3_ref,
    rank4_ref,
    rank7_ref,
    grad_one_ref,
    dz_own_ref,
    dz_first_ref,
    dz_second_ref,
    text_grad_own_ref,
    mine_ref,
    theirs_ref,
    text_mine_ref,
    text_theirs_ref,
    key_total,
    value_total,
    ga3_ref,
    gb3_ref,
    ga4_ref,
    gb4_ref,
    ga7_ref,
    gb7_ref,
    *scratch,
):
    step = pl.program_id(0)
    late = scratch[7:12]
    late_sems = scratch[13]
    late_copies = [
        pltpu.make_async_copy(source, target, late_sems.at[number])
        for number, (source, target) in enumerate(
            zip((query_in_own_ref, query_in_other_ref, stream_one_ref, z_own_ref, z_other_ref), late)
        )
    ]
    query_in_own_ref, query_in_other_ref, stream_one_ref, z_own_ref, z_other_ref = late
    grad_one_copy = pltpu.make_async_copy(scratch[12], grad_one_ref, late_sems.at[5])
    ready = fetch_weights(
        step,
        (2, 1, 0),
        (out_weight_ref, query_weight_ref, cross_weight_ref),
        gathered_ref,
        scratch[:6],
        scratch[6],
        (late_copies[:2], late_copies[2:], ()),
    )
    local = z_own_ref.shape[1]
    tiles = local // (TILE_HEADS * HEAD_DIM)
    masks = tile_masks()
    scale = jnp.asarray(HEAD_DIM**-0.5, LOW)

    @pl.when(step == 0)
    def _():
        key_total[...] = jnp.zeros_like(key_total)
        value_total[...] = jnp.zeros_like(value_total)
        for ref in (ga3_ref, gb3_ref, ga4_ref, gb4_ref, ga7_ref, gb7_ref):
            ref[...] = jnp.zeros_like(ref)

    def out_back(grad, own, other, which, down, down_other, up, ga_ref, gb_ref, rank):
        grad_rank = low_rank(up, grad)
        ga_ref[:, :local] += mm(grad_rank, own)
        ga_ref[:, local:] += mm(grad_rank, other)
        gb_ref[...] += mm(rank, grad)
        weight_own, weight_other_ref = ready(which)
        first, second = halves_of(weight_other_ref, local)
        middle = grad.shape[1] // 2
        grad_own = mm_nt(grad, weight_own[...]) + mm_tn(grad_rank, down)
        grad_other = (
            mm_nt(grad[:, :middle], first)
            + mm_nt(grad[:, middle:], second)
            + mm_tn(grad_rank, down_other)
        )
        return grad_own.astype(LOW), grad_other.astype(LOW)

    grad = grad_ref[...]
    dz2_own, dz2_other = out_back(
        grad.astype(LOW),
        z2_own_ref[...],
        z2_other_ref[...],
        2,
        down7_ref[0, 0],
        down7_other_ref[...],
        up7_ref[0, 0],
        ga7_ref,
        gb7_ref,
        rank7_ref[...],
    )

    def text_back(query, dz2, keys, values, part):
        query_grads = []
        for tile in range(tiles):
            key_tile = text_tile(keys, tile, masks)
            value_tile = text_tile(values, tile, masks)
            one_query = query[:, tile_span(tile)] * scale
            one_grad = dz2[:, tile_span(tile)]
            probs = text_weights(key_tile, one_query)
            prob_grads = mm_nt(value_tile, one_grad)
            inner = by_head(probs * prob_grads, jnp.sum)
            score_grads = (probs * (prob_grads - inner)).astype(LOW)
            query_grads.append((mm_tn(score_grads, key_tile) * HEAD_DIM**-0.5).astype(LOW))
            key_total[part, tile] += mm(score_grads, one_query)
            value_total[part, tile] += mm(probs.astype(LOW), one_grad)
        return jnp.concatenate(query_grads, axis=1)

    for copy in late_copies[:2]:
        copy.wait()
    dq_own = text_back(query_in_own_ref[...], dz2_own, text_own_ref[0], text_own_ref[1], 0)
    dq_other = text_back(query_in_other_ref[...], dz2_other, text_other_ref[0], text_other_ref[1], 1)

    for copy in late_copies[2:]:
        copy.wait()
    rows_two, normed, inverse = norm_rows(stream_one_ref[...], gain_two_ref[...])
    rows_two = rows_two.astype(LOW)
    rank = rank4_ref[...]
    grad_rank = (mm_nt(up4_ref[0, 0], dq_own) + mm_nt(up4_other_ref[...], dq_other)).astype(LOW)
    ga4_ref[...] += mm(grad_rank, rows_two)
    gb4_ref[:, :local] += mm(rank, dq_own)
    gb4_ref[:, local:] += mm(rank, dq_other)
    query_own_ref, query_other_ref = ready(1)
    grad_rows = (
        mm_nt(dq_own, query_own_ref[...])
        + mm_nt(dq_other, full_of(query_other_ref))
        + mm_tn(grad_rank, down4_ref[0, 0])
    )
    grad = grad + norm_back(grad_rows, gain_two_ref[...], normed, inverse)
    scratch[12][...] = grad
    grad_one_copy.start()
    dz_own, dz_other = out_back(
        grad.astype(LOW),
        z_own_ref[...],
        z_other_ref[...],
        0,
        down3_ref[0, 0],
        down3_other_ref[...],
        up3_ref[0, 0],
        ga3_ref,
        gb3_ref,
        rank3_ref[...],
    )
    dz_own_ref[...] = dz_own
    half = dz_first_ref.shape[0]
    dz_first_ref[...] = dz_other[:half]
    dz_second_ref[...] = dz_other[half:]
    grad_one_copy.wait()

    @pl.when(step == last)
    def _():
        split_columns(meta, mine_ref, theirs_ref, 0, ga4_ref)
        own_columns(mine_ref, theirs_ref, local, gb4_ref)
        own_columns(mine_ref, theirs_ref, 2 * local, ga3_ref)
        own_columns(mine_ref, theirs_ref, 3 * local, ga7_ref)
        split_columns(meta, mine_ref, theirs_ref, 4 * local, gb3_ref)
        split_columns(meta, mine_ref, theirs_ref, 5 * local, gb7_ref)
        texts = text_ref.shape[0]
        for slot, total in enumerate((key_total, value_total)):
            for part in (0, 1):
                for tile in range(tiles):
                    stacked = total[part, tile]
                    rows = 0.0
                    for head, mask in enumerate(masks):
                        rows = rows + stacked[HEAD_DIM * head : HEAD_DIM * (head + 1)] * mask.astype(WIDE)
                    if part == 0:
                        text_grad_own_ref[slot, :, tile_span(tile)] = rows
                    else:
                        text_theirs_ref[texts * slot : texts * (slot + 1), tile_span(tile)] = rows.astype(LOW)
        text = text_ref[...]
        factors = ((down5_ref, up5_ref, up5_other_ref), (down6_ref, up6_ref, up6_other_ref))
        for slot, (down_ref, up_ref, up_other_ref) in enumerate(factors):
            grad_own = text_grad_own_ref[slot].astype(LOW)
            grad_other = text_theirs_ref[texts * slot : texts * (slot + 1)]
            rank = low_rank(down_ref[0, 0], text)
            grad_rank = mm_nt(up_ref[0, 0], grad_own) + mm_nt(up_other_ref[...], grad_other)
            ga4_ref[...] = mm(grad_rank.astype(LOW), text)
            first = slice(2 * texts + RANK_UNIT * slot, 2 * texts + RANK_UNIT * (slot + 1))
            second = slice(2 * texts + RANK_UNIT * (2 + slot), 2 * texts + RANK_UNIT * (3 + slot))
            split_columns(meta, text_mine_ref.at[:, pl.ds(slot * local, local)], text_theirs_ref.at[first], 0, ga4_ref)
            text_mine_ref[:, (2 + slot) * local : (3 + slot) * local] = mm(rank, grad_own)
            text_theirs_ref[second] = mm(rank, grad_other).astype(LOW)


def middle_back(
    meta, grad, stream_one, z_own, z_other, q_own, q_other, z2_own, z2_other,
    weights, gathered, tables, packed, text_own, text_other, gain, text, ranks,
):
    frames, width = grad.shape
    local = z_own.shape[1]
    tiles = local // (TILE_HEADS * HEAD_DIM)
    wide = whole((frames, width))
    narrow = whole((frames, local))
    specs, args = middle_specs(weights, gathered, tables, packed)
    rank = (RANK_UNIT, width)
    packs = (RANK_UNIT, 6 * local)
    text_packs = (RANK_UNIT, 4 * local)
    text_rows = (2 * text.shape[0] + 4 * RANK_UNIT, local)
    _, _, cross_down, cross_up = tables
    return call(
        lambda m, *refs: middle_back_body(m, 0, *refs),
        (1,),
        [wide, IN_PLACE]
        + [IN_PLACE] * 4
        + [narrow] * 2
        + specs
        + [whole(text_own.shape), whole(text_other.shape), whole((1, width)), whole(text.shape)]
        + [chosen(cross_down, 1, 5), chosen(cross_down, 2, 6), chosen(cross_up, 1, 5), chosen(cross_up, 2, 6)]
        + [whole((RANK_UNIT, local), (0, 3)), whole((RANK_UNIT, local), (0, 4))]
        + [whole((RANK_UNIT, frames))] * 3,
        (IN_PLACE, narrow, whole((frames // 2, local)), whole((frames // 2, local)), whole(text_own.shape))
        + (whole(packs), whole(packs), whole(text_packs), whole(text_rows)),
        (
            shaped((frames, width), WIDE),
            shaped((frames, local), LOW),
            shaped((frames // 2, local), LOW),
            shaped((frames // 2, local), LOW),
            shaped(text_own.shape, WIDE),
            shaped(packs, WIDE),
            shaped(packs, LOW),
            shaped(text_packs, WIDE),
            shaped(text_rows, LOW),
        ),
        [
            pltpu.VMEM((2, tiles, TILE_HEADS * HEAD_DIM, TILE_HEADS * HEAD_DIM), WIDE),
            pltpu.VMEM((2, tiles, TILE_HEADS * HEAD_DIM, TILE_HEADS * HEAD_DIM), WIDE),
        ]
        + [pltpu.VMEM(rank, WIDE)] * 6
        + middle_scratch(weights, gathered)
        + [pltpu.VMEM((frames, local), LOW)] * 2
        + [pltpu.VMEM((frames, width), WIDE)]
        + [pltpu.VMEM((frames, local), LOW)] * 2
        + [pltpu.VMEM((frames, width), WIDE), pltpu.SemaphoreType.DMA((6,))],
        6 * frames * width * width,
        6 * width * width + 24 * frames * width,
        "middle_back",
        (meta, grad, stream_one, z_own, z_other, q_own, q_other, z2_own, z2_other)
        + args
        + (text_own, text_other, gain, text)
        + (cross_down, cross_down, cross_up, cross_up, packed, packed)
        + tuple(ranks),
    )


def feed_tile(
    rows_ref, cot_ref, up_weight, down_weight, up_rank, down_rank,
    ga9_ref, gb8_ref, branch, grad_rows, rank9, grad_rank8, rank8, grad_rank9,
):
    frames = rows_ref.shape[0]
    block = min(256, frames)
    low_pre = mm_tn(rank8[...], up_rank)
    low_grad = mm_tn(grad_rank9[...], down_rank)
    hidden_blocks = []
    grad_blocks = []
    for first in range(0, frames, block):
        span = slice(first, first + block)
        pre = mm(rows_ref[span], up_weight) + low_pre[span]
        grad_hidden = mm_nt(cot_ref[span], down_weight) + low_grad[span]
        hidden, slope = gelu_parts(pre)
        hidden = hidden.astype(LOW)
        grad_pre = (grad_hidden * slope).astype(LOW)
        branch[span] += mm(hidden, down_weight)
        grad_rows[span] += mm_nt(grad_pre, up_weight)
        hidden_blocks.append(hidden)
        grad_blocks.append(grad_pre)
    hidden = jnp.concatenate(hidden_blocks, axis=0)
    grad_pre = jnp.concatenate(grad_blocks, axis=0)
    rank9[...] += mm_nt(down_rank, hidden)
    grad_rank8[...] += mm_nt(up_rank, grad_pre)
    ga9_ref[...] = mm(grad_rank9[...], hidden).astype(ga9_ref.dtype)
    gb8_ref[...] = mm(rank8[...], grad_pre).astype(gb8_ref.dtype)


def feed_own_body(
    _, rows_ref, cot_ref, up_weight_ref, down_weight_ref, up_rank_ref, down_rank_ref,
    down8_ref, up9_ref,
    branch_ref, grad_rows_ref, rank9_ref, grad_rank8_ref, rank8, grad_rank9, ga9_ref, gb8_ref,
):
    @pl.when(pl.program_id(0) == 0)
    def _():
        rank8[...] = low_rank(down8_ref[0], rows_ref[...])
        grad_rank9[...] = low_rank(up9_ref[0], cot_ref[...])
        for ref in (branch_ref, grad_rows_ref, rank9_ref, grad_rank8_ref):
            ref[...] = jnp.zeros_like(ref)

    feed_tile(
        rows_ref, cot_ref, up_weight_ref[...], down_weight_ref[...], up_rank_ref[0], down_rank_ref[0],
        ga9_ref, gb8_ref, branch_ref, grad_rows_ref, rank9_ref, grad_rank8_ref, rank8, grad_rank9,
    )


def table_tile(tile, slot):
    return pl.BlockSpec((1, RANK_UNIT, tile), lambda t, m: (m[slot], 0, t))


def feed_own(meta, rows, cot, up_weight, down_weight, input_down, input_up, output_down, output_up, tile):
    frames, width = rows.shape
    hidden = up_weight.shape[1]
    grads = pl.BlockSpec((RANK_UNIT, tile), lambda t, m: (0, t))
    picked = pl.BlockSpec((1, RANK_UNIT, width), lambda t, m: (m[8], 0, 0))
    picked_out = pl.BlockSpec((1, RANK_UNIT, width), lambda t, m: (m[9], 0, 0))
    rank = (RANK_UNIT, frames)
    return call(
        feed_own_body,
        (hidden // tile,),
        [
            whole((frames, width)),
            whole((frames, width)),
            pl.BlockSpec((width, tile), lambda t, m: (0, t)),
            pl.BlockSpec((tile, width), lambda t, m: (t, 0)),
            table_tile(tile, 8),
            table_tile(tile, 9),
            picked,
            picked_out,
        ],
        (whole((frames, width)), whole((frames, width))) + (whole(rank),) * 4 + (grads, grads),
        (
            shaped((frames, width), WIDE),
            shaped((frames, width), WIDE),
            shaped(rank, WIDE),
            shaped(rank, WIDE),
            shaped(rank, LOW),
            shaped(rank, LOW),
            shaped((RANK_UNIT, hidden), WIDE),
            shaped((RANK_UNIT, hidden), WIDE),
        ),
        [],
        8 * frames * width * hidden,
        4 * width * hidden + 12 * frames * width,
        "feed_own",
        (meta, rows, cot, up_weight, down_weight, input_up, output_down, input_down, output_up),
    )


def feed_other_body(
    meta, last, rows_ref, cot_ref, up_weight_ref, down_weight_ref, up_rank_ref, down_rank_ref,
    down8_ref, up9_ref, branch_in_ref, grad_rows_in_ref, rank9_in_ref, grad_rank8_in_ref, rank8, grad_rank9,
    stream_ref, gain_ref,
    out_ref, grad_ref, mine_ref, theirs_ref,
    branch, grad_rows, rank9, grad_rank8, ga8_ref, gb9_ref, branch_in, grad_rows_in, stream_in, sems,
):
    step = pl.program_id(0)
    copies = [
        pltpu.make_async_copy(source, target, sems.at[i])
        for i, (source, target) in enumerate(
            ((branch_in_ref, branch_in), (grad_rows_in_ref, grad_rows_in), (stream_ref, stream_in))
        )
    ]

    @pl.when(step == 0)
    def _():
        for copy in copies:
            copy.start()
        branch[...] = jnp.zeros_like(branch)
        grad_rows[...] = jnp.zeros_like(grad_rows)
        rank9[...] = rank9_in_ref[...]
        grad_rank8[...] = grad_rank8_in_ref[...]

    shards, _, depth, tile = up_weight_ref.shape
    hidden = (last + 1) * tile
    first = pl.multiple_of(step * tile, 128)
    gb8_ref = theirs_ref.at[:, pl.ds(first, tile)]
    ga9_ref = theirs_ref.at[:, pl.ds(pl.multiple_of(hidden + first, 128), tile)]
    up_weight = up_weight_ref[...].reshape(shards * depth, tile)
    down_weight = down_weight_ref[...].reshape(tile, down_weight_ref.shape[3])
    feed_tile(
        rows_ref, cot_ref, up_weight, down_weight, up_rank_ref[...], down_rank_ref[...],
        ga9_ref, gb8_ref, branch, grad_rows, rank9, grad_rank8, rank8, grad_rank9,
    )

    @pl.when(step == last)
    def _():
        for copy in copies:
            copy.wait()
        frames = rows_ref.shape[0]
        block = min(128, frames)
        last8 = grad_rank8[...].astype(LOW)
        last9 = rank9[...].astype(LOW)
        ga8_ref[...] = mm(last8, rows_ref[...])
        gb9_ref[...] = mm(last9, cot_ref[...])
        half = ga8_ref.shape[1] // 2
        split_columns(meta, mine_ref, theirs_ref, 0, ga8_ref, 2 * hidden)
        split_columns(meta, mine_ref, theirs_ref, half, gb9_ref, 2 * hidden)
        for first in range(0, frames, block):
            span = slice(first, first + block)
            stream = stream_in[span]
            out = stream + (branch[span] + branch_in[span]) + mm_tn(last9[:, span], up9_ref[0])
            out_ref[span] = out.astype(LOW)
            _, normed, inverse = norm_rows(stream, gain_ref[...])
            grad = grad_rows[span] + grad_rows_in[span] + mm_tn(last8[:, span], down8_ref[0])
            grad_ref[span] = cot_ref[span].astype(WIDE) + norm_back(
                grad, gain_ref[...], normed, inverse
            )


def feed_other(
    meta, rows, cot, gathered, packed, first_pack, input_down, output_up, carried, stream, gain, tile
):
    frames, width = rows.shape
    shards, quarters, depth, _ = gathered.shape
    hidden = quarters // 2 * width
    per_half = width // tile
    own_shards = tile // (quarters // 2 * depth)
    down_first = quarters // 2
    picked = pl.BlockSpec((1, RANK_UNIT, width), lambda t, m: (m[8], 0, 0))
    picked_out = pl.BlockSpec((1, RANK_UNIT, width), lambda t, m: (m[9], 0, 0))
    rank = (RANK_UNIT, frames)
    steps = hidden // tile
    full = whole((frames, width))
    wide = pltpu.VMEM((frames, width), WIDE)
    return call(
        lambda m, *refs: feed_other_body(m, steps - 1, *refs),
        (steps,),
        [
            full,
            full,
            pl.BlockSpec(
                (shards, 1, depth, tile),
                lambda t, m: (0, down_first + t // per_half, 0, t % per_half),
            ),
            pl.BlockSpec((own_shards, down_first, depth, width), lambda t, m: (t, 0, 0, 0)),
            pl.BlockSpec((RANK_UNIT, tile), lambda t, m: (0, first_pack // tile + t)),
            pl.BlockSpec((RANK_UNIT, tile), lambda t, m: (0, (first_pack + hidden) // tile + t)),
            picked,
            picked_out,
            IN_PLACE,
            IN_PLACE,
            whole(rank),
            whole(rank),
            whole(rank),
            whole(rank),
            IN_PLACE,
            whole((1, width)),
        ],
        (full, full, whole((RANK_UNIT, width)), whole((RANK_UNIT, 2 * hidden + width))),
        (
            shaped((frames, width), LOW),
            shaped((frames, width), WIDE),
            shaped((RANK_UNIT, width), WIDE),
            shaped((RANK_UNIT, 2 * hidden + width), LOW),
        ),
        [
            wide,
            wide,
            pltpu.VMEM(rank, WIDE),
            pltpu.VMEM(rank, WIDE),
            pltpu.VMEM((RANK_UNIT, width), WIDE),
            pltpu.VMEM((RANK_UNIT, width), WIDE),
            wide,
            wide,
            wide,
            pltpu.SemaphoreType.DMA((3,)),
        ],
        8 * frames * width * hidden,
        4 * width * hidden + 24 * frames * width,
        "feed_other",
        (meta, rows, cot, gathered, gathered, packed, packed, input_down, output_up)
        + tuple(carried)
        + (stream, gain),
    )


def last_norm_body(_, half, slot_part, x_ref, own_ref, first_ref, second_ref, grad_ref, gain_ref, *refs):
    plan, slots, carried, outs = slot_part
    step = pl.program_id(0)
    everyone_ref, label_ref = refs[:2]
    earlier = refs[2 : 2 + len(carried)]
    out_ref = refs[-6 - outs]
    scratch = refs[-5:]

    @pl.when(step == 0)
    def _():
        for copy in slot_copies(scratch[1].shape[3], len(plan), everyone_ref, scratch[1], scratch[3]):
            copy.start()

    _, normed, inverse = norm_rows(x_ref[...].astype(WIDE), gain_ref[...])
    other = jnp.where(step < half, first_ref[...].astype(WIDE), second_ref[...].astype(WIDE))
    total = own_ref[...] + other
    out_ref[...] = grad_ref[...] + norm_back(total, gain_ref[...], normed, inverse)

    @pl.when(step == 2 * half - 1)
    def _():
        slot_work(plan, slots, carried, everyone_ref, label_ref, earlier, refs[-5 - outs : -5], scratch)


def last_norm(meta, x, own, received, grad, gain, everyone, plan, outs, slots, unit, carried, after):
    frames, width = x.shape
    block = min(256, frames // 2)
    half = frames // 2 // block
    rows = pl.BlockSpec((block, width), lambda t, _: (t, 0))
    first = pl.BlockSpec((block, width), lambda t, _: (jnp.minimum(t, half - 1), 0))
    second = pl.BlockSpec((block, width), lambda t, _: (jnp.maximum(t - half, 0), 0))
    slot_part = (plan, slots, tuple(carried), len(outs))
    return call(
        lambda m, *refs: last_norm_body(m, half, slot_part, *refs),
        (2 * half,),
        [rows, rows, first, second, rows, whole((1, width))]
        + slot_specs(everyone, carried)
        + [IN_PLACE] * len(after),
        (rows,) + (IN_PLACE,) * len(outs),
        (shaped(x.shape, WIDE),) + slot_shapes(everyone, outs, slots),
        slot_scratch(everyone, plan, slots, unit, carried),
        20 * x.size,
        16 * x.size,
        "last_norm",
        (meta, x, own, *received, grad, gain, everyone, everyone, *carried.values(), *after),
    )


def on_pair(
    inputs,
    encoder_text_states,
    cotangent,
    clip_adapter_index,
    self_norm_gain,
    cross_norm_gain,
    feed_norm_gain,
    self_query_key_value_weight,
    self_output_weight,
    cross_query_weight,
    cross_key_value_weight,
    cross_output_weight,
    up_weight,
    down_weight,
    self_first_factors,
    self_second_factors,
    cross_first_factors,
    cross_second_factors,
    attention_first_factors,
    attention_second_factors,
    input_first_factors,
    input_second_factors,
    output_first_factors,
    output_second_factors,
):
    x = inputs[0]
    text = encoder_text_states[0]
    cot = cotangent[0]
    width = x.shape[1]
    local = self_output_weight.shape[0]
    hidden = up_weight.shape[1]
    slots = input_first_factors.shape[0]
    group_count = lax.axis_size("dp")
    place = lax.axis_index("dp")
    side = lax.axis_index("tensor")
    picks = clip_adapter_index[0]
    meta = jnp.concatenate([picks, jnp.stack([side, place]).astype(jnp.int32)])
    gain_one, gain_two, gain_three = (
        vec.reshape(1, width) for vec in (self_norm_gain, cross_norm_gain, feed_norm_gain)
    )

    def swap(array):
        return lax.ppermute(array, "tensor", [(0, 1), (1, 0)])

    depth = width // group_count
    step = local // group_count

    def share(weight, size):
        return lax.dynamic_slice_in_dim(weight, place * size, size, axis=0)

    def side_by_side(rows, count):
        return rows.reshape(rows.shape[0], count, -1).transpose(1, 0, 2)

    out_share = side_by_side(share(self_output_weight, step), 2).reshape(depth, local)
    query_share = share(cross_query_weight, depth)
    cross_share = side_by_side(share(cross_output_weight, step), 2).reshape(depth, local)
    share_one = jnp.stack([swap(out_share), swap(query_share), swap(cross_share)])
    rows_one = first_norm(meta, x, gain_one)
    share_one, rows_one = lax.optimization_barrier((share_one, rows_one))
    gathered_one = lax.all_gather(share_one, "dp", axis=0)
    rows_one_other = swap(rows_one)
    factors = picked_factors(
        meta,
        [
            (attention_first_factors, 0, 3),
            (attention_first_factors, 1, 7),
            (cross_second_factors, 0, 4),
            (cross_second_factors, 1, 5),
            (cross_second_factors, 2, 6),
            (input_second_factors, None, 8),
            (output_first_factors, None, 9),
        ],
    )
    packed = swap(factors)
    first_pack = 5 * local

    heads_own, ranks_own = project_heads(
        meta, rows_one, self_query_key_value_weight, self_first_factors, self_second_factors, 0, 0, "own_heads"
    )
    part_own = self_forward_own(meta, heads_own, factors)
    text_own, _ = project_heads(
        meta, text, cross_key_value_weight, cross_first_factors, cross_second_factors, 5, 1, "text_heads"
    )
    text_other = swap(text_own)
    share_two = feed_share(
        meta, down_weight, up_weight, depth, (part_own, text_own, rows_one_other)
    )
    heads_other, ranks_other = project_heads(
        meta, rows_one_other, self_query_key_value_weight, self_first_factors, self_second_factors,
        0, 0, "other_heads", (share_two,),
    )
    z_own_frames, z_other_frames, log_own, log_other = self_forward(meta, part_own, heads_own, heads_other)
    share_two, z_other_frames = lax.optimization_barrier((swap(share_two), z_other_frames))
    gathered_two = lax.all_gather(share_two, "dp", axis=0)
    z_other_heads = swap(z_other_frames)
    weights = (self_output_weight, cross_query_weight, cross_output_weight)
    tables = (attention_first_factors, attention_second_factors, cross_first_factors, cross_second_factors)
    stream_one, stream_two, rows_three, q_own, q_other, z2_own, z2_other, *middle_ranks = middle_forward(
        meta, x, z_own_frames, z_other_heads, weights, gathered_one, tables, packed,
        text_own, text_other, (gain_two, gain_three),
    )
    tile = local
    *carried, ga9_own, gb8_own = feed_own(
        meta, rows_three, cot, up_weight, down_weight, input_first_factors, input_second_factors,
        output_first_factors, output_second_factors, tile,
    )
    output, grad_two, feed_mine, feed_theirs = feed_other(
        meta, rows_three, cot, gathered_two, packed, first_pack, input_first_factors,
        output_second_factors, carried, stream_two, gain_three, tile,
    )

    feed_received = swap(feed_theirs)

    (
        grad_one, dz_own_heads, *dz_other_heads, text_grad_own, middle_mine, middle_theirs,
        text_mine_rank, text_theirs,
    ) = middle_back(
        meta, grad_two, stream_one, z_own_frames, z_other_heads, q_own, q_other, z2_own, z2_other,
        weights, gathered_one, tables, packed, text_own, text_other, gain_two, text, middle_ranks,
    )
    feed_received, middle_theirs, *dz_other_heads = lax.optimization_barrier(
        (feed_received, middle_theirs, *dz_other_heads)
    )
    *dz_other_frames, text_theirs = lax.optimization_barrier(
        (*[swap(half) for half in dz_other_heads], text_theirs)
    )

    unit = local
    hidden_units = hidden // unit
    labels = jnp.zeros((RANK_UNIT, 2 * HEAD_DIM), LOW).at[:, : picks.shape[0]].set(picks.astype(LOW)[None])
    early = jnp.concatenate(
        [
            join(middle_mine, [swap(middle_theirs)]),
            join(feed_mine, [feed_received[:, 2 * hidden :]]),
            join(jnp.concatenate([gb8_own, ga9_own], axis=1), [feed_received[:, : 2 * hidden]]),
            labels,
        ],
        axis=1,
    )
    early_all = lax.all_gather(early, "dp", axis=0)
    grads_part, *prepared = self_back_own(meta, heads_own, z_own_frames, log_own, dz_own_heads)
    grads_own, grads_other = self_back(
        meta, grads_part, prepared, heads_other, z_other_frames, log_other, dz_other_frames, early
    )
    text_received, grads_own = lax.optimization_barrier((swap(text_theirs), grads_own))
    texts = text.shape[0]
    text_grad_other = text_received[: 2 * texts].reshape(text_grad_own.shape)
    text_received_rank = side_by_side(
        text_received[2 * texts :].reshape(4, RANK_UNIT, local).transpose(1, 0, 2).reshape(RANK_UNIT, -1), 1
    )[0]
    text_heads_grad = (text_grad_own + text_grad_other.astype(WIDE)).astype(LOW)
    mine, theirs = first_grads(
        meta, [rows_one, rows_one_other], [grads_own, grads_other], self_second_factors, 0, "self_first"
    )
    seconds = second_grads(meta, [ranks_own, ranks_other], [grads_own, grads_other], "self_second", theirs)
    theirs, seconds = lax.optimization_barrier((swap(theirs), seconds))
    partial_other = [
        project_back_heads(
            meta, grads_other, self_query_key_value_weight, self_first_factors, self_second_factors,
            0, 0, LOW, "other_back", seconds, (part, 2),
        )
        for part in range(2)
    ]
    received = [swap(part) for part in partial_other]
    labels = lax.dynamic_index_in_dim(early_all[:, :, -2 * HEAD_DIM :], place, axis=0, keepdims=False)
    late = jnp.concatenate(
        [join(mine, [theirs]), seconds, join(text_mine_rank, [text_received_rank]), labels], axis=1
    )
    late_all = lax.all_gather(late, "dp", axis=0)
    text_rows = project_back_heads(
        meta, text_heads_grad, cross_key_value_weight, cross_first_factors, cross_second_factors,
        5, 1, WIDE, "text_back", partial_other[1],
    )
    text_halves = (text_rows[:, : width // 2], text_rows[:, width // 2 :])
    text_mine = jnp.where(side == 0, text_halves[0], text_halves[1])
    text_theirs = jnp.where(side == 0, text_halves[1], text_halves[0])
    text_received = swap(text_theirs.astype(LOW))
    partial_own = project_back_heads(
        meta, grads_own, self_query_key_value_weight, self_first_factors, self_second_factors,
        0, 0, WIDE, "own_back", late,
    )
    sum_query_a, sum_query_b, sum_out_a, sum_out_b, sum_up_a, sum_down_b, sum_up_b, sum_down_a = slot_sums(
        meta,
        early_all,
        [(4, 0, 0), (4, 1, 0), (3, 2, 0), (7, 2, 1), (3, 3, 0), (7, 3, 1), (8, 4, 0), (9, 5, 0)]
        + [(8, 6, i) for i in range(hidden_units)]
        + [(9, 7, i) for i in range(hidden_units)],
        [(1, unit), (1, unit), (2, unit), (2, unit), (None, unit), (None, unit), (None, hidden), (None, hidden)],
        slots, unit, {}, "early_slots", (partial_own,),
    )
    *received, text_received, sum_up_a = lax.optimization_barrier((*received, text_received, sum_up_a))
    text_grad = text_mine + text_received.astype(WIDE)
    input_grad, sum_self_a, sum_self_b, sum_cross_a, sum_cross_b = last_norm(
        meta, x, partial_own, received, grad_one, gain_one,
        late_all,
        [(0, 0, 0), (1, 0, 1), (2, 0, 2), (0, 1, 0), (1, 1, 1), (2, 1, 2)]
        + [(5, 2, 1), (6, 2, 2), (5, 3, 1), (6, 3, 2)],
        [(3, unit), (3, unit), (3, unit), (3, unit)],
        slots, unit, {2: sum_query_a, 3: sum_query_b}, (sum_up_a,),
    )
    return (
        output[None],
        input_grad[None],
        text_grad[None],
        sum_self_a,
        sum_self_b,
        sum_cross_a,
        sum_cross_b,
        sum_out_a,
        sum_out_b,
        sum_up_a,
        sum_up_b,
        sum_down_a,
        sum_down_b,
    )


def solution(mesh):
    in_specs = (
        P("dp", "tensor", None),
        P("dp", None, None),
        P("dp", "tensor", None),
        P("dp", None),
        P(),
        P(),
        P(),
        P(None, None, "tensor"),
        P("tensor", None),
        P(None, "tensor"),
        P(None, None, "tensor"),
        P("tensor", None),
        P(None, "tensor"),
        P("tensor", None),
        P(),
        P(None, None, None, "tensor"),
        P(),
        P(None, None, None, "tensor"),
        P(None, None, None, "tensor"),
        P(),
        P(),
        P(None, None, "tensor"),
        P(None, None, "tensor"),
        P(),
    )
    out_specs = (
        P("dp", "tensor", None),
        P("dp", "tensor", None),
        P("dp", None, "tensor"),
        P(None, None, None, "tensor"),
        P(None, None, None, "tensor"),
        P(None, None, None, "tensor"),
        P(None, None, None, "tensor"),
        P(None, None, None, "tensor"),
        P(None, None, None, "tensor"),
        P(None, None, "tensor"),
        P(None, None, "tensor"),
        P(None, None, "tensor"),
        P(None, None, "tensor"),
    )
    layer = on_pair if mesh.shape["tensor"] == 2 else on_device
    return jax.shard_map(
        layer, mesh=mesh, in_specs=in_specs, out_specs=out_specs, check_vma=False
    )
```

```python
import jax
import jax.numpy as jnp
from jax import lax
from jax.experimental import pallas as pl
from jax.experimental.pallas import tpu as pltpu
from jax.sharding import PartitionSpec as P

HEAD_DIM = 64


epsilon = 1e-05


def split_dot(form, wide_part, narrow_part):
    high_part = wide_part.astype(jnp.bfloat16)
    rest_part = (wide_part - high_part.astype(jnp.float32)).astype(jnp.bfloat16)
    first = jnp.einsum(form, high_part, narrow_part, preferred_element_type=jnp.float32)
    return first + jnp.einsum(form, rest_part, narrow_part, preferred_element_type=jnp.float32)


def layer_norm(stream, gain_vec):
    centred = stream - jnp.mean(stream, axis=-1, keepdims=True)
    inverse = lax.rsqrt(jnp.mean(centred * centred, axis=-1, keepdims=True) + epsilon)
    normed = centred * inverse
    return (normed * gain_vec, normed, inverse)


def norm_back(grad_out, gain_vec, normed, inverse):
    grad_norm = grad_out * gain_vec
    mean_grad = jnp.mean(grad_norm, axis=-1, keepdims=True)
    mean_cross = jnp.mean(grad_norm * normed, axis=-1, keepdims=True)
    return inverse * (grad_norm - mean_grad - normed * mean_cross)


def spread_rows(local_rows):
    return lax.all_gather(local_rows.astype(jnp.bfloat16), "tensor", axis=1, tiled=True)


def reduce_grads(partial_sum):
    return lax.psum_scatter(
        partial_sum.astype(jnp.bfloat16), "tensor", scatter_dimension=1, tiled=True
    ).astype(jnp.float32)


def project_rows(act_rows, weight, output_choice, input_choice):
    low_rank = jnp.einsum(
        "ctd,crd->ctr", act_rows, output_choice, preferred_element_type=jnp.float32
    )
    result = jnp.einsum("ctd,de->cte", act_rows, weight, preferred_element_type=jnp.float32)
    result = result + split_dot("ctr,cre->cte", low_rank, input_choice)
    return (result, low_rank)


def project_back(grad_low, act_rows, weight, output_choice, input_choice, low_rank):
    grad_rank = jnp.einsum(
        "cte,cre->ctr", grad_low, input_choice, preferred_element_type=jnp.float32
    )
    grad_rows = jnp.einsum("cte,de->ctd", grad_low, weight, preferred_element_type=jnp.float32)
    grad_rows = grad_rows + split_dot("ctr,crd->ctd", grad_rank, output_choice)
    grad_down = split_dot("ctr,ctd->crd", grad_rank, act_rows)
    grad_up = split_dot("ctr,cte->cre", low_rank, grad_low)
    return (grad_rows, grad_down, grad_up)


def causal_frames(first_row, block_rows, key_count):
    query_at = first_row + jnp.arange(block_rows, dtype=jnp.int32)[:, None]
    key_at = jnp.arange(key_count, dtype=jnp.int32)[None, :]
    return key_at <= query_at


def attention_forward(queries, key_rows, value_rows, causal):
    frames = queries.shape[1]
    key_count = key_rows.shape[1]
    block_rows = min(512, frames)
    score_scale = HEAD_DIM ** (-0.5)
    outputs = []
    log_totals = []
    for first_row in range(0, frames, block_rows):
        key_end = first_row + block_rows if causal else key_count
        query_block = queries[:, first_row : first_row + block_rows]
        scores = (
            jnp.einsum(
                "cbhe,ckhe->chbk",
                query_block,
                key_rows[:, :key_end],
                preferred_element_type=jnp.float32,
            )
            * score_scale
        )
        if causal:
            scores = jnp.where(causal_frames(first_row, block_rows, key_end), scores, -1e30)
        largest = jnp.max(scores, axis=-1, keepdims=True)
        exponent = jnp.exp(scores - largest)
        summed = jnp.sum(exponent, axis=-1, keepdims=True)
        prob_low = (exponent / summed).astype(jnp.bfloat16)
        outputs.append(
            jnp.einsum(
                "chbk,ckhe->cbhe",
                prob_low,
                value_rows[:, :key_end],
                preferred_element_type=jnp.float32,
            )
        )
        log_totals.append(largest + jnp.log(summed))
    return (jnp.concatenate(outputs, axis=1), jnp.concatenate(log_totals, axis=2))


def attention_back(queries, key_rows, value_rows, log_totals, grad_mixed, causal):
    frames = queries.shape[1]
    key_count = key_rows.shape[1]
    block_rows = min(512, frames)
    score_scale = HEAD_DIM ** (-0.5)
    grad_keys = jnp.zeros(key_rows.shape, jnp.float32)
    grad_values = jnp.zeros(value_rows.shape, jnp.float32)
    grad_queries = []
    for first_row in range(0, frames, block_rows):
        key_end = first_row + block_rows if causal else key_count
        key_part = key_rows[:, :key_end]
        value_part = value_rows[:, :key_end]
        query_block = queries[:, first_row : first_row + block_rows]
        grad_block = grad_mixed[:, first_row : first_row + block_rows]
        scores = (
            jnp.einsum("cbhe,ckhe->chbk", query_block, key_part, preferred_element_type=jnp.float32)
            * score_scale
        )
        if causal:
            scores = jnp.where(causal_frames(first_row, block_rows, key_end), scores, -1e30)
        probs = jnp.exp(scores - log_totals[:, :, first_row : first_row + block_rows])
        grad_values = grad_values.at[:, :key_end].add(
            jnp.einsum(
                "chbk,cbhe->ckhe",
                probs.astype(jnp.bfloat16),
                grad_block,
                preferred_element_type=jnp.float32,
            )
        )
        grad_probs = jnp.einsum(
            "cbhe,ckhe->chbk", grad_block, value_part, preferred_element_type=jnp.float32
        )
        inner_sum = jnp.sum(probs * grad_probs, axis=-1, keepdims=True)
        grad_scores = (probs * (grad_probs - inner_sum)).astype(jnp.bfloat16)
        grad_queries.append(
            jnp.einsum("chbk,ckhe->cbhe", grad_scores, key_part, preferred_element_type=jnp.float32)
            * score_scale
        )
        grad_keys = grad_keys.at[:, :key_end].add(
            jnp.einsum(
                "chbk,cbhe->ckhe", grad_scores, query_block, preferred_element_type=jnp.float32
            )
            * score_scale
        )
    return (jnp.concatenate(grad_queries, axis=1), grad_keys, grad_values)


def gelu_exact(pre_act):
    return jax.nn.gelu(pre_act, approximate=False)


def on_device(
    inputs,
    encoder_text_states,
    cotangent,
    clip_adapter_index,
    self_norm_gain,
    cross_norm_gain,
    feed_norm_gain,
    self_query_key_value_weight,
    self_output_weight,
    cross_query_weight,
    cross_key_value_weight,
    cross_output_weight,
    up_weight,
    down_weight,
    self_first_factors,
    self_second_factors,
    cross_first_factors,
    cross_second_factors,
    attention_first_factors,
    attention_second_factors,
    input_first_factors,
    input_second_factors,
    output_first_factors,
    output_second_factors,
):
    adapter_slot_count = input_first_factors.shape[0]
    chooser = (
        clip_adapter_index[:, :, None]
        == jnp.arange(adapter_slot_count, dtype=jnp.int32)[None, None, :]
    ).astype(jnp.bfloat16)
    local_heads = self_output_weight.shape[0] // HEAD_DIM

    def choose_adapter_slot(adapter_slot_table, column_index):
        return jnp.einsum(
            "cn,npq->cpq",
            chooser[:, column_index],
            adapter_slot_table,
            preferred_element_type=jnp.float32,
        ).astype(jnp.bfloat16)

    def slot_grads(grad_pick, column_index):
        return split_dot("cpq,cn->npq", grad_pick, chooser[:, column_index])

    def split_heads(stacked):
        return stacked.reshape(stacked.shape[0], stacked.shape[1], local_heads, HEAD_DIM)

    def join_heads(stacked):
        return stacked.reshape(stacked.shape[0], stacked.shape[1], local_heads * HEAD_DIM)

    def out_forward(mixed_in, inner_layer):
        column_index = 3 + 4 * inner_layer
        input_choice = choose_adapter_slot(attention_second_factors[inner_layer], column_index)
        weight = self_output_weight if inner_layer == 0 else cross_output_weight
        output_choice = choose_adapter_slot(attention_first_factors[inner_layer], column_index)
        partial_out, low_rank = project_rows(mixed_in, weight, output_choice, input_choice)
        branch = lax.psum_scatter(
            partial_out.astype(jnp.bfloat16), "tensor", scatter_dimension=1, tiled=True
        ).astype(jnp.float32)
        kept_data = (mixed_in, weight, output_choice, input_choice, low_rank)
        return (branch, kept_data)

    def out_back(grad_stream, kept_data):
        mixed_in, weight, output_choice, input_choice, low_rank = kept_data
        grad_low = grad_stream.astype(jnp.bfloat16)
        grad_full = lax.all_gather(grad_low, "tensor", axis=1, tiled=True)
        grad_rows, grad_down, grad_up = project_back(
            grad_full, mixed_in, weight, output_choice, input_choice, low_rank
        )
        grad_mixed = grad_rows.astype(jnp.bfloat16)
        return (grad_mixed, grad_down, grad_up)

    stream = inputs.astype(jnp.float32)
    normed_value, normed_one, inverse_one = layer_norm(stream, self_norm_gain)
    rows_one = spread_rows(normed_value)
    self_down_factor = [
        choose_adapter_slot(self_first_factors[slot_number], slot_number)
        for slot_number in range(3)
    ]
    self_up_factor = [
        choose_adapter_slot(self_second_factors[slot_number], slot_number)
        for slot_number in range(3)
    ]
    self_parts = [
        project_rows(
            rows_one,
            self_query_key_value_weight[slot_number],
            self_down_factor[slot_number],
            self_up_factor[slot_number],
        )
        for slot_number in range(3)
    ]
    self_heads = [
        split_heads(self_parts[slot_number][0].astype(jnp.bfloat16)) for slot_number in range(3)
    ]
    mixed_one, totals_one = attention_forward(self_heads[0], self_heads[1], self_heads[2], True)
    mixed_one = join_heads(mixed_one).astype(jnp.bfloat16)
    branch_one, kept_one = out_forward(mixed_one, 0)
    stream_one = stream + branch_one
    normed_value, normed_two, inverse_two = layer_norm(stream_one, cross_norm_gain)
    rows_two = spread_rows(normed_value)
    cross_down_factor = [
        choose_adapter_slot(cross_first_factors[slot_number], 4 + slot_number)
        for slot_number in range(3)
    ]
    cross_up_factor = [
        choose_adapter_slot(cross_second_factors[slot_number], 4 + slot_number)
        for slot_number in range(3)
    ]
    query_full, query_rank = project_rows(
        rows_two, cross_query_weight, cross_down_factor[0], cross_up_factor[0]
    )
    key_full, key_rank = project_rows(
        encoder_text_states, cross_key_value_weight[0], cross_down_factor[1], cross_up_factor[1]
    )
    value_full, value_rank = project_rows(
        encoder_text_states, cross_key_value_weight[1], cross_down_factor[2], cross_up_factor[2]
    )
    query_two = split_heads(query_full.astype(jnp.bfloat16))
    key_two = split_heads(key_full.astype(jnp.bfloat16))
    value_two = split_heads(value_full.astype(jnp.bfloat16))
    mixed_two, totals_two = attention_forward(query_two, key_two, value_two, False)
    mixed_two = join_heads(mixed_two).astype(jnp.bfloat16)
    branch_two, kept_two = out_forward(mixed_two, 1)
    stream_two = stream_one + branch_two
    normed_value, normed_three, inverse_three = layer_norm(stream_two, feed_norm_gain)
    rows_three = spread_rows(normed_value)
    input_second_choice = choose_adapter_slot(input_first_factors, 8)
    input_first_choice = choose_adapter_slot(input_second_factors, 8)
    before, up_rank = project_rows(rows_three, up_weight, input_second_choice, input_first_choice)
    gelu_value, gelu_pull = jax.vjp(gelu_exact, before)
    hidden = gelu_value.astype(jnp.bfloat16)
    output_second_choice = choose_adapter_slot(output_first_factors, 9)
    output_first_choice = choose_adapter_slot(output_second_factors, 9)
    partial_out, down_rank = project_rows(
        hidden, down_weight, output_second_choice, output_first_choice
    )
    branch_three = lax.psum_scatter(
        partial_out.astype(jnp.bfloat16), "tensor", scatter_dimension=1, tiled=True
    ).astype(jnp.float32)
    output = (stream_two + branch_three).astype(jnp.bfloat16)
    grad_full = lax.all_gather(cotangent, "tensor", axis=1, tiled=True)
    grad_hidden, grad_down_a, grad_down_b = project_back(
        grad_full, hidden, down_weight, output_second_choice, output_first_choice, down_rank
    )
    grad_before = gelu_pull(grad_hidden)[0].astype(jnp.bfloat16)
    grad_rows, grad_up_a, grad_up_b = project_back(
        grad_before, rows_three, up_weight, input_second_choice, input_first_choice, up_rank
    )
    grad_stream = cotangent.astype(jnp.float32) + norm_back(
        reduce_grads(grad_rows), feed_norm_gain, normed_three, inverse_three
    )
    grad_mixed, grad_out_a_two, grad_out_b_two = out_back(grad_stream, kept_two)
    grad_query, grad_key, grad_value = attention_back(
        query_two, key_two, value_two, totals_two, split_heads(grad_mixed), False
    )
    grad_query = join_heads(grad_query).astype(jnp.bfloat16)
    grad_key = join_heads(grad_key).astype(jnp.bfloat16)
    grad_value = join_heads(grad_value).astype(jnp.bfloat16)
    grad_rows_query, cross_grad_a_zero, cross_grad_b_zero = project_back(
        grad_query,
        rows_two,
        cross_query_weight,
        cross_down_factor[0],
        cross_up_factor[0],
        query_rank,
    )
    grad_text_key, cross_grad_a_one, cross_grad_b_one = project_back(
        grad_key,
        encoder_text_states,
        cross_key_value_weight[0],
        cross_down_factor[1],
        cross_up_factor[1],
        key_rank,
    )
    grad_text_value, cross_grad_a_two, cross_grad_b_two = project_back(
        grad_value,
        encoder_text_states,
        cross_key_value_weight[1],
        cross_down_factor[2],
        cross_up_factor[2],
        value_rank,
    )
    normed_grad, text_grad = (
        lax.psum_scatter(
            grad_rows_query.astype(jnp.bfloat16), "tensor", scatter_dimension=1, tiled=True
        ).astype(jnp.float32),
        lax.psum_scatter(
            (grad_text_key + grad_text_value).astype(jnp.bfloat16),
            "tensor",
            scatter_dimension=2,
            tiled=True,
        ).astype(jnp.float32),
    )
    grad_stream = grad_stream + norm_back(normed_grad, cross_norm_gain, normed_two, inverse_two)
    grad_mixed, grad_out_a_one, grad_out_b_one = out_back(grad_stream, kept_one)
    grad_query, grad_key, grad_value = attention_back(
        self_heads[0], self_heads[1], self_heads[2], totals_one, split_heads(grad_mixed), True
    )
    self_grads = [
        join_heads(grad_query).astype(jnp.bfloat16),
        join_heads(grad_key).astype(jnp.bfloat16),
        join_heads(grad_value).astype(jnp.bfloat16),
    ]
    self_rows_total = jnp.zeros(rows_one.shape, jnp.float32)
    self_grad_a = []
    self_grad_b = []
    for slot_number in range(3):
        grad_rows, grad_a_part, grad_b_part = project_back(
            self_grads[slot_number],
            rows_one,
            self_query_key_value_weight[slot_number],
            self_down_factor[slot_number],
            self_up_factor[slot_number],
            self_parts[slot_number][1],
        )
        self_rows_total = self_rows_total + grad_rows
        self_grad_a.append(slot_grads(grad_a_part, slot_number))
        self_grad_b.append(slot_grads(grad_b_part, slot_number))
    input_grad = grad_stream + norm_back(
        reduce_grads(self_rows_total), self_norm_gain, normed_one, inverse_one
    )
    sum_self_a = jnp.stack(self_grad_a)
    sum_self_b = jnp.stack(self_grad_b)
    sum_cross_a = jnp.stack(
        [
            slot_grads(cross_grad_a_zero, 4),
            slot_grads(cross_grad_a_one, 5),
            slot_grads(cross_grad_a_two, 6),
        ]
    )
    sum_cross_b = jnp.stack(
        [
            slot_grads(cross_grad_b_zero, 4),
            slot_grads(cross_grad_b_one, 5),
            slot_grads(cross_grad_b_two, 6),
        ]
    )
    sum_out_a = jnp.stack([slot_grads(grad_out_a_one, 3), slot_grads(grad_out_a_two, 7)])
    sum_out_b = jnp.stack([slot_grads(grad_out_b_one, 3), slot_grads(grad_out_b_two, 7)])
    sum_up_a = slot_grads(grad_up_a, 8)
    sum_up_b = slot_grads(grad_up_b, 8)
    sum_down_a = slot_grads(grad_down_a, 9)
    sum_down_b = slot_grads(grad_down_b, 9)
    sum_self_a, sum_cross_a, sum_out_b, sum_up_a, sum_down_b = (
        lax.psum_scatter(
            sum_self_a.astype(jnp.bfloat16), "tensor", scatter_dimension=3, tiled=True
        ).astype(jnp.float32),
        lax.psum_scatter(
            sum_cross_a.astype(jnp.bfloat16), "tensor", scatter_dimension=3, tiled=True
        ).astype(jnp.float32),
        lax.psum_scatter(
            sum_out_b.astype(jnp.bfloat16), "tensor", scatter_dimension=3, tiled=True
        ).astype(jnp.float32),
        lax.psum_scatter(
            sum_up_a.astype(jnp.bfloat16), "tensor", scatter_dimension=2, tiled=True
        ).astype(jnp.float32),
        lax.psum_scatter(
            sum_down_b.astype(jnp.bfloat16), "tensor", scatter_dimension=2, tiled=True
        ).astype(jnp.float32),
    )
    totals = (
        lax.psum(sum_self_a.astype(jnp.bfloat16), "dp").astype(jnp.float32),
        lax.psum(sum_self_b.astype(jnp.bfloat16), "dp").astype(jnp.float32),
        lax.psum(sum_cross_a.astype(jnp.bfloat16), "dp").astype(jnp.float32),
        lax.psum(sum_cross_b.astype(jnp.bfloat16), "dp").astype(jnp.float32),
        lax.psum(sum_out_a.astype(jnp.bfloat16), "dp").astype(jnp.float32),
        lax.psum(sum_out_b.astype(jnp.bfloat16), "dp").astype(jnp.float32),
        lax.psum(sum_up_a.astype(jnp.bfloat16), "dp").astype(jnp.float32),
        lax.psum(sum_up_b.astype(jnp.bfloat16), "dp").astype(jnp.float32),
        lax.psum(sum_down_a.astype(jnp.bfloat16), "dp").astype(jnp.float32),
        lax.psum(sum_down_b.astype(jnp.bfloat16), "dp").astype(jnp.float32),
    )
    return (
        output,
        input_grad,
        text_grad,
        totals[0],
        totals[1],
        totals[2],
        totals[3],
        totals[4],
        totals[5],
        totals[6],
        totals[7],
        totals[8],
        totals[9],
    )


LOW = jnp.bfloat16
WIDE = jnp.float32
VMEM_BYTES = 58 * 1024 * 1024
RANK_UNIT = 16
COST_SCALE = 1


def mm(left, right, left_dim=1, right_dim=0):
    return lax.dot_general(
        left, right, (((left_dim,), (right_dim,)), ((), ())), preferred_element_type=WIDE
    )


def mm_nt(left, right):
    return mm(left, right, 1, 1)


def mm_tn(left, right):
    return mm(left, right, 0, 0)


def low_rank(factor, rows):
    return mm_nt(factor, rows).astype(LOW)


def norm_rows(rows, gain):
    centred = rows - jnp.mean(rows, axis=-1, keepdims=True)
    inverse = lax.rsqrt(jnp.mean(centred * centred, axis=-1, keepdims=True) + epsilon)
    normed = centred * inverse
    return normed * gain, normed, inverse


def lane_halves():
    lane = lax.broadcasted_iota(jnp.int32, (1, 2 * HEAD_DIM), 1)
    return lane < HEAD_DIM


def half_masks():
    left = lane_halves()
    first = jnp.where(left, 1.0, 0.0)
    return first.astype(LOW), (1.0 - first).astype(LOW)


def gelu_parts(pre):
    bell = jnp.exp(-0.5 * pre * pre)
    step = 1.0 / (1.0 + (0.3275911 * 0.7071067811865476) * jnp.abs(pre))
    tail = step * (
        0.5 * 0.254829592
        + step
        * (
            0.5 * -0.284496736
            + step
            * (0.5 * 1.421413741 + step * (0.5 * -1.453152027 + step * (0.5 * 1.061405429)))
        )
    )
    tail = tail * bell
    phi = jnp.where(pre >= 0.0, 1.0 - tail, tail)
    return pre * phi, phi + pre * bell * 0.3989422804014327


def whole(shape, where=None):
    place = (0,) * len(shape) if where is None else where
    return pl.BlockSpec(shape, lambda *_: place, pipeline_mode=pl.Buffered(1))


def call(body, grid, in_specs, out_specs, out_shape, scratch, flops, moved, name, args):
    return pl.pallas_call(
        body,
        grid_spec=pltpu.PrefetchScalarGridSpec(
            num_scalar_prefetch=1,
            grid=grid,
            in_specs=in_specs,
            out_specs=out_specs,
            scratch_shapes=scratch,
        ),
        out_shape=out_shape,
        compiler_params=pltpu.CompilerParams(
            dimension_semantics=("arbitrary",) * len(grid), vmem_limit_bytes=VMEM_BYTES
        ),
        cost_estimate=pl.CostEstimate(
            flops=flops // COST_SCALE, bytes_accessed=moved // COST_SCALE, transcendentals=0
        ),
        name=name,
    )(*args)


def shaped(shape, dtype):
    return jax.ShapeDtypeStruct(shape, dtype)


IN_PLACE = pl.BlockSpec(memory_space=pl.ANY)


def factors_body(_, *refs):
    out_ref = refs[-1]
    first = 0
    for ref in refs[:-1]:
        size = ref.shape[-1]
        out_ref[:, first : first + size] = ref[...]
        first += size


def picked_factors(meta, sources):
    specs = []
    total = 0
    for table, entry, slot in sources:
        if entry is None:
            spec = pl.BlockSpec((None,) + table.shape[1:], lambda t, m, slot=slot: (m[slot], 0, 0))
        else:
            spec = pl.BlockSpec(
                (None, None) + table.shape[2:], lambda t, m, entry=entry, slot=slot: (entry, m[slot], 0, 0)
            )
        specs.append(spec)
        total += table.shape[-1]
    shape = (RANK_UNIT, total)
    return call(
        factors_body, (1,), specs, whole(shape), shaped(shape, LOW), [], 0, 4 * RANK_UNIT * total,
        "picked_factors", (meta,) + tuple(table for table, _, _ in sources),
    )


def share_body(_, parts, down_ref, up_ref, *refs):
    out_ref = refs[-1]
    step = pl.program_id(0)

    @pl.when(step < parts)
    def _():
        out_ref[0] = down_ref[...]

    @pl.when(step >= parts)
    def _():
        out_ref[0] = up_ref[...]


def feed_share(meta, down_weight, up_weight, depth, after):
    hidden, width = down_weight.shape
    parts = hidden // width
    return call(
        lambda m, *refs: share_body(m, parts, *refs),
        (2 * parts,),
        [
            pl.BlockSpec(
                (depth, width), lambda t, m: (m[11] * parts + jnp.minimum(t, parts - 1), 0)
            ),
            pl.BlockSpec((depth, width), lambda t, m: (m[11], jnp.maximum(t - parts, 0))),
        ]
        + [IN_PLACE] * len(after),
        pl.BlockSpec((1, depth, width), lambda t, m: (t, 0, 0)),
        shaped((2 * parts, depth, width), LOW),
        [],
        0,
        8 * parts * depth * width,
        "feed_share",
        (meta, down_weight, up_weight, *after),
    )


def first_norm_body(_, x_ref, gain_ref, out_ref):
    rows, _, _ = norm_rows(x_ref[...].astype(WIDE), gain_ref[...])
    out_ref[...] = rows.astype(LOW)


def first_norm(meta, x, gain):
    frames, width = x.shape
    block = min(256, frames)
    rows = pl.BlockSpec((block, width), lambda t, _: (t, 0))
    return call(
        first_norm_body,
        (frames // block,),
        [rows, whole((1, width))],
        rows,
        shaped(x.shape, LOW),
        [],
        10 * x.size,
        4 * x.size,
        "first_norm",
        (meta, x, gain),
    )


def project_body(_, act_ref, weight_ref, down_ref, up_ref, *refs):
    out_ref, rank_ref = refs[-2:]
    act = act_ref[...]
    rank = low_rank(down_ref[0, 0], act)
    rank_ref[0] = rank
    out_ref[0] = (mm(act, weight_ref[0]) + mm_tn(rank, up_ref[0, 0])).astype(LOW)


def project_heads(meta, act, weights, down, up, slots, skip, name, after=()):
    rows, width = act.shape
    count, _, local = weights.shape
    first_slot = slots
    return call(
        project_body,
        (count,),
        [
            whole((rows, width)),
            pl.BlockSpec((1, width, local), lambda j, m: (j, 0, 0)),
            pl.BlockSpec((1, 1, RANK_UNIT, width), lambda j, m: (j + skip, m[first_slot + j], 0, 0)),
            pl.BlockSpec((1, 1, RANK_UNIT, local), lambda j, m: (j + skip, m[first_slot + j], 0, 0)),
        ]
        + [IN_PLACE] * len(after),
        (
            pl.BlockSpec((1, rows, local), lambda j, m: (j, 0, 0)),
            pl.BlockSpec((1, RANK_UNIT, rows), lambda j, m: (j, 0, 0)),
        ),
        (shaped((count, rows, local), LOW), shaped((count, RANK_UNIT, rows), LOW)),
        [],
        2 * rows * width * local * count,
        2 * (weights.size + act.size + count * rows * local),
        name,
        (meta, act, weights, down, up, *after),
    )


def project_back_body(_, last, grad_ref, weight_ref, down_ref, up_ref, after_ref, out_ref, total_ref):
    step = pl.program_id(0)
    grad = grad_ref[0]
    grad_rank = low_rank(up_ref[0, 0], grad)
    part = mm_nt(grad, weight_ref[0]) + mm_tn(grad_rank, down_ref[0, 0])

    @pl.when(step == 0)
    def _():
        total_ref[...] = part

    @pl.when(step > 0)
    def _():
        total_ref[...] += part

    @pl.when(step == last)
    def _():
        out_ref[...] = total_ref[...].astype(out_ref.dtype)


def project_back_heads(meta, grads, weights, down, up, slots, skip, kind, name, after, part=(0, 1)):
    count, width, local = weights.shape
    which, parts = part
    rows = grads.shape[1] // parts
    return call(
        lambda m, *refs: project_back_body(m, count - 1, *refs),
        (count,),
        [
            pl.BlockSpec((1, rows, local), lambda j, m: (j, which, 0)),
            pl.BlockSpec((1, width, local), lambda j, m: (j, 0, 0)),
            pl.BlockSpec((1, 1, RANK_UNIT, width), lambda j, m: (j + skip, m[slots + j], 0, 0)),
            pl.BlockSpec((1, 1, RANK_UNIT, local), lambda j, m: (j + skip, m[slots + j], 0, 0)),
            IN_PLACE,
        ],
        whole((rows, width)),
        shaped((rows, width), kind),
        [pltpu.VMEM((rows, width), WIDE)],
        2 * rows * width * local * count,
        2 * (weights.size + count * rows * local) + 4 * rows * width,
        name,
        (meta, grads, weights, down, up, after),
    )


def first_grads_body(meta, count, parts, *refs):
    ups = refs[2 * parts : 2 * parts + count]
    mine_ref, theirs_ref, ga, act_scratch, grad_scratch, sems = refs[-6:]
    half = ga.shape[1] // 2
    copies = []
    for part in range(parts):
        pairs = ((refs[parts + part], grad_scratch.at[part]), (refs[part], act_scratch.at[part]))
        copies.append(
            [pltpu.make_async_copy(*pair, sems.at[2 * part + number]) for number, pair in enumerate(pairs)]
        )
        for copy in copies[-1]:
            copy.start()
    for part in range(parts):
        copies[part][0].wait()
        grad_rank = jnp.concatenate(
            [low_rank(ups[j][0, 0], grad_scratch[part, j]) for j in range(count)], axis=0
        )
        copies[part][1].wait()
        product = mm(grad_rank, act_scratch[part])
        if part == 0:
            ga[...] = product
        else:
            ga[...] += product
    side = meta[10]
    for j in range(count):
        rows = slice(RANK_UNIT * j, RANK_UNIT * (j + 1))
        span = slice(j * half, (j + 1) * half)
        mine_ref[:, span] = ga[rows, pl.ds(pl.multiple_of(side * half, 128), half)]
        theirs = ga[rows, pl.ds(pl.multiple_of((1 - side) * half, 128), half)]
        theirs_ref[:, span] = theirs.astype(LOW)


def first_grads(meta, acts, grads, up, slots, name):
    rows, width = acts[0].shape
    count, _, local = grads[0].shape
    parts = len(acts)

    def table(j):
        return pl.BlockSpec(
            (1, 1, RANK_UNIT, local), lambda t, m: (j, m[slots + j], 0, 0), pipeline_mode=pl.Buffered(1)
        )

    shape = (RANK_UNIT, count * width // 2)
    return call(
        lambda m, *refs: first_grads_body(m, count, parts, *refs),
        (1,),
        [IN_PLACE] * (2 * parts) + [table(j) for j in range(count)],
        (whole(shape), whole(shape)),
        (shaped(shape, WIDE), shaped(shape, LOW)),
        [
            pltpu.VMEM((RANK_UNIT * count, width), WIDE),
            pltpu.VMEM((parts, rows, width), LOW),
            pltpu.VMEM((parts, count, rows, local), LOW),
            pltpu.SemaphoreType.DMA((2 * parts,)),
        ],
        4 * parts * rows * (width + local) * RANK_UNIT * count,
        2 * parts * rows * (width + count * local),
        name,
        (meta, *acts, *grads, *([up] * count)),
    )


def second_grads_body(_, parts, *refs):
    out_ref, grad_scratch, sems = refs[-3:]
    count, _, local = refs[parts].shape
    copies = [
        pltpu.make_async_copy(refs[parts + part].at[j], grad_scratch.at[part, j], sems.at[part * count + j])
        for part in range(parts)
        for j in range(count)
    ]
    for j in range(count):
        for part in range(parts):
            copies[part * count + j].start()
    for j in range(count):
        total = None
        for part in range(parts):
            copies[part * count + j].wait()
            product = mm(refs[part][j], grad_scratch[part, j])
            total = product if total is None else total + product
        out_ref[:, j * local : (j + 1) * local] = total.astype(LOW)


def second_grads(meta, ranks, grads, name, after):
    count, rows, local = grads[0].shape
    parts = len(ranks)
    shape = (RANK_UNIT, count * local)
    return call(
        lambda m, *refs: second_grads_body(m, parts, *refs),
        (1,),
        [whole(ranks[0].shape)] * parts + [IN_PLACE] * (parts + 1),
        whole(shape),
        shaped(shape, LOW),
        [pltpu.VMEM((parts, count, rows, local), LOW), pltpu.SemaphoreType.DMA((parts * count,))],
        2 * parts * rows * local * RANK_UNIT * count,
        2 * parts * rows * count * local,
        name,
        (meta, *ranks, *grads, after),
    )


def split_columns(meta, mine_ref, theirs_ref, first, array, skip=0):
    half = array.shape[-1] // 2
    side = meta[10]
    mine_ref[:, first : first + half] = array[:, pl.ds(pl.multiple_of(side * half, 128), half)]
    theirs = array[:, pl.ds(pl.multiple_of((1 - side) * half, 128), half)]
    theirs_ref[:, skip + first : skip + first + half] = theirs.astype(LOW)


def own_columns(mine_ref, theirs_ref, first, array):
    half = array.shape[-1] // 2
    span = slice(first, first + half)
    mine_ref[:, span] = array[:, :half]
    theirs_ref[:, span] = array[:, half:].astype(LOW)


def join(mine, received):
    both = jnp.concatenate(received, axis=1).astype(WIDE)
    width = both.shape[1]
    return (mine + jnp.pad(both, ((0, 0), (0, mine.shape[1] - width)))).astype(LOW)


def clip_names(label_ref):
    clips, rank, width = label_ref.shape
    return label_ref[...].reshape(clips * rank, width).astype(WIDE).T


def slot_take(names, slots, rank):
    source = lax.broadcasted_iota(jnp.int32, names.shape, 1)
    target = (source & (rank - 1)) + rank * names.astype(jnp.int32)
    place = lax.broadcasted_iota(jnp.int32, (slots * rank, names.shape[1]), 0)
    return jnp.where(place == target, 1.0, 0.0).astype(LOW)


def slot_copies(unit, count, everyone_ref, arrived, in_sems):
    return [
        pltpu.make_async_copy(
            everyone_ref.at[:, :, pl.ds(unit * number, unit)], arrived.at[number], in_sems.at[number]
        )
        for number in range(count)
    ]


def slot_work(plan, slots, carried, everyone_ref, label_ref, earlier, out_refs, scratch):
    names, arrived, totals, in_sems, out_sems = scratch
    clips, rank, unit = arrived.shape[1:]
    incoming = slot_copies(unit, len(plan), everyone_ref, arrived, in_sems)
    names[...] = clip_names(label_ref)
    outgoing = []
    for number, (which, ref) in enumerate(zip(carried, earlier)):
        copy = pltpu.make_async_copy(ref.at[0], out_refs[which].at[0], out_sems.at[len(plan) + number])
        copy.start()
        outgoing.append(copy)
    for number, (column, which, place) in enumerate(plan):
        incoming[number].wait()
        take = slot_take(names[column : column + 1], slots, rank)
        total = mm(take, arrived[number].reshape(clips * rank, unit))
        totals[number] = total.reshape(slots, rank, unit)
        out_ref = out_refs[which]
        target = out_ref.at[place] if len(out_ref.shape) == 4 else out_ref.at[:, :, pl.ds(unit * place, unit)]
        copy = pltpu.make_async_copy(totals.at[number], target, out_sems.at[number])
        copy.start()
        outgoing.append(copy)
    for copy in outgoing:
        copy.wait()


def slot_scratch(everyone, plan, slots, unit, carried):
    clips, rank, _ = everyone.shape
    units = len(plan)
    return [
        pltpu.VMEM((2 * HEAD_DIM, clips * rank), WIDE),
        pltpu.VMEM((units, clips, rank, unit), LOW),
        pltpu.VMEM((units, slots, rank, unit), WIDE),
        pltpu.SemaphoreType.DMA((units,)),
        pltpu.SemaphoreType.DMA((units + len(carried),)),
    ]


def slot_specs(labelled, carried):
    clips, rank, total = labelled.shape
    label_width = 2 * HEAD_DIM
    return [IN_PLACE, whole((clips, rank, label_width), (0, 0, total // label_width - 1))] + [
        whole(array.shape) for array in carried.values()
    ]


def slot_shapes(everyone, outs, slots):
    rank = everyone.shape[1]
    return tuple(
        shaped((slots, rank, width) if stack is None else (stack, slots, rank, width), WIDE)
        for stack, width in outs
    )


def slot_sum_body(_, plan, slots, carried, outs, everyone_ref, label_ref, *refs):
    scratch = refs[-5:]
    for copy in slot_copies(scratch[1].shape[3], len(plan), everyone_ref, scratch[1], scratch[3]):
        copy.start()
    slot_work(
        plan, slots, carried, everyone_ref, label_ref, refs[: len(carried)], refs[-5 - outs : -5], scratch
    )


def slot_sums(meta, everyone, plan, outs, slots, unit, carried, name, after):
    return call(
        lambda m, *refs: slot_sum_body(m, plan, slots, tuple(carried), len(outs), *refs),
        (1,),
        slot_specs(everyone, carried) + [IN_PLACE] * len(after),
        (IN_PLACE,) * len(outs),
        slot_shapes(everyone, outs, slots),
        slot_scratch(everyone, plan, slots, unit, carried),
        0,
        2 * everyone.size,
        name,
        (meta, everyone, everyone, *carried.values(), *after),
    )


def causal_keep(rows):
    key_at = lax.broadcasted_iota(jnp.int32, (rows, rows), 0)
    return key_at <= lax.broadcasted_iota(jnp.int32, (rows, rows), 1)


def turned(rows):
    return rows.astype(WIDE).T.astype(LOW)


def forward_block(query, keys, value_turned, diagonal, earlier=None):
    score = mm_nt(keys, query)
    if diagonal:
        score = jnp.where(causal_keep(score.shape[0]), score, -1e30)
    largest = jnp.max(score, axis=0, keepdims=True)
    if earlier is not None:
        largest = jnp.maximum(largest, earlier[0])
    mixed = mm(value_turned, jnp.exp(score - largest).astype(LOW))
    if earlier is not None:
        mixed = mixed + earlier[1] * jnp.exp(earlier[0] - largest)
    return largest, mixed


def values_of(rows_ref):
    values = turned(rows_ref[2])
    ones = jnp.ones((RANK_UNIT, values.shape[1]), LOW)
    return [
        jnp.concatenate([values[HEAD_DIM * which : HEAD_DIM * (which + 1)], ones], axis=0)
        for which in (0, 1)
    ]


def forward_finish(blocks, out_ref, log_ref):
    mixes = []
    totals = []
    for largest, mixed in blocks:
        summed = mixed[HEAD_DIM : HEAD_DIM + 1]
        mixes.append(mixed[:HEAD_DIM] * (1.0 / summed))
        totals.append(jnp.broadcast_to(jnp.log(summed) + largest, (HEAD_DIM, summed.shape[1])))
    out_ref[...] = jnp.concatenate(mixes, axis=0).T.astype(LOW)
    log_ref[...] = jnp.concatenate(totals, axis=0).T


MIXED_ROWS = HEAD_DIM + RANK_UNIT
PART_ROWS = MIXED_ROWS + 8


def self_forward_own_body(_, own_ref, part_ref):
    masks = half_masks()
    query = own_ref[0] * jnp.asarray(HEAD_DIM**-0.5, LOW)
    values = values_of(own_ref)
    for which in (0, 1):
        largest, mixed = forward_block(query * masks[which], own_ref[1], values[which], True)
        part_ref[0, which, :MIXED_ROWS] = mixed
        part_ref[0, which, MIXED_ROWS:] = jnp.broadcast_to(largest, (8, largest.shape[1]))


def self_forward_own(meta, own, after):
    _, half, local = own.shape
    pair = 2 * HEAD_DIM
    shape = (local // pair, 2, PART_ROWS, half)
    return call(
        lambda m, own_ref, after_ref, part_ref: self_forward_own_body(m, own_ref, part_ref),
        (local // pair,),
        [pl.BlockSpec((3, half, pair), lambda p, m: (0, 0, p)), IN_PLACE],
        pl.BlockSpec((1,) + shape[1:], lambda p, m: (p, 0, 0, 0)),
        shaped(shape, WIDE),
        [],
        4 * half * half * local,
        10 * half * local,
        "self_forward_own",
        (meta, own, after),
    )


def self_forward_body(
    meta, part_ref, own_ref, other_ref, out_own_ref, out_other_ref, log_own_ref, log_other_ref, keys, values, queries
):
    side = meta[10]
    masks = half_masks()
    for slot, ref in ((0, own_ref), (1, other_ref)):
        keys[slot] = ref[1]
        queries[slot] = ref[0] * jnp.asarray(HEAD_DIM**-0.5, LOW)
        for which, value in enumerate(values_of(ref)):
            values[slot, which] = value
    blocks = []
    for which in (0, 1):
        own = (part_ref[0, which, MIXED_ROWS : MIXED_ROWS + 1], part_ref[0, which, :MIXED_ROWS])
        other = forward_block(queries[1] * masks[which], keys[1], values[1, which], True)
        earlier = (jnp.where(side == 0, other[0], own[0]), jnp.where(side == 0, other[1], own[1]))
        later = forward_block(
            queries[1 - side] * masks[which], keys[side], values[side, which], False, earlier
        )
        blocks.append(
            (
                (jnp.where(side == 0, own[0], later[0]), jnp.where(side == 0, own[1], later[1])),
                (jnp.where(side == 0, later[0], other[0]), jnp.where(side == 0, later[1], other[1])),
            )
        )
    forward_finish([blocks[0][0], blocks[1][0]], out_own_ref, log_own_ref)
    forward_finish([blocks[0][1], blocks[1][1]], out_other_ref, log_other_ref)


def self_forward(meta, part, own, other):
    _, half, local = own.shape
    pair = 2 * HEAD_DIM
    three = pl.BlockSpec((3, half, pair), lambda p, m: (0, 0, p))
    one = pl.BlockSpec((half, pair), lambda p, m: (0, p))
    rows = shaped((half, local), LOW)
    logs = shaped((half, local), WIDE)
    return call(
        self_forward_body,
        (local // pair,),
        [pl.BlockSpec((1,) + part.shape[1:], lambda p, m: (p, 0, 0, 0)), three, three],
        (one, one, one, one),
        (rows, rows, logs, logs),
        [
            pltpu.VMEM((2, half, pair), LOW),
            pltpu.VMEM((2, 2, MIXED_ROWS, half), LOW),
            pltpu.VMEM((2, half, pair), LOW),
        ],
        12 * half * half * local,
        20 * half * local,
        "self_forward",
        (meta, part, own, other),
    )


def three_parts(column):
    high = column.astype(LOW)
    rest = column - high.astype(WIDE)
    middle = rest.astype(LOW)
    return high, middle, (rest - middle.astype(WIDE)).astype(LOW)


def back_prepare_keys(slot, rows_ref, scratch):
    key_turned, _, _, _, key_wide, _, value_wide = scratch
    lane = lax.broadcasted_iota(jnp.int32, (1, 2 * HEAD_DIM), 1)
    key_turned[slot] = turned(rows_ref[1])
    for which in (0, 1):
        spare = HEAD_DIM * (1 - which)
        marked = jnp.where((lane >= spare) & (lane < spare + 3), 1.0, 0.0).astype(LOW)
        key_wide[slot, which] = rows_ref[1] * (1 - marked) + marked
        value_wide[slot, which] = rows_ref[2] * (1 - marked) + marked


def back_prepare_queries(slot, rows_ref, mixed_ref, logs_ref, grad_refs, scratch):
    _, query_turned, grad_turned, query_wide, _, grad_wide, _ = scratch
    masks = half_masks()
    lane = lax.broadcasted_iota(jnp.int32, (1, 2 * HEAD_DIM), 1)
    grad = jnp.concatenate([ref[...] for ref in grad_refs], axis=0)
    product = grad.astype(WIDE) * mixed_ref[...].astype(WIDE)
    query = rows_ref[0] * jnp.asarray(HEAD_DIM**-0.5, LOW)
    logs = logs_ref[...]
    query_turned[slot] = turned(query)
    grad_turned[slot] = turned(grad)
    for which in (0, 1):
        spare = HEAD_DIM * (1 - which)
        marks = [jnp.where(lane == spare + i, 1.0, 0.0).astype(LOW) for i in range(3)]
        inner = jnp.sum(product * masks[which].astype(WIDE), axis=-1, keepdims=True)
        query_rows = query * masks[which]
        for part, mark in zip(three_parts(logs[:, HEAD_DIM * which : HEAD_DIM * which + 1]), marks):
            query_rows = query_rows - part * mark
        query_wide[slot, which] = query_rows
        grad_rows = grad * masks[which]
        for part, mark in zip(three_parts(inner), marks):
            grad_rows = grad_rows - part * mark
        grad_wide[slot, which] = grad_rows


def back_block(queries, query_slot, keys, key_slot, diagonal, totals):
    _, query_turned, grad_turned, query_wide, _, grad_wide, _ = queries
    key_turned, _, _, _, key_wide, _, value_wide = keys
    half = key_turned.shape[2]
    for which in (0, 1):
        head = slice(HEAD_DIM * which, HEAD_DIM * (which + 1))
        score = mm_nt(key_wide[0, which], query_wide[0, which])
        if diagonal:
            score = jnp.where(causal_keep(half), score, -1e30)
        prob = jnp.exp(score)
        prob_grad = mm_nt(value_wide[0, which], grad_wide[0, which])
        score_grad = (prob * prob_grad).astype(LOW)
        totals[2, key_slot, head] += mm_nt(grad_turned[0, head], prob.astype(LOW))
        totals[1, key_slot, head] += mm_nt(query_turned[0, head], score_grad)
        totals[0, query_slot, head] += mm(key_turned[0, head], score_grad)


def self_back_own_body(_, own_ref, z_ref, log_ref, grad_ref, out_ref, *refs):
    prepared = refs[:-1]
    totals = refs[-1]
    totals[...] = jnp.zeros_like(totals)
    back_prepare_keys(0, own_ref, prepared)
    back_prepare_queries(0, own_ref, z_ref, log_ref, (grad_ref,), prepared)
    back_block(prepared, 0, prepared, 0, True, totals)
    out_ref[...] = totals[:, 0]


def prepared_specs(half):
    pair = 2 * HEAD_DIM
    return (pl.BlockSpec((1, pair, half), lambda p, m: (0, p, 0)),) * 3 + (
        pl.BlockSpec((1, 2, half, pair), lambda p, m: (0, 0, 0, p)),
    ) * 4


def self_back_own(meta, own, z_own, log_own, grad_own):
    _, half, local = own.shape
    pair = 2 * HEAD_DIM
    three = pl.BlockSpec((3, half, pair), lambda p, m: (0, 0, p))
    one = pl.BlockSpec((half, pair), lambda p, m: (0, p))
    return call(
        self_back_own_body,
        (local // pair,),
        [three, one, one, one],
        (pl.BlockSpec((3, pair, half), lambda p, m: (0, p, 0)),) + prepared_specs(half),
        (shaped((3, local, half), WIDE),)
        + (shaped((1, local, half), LOW),) * 3
        + (shaped((1, 2, half, local), LOW),) * 4,
        [pltpu.VMEM((3, 1, pair, half), WIDE)],
        100 * half * half * local,
        50 * half * local,
        "self_back_own",
        (meta, own, z_own, log_own, grad_own),
    )


def self_back_body(
    meta,
    part_ref,
    *refs,
):
    own = refs[:7]
    other_ref, z_ref, log_ref, grad_first_ref, grad_second_ref, _, out_own_ref, out_other_ref = refs[7:15]
    other = refs[15:22]
    totals = refs[22]
    side = meta[10]
    totals[:, 0] = part_ref[...]
    totals[:, 1] = jnp.zeros_like(totals[:, 1])
    back_prepare_keys(0, other_ref, other)
    back_prepare_queries(0, other_ref, z_ref, log_ref, (grad_first_ref, grad_second_ref), other)
    back_block(other, 1, other, 1, True, totals)

    @pl.when(side == 0)
    def _():
        back_block(other, 1, own, 0, False, totals)

    @pl.when(side != 0)
    def _():
        back_block(own, 0, other, 1, False, totals)

    for slot, ref in ((0, out_own_ref), (1, out_other_ref)):
        ref[0] = (totals[0, slot].T * HEAD_DIM**-0.5).astype(LOW)
        ref[1] = totals[1, slot].T.astype(LOW)
        ref[2] = totals[2, slot].T.astype(LOW)


def self_back(meta, part, prepared, other, z_other, log_other, grads_other, after):
    _, half, local = other.shape
    pair = 2 * HEAD_DIM
    three = pl.BlockSpec((3, half, pair), lambda p, m: (0, 0, p))
    one = pl.BlockSpec((half, pair), lambda p, m: (0, p))
    return call(
        self_back_body,
        (local // pair,),
        [pl.BlockSpec((3, pair, half), lambda p, m: (0, p, 0)), *prepared_specs(half), three, one, one]
        + [pl.BlockSpec((half // 2, pair), lambda p, m: (0, p))] * 2
        + [IN_PLACE],
        (three, three),
        (shaped(other.shape, LOW), shaped(other.shape, LOW)),
        [pltpu.VMEM((1, pair, half), LOW)] * 3
        + [pltpu.VMEM((1, 2, half, pair), LOW)] * 4
        + [pltpu.VMEM((3, 2, pair, half), WIDE)],
        200 * half * half * local,
        60 * half * local,
        "self_back",
        (meta, part, *prepared, other, z_other, log_other, *grads_other, after),
    )


def halves_of(ref, local):
    step = ref.shape[1] // 2
    return (
        ref[:, :step, :].reshape(local, ref.shape[2]),
        ref[:, step:, :].reshape(local, ref.shape[2]),
    )


def full_of(ref):
    return ref[...].reshape(ref.shape[0] * ref.shape[1], ref.shape[2])


def fetch_weights(step, order, sources, gathered, held, sems, between=()):
    copies = {}
    for which in order:
        copies[which] = (
            pltpu.make_async_copy(sources[which], held[2 * which], sems.at[2 * which]),
            pltpu.make_async_copy(gathered.at[:, which], held[2 * which + 1], sems.at[2 * which + 1]),
        )

    @pl.when(step == 0)
    def _():
        for place, which in enumerate(order):
            for copy in copies[which]:
                copy.start()
            for copy in between[place] if between else ():
                copy.start()

    def ready(which):
        @pl.when(step == 0)
        def _():
            for copy in copies[which]:
                copy.wait()

        return held[2 * which], held[2 * which + 1]

    return ready


TILE_HEADS = 4


def tile_span(tile):
    return slice(TILE_HEADS * HEAD_DIM * tile, TILE_HEADS * HEAD_DIM * (tile + 1))


def tile_masks():
    lane = lax.broadcasted_iota(jnp.int32, (1, TILE_HEADS * HEAD_DIM), 1)
    return [jnp.where(lane // HEAD_DIM == head, 1.0, 0.0).astype(LOW) for head in range(TILE_HEADS)]


def text_tile(rows, tile, masks):
    part = rows[:, tile_span(tile)]
    return jnp.concatenate([part * mask for mask in masks], axis=0)


def by_head(values, reduce):
    keys, rows = values.shape
    apart = values.reshape(TILE_HEADS, keys // TILE_HEADS, rows)
    reduced = reduce(apart, axis=1, keepdims=True)
    return jnp.broadcast_to(reduced, apart.shape).reshape(keys, rows)


def text_weights(key_tile, query):
    scores = mm_nt(key_tile, query)
    weights = jnp.exp(scores - by_head(scores, jnp.max))
    return weights * (1.0 / by_head(weights, jnp.sum))


def mix_text(query, keys, values):
    masks = tile_masks()
    mixed = []
    for tile in range(query.shape[1] // (TILE_HEADS * HEAD_DIM)):
        one_query = query[:, tile_span(tile)] * jnp.asarray(HEAD_DIM**-0.5, LOW)
        weights = text_weights(text_tile(keys, tile, masks), one_query)
        mixed.append(mm_tn(weights.astype(LOW), text_tile(values, tile, masks)).astype(LOW))
    return jnp.concatenate(mixed, axis=1)


def middle_forward_body(
    _,
    x_ref,
    z_own_ref,
    z_other_ref,
    out_weight_ref,
    query_weight_ref,
    cross_weight_ref,
    gathered_ref,
    down3_ref,
    down3_other_ref,
    up3_ref,
    down4_ref,
    up4_ref,
    up4_other_ref,
    down7_ref,
    down7_other_ref,
    up7_ref,
    text_own_ref,
    text_other_ref,
    gain_two_ref,
    gain_three_ref,
    stream_one_ref,
    stream_two_ref,
    rows_three_ref,
    query_out_own_ref,
    query_out_other_ref,
    z2_own_ref,
    z2_other_ref,
    rank3_ref,
    rank4_ref,
    rank7_ref,
    *scratch,
):
    local = z_own_ref.shape[1]
    ready = fetch_weights(
        pl.program_id(0),
        (0, 1, 2),
        (out_weight_ref, query_weight_ref, cross_weight_ref),
        gathered_ref,
        scratch[:6],
        scratch[6],
    )

    def out_product(own, other, which, down, down_other, up, rank_ref):
        rank = (mm_nt(down, own) + mm_nt(down_other, other)).astype(LOW)
        rank_ref[...] = rank
        weight_own, weight_other_ref = ready(which)
        first, second = halves_of(weight_other_ref, local)
        product = mm(own, weight_own[...]) + mm_tn(rank, up)
        return product + jnp.concatenate([mm(other, first), mm(other, second)], axis=1)

    stream = x_ref[...].astype(WIDE) + out_product(
        z_own_ref[...],
        z_other_ref[...],
        0,
        down3_ref[0, 0],
        down3_other_ref[...],
        up3_ref[0, 0],
        rank3_ref,
    )
    stream_one_ref[...] = stream
    rows_two = norm_rows(stream, gain_two_ref[...])[0].astype(LOW)
    rank = low_rank(down4_ref[0, 0], rows_two)
    rank4_ref[...] = rank
    query_own_ref, query_other_ref = ready(1)
    query_own = (mm(rows_two, query_own_ref[...]) + mm_tn(rank, up4_ref[0, 0])).astype(LOW)
    query_other = (
        mm(rows_two, full_of(query_other_ref)) + mm_tn(rank, up4_other_ref[...])
    ).astype(LOW)
    query_out_own_ref[...] = query_own
    query_out_other_ref[...] = query_other
    z2_own = mix_text(query_own, text_own_ref[0], text_own_ref[1])
    z2_other = mix_text(query_other, text_other_ref[0], text_other_ref[1])
    z2_own_ref[...] = z2_own
    z2_other_ref[...] = z2_other
    stream = stream + out_product(
        z2_own,
        z2_other,
        2,
        down7_ref[0, 0],
        down7_other_ref[...],
        up7_ref[0, 0],
        rank7_ref,
    )
    stream_two_ref[...] = stream
    rows_three_ref[...] = norm_rows(stream, gain_three_ref[...])[0].astype(LOW)


def chosen(table, entry, slot):
    shape = (1, 1) + table.shape[2:]
    return pl.BlockSpec(
        shape, lambda t, m: (entry, m[slot], 0, 0), pipeline_mode=pl.Buffered(1)
    )


def middle_specs(weights, gathered, tables, packed):
    attention_down, attention_up, cross_down, cross_up = tables
    rank = (RANK_UNIT, gathered.shape[3])
    specs = [
        IN_PLACE,
        IN_PLACE,
        IN_PLACE,
        IN_PLACE,
        chosen(attention_down, 0, 3),
        whole(rank, (0, 0)),
        chosen(attention_up, 0, 3),
        chosen(cross_down, 0, 4),
        chosen(cross_up, 0, 4),
        whole(rank, (0, 2)),
        chosen(attention_down, 1, 7),
        whole(rank, (0, 1)),
        chosen(attention_up, 1, 7),
    ]
    args = weights + (
        gathered,
        attention_down,
        packed,
        attention_up,
        cross_down,
        cross_up,
        packed,
        attention_down,
        packed,
        attention_up,
    )
    return specs, args


def middle_scratch(weights, gathered):
    shards, _, depth, local = gathered.shape
    held = []
    for weight in weights:
        held += [pltpu.VMEM(weight.shape, LOW), pltpu.VMEM((shards, depth, local), LOW)]
    return held + [pltpu.SemaphoreType.DMA((2 * len(weights),))]


def middle_forward(meta, x, z_own, z_other, weights, gathered, tables, packed, text_own, text_other, gains):
    frames, width = x.shape
    local = z_own.shape[1]
    block = min(512, frames)
    wide = pl.BlockSpec((block, width), lambda t, m: (t, 0))
    narrow = pl.BlockSpec((block, local), lambda t, m: (t, 0))
    ranks = pl.BlockSpec((RANK_UNIT, block), lambda t, m: (0, t))
    specs, args = middle_specs(weights, gathered, tables, packed)
    return call(
        middle_forward_body,
        (frames // block,),
        [wide, narrow, narrow]
        + specs
        + [whole(text_own.shape), whole(text_other.shape), whole((1, width)), whole((1, width))],
        (wide, wide, wide, narrow, narrow, narrow, narrow) + (ranks,) * 3,
        (
            shaped((frames, width), WIDE),
            shaped((frames, width), WIDE),
            shaped((frames, width), LOW),
            shaped((frames, local), LOW),
            shaped((frames, local), LOW),
            shaped((frames, local), LOW),
            shaped((frames, local), LOW),
        )
        + (shaped((RANK_UNIT, frames), LOW),) * 3,
        middle_scratch(weights, gathered),
        6 * frames * width * width,
        6 * width * width + 20 * frames * width,
        "middle_forward",
        (meta, x, z_own, z_other) + args + (text_own, text_other) + gains,
    )


def middle_back_body(
    meta,
    last,
    grad_ref,
    stream_one_ref,
    z_own_ref,
    z_other_ref,
    query_in_own_ref,
    query_in_other_ref,
    z2_own_ref,
    z2_other_ref,
    out_weight_ref,
    query_weight_ref,
    cross_weight_ref,
    gathered_ref,
    down3_ref,
    down3_other_ref,
    up3_ref,
    down4_ref,
    up4_ref,
    up4_other_ref,
    down7_ref,
    down7_other_ref,
    up7_ref,
    text_own_ref,
    text_other_ref,
    gain_two_ref,
    text_ref,
    down5_ref,
    down6_ref,
    up5_ref,
    up6_ref,
    up5_other_ref,
    up6_other_ref,
    rank3_ref,
    rank4_ref,
    rank7_ref,
    grad_one_ref,
    dz_own_ref,
    dz_first_ref,
    dz_second_ref,
    text_grad_own_ref,
    mine_ref,
    theirs_ref,
    text_mine_ref,
    text_theirs_ref,
    key_total,
    value_total,
    ga3_ref,
    gb3_ref,
    ga4_ref,
    gb4_ref,
    ga7_ref,
    gb7_ref,
    *scratch,
):
    step = pl.program_id(0)
    late = scratch[7:12]
    late_sems = scratch[13]
    late_copies = [
        pltpu.make_async_copy(source, target, late_sems.at[number])
        for number, (source, target) in enumerate(
            zip((query_in_own_ref, query_in_other_ref, stream_one_ref, z_own_ref, z_other_ref), late)
        )
    ]
    query_in_own_ref, query_in_other_ref, stream_one_ref, z_own_ref, z_other_ref = late
    grad_one_copy = pltpu.make_async_copy(scratch[12], grad_one_ref, late_sems.at[5])
    ready = fetch_weights(
        step,
        (2, 1, 0),
        (out_weight_ref, query_weight_ref, cross_weight_ref),
        gathered_ref,
        scratch[:6],
        scratch[6],
        (late_copies[:2], late_copies[2:], ()),
    )
    local = z_own_ref.shape[1]
    tiles = local // (TILE_HEADS * HEAD_DIM)
    masks = tile_masks()
    scale = jnp.asarray(HEAD_DIM**-0.5, LOW)

    @pl.when(step == 0)
    def _():
        key_total[...] = jnp.zeros_like(key_total)
        value_total[...] = jnp.zeros_like(value_total)
        for ref in (ga3_ref, gb3_ref, ga4_ref, gb4_ref, ga7_ref, gb7_ref):
            ref[...] = jnp.zeros_like(ref)

    def out_back(grad, own, other, which, down, down_other, up, ga_ref, gb_ref, rank):
        grad_rank = low_rank(up, grad)
        ga_ref[:, :local] += mm(grad_rank, own)
        ga_ref[:, local:] += mm(grad_rank, other)
        gb_ref[...] += mm(rank, grad)
        weight_own, weight_other_ref = ready(which)
        first, second = halves_of(weight_other_ref, local)
        middle = grad.shape[1] // 2
        grad_own = mm_nt(grad, weight_own[...]) + mm_tn(grad_rank, down)
        grad_other = (
            mm_nt(grad[:, :middle], first)
            + mm_nt(grad[:, middle:], second)
            + mm_tn(grad_rank, down_other)
        )
        return grad_own.astype(LOW), grad_other.astype(LOW)

    grad = grad_ref[...]
    dz2_own, dz2_other = out_back(
        grad.astype(LOW),
        z2_own_ref[...],
        z2_other_ref[...],
        2,
        down7_ref[0, 0],
        down7_other_ref[...],
        up7_ref[0, 0],
        ga7_ref,
        gb7_ref,
        rank7_ref[...],
    )

    def text_back(query, dz2, keys, values, part):
        query_grads = []
        for tile in range(tiles):
            key_tile = text_tile(keys, tile, masks)
            value_tile = text_tile(values, tile, masks)
            one_query = query[:, tile_span(tile)] * scale
            one_grad = dz2[:, tile_span(tile)]
            probs = text_weights(key_tile, one_query)
            prob_grads = mm_nt(value_tile, one_grad)
            inner = by_head(probs * prob_grads, jnp.sum)
            score_grads = (probs * (prob_grads - inner)).astype(LOW)
            query_grads.append((mm_tn(score_grads, key_tile) * HEAD_DIM**-0.5).astype(LOW))
            key_total[part, tile] += mm(score_grads, one_query)
            value_total[part, tile] += mm(probs.astype(LOW), one_grad)
        return jnp.concatenate(query_grads, axis=1)

    for copy in late_copies[:2]:
        copy.wait()
    dq_own = text_back(query_in_own_ref[...], dz2_own, text_own_ref[0], text_own_ref[1], 0)
    dq_other = text_back(query_in_other_ref[...], dz2_other, text_other_ref[0], text_other_ref[1], 1)

    for copy in late_copies[2:]:
        copy.wait()
    rows_two, normed, inverse = norm_rows(stream_one_ref[...], gain_two_ref[...])
    rows_two = rows_two.astype(LOW)
    rank = rank4_ref[...]
    grad_rank = (mm_nt(up4_ref[0, 0], dq_own) + mm_nt(up4_other_ref[...], dq_other)).astype(LOW)
    ga4_ref[...] += mm(grad_rank, rows_two)
    gb4_ref[:, :local] += mm(rank, dq_own)
    gb4_ref[:, local:] += mm(rank, dq_other)
    query_own_ref, query_other_ref = ready(1)
    grad_rows = (
        mm_nt(dq_own, query_own_ref[...])
        + mm_nt(dq_other, full_of(query_other_ref))
        + mm_tn(grad_rank, down4_ref[0, 0])
    )
    grad = grad + norm_back(grad_rows, gain_two_ref[...], normed, inverse)
    scratch[12][...] = grad
    grad_one_copy.start()
    dz_own, dz_other = out_back(
        grad.astype(LOW),
        z_own_ref[...],
        z_other_ref[...],
        0,
        down3_ref[0, 0],
        down3_other_ref[...],
        up3_ref[0, 0],
        ga3_ref,
        gb3_ref,
        rank3_ref[...],
    )
    dz_own_ref[...] = dz_own
    half = dz_first_ref.shape[0]
    dz_first_ref[...] = dz_other[:half]
    dz_second_ref[...] = dz_other[half:]
    grad_one_copy.wait()

    @pl.when(step == last)
    def _():
        split_columns(meta, mine_ref, theirs_ref, 0, ga4_ref)
        own_columns(mine_ref, theirs_ref, local, gb4_ref)
        own_columns(mine_ref, theirs_ref, 2 * local, ga3_ref)
        own_columns(mine_ref, theirs_ref, 3 * local, ga7_ref)
        split_columns(meta, mine_ref, theirs_ref, 4 * local, gb3_ref)
        split_columns(meta, mine_ref, theirs_ref, 5 * local, gb7_ref)
        texts = text_ref.shape[0]
        for slot, total in enumerate((key_total, value_total)):
            for part in (0, 1):
                for tile in range(tiles):
                    stacked = total[part, tile]
                    rows = 0.0
                    for head, mask in enumerate(masks):
                        rows = rows + stacked[HEAD_DIM * head : HEAD_DIM * (head + 1)] * mask.astype(WIDE)
                    if part == 0:
                        text_grad_own_ref[slot, :, tile_span(tile)] = rows
                    else:
                        text_theirs_ref[texts * slot : texts * (slot + 1), tile_span(tile)] = rows.astype(LOW)
        text = text_ref[...]
        factors = ((down5_ref, up5_ref, up5_other_ref), (down6_ref, up6_ref, up6_other_ref))
        for slot, (down_ref, up_ref, up_other_ref) in enumerate(factors):
            grad_own = text_grad_own_ref[slot].astype(LOW)
            grad_other = text_theirs_ref[texts * slot : texts * (slot + 1)]
            rank = low_rank(down_ref[0, 0], text)
            grad_rank = mm_nt(up_ref[0, 0], grad_own) + mm_nt(up_other_ref[...], grad_other)
            ga4_ref[...] = mm(grad_rank.astype(LOW), text)
            first = slice(2 * texts + RANK_UNIT * slot, 2 * texts + RANK_UNIT * (slot + 1))
            second = slice(2 * texts + RANK_UNIT * (2 + slot), 2 * texts + RANK_UNIT * (3 + slot))
            split_columns(meta, text_mine_ref.at[:, pl.ds(slot * local, local)], text_theirs_ref.at[first], 0, ga4_ref)
            text_mine_ref[:, (2 + slot) * local : (3 + slot) * local] = mm(rank, grad_own)
            text_theirs_ref[second] = mm(rank, grad_other).astype(LOW)


def middle_back(
    meta, grad, stream_one, z_own, z_other, q_own, q_other, z2_own, z2_other,
    weights, gathered, tables, packed, text_own, text_other, gain, text, ranks,
):
    frames, width = grad.shape
    local = z_own.shape[1]
    tiles = local // (TILE_HEADS * HEAD_DIM)
    wide = whole((frames, width))
    narrow = whole((frames, local))
    specs, args = middle_specs(weights, gathered, tables, packed)
    rank = (RANK_UNIT, width)
    packs = (RANK_UNIT, 6 * local)
    text_packs = (RANK_UNIT, 4 * local)
    text_rows = (2 * text.shape[0] + 4 * RANK_UNIT, local)
    _, _, cross_down, cross_up = tables
    return call(
        lambda m, *refs: middle_back_body(m, 0, *refs),
        (1,),
        [wide, IN_PLACE]
        + [IN_PLACE] * 4
        + [narrow] * 2
        + specs
        + [whole(text_own.shape), whole(text_other.shape), whole((1, width)), whole(text.shape)]
        + [chosen(cross_down, 1, 5), chosen(cross_down, 2, 6), chosen(cross_up, 1, 5), chosen(cross_up, 2, 6)]
        + [whole((RANK_UNIT, local), (0, 3)), whole((RANK_UNIT, local), (0, 4))]
        + [whole((RANK_UNIT, frames))] * 3,
        (IN_PLACE, narrow, whole((frames // 2, local)), whole((frames // 2, local)), whole(text_own.shape))
        + (whole(packs), whole(packs), whole(text_packs), whole(text_rows)),
        (
            shaped((frames, width), WIDE),
            shaped((frames, local), LOW),
            shaped((frames // 2, local), LOW),
            shaped((frames // 2, local), LOW),
            shaped(text_own.shape, WIDE),
            shaped(packs, WIDE),
            shaped(packs, LOW),
            shaped(text_packs, WIDE),
            shaped(text_rows, LOW),
        ),
        [
            pltpu.VMEM((2, tiles, TILE_HEADS * HEAD_DIM, TILE_HEADS * HEAD_DIM), WIDE),
            pltpu.VMEM((2, tiles, TILE_HEADS * HEAD_DIM, TILE_HEADS * HEAD_DIM), WIDE),
        ]
        + [pltpu.VMEM(rank, WIDE)] * 6
        + middle_scratch(weights, gathered)
        + [pltpu.VMEM((frames, local), LOW)] * 2
        + [pltpu.VMEM((frames, width), WIDE)]
        + [pltpu.VMEM((frames, local), LOW)] * 2
        + [pltpu.VMEM((frames, width), WIDE), pltpu.SemaphoreType.DMA((6,))],
        6 * frames * width * width,
        6 * width * width + 24 * frames * width,
        "middle_back",
        (meta, grad, stream_one, z_own, z_other, q_own, q_other, z2_own, z2_other)
        + args
        + (text_own, text_other, gain, text)
        + (cross_down, cross_down, cross_up, cross_up, packed, packed)
        + tuple(ranks),
    )


def feed_tile(
    rows_ref, cot_ref, up_weight, down_weight, up_rank, down_rank,
    ga9_ref, gb8_ref, branch, grad_rows, rank9, grad_rank8, rank8, grad_rank9,
):
    frames = rows_ref.shape[0]
    block = min(256, frames)
    low_pre = mm_tn(rank8[...], up_rank)
    low_grad = mm_tn(grad_rank9[...], down_rank)
    hidden_blocks = []
    grad_blocks = []
    for first in range(0, frames, block):
        span = slice(first, first + block)
        pre = mm(rows_ref[span], up_weight) + low_pre[span]
        grad_hidden = mm_nt(cot_ref[span], down_weight) + low_grad[span]
        hidden, slope = gelu_parts(pre)
        hidden = hidden.astype(LOW)
        grad_pre = (grad_hidden * slope).astype(LOW)
        branch[span] += mm(hidden, down_weight)
        grad_rows[span] += mm_nt(grad_pre, up_weight)
        hidden_blocks.append(hidden)
        grad_blocks.append(grad_pre)
    hidden = jnp.concatenate(hidden_blocks, axis=0)
    grad_pre = jnp.concatenate(grad_blocks, axis=0)
    rank9[...] += mm_nt(down_rank, hidden)
    grad_rank8[...] += mm_nt(up_rank, grad_pre)
    ga9_ref[...] = mm(grad_rank9[...], hidden).astype(ga9_ref.dtype)
    gb8_ref[...] = mm(rank8[...], grad_pre).astype(gb8_ref.dtype)


def feed_own_body(
    _, rows_ref, cot_ref, up_weight_ref, down_weight_ref, up_rank_ref, down_rank_ref,
    down8_ref, up9_ref,
    branch_ref, grad_rows_ref, rank9_ref, grad_rank8_ref, rank8, grad_rank9, ga9_ref, gb8_ref,
):
    @pl.when(pl.program_id(0) == 0)
    def _():
        rank8[...] = low_rank(down8_ref[0], rows_ref[...])
        grad_rank9[...] = low_rank(up9_ref[0], cot_ref[...])
        for ref in (branch_ref, grad_rows_ref, rank9_ref, grad_rank8_ref):
            ref[...] = jnp.zeros_like(ref)

    feed_tile(
        rows_ref, cot_ref, up_weight_ref[...], down_weight_ref[...], up_rank_ref[0], down_rank_ref[0],
        ga9_ref, gb8_ref, branch_ref, grad_rows_ref, rank9_ref, grad_rank8_ref, rank8, grad_rank9,
    )


def table_tile(tile, slot):
    return pl.BlockSpec((1, RANK_UNIT, tile), lambda t, m: (m[slot], 0, t))


def feed_own(meta, rows, cot, up_weight, down_weight, input_down, input_up, output_down, output_up, tile):
    frames, width = rows.shape
    hidden = up_weight.shape[1]
    grads = pl.BlockSpec((RANK_UNIT, tile), lambda t, m: (0, t))
    picked = pl.BlockSpec((1, RANK_UNIT, width), lambda t, m: (m[8], 0, 0))
    picked_out = pl.BlockSpec((1, RANK_UNIT, width), lambda t, m: (m[9], 0, 0))
    rank = (RANK_UNIT, frames)
    return call(
        feed_own_body,
        (hidden // tile,),
        [
            whole((frames, width)),
            whole((frames, width)),
            pl.BlockSpec((width, tile), lambda t, m: (0, t)),
            pl.BlockSpec((tile, width), lambda t, m: (t, 0)),
            table_tile(tile, 8),
            table_tile(tile, 9),
            picked,
            picked_out,
        ],
        (whole((frames, width)), whole((frames, width))) + (whole(rank),) * 4 + (grads, grads),
        (
            shaped((frames, width), WIDE),
            shaped((frames, width), WIDE),
            shaped(rank, WIDE),
            shaped(rank, WIDE),
            shaped(rank, LOW),
            shaped(rank, LOW),
            shaped((RANK_UNIT, hidden), WIDE),
            shaped((RANK_UNIT, hidden), WIDE),
        ),
        [],
        8 * frames * width * hidden,
        4 * width * hidden + 12 * frames * width,
        "feed_own",
        (meta, rows, cot, up_weight, down_weight, input_up, output_down, input_down, output_up),
    )


def feed_other_body(
    meta, last, rows_ref, cot_ref, up_weight_ref, down_weight_ref, up_rank_ref, down_rank_ref,
    down8_ref, up9_ref, branch_in_ref, grad_rows_in_ref, rank9_in_ref, grad_rank8_in_ref, rank8, grad_rank9,
    stream_ref, gain_ref,
    out_ref, grad_ref, mine_ref, theirs_ref,
    branch, grad_rows, rank9, grad_rank8, ga8_ref, gb9_ref, branch_in, grad_rows_in, stream_in, sems,
    out_held, grad_held, out_sems,
):
    step = pl.program_id(0)
    copies = [
        pltpu.make_async_copy(source, target, sems.at[i])
        for i, (source, target) in enumerate(
            ((branch_in_ref, branch_in), (grad_rows_in_ref, grad_rows_in), (stream_ref, stream_in))
        )
    ]

    @pl.when(step == 0)
    def _():
        for copy in copies:
            copy.start()
        branch[...] = jnp.zeros_like(branch)
        grad_rows[...] = jnp.zeros_like(grad_rows)
        rank9[...] = rank9_in_ref[...]
        grad_rank8[...] = grad_rank8_in_ref[...]

    shards, _, depth, tile = up_weight_ref.shape
    hidden = (last + 1) * tile
    first = pl.multiple_of(step * tile, 128)
    gb8_ref = theirs_ref.at[:, pl.ds(first, tile)]
    ga9_ref = theirs_ref.at[:, pl.ds(pl.multiple_of(hidden + first, 128), tile)]
    up_weight = up_weight_ref[...].reshape(shards * depth, tile)
    down_weight = down_weight_ref[...].reshape(tile, down_weight_ref.shape[3])
    feed_tile(
        rows_ref, cot_ref, up_weight, down_weight, up_rank_ref[...], down_rank_ref[...],
        ga9_ref, gb8_ref, branch, grad_rows, rank9, grad_rank8, rank8, grad_rank9,
    )

    @pl.when(step == last)
    def _():
        for copy in copies:
            copy.wait()
        frames = rows_ref.shape[0]
        block = min(128, frames)
        last8 = grad_rank8[...].astype(LOW)
        last9 = rank9[...].astype(LOW)
        ga8_ref[...] = mm(last8, rows_ref[...])
        gb9_ref[...] = mm(last9, cot_ref[...])
        half = ga8_ref.shape[1] // 2
        split_columns(meta, mine_ref, theirs_ref, 0, ga8_ref, 2 * hidden)
        split_columns(meta, mine_ref, theirs_ref, half, gb9_ref, 2 * hidden)
        flushes = []
        for first in range(0, frames, block):
            span = slice(first, first + block)
            stream = stream_in[span]
            out = stream + (branch[span] + branch_in[span]) + mm_tn(last9[:, span], up9_ref[0])
            out_held[span] = out.astype(LOW)
            flushes.append(pltpu.make_async_copy(out_held.at[span], out_ref.at[span], out_sems.at[len(flushes)]))
            flushes[-1].start()
            _, normed, inverse = norm_rows(stream, gain_ref[...])
            grad = grad_rows[span] + grad_rows_in[span] + mm_tn(last8[:, span], down8_ref[0])
            grad_held[span] = cot_ref[span].astype(WIDE) + norm_back(
                grad, gain_ref[...], normed, inverse
            )
            flushes.append(pltpu.make_async_copy(grad_held.at[span], grad_ref.at[span], out_sems.at[len(flushes)]))
            flushes[-1].start()
        for copy in flushes:
            copy.wait()


def feed_other(
    meta, rows, cot, gathered, packed, first_pack, input_down, output_up, carried, stream, gain, tile
):
    frames, width = rows.shape
    shards, quarters, depth, _ = gathered.shape
    hidden = quarters // 2 * width
    per_half = width // tile
    own_shards = tile // (quarters // 2 * depth)
    down_first = quarters // 2
    picked = pl.BlockSpec((1, RANK_UNIT, width), lambda t, m: (m[8], 0, 0))
    picked_out = pl.BlockSpec((1, RANK_UNIT, width), lambda t, m: (m[9], 0, 0))
    rank = (RANK_UNIT, frames)
    steps = hidden // tile
    full = whole((frames, width))
    wide = pltpu.VMEM((frames, width), WIDE)
    return call(
        lambda m, *refs: feed_other_body(m, steps - 1, *refs),
        (steps,),
        [
            full,
            full,
            pl.BlockSpec(
                (shards, 1, depth, tile),
                lambda t, m: (0, down_first + t // per_half, 0, t % per_half),
            ),
            pl.BlockSpec((own_shards, down_first, depth, width), lambda t, m: (t, 0, 0, 0)),
            pl.BlockSpec((RANK_UNIT, tile), lambda t, m: (0, first_pack // tile + t)),
            pl.BlockSpec((RANK_UNIT, tile), lambda t, m: (0, (first_pack + hidden) // tile + t)),
            picked,
            picked_out,
            IN_PLACE,
            IN_PLACE,
            whole(rank),
            whole(rank),
            whole(rank),
            whole(rank),
            IN_PLACE,
            whole((1, width)),
        ],
        (IN_PLACE, IN_PLACE, whole((RANK_UNIT, width)), whole((RANK_UNIT, 2 * hidden + width))),
        (
            shaped((frames, width), LOW),
            shaped((frames, width), WIDE),
            shaped((RANK_UNIT, width), WIDE),
            shaped((RANK_UNIT, 2 * hidden + width), LOW),
        ),
        [
            wide,
            wide,
            pltpu.VMEM(rank, WIDE),
            pltpu.VMEM(rank, WIDE),
            pltpu.VMEM((RANK_UNIT, width), WIDE),
            pltpu.VMEM((RANK_UNIT, width), WIDE),
            wide,
            wide,
            wide,
            pltpu.SemaphoreType.DMA((3,)),
            pltpu.VMEM((frames, width), LOW),
            wide,
            pltpu.SemaphoreType.DMA((2 * (frames // min(128, frames)),)),
        ],
        8 * frames * width * hidden,
        4 * width * hidden + 24 * frames * width,
        "feed_other",
        (meta, rows, cot, gathered, gathered, packed, packed, input_down, output_up)
        + tuple(carried)
        + (stream, gain),
    )


def last_norm_body(_, half, slot_part, x_ref, own_ref, first_ref, second_ref, grad_ref, gain_ref, *refs):
    plan, slots, carried, outs = slot_part
    step = pl.program_id(0)
    everyone_ref, label_ref = refs[:2]
    earlier = refs[2 : 2 + len(carried)]
    out_ref = refs[-6 - outs]
    scratch = refs[-5:]

    @pl.when(step == 0)
    def _():
        for copy in slot_copies(scratch[1].shape[3], len(plan), everyone_ref, scratch[1], scratch[3]):
            copy.start()

    _, normed, inverse = norm_rows(x_ref[...].astype(WIDE), gain_ref[...])
    other = jnp.where(step < half, first_ref[...].astype(WIDE), second_ref[...].astype(WIDE))
    total = own_ref[...] + other
    out_ref[...] = grad_ref[...] + norm_back(total, gain_ref[...], normed, inverse)

    @pl.when(step == 2 * half - 1)
    def _():
        slot_work(plan, slots, carried, everyone_ref, label_ref, earlier, refs[-5 - outs : -5], scratch)


def last_norm(meta, x, own, received, grad, gain, everyone, labelled, plan, outs, slots, unit, carried, after):
    frames, width = x.shape
    block = min(256, frames // 2)
    half = frames // 2 // block
    rows = pl.BlockSpec((block, width), lambda t, _: (t, 0))
    first = pl.BlockSpec((block, width), lambda t, _: (jnp.minimum(t, half - 1), 0))
    second = pl.BlockSpec((block, width), lambda t, _: (jnp.maximum(t - half, 0), 0))
    slot_part = (plan, slots, tuple(carried), len(outs))
    return call(
        lambda m, *refs: last_norm_body(m, half, slot_part, *refs),
        (2 * half,),
        [rows, rows, first, second, rows, whole((1, width))]
        + slot_specs(labelled, carried)
        + [IN_PLACE] * len(after),
        (rows,) + (IN_PLACE,) * len(outs),
        (shaped(x.shape, WIDE),) + slot_shapes(everyone, outs, slots),
        slot_scratch(everyone, plan, slots, unit, carried),
        20 * x.size,
        16 * x.size,
        "last_norm",
        (meta, x, own, *received, grad, gain, everyone, labelled, *carried.values(), *after),
    )


def on_pair(
    inputs,
    encoder_text_states,
    cotangent,
    clip_adapter_index,
    self_norm_gain,
    cross_norm_gain,
    feed_norm_gain,
    self_query_key_value_weight,
    self_output_weight,
    cross_query_weight,
    cross_key_value_weight,
    cross_output_weight,
    up_weight,
    down_weight,
    self_first_factors,
    self_second_factors,
    cross_first_factors,
    cross_second_factors,
    attention_first_factors,
    attention_second_factors,
    input_first_factors,
    input_second_factors,
    output_first_factors,
    output_second_factors,
):
    x = inputs[0]
    text = encoder_text_states[0]
    cot = cotangent[0]
    width = x.shape[1]
    local = self_output_weight.shape[0]
    hidden = up_weight.shape[1]
    slots = input_first_factors.shape[0]
    group_count = lax.axis_size("dp")
    place = lax.axis_index("dp")
    side = lax.axis_index("tensor")
    picks = clip_adapter_index[0]
    meta = jnp.concatenate([picks, jnp.stack([side, place]).astype(jnp.int32)])
    gain_one, gain_two, gain_three = (
        vec.reshape(1, width) for vec in (self_norm_gain, cross_norm_gain, feed_norm_gain)
    )

    def swap(array):
        return lax.ppermute(array, "tensor", [(0, 1), (1, 0)])

    depth = width // group_count
    step = local // group_count

    def share(weight, size):
        return lax.dynamic_slice_in_dim(weight, place * size, size, axis=0)

    def side_by_side(rows, count):
        return rows.reshape(rows.shape[0], count, -1).transpose(1, 0, 2)

    out_share = side_by_side(share(self_output_weight, step), 2).reshape(depth, local)
    query_share = share(cross_query_weight, depth)
    cross_share = side_by_side(share(cross_output_weight, step), 2).reshape(depth, local)
    share_one = jnp.stack([swap(out_share), swap(query_share), swap(cross_share)])
    rows_one = first_norm(meta, x, gain_one)
    share_one, rows_one = lax.optimization_barrier((share_one, rows_one))
    gathered_one = lax.all_gather(share_one, "dp", axis=0)
    rows_one_other = swap(rows_one)
    factors = picked_factors(
        meta,
        [
            (attention_first_factors, 0, 3),
            (attention_first_factors, 1, 7),
            (cross_second_factors, 0, 4),
            (cross_second_factors, 1, 5),
            (cross_second_factors, 2, 6),
            (input_second_factors, None, 8),
            (output_first_factors, None, 9),
        ],
    )
    packed = swap(factors)
    first_pack = 5 * local

    heads_own, ranks_own = project_heads(
        meta, rows_one, self_query_key_value_weight, self_first_factors, self_second_factors, 0, 0, "own_heads"
    )
    part_own = self_forward_own(meta, heads_own, factors)
    text_own, _ = project_heads(
        meta, text, cross_key_value_weight, cross_first_factors, cross_second_factors, 5, 1, "text_heads"
    )
    text_other = swap(text_own)
    share_two = feed_share(
        meta, down_weight, up_weight, depth, (part_own, text_own, rows_one_other)
    )
    heads_other, ranks_other = project_heads(
        meta, rows_one_other, self_query_key_value_weight, self_first_factors, self_second_factors,
        0, 0, "other_heads", (share_two,),
    )
    z_own_frames, z_other_frames, log_own, log_other = self_forward(meta, part_own, heads_own, heads_other)
    share_two, z_other_frames = lax.optimization_barrier((swap(share_two), z_other_frames))
    gathered_two = lax.all_gather(share_two, "dp", axis=0)
    z_other_heads = swap(z_other_frames)
    weights = (self_output_weight, cross_query_weight, cross_output_weight)
    tables = (attention_first_factors, attention_second_factors, cross_first_factors, cross_second_factors)
    stream_one, stream_two, rows_three, q_own, q_other, z2_own, z2_other, *middle_ranks = middle_forward(
        meta, x, z_own_frames, z_other_heads, weights, gathered_one, tables, packed,
        text_own, text_other, (gain_two, gain_three),
    )
    tile = local
    *carried, ga9_own, gb8_own = feed_own(
        meta, rows_three, cot, up_weight, down_weight, input_first_factors, input_second_factors,
        output_first_factors, output_second_factors, tile,
    )
    output, grad_two, feed_mine, feed_theirs = feed_other(
        meta, rows_three, cot, gathered_two, packed, first_pack, input_first_factors,
        output_second_factors, carried, stream_two, gain_three, tile,
    )

    feed_received = swap(feed_theirs)

    (
        grad_one, dz_own_heads, *dz_other_heads, text_grad_own, middle_mine, middle_theirs,
        text_mine_rank, text_theirs,
    ) = middle_back(
        meta, grad_two, stream_one, z_own_frames, z_other_heads, q_own, q_other, z2_own, z2_other,
        weights, gathered_one, tables, packed, text_own, text_other, gain_two, text, middle_ranks,
    )
    feed_received, middle_theirs, *dz_other_heads = lax.optimization_barrier(
        (feed_received, middle_theirs, *dz_other_heads)
    )
    *dz_other_frames, text_theirs = lax.optimization_barrier(
        (*[swap(half) for half in dz_other_heads], text_theirs)
    )

    unit = local
    hidden_units = hidden // unit
    labels = jnp.zeros((RANK_UNIT, 2 * HEAD_DIM), LOW).at[:, : picks.shape[0]].set(picks.astype(LOW)[None])
    early = jnp.concatenate(
        [
            join(middle_mine, [swap(middle_theirs)]),
            join(feed_mine, [feed_received[:, 2 * hidden :]]),
            join(jnp.concatenate([gb8_own, ga9_own], axis=1), [feed_received[:, : 2 * hidden]]),
            labels,
        ],
        axis=1,
    )
    early_all = lax.all_gather(early, "dp", axis=0)
    grads_part, *prepared = self_back_own(meta, heads_own, z_own_frames, log_own, dz_own_heads)
    grads_own, grads_other = self_back(
        meta, grads_part, prepared, heads_other, z_other_frames, log_other, dz_other_frames, early
    )
    text_received, grads_own = lax.optimization_barrier((swap(text_theirs), grads_own))
    texts = text.shape[0]
    text_grad_other = text_received[: 2 * texts].reshape(text_grad_own.shape)
    text_received_rank = side_by_side(
        text_received[2 * texts :].reshape(4, RANK_UNIT, local).transpose(1, 0, 2).reshape(RANK_UNIT, -1), 1
    )[0]
    text_heads_grad = (text_grad_own + text_grad_other.astype(WIDE)).astype(LOW)
    mine, theirs = first_grads(
        meta, [rows_one, rows_one_other], [grads_own, grads_other], self_second_factors, 0, "self_first"
    )
    seconds = second_grads(meta, [ranks_own, ranks_other], [grads_own, grads_other], "self_second", theirs)
    theirs, seconds = lax.optimization_barrier((swap(theirs), seconds))
    partial_other = [
        project_back_heads(
            meta, grads_other, self_query_key_value_weight, self_first_factors, self_second_factors,
            0, 0, LOW, "other_back", seconds, (part, 2),
        )
        for part in range(2)
    ]
    received = [swap(part) for part in partial_other]
    late = jnp.concatenate(
        [join(mine, [theirs]), seconds, join(text_mine_rank, [text_received_rank])], axis=1
    )
    late, early_all = lax.optimization_barrier((late, early_all))
    late_all = lax.all_gather(late, "dp", axis=0)
    text_rows = project_back_heads(
        meta, text_heads_grad, cross_key_value_weight, cross_first_factors, cross_second_factors,
        5, 1, WIDE, "text_back", partial_other[1],
    )
    text_halves = (text_rows[:, : width // 2], text_rows[:, width // 2 :])
    text_mine = jnp.where(side == 0, text_halves[0], text_halves[1])
    text_theirs = jnp.where(side == 0, text_halves[1], text_halves[0])
    text_received = swap(text_theirs.astype(LOW))
    partial_own = project_back_heads(
        meta, grads_own, self_query_key_value_weight, self_first_factors, self_second_factors,
        0, 0, WIDE, "own_back", late,
    )
    sum_query_a, sum_query_b, sum_out_a, sum_out_b, sum_up_a, sum_down_b, sum_up_b, sum_down_a = slot_sums(
        meta,
        early_all,
        [(4, 0, 0), (4, 1, 0), (3, 2, 0), (7, 2, 1), (3, 3, 0), (7, 3, 1), (8, 4, 0), (9, 5, 0)]
        + [(8, 6, i) for i in range(hidden_units)]
        + [(9, 7, i) for i in range(hidden_units)],
        [(1, unit), (1, unit), (2, unit), (2, unit), (None, unit), (None, unit), (None, hidden), (None, hidden)],
        slots, unit, {}, "early_slots", (partial_own,),
    )
    *received, text_received, sum_up_a = lax.optimization_barrier((*received, text_received, sum_up_a))
    text_grad = text_mine + text_received.astype(WIDE)
    input_grad, sum_self_a, sum_self_b, sum_cross_a, sum_cross_b = last_norm(
        meta, x, partial_own, received, grad_one, gain_one,
        late_all,
        early_all,
        [(0, 0, 0), (1, 0, 1), (2, 0, 2), (0, 1, 0), (1, 1, 1), (2, 1, 2)]
        + [(5, 2, 1), (6, 2, 2), (5, 3, 1), (6, 3, 2)],
        [(3, unit), (3, unit), (3, unit), (3, unit)],
        slots, unit, {2: sum_query_a, 3: sum_query_b}, (sum_up_a,),
    )
    return (
        output[None],
        input_grad[None],
        text_grad[None],
        sum_self_a,
        sum_self_b,
        sum_cross_a,
        sum_cross_b,
        sum_out_a,
        sum_out_b,
        sum_up_a,
        sum_up_b,
        sum_down_a,
        sum_down_b,
    )


def solution(mesh):
    in_specs = (
        P("dp", "tensor", None),
        P("dp", None, None),
        P("dp", "tensor", None),
        P("dp", None),
        P(),
        P(),
        P(),
        P(None, None, "tensor"),
        P("tensor", None),
        P(None, "tensor"),
        P(None, None, "tensor"),
        P("tensor", None),
        P(None, "tensor"),
        P("tensor", None),
        P(),
        P(None, None, None, "tensor"),
        P(),
        P(None, None, None, "tensor"),
        P(None, None, None, "tensor"),
        P(),
        P(),
        P(None, None, "tensor"),
        P(None, None, "tensor"),
        P(),
    )
    out_specs = (
        P("dp", "tensor", None),
        P("dp", "tensor", None),
        P("dp", None, "tensor"),
        P(None, None, None, "tensor"),
        P(None, None, None, "tensor"),
        P(None, None, None, "tensor"),
        P(None, None, None, "tensor"),
        P(None, None, None, "tensor"),
        P(None, None, None, "tensor"),
        P(None, None, "tensor"),
        P(None, None, "tensor"),
        P(None, None, "tensor"),
        P(None, None, "tensor"),
    )
    layer = on_pair if mesh.shape["tensor"] == 2 else on_device
    return jax.shard_map(
        layer, mesh=mesh, in_specs=in_specs, out_specs=out_specs, check_vma=False
    )
```

```python
import jax
import jax.numpy as jnp
from jax import lax
from jax.experimental import pallas as pl
from jax.experimental.pallas import tpu as pltpu
from jax.sharding import PartitionSpec as P

HEAD_DIM = 64


epsilon = 1e-05


def split_dot(form, wide_part, narrow_part):
    high_part = wide_part.astype(jnp.bfloat16)
    rest_part = (wide_part - high_part.astype(jnp.float32)).astype(jnp.bfloat16)
    first = jnp.einsum(form, high_part, narrow_part, preferred_element_type=jnp.float32)
    return first + jnp.einsum(form, rest_part, narrow_part, preferred_element_type=jnp.float32)


def layer_norm(stream, gain_vec):
    centred = stream - jnp.mean(stream, axis=-1, keepdims=True)
    inverse = lax.rsqrt(jnp.mean(centred * centred, axis=-1, keepdims=True) + epsilon)
    normed = centred * inverse
    return (normed * gain_vec, normed, inverse)


def norm_back(grad_out, gain_vec, normed, inverse):
    grad_norm = grad_out * gain_vec
    mean_grad = jnp.mean(grad_norm, axis=-1, keepdims=True)
    mean_cross = jnp.mean(grad_norm * normed, axis=-1, keepdims=True)
    return inverse * (grad_norm - mean_grad - normed * mean_cross)


def spread_rows(local_rows):
    return lax.all_gather(local_rows.astype(jnp.bfloat16), "tensor", axis=1, tiled=True)


def reduce_grads(partial_sum):
    return lax.psum_scatter(
        partial_sum.astype(jnp.bfloat16), "tensor", scatter_dimension=1, tiled=True
    ).astype(jnp.float32)


def project_rows(act_rows, weight, output_choice, input_choice):
    low_rank = jnp.einsum(
        "ctd,crd->ctr", act_rows, output_choice, preferred_element_type=jnp.float32
    )
    result = jnp.einsum("ctd,de->cte", act_rows, weight, preferred_element_type=jnp.float32)
    result = result + split_dot("ctr,cre->cte", low_rank, input_choice)
    return (result, low_rank)


def project_back(grad_low, act_rows, weight, output_choice, input_choice, low_rank):
    grad_rank = jnp.einsum(
        "cte,cre->ctr", grad_low, input_choice, preferred_element_type=jnp.float32
    )
    grad_rows = jnp.einsum("cte,de->ctd", grad_low, weight, preferred_element_type=jnp.float32)
    grad_rows = grad_rows + split_dot("ctr,crd->ctd", grad_rank, output_choice)
    grad_down = split_dot("ctr,ctd->crd", grad_rank, act_rows)
    grad_up = split_dot("ctr,cte->cre", low_rank, grad_low)
    return (grad_rows, grad_down, grad_up)


def causal_frames(first_row, block_rows, key_count):
    query_at = first_row + jnp.arange(block_rows, dtype=jnp.int32)[:, None]
    key_at = jnp.arange(key_count, dtype=jnp.int32)[None, :]
    return key_at <= query_at


def attention_forward(queries, key_rows, value_rows, causal):
    frames = queries.shape[1]
    key_count = key_rows.shape[1]
    block_rows = min(512, frames)
    score_scale = HEAD_DIM ** (-0.5)
    outputs = []
    log_totals = []
    for first_row in range(0, frames, block_rows):
        key_end = first_row + block_rows if causal else key_count
        query_block = queries[:, first_row : first_row + block_rows]
        scores = (
            jnp.einsum(
                "cbhe,ckhe->chbk",
                query_block,
                key_rows[:, :key_end],
                preferred_element_type=jnp.float32,
            )
            * score_scale
        )
        if causal:
            scores = jnp.where(causal_frames(first_row, block_rows, key_end), scores, -1e30)
        largest = jnp.max(scores, axis=-1, keepdims=True)
        exponent = jnp.exp(scores - largest)
        summed = jnp.sum(exponent, axis=-1, keepdims=True)
        prob_low = (exponent / summed).astype(jnp.bfloat16)
        outputs.append(
            jnp.einsum(
                "chbk,ckhe->cbhe",
                prob_low,
                value_rows[:, :key_end],
                preferred_element_type=jnp.float32,
            )
        )
        log_totals.append(largest + jnp.log(summed))
    return (jnp.concatenate(outputs, axis=1), jnp.concatenate(log_totals, axis=2))


def attention_back(queries, key_rows, value_rows, log_totals, grad_mixed, causal):
    frames = queries.shape[1]
    key_count = key_rows.shape[1]
    block_rows = min(512, frames)
    score_scale = HEAD_DIM ** (-0.5)
    grad_keys = jnp.zeros(key_rows.shape, jnp.float32)
    grad_values = jnp.zeros(value_rows.shape, jnp.float32)
    grad_queries = []
    for first_row in range(0, frames, block_rows):
        key_end = first_row + block_rows if causal else key_count
        key_part = key_rows[:, :key_end]
        value_part = value_rows[:, :key_end]
        query_block = queries[:, first_row : first_row + block_rows]
        grad_block = grad_mixed[:, first_row : first_row + block_rows]
        scores = (
            jnp.einsum("cbhe,ckhe->chbk", query_block, key_part, preferred_element_type=jnp.float32)
            * score_scale
        )
        if causal:
            scores = jnp.where(causal_frames(first_row, block_rows, key_end), scores, -1e30)
        probs = jnp.exp(scores - log_totals[:, :, first_row : first_row + block_rows])
        grad_values = grad_values.at[:, :key_end].add(
            jnp.einsum(
                "chbk,cbhe->ckhe",
                probs.astype(jnp.bfloat16),
                grad_block,
                preferred_element_type=jnp.float32,
            )
        )
        grad_probs = jnp.einsum(
            "cbhe,ckhe->chbk", grad_block, value_part, preferred_element_type=jnp.float32
        )
        inner_sum = jnp.sum(probs * grad_probs, axis=-1, keepdims=True)
        grad_scores = (probs * (grad_probs - inner_sum)).astype(jnp.bfloat16)
        grad_queries.append(
            jnp.einsum("chbk,ckhe->cbhe", grad_scores, key_part, preferred_element_type=jnp.float32)
            * score_scale
        )
        grad_keys = grad_keys.at[:, :key_end].add(
            jnp.einsum(
                "chbk,cbhe->ckhe", grad_scores, query_block, preferred_element_type=jnp.float32
            )
            * score_scale
        )
    return (jnp.concatenate(grad_queries, axis=1), grad_keys, grad_values)


def gelu_exact(pre_act):
    return jax.nn.gelu(pre_act, approximate=False)


def on_device(
    inputs,
    encoder_text_states,
    cotangent,
    clip_adapter_index,
    self_norm_gain,
    cross_norm_gain,
    feed_norm_gain,
    self_query_key_value_weight,
    self_output_weight,
    cross_query_weight,
    cross_key_value_weight,
    cross_output_weight,
    up_weight,
    down_weight,
    self_first_factors,
    self_second_factors,
    cross_first_factors,
    cross_second_factors,
    attention_first_factors,
    attention_second_factors,
    input_first_factors,
    input_second_factors,
    output_first_factors,
    output_second_factors,
):
    adapter_slot_count = input_first_factors.shape[0]
    chooser = (
        clip_adapter_index[:, :, None]
        == jnp.arange(adapter_slot_count, dtype=jnp.int32)[None, None, :]
    ).astype(jnp.bfloat16)
    local_heads = self_output_weight.shape[0] // HEAD_DIM

    def choose_adapter_slot(adapter_slot_table, column_index):
        return jnp.einsum(
            "cn,npq->cpq",
            chooser[:, column_index],
            adapter_slot_table,
            preferred_element_type=jnp.float32,
        ).astype(jnp.bfloat16)

    def slot_grads(grad_pick, column_index):
        return split_dot("cpq,cn->npq", grad_pick, chooser[:, column_index])

    def split_heads(stacked):
        return stacked.reshape(stacked.shape[0], stacked.shape[1], local_heads, HEAD_DIM)

    def join_heads(stacked):
        return stacked.reshape(stacked.shape[0], stacked.shape[1], local_heads * HEAD_DIM)

    def out_forward(mixed_in, inner_layer):
        column_index = 3 + 4 * inner_layer
        input_choice = choose_adapter_slot(attention_second_factors[inner_layer], column_index)
        weight = self_output_weight if inner_layer == 0 else cross_output_weight
        output_choice = choose_adapter_slot(attention_first_factors[inner_layer], column_index)
        partial_out, low_rank = project_rows(mixed_in, weight, output_choice, input_choice)
        branch = lax.psum_scatter(
            partial_out.astype(jnp.bfloat16), "tensor", scatter_dimension=1, tiled=True
        ).astype(jnp.float32)
        kept_data = (mixed_in, weight, output_choice, input_choice, low_rank)
        return (branch, kept_data)

    def out_back(grad_stream, kept_data):
        mixed_in, weight, output_choice, input_choice, low_rank = kept_data
        grad_low = grad_stream.astype(jnp.bfloat16)
        grad_full = lax.all_gather(grad_low, "tensor", axis=1, tiled=True)
        grad_rows, grad_down, grad_up = project_back(
            grad_full, mixed_in, weight, output_choice, input_choice, low_rank
        )
        grad_mixed = grad_rows.astype(jnp.bfloat16)
        return (grad_mixed, grad_down, grad_up)

    stream = inputs.astype(jnp.float32)
    normed_value, normed_one, inverse_one = layer_norm(stream, self_norm_gain)
    rows_one = spread_rows(normed_value)
    self_down_factor = [
        choose_adapter_slot(self_first_factors[slot_number], slot_number)
        for slot_number in range(3)
    ]
    self_up_factor = [
        choose_adapter_slot(self_second_factors[slot_number], slot_number)
        for slot_number in range(3)
    ]
    self_parts = [
        project_rows(
            rows_one,
            self_query_key_value_weight[slot_number],
            self_down_factor[slot_number],
            self_up_factor[slot_number],
        )
        for slot_number in range(3)
    ]
    self_heads = [
        split_heads(self_parts[slot_number][0].astype(jnp.bfloat16)) for slot_number in range(3)
    ]
    mixed_one, totals_one = attention_forward(self_heads[0], self_heads[1], self_heads[2], True)
    mixed_one = join_heads(mixed_one).astype(jnp.bfloat16)
    branch_one, kept_one = out_forward(mixed_one, 0)
    stream_one = stream + branch_one
    normed_value, normed_two, inverse_two = layer_norm(stream_one, cross_norm_gain)
    rows_two = spread_rows(normed_value)
    cross_down_factor = [
        choose_adapter_slot(cross_first_factors[slot_number], 4 + slot_number)
        for slot_number in range(3)
    ]
    cross_up_factor = [
        choose_adapter_slot(cross_second_factors[slot_number], 4 + slot_number)
        for slot_number in range(3)
    ]
    query_full, query_rank = project_rows(
        rows_two, cross_query_weight, cross_down_factor[0], cross_up_factor[0]
    )
    key_full, key_rank = project_rows(
        encoder_text_states, cross_key_value_weight[0], cross_down_factor[1], cross_up_factor[1]
    )
    value_full, value_rank = project_rows(
        encoder_text_states, cross_key_value_weight[1], cross_down_factor[2], cross_up_factor[2]
    )
    query_two = split_heads(query_full.astype(jnp.bfloat16))
    key_two = split_heads(key_full.astype(jnp.bfloat16))
    value_two = split_heads(value_full.astype(jnp.bfloat16))
    mixed_two, totals_two = attention_forward(query_two, key_two, value_two, False)
    mixed_two = join_heads(mixed_two).astype(jnp.bfloat16)
    branch_two, kept_two = out_forward(mixed_two, 1)
    stream_two = stream_one + branch_two
    normed_value, normed_three, inverse_three = layer_norm(stream_two, feed_norm_gain)
    rows_three = spread_rows(normed_value)
    input_second_choice = choose_adapter_slot(input_first_factors, 8)
    input_first_choice = choose_adapter_slot(input_second_factors, 8)
    before, up_rank = project_rows(rows_three, up_weight, input_second_choice, input_first_choice)
    gelu_value, gelu_pull = jax.vjp(gelu_exact, before)
    hidden = gelu_value.astype(jnp.bfloat16)
    output_second_choice = choose_adapter_slot(output_first_factors, 9)
    output_first_choice = choose_adapter_slot(output_second_factors, 9)
    partial_out, down_rank = project_rows(
        hidden, down_weight, output_second_choice, output_first_choice
    )
    branch_three = lax.psum_scatter(
        partial_out.astype(jnp.bfloat16), "tensor", scatter_dimension=1, tiled=True
    ).astype(jnp.float32)
    output = (stream_two + branch_three).astype(jnp.bfloat16)
    grad_full = lax.all_gather(cotangent, "tensor", axis=1, tiled=True)
    grad_hidden, grad_down_a, grad_down_b = project_back(
        grad_full, hidden, down_weight, output_second_choice, output_first_choice, down_rank
    )
    grad_before = gelu_pull(grad_hidden)[0].astype(jnp.bfloat16)
    grad_rows, grad_up_a, grad_up_b = project_back(
        grad_before, rows_three, up_weight, input_second_choice, input_first_choice, up_rank
    )
    grad_stream = cotangent.astype(jnp.float32) + norm_back(
        reduce_grads(grad_rows), feed_norm_gain, normed_three, inverse_three
    )
    grad_mixed, grad_out_a_two, grad_out_b_two = out_back(grad_stream, kept_two)
    grad_query, grad_key, grad_value = attention_back(
        query_two, key_two, value_two, totals_two, split_heads(grad_mixed), False
    )
    grad_query = join_heads(grad_query).astype(jnp.bfloat16)
    grad_key = join_heads(grad_key).astype(jnp.bfloat16)
    grad_value = join_heads(grad_value).astype(jnp.bfloat16)
    grad_rows_query, cross_grad_a_zero, cross_grad_b_zero = project_back(
        grad_query,
        rows_two,
        cross_query_weight,
        cross_down_factor[0],
        cross_up_factor[0],
        query_rank,
    )
    grad_text_key, cross_grad_a_one, cross_grad_b_one = project_back(
        grad_key,
        encoder_text_states,
        cross_key_value_weight[0],
        cross_down_factor[1],
        cross_up_factor[1],
        key_rank,
    )
    grad_text_value, cross_grad_a_two, cross_grad_b_two = project_back(
        grad_value,
        encoder_text_states,
        cross_key_value_weight[1],
        cross_down_factor[2],
        cross_up_factor[2],
        value_rank,
    )
    normed_grad, text_grad = (
        lax.psum_scatter(
            grad_rows_query.astype(jnp.bfloat16), "tensor", scatter_dimension=1, tiled=True
        ).astype(jnp.float32),
        lax.psum_scatter(
            (grad_text_key + grad_text_value).astype(jnp.bfloat16),
            "tensor",
            scatter_dimension=2,
            tiled=True,
        ).astype(jnp.float32),
    )
    grad_stream = grad_stream + norm_back(normed_grad, cross_norm_gain, normed_two, inverse_two)
    grad_mixed, grad_out_a_one, grad_out_b_one = out_back(grad_stream, kept_one)
    grad_query, grad_key, grad_value = attention_back(
        self_heads[0], self_heads[1], self_heads[2], totals_one, split_heads(grad_mixed), True
    )
    self_grads = [
        join_heads(grad_query).astype(jnp.bfloat16),
        join_heads(grad_key).astype(jnp.bfloat16),
        join_heads(grad_value).astype(jnp.bfloat16),
    ]
    self_rows_total = jnp.zeros(rows_one.shape, jnp.float32)
    self_grad_a = []
    self_grad_b = []
    for slot_number in range(3):
        grad_rows, grad_a_part, grad_b_part = project_back(
            self_grads[slot_number],
            rows_one,
            self_query_key_value_weight[slot_number],
            self_down_factor[slot_number],
            self_up_factor[slot_number],
            self_parts[slot_number][1],
        )
        self_rows_total = self_rows_total + grad_rows
        self_grad_a.append(slot_grads(grad_a_part, slot_number))
        self_grad_b.append(slot_grads(grad_b_part, slot_number))
    input_grad = grad_stream + norm_back(
        reduce_grads(self_rows_total), self_norm_gain, normed_one, inverse_one
    )
    sum_self_a = jnp.stack(self_grad_a)
    sum_self_b = jnp.stack(self_grad_b)
    sum_cross_a = jnp.stack(
        [
            slot_grads(cross_grad_a_zero, 4),
            slot_grads(cross_grad_a_one, 5),
            slot_grads(cross_grad_a_two, 6),
        ]
    )
    sum_cross_b = jnp.stack(
        [
            slot_grads(cross_grad_b_zero, 4),
            slot_grads(cross_grad_b_one, 5),
            slot_grads(cross_grad_b_two, 6),
        ]
    )
    sum_out_a = jnp.stack([slot_grads(grad_out_a_one, 3), slot_grads(grad_out_a_two, 7)])
    sum_out_b = jnp.stack([slot_grads(grad_out_b_one, 3), slot_grads(grad_out_b_two, 7)])
    sum_up_a = slot_grads(grad_up_a, 8)
    sum_up_b = slot_grads(grad_up_b, 8)
    sum_down_a = slot_grads(grad_down_a, 9)
    sum_down_b = slot_grads(grad_down_b, 9)
    sum_self_a, sum_cross_a, sum_out_b, sum_up_a, sum_down_b = (
        lax.psum_scatter(
            sum_self_a.astype(jnp.bfloat16), "tensor", scatter_dimension=3, tiled=True
        ).astype(jnp.float32),
        lax.psum_scatter(
            sum_cross_a.astype(jnp.bfloat16), "tensor", scatter_dimension=3, tiled=True
        ).astype(jnp.float32),
        lax.psum_scatter(
            sum_out_b.astype(jnp.bfloat16), "tensor", scatter_dimension=3, tiled=True
        ).astype(jnp.float32),
        lax.psum_scatter(
            sum_up_a.astype(jnp.bfloat16), "tensor", scatter_dimension=2, tiled=True
        ).astype(jnp.float32),
        lax.psum_scatter(
            sum_down_b.astype(jnp.bfloat16), "tensor", scatter_dimension=2, tiled=True
        ).astype(jnp.float32),
    )
    totals = (
        lax.psum(sum_self_a.astype(jnp.bfloat16), "dp").astype(jnp.float32),
        lax.psum(sum_self_b.astype(jnp.bfloat16), "dp").astype(jnp.float32),
        lax.psum(sum_cross_a.astype(jnp.bfloat16), "dp").astype(jnp.float32),
        lax.psum(sum_cross_b.astype(jnp.bfloat16), "dp").astype(jnp.float32),
        lax.psum(sum_out_a.astype(jnp.bfloat16), "dp").astype(jnp.float32),
        lax.psum(sum_out_b.astype(jnp.bfloat16), "dp").astype(jnp.float32),
        lax.psum(sum_up_a.astype(jnp.bfloat16), "dp").astype(jnp.float32),
        lax.psum(sum_up_b.astype(jnp.bfloat16), "dp").astype(jnp.float32),
        lax.psum(sum_down_a.astype(jnp.bfloat16), "dp").astype(jnp.float32),
        lax.psum(sum_down_b.astype(jnp.bfloat16), "dp").astype(jnp.float32),
    )
    return (
        output,
        input_grad,
        text_grad,
        totals[0],
        totals[1],
        totals[2],
        totals[3],
        totals[4],
        totals[5],
        totals[6],
        totals[7],
        totals[8],
        totals[9],
    )


LOW = jnp.bfloat16
WIDE = jnp.float32
VMEM_BYTES = 58 * 1024 * 1024
RANK_UNIT = 16
COST_SCALE = 1


def mm(left, right, left_dim=1, right_dim=0):
    return lax.dot_general(
        left, right, (((left_dim,), (right_dim,)), ((), ())), preferred_element_type=WIDE
    )


def mm_nt(left, right):
    return mm(left, right, 1, 1)


def mm_tn(left, right):
    return mm(left, right, 0, 0)


def low_rank(factor, rows):
    return mm_nt(factor, rows).astype(LOW)


def norm_rows(rows, gain):
    centred = rows - jnp.mean(rows, axis=-1, keepdims=True)
    inverse = lax.rsqrt(jnp.mean(centred * centred, axis=-1, keepdims=True) + epsilon)
    normed = centred * inverse
    return normed * gain, normed, inverse


def lane_halves():
    lane = lax.broadcasted_iota(jnp.int32, (1, 2 * HEAD_DIM), 1)
    return lane < HEAD_DIM


def half_masks():
    left = lane_halves()
    first = jnp.where(left, 1.0, 0.0)
    return first.astype(LOW), (1.0 - first).astype(LOW)


def gelu_parts(pre):
    bell = jnp.exp(-0.5 * pre * pre)
    step = 1.0 / (1.0 + (0.3275911 * 0.7071067811865476) * jnp.abs(pre))
    tail = step * (
        0.5 * 0.254829592
        + step
        * (
            0.5 * -0.284496736
            + step
            * (0.5 * 1.421413741 + step * (0.5 * -1.453152027 + step * (0.5 * 1.061405429)))
        )
    )
    tail = tail * bell
    phi = jnp.where(pre >= 0.0, 1.0 - tail, tail)
    return pre * phi, phi + pre * bell * 0.3989422804014327


def whole(shape, where=None):
    place = (0,) * len(shape) if where is None else where
    return pl.BlockSpec(shape, lambda *_: place, pipeline_mode=pl.Buffered(1))


def call(body, grid, in_specs, out_specs, out_shape, scratch, flops, moved, name, args):
    return pl.pallas_call(
        body,
        grid_spec=pltpu.PrefetchScalarGridSpec(
            num_scalar_prefetch=1,
            grid=grid,
            in_specs=in_specs,
            out_specs=out_specs,
            scratch_shapes=scratch,
        ),
        out_shape=out_shape,
        compiler_params=pltpu.CompilerParams(
            dimension_semantics=("arbitrary",) * len(grid), vmem_limit_bytes=VMEM_BYTES
        ),
        cost_estimate=pl.CostEstimate(
            flops=flops // COST_SCALE, bytes_accessed=moved // COST_SCALE, transcendentals=0
        ),
        name=name,
    )(*args)


def shaped(shape, dtype):
    return jax.ShapeDtypeStruct(shape, dtype)


IN_PLACE = pl.BlockSpec(memory_space=pl.ANY)


def factors_body(_, *refs):
    out_ref = refs[-1]
    first = 0
    for ref in refs[:-1]:
        size = ref.shape[-1]
        out_ref[:, first : first + size] = ref[...]
        first += size


def picked_factors(meta, sources):
    specs = []
    total = 0
    for table, entry, slot in sources:
        if entry is None:
            spec = pl.BlockSpec((None,) + table.shape[1:], lambda t, m, slot=slot: (m[slot], 0, 0))
        else:
            spec = pl.BlockSpec(
                (None, None) + table.shape[2:], lambda t, m, entry=entry, slot=slot: (entry, m[slot], 0, 0)
            )
        specs.append(spec)
        total += table.shape[-1]
    shape = (RANK_UNIT, total)
    return call(
        factors_body, (1,), specs, whole(shape), shaped(shape, LOW), [], 0, 4 * RANK_UNIT * total,
        "picked_factors", (meta,) + tuple(table for table, _, _ in sources),
    )


def share_body(_, parts, down_ref, up_ref, *refs):
    out_ref = refs[-1]
    step = pl.program_id(0)

    @pl.when(step < parts)
    def _():
        out_ref[0] = down_ref[...]

    @pl.when(step >= parts)
    def _():
        out_ref[0] = up_ref[...]


def feed_share(meta, down_weight, up_weight, depth, after):
    hidden, width = down_weight.shape
    parts = hidden // width
    return call(
        lambda m, *refs: share_body(m, parts, *refs),
        (2 * parts,),
        [
            pl.BlockSpec(
                (depth, width), lambda t, m: (m[11] * parts + jnp.minimum(t, parts - 1), 0)
            ),
            pl.BlockSpec((depth, width), lambda t, m: (m[11], jnp.maximum(t - parts, 0))),
        ]
        + [IN_PLACE] * len(after),
        pl.BlockSpec((1, depth, width), lambda t, m: (t, 0, 0)),
        shaped((2 * parts, depth, width), LOW),
        [],
        0,
        8 * parts * depth * width,
        "feed_share",
        (meta, down_weight, up_weight, *after),
    )


def first_norm_body(_, x_ref, gain_ref, out_ref):
    rows, _, _ = norm_rows(x_ref[...].astype(WIDE), gain_ref[...])
    out_ref[...] = rows.astype(LOW)


def first_norm(meta, x, gain):
    frames, width = x.shape
    block = min(256, frames)
    rows = pl.BlockSpec((block, width), lambda t, _: (t, 0))
    return call(
        first_norm_body,
        (frames // block,),
        [rows, whole((1, width))],
        rows,
        shaped(x.shape, LOW),
        [],
        10 * x.size,
        4 * x.size,
        "first_norm",
        (meta, x, gain),
    )


def project_body(_, act_ref, weight_ref, down_ref, up_ref, *refs):
    out_ref, rank_ref = refs[-2:]
    act = act_ref[...]
    rank = low_rank(down_ref[0, 0], act)
    rank_ref[0] = rank
    out_ref[0] = (mm(act, weight_ref[0]) + mm_tn(rank, up_ref[0, 0])).astype(LOW)


def project_heads(meta, act, weights, down, up, slots, skip, name, after=()):
    rows, width = act.shape
    count, _, local = weights.shape
    first_slot = slots
    return call(
        project_body,
        (count,),
        [
            whole((rows, width)),
            pl.BlockSpec((1, width, local), lambda j, m: (j, 0, 0)),
            pl.BlockSpec((1, 1, RANK_UNIT, width), lambda j, m: (j + skip, m[first_slot + j], 0, 0)),
            pl.BlockSpec((1, 1, RANK_UNIT, local), lambda j, m: (j + skip, m[first_slot + j], 0, 0)),
        ]
        + [IN_PLACE] * len(after),
        (
            pl.BlockSpec((1, rows, local), lambda j, m: (j, 0, 0)),
            pl.BlockSpec((1, RANK_UNIT, rows), lambda j, m: (j, 0, 0)),
        ),
        (shaped((count, rows, local), LOW), shaped((count, RANK_UNIT, rows), LOW)),
        [],
        2 * rows * width * local * count,
        2 * (weights.size + act.size + count * rows * local),
        name,
        (meta, act, weights, down, up, *after),
    )


def project_back_body(_, last, grad_ref, weight_ref, down_ref, up_ref, after_ref, out_ref, total_ref):
    step = pl.program_id(0)
    grad = grad_ref[0]
    grad_rank = low_rank(up_ref[0, 0], grad)
    part = mm_nt(grad, weight_ref[0]) + mm_tn(grad_rank, down_ref[0, 0])

    @pl.when(step == 0)
    def _():
        total_ref[...] = part

    @pl.when(step > 0)
    def _():
        total_ref[...] += part

    @pl.when(step == last)
    def _():
        out_ref[...] = total_ref[...].astype(out_ref.dtype)


def project_back_heads(meta, grads, weights, down, up, slots, skip, kind, name, after, part=(0, 1)):
    count, width, local = weights.shape
    which, parts = part
    rows = grads.shape[1] // parts
    return call(
        lambda m, *refs: project_back_body(m, count - 1, *refs),
        (count,),
        [
            pl.BlockSpec((1, rows, local), lambda j, m: (j, which, 0)),
            pl.BlockSpec((1, width, local), lambda j, m: (j, 0, 0)),
            pl.BlockSpec((1, 1, RANK_UNIT, width), lambda j, m: (j + skip, m[slots + j], 0, 0)),
            pl.BlockSpec((1, 1, RANK_UNIT, local), lambda j, m: (j + skip, m[slots + j], 0, 0)),
            IN_PLACE,
        ],
        whole((rows, width)),
        shaped((rows, width), kind),
        [pltpu.VMEM((rows, width), WIDE)],
        2 * rows * width * local * count,
        2 * (weights.size + count * rows * local) + 4 * rows * width,
        name,
        (meta, grads, weights, down, up, after),
    )


def first_grads_body(meta, count, parts, *refs):
    ups = refs[2 * parts : 2 * parts + count]
    mine_ref, theirs_ref, ga, act_scratch, grad_scratch, sems = refs[-6:]
    half = ga.shape[1] // 2
    copies = []
    for part in range(parts):
        pairs = ((refs[parts + part], grad_scratch.at[part]), (refs[part], act_scratch.at[part]))
        copies.append(
            [pltpu.make_async_copy(*pair, sems.at[2 * part + number]) for number, pair in enumerate(pairs)]
        )
        for copy in copies[-1]:
            copy.start()
    for part in range(parts):
        copies[part][0].wait()
        grad_rank = jnp.concatenate(
            [low_rank(ups[j][0, 0], grad_scratch[part, j]) for j in range(count)], axis=0
        )
        copies[part][1].wait()
        product = mm(grad_rank, act_scratch[part])
        if part == 0:
            ga[...] = product
        else:
            ga[...] += product
    side = meta[10]
    for j in range(count):
        rows = slice(RANK_UNIT * j, RANK_UNIT * (j + 1))
        span = slice(j * half, (j + 1) * half)
        mine_ref[:, span] = ga[rows, pl.ds(pl.multiple_of(side * half, 128), half)]
        theirs = ga[rows, pl.ds(pl.multiple_of((1 - side) * half, 128), half)]
        theirs_ref[:, span] = theirs.astype(LOW)


def first_grads(meta, acts, grads, up, slots, name):
    rows, width = acts[0].shape
    count, _, local = grads[0].shape
    parts = len(acts)

    def table(j):
        return pl.BlockSpec(
            (1, 1, RANK_UNIT, local), lambda t, m: (j, m[slots + j], 0, 0), pipeline_mode=pl.Buffered(1)
        )

    shape = (RANK_UNIT, count * width // 2)
    return call(
        lambda m, *refs: first_grads_body(m, count, parts, *refs),
        (1,),
        [IN_PLACE] * (2 * parts) + [table(j) for j in range(count)],
        (whole(shape), whole(shape)),
        (shaped(shape, WIDE), shaped(shape, LOW)),
        [
            pltpu.VMEM((RANK_UNIT * count, width), WIDE),
            pltpu.VMEM((parts, rows, width), LOW),
            pltpu.VMEM((parts, count, rows, local), LOW),
            pltpu.SemaphoreType.DMA((2 * parts,)),
        ],
        4 * parts * rows * (width + local) * RANK_UNIT * count,
        2 * parts * rows * (width + count * local),
        name,
        (meta, *acts, *grads, *([up] * count)),
    )


def second_grads_body(_, parts, *refs):
    out_ref, grad_scratch, sems = refs[-3:]
    count, _, local = refs[parts].shape
    copies = [
        pltpu.make_async_copy(refs[parts + part].at[j], grad_scratch.at[part, j], sems.at[part * count + j])
        for part in range(parts)
        for j in range(count)
    ]
    for j in range(count):
        for part in range(parts):
            copies[part * count + j].start()
    for j in range(count):
        total = None
        for part in range(parts):
            copies[part * count + j].wait()
            product = mm(refs[part][j], grad_scratch[part, j])
            total = product if total is None else total + product
        out_ref[:, j * local : (j + 1) * local] = total.astype(LOW)


def second_grads(meta, ranks, grads, name, after):
    count, rows, local = grads[0].shape
    parts = len(ranks)
    shape = (RANK_UNIT, count * local)
    return call(
        lambda m, *refs: second_grads_body(m, parts, *refs),
        (1,),
        [whole(ranks[0].shape)] * parts + [IN_PLACE] * (parts + 1),
        whole(shape),
        shaped(shape, LOW),
        [pltpu.VMEM((parts, count, rows, local), LOW), pltpu.SemaphoreType.DMA((parts * count,))],
        2 * parts * rows * local * RANK_UNIT * count,
        2 * parts * rows * count * local,
        name,
        (meta, *ranks, *grads, after),
    )


def split_columns(meta, mine_ref, theirs_ref, first, array, skip=0):
    half = array.shape[-1] // 2
    side = meta[10]
    mine_ref[:, first : first + half] = array[:, pl.ds(pl.multiple_of(side * half, 128), half)]
    theirs = array[:, pl.ds(pl.multiple_of((1 - side) * half, 128), half)]
    theirs_ref[:, skip + first : skip + first + half] = theirs.astype(LOW)


def own_columns(mine_ref, theirs_ref, first, array):
    half = array.shape[-1] // 2
    span = slice(first, first + half)
    mine_ref[:, span] = array[:, :half]
    theirs_ref[:, span] = array[:, half:].astype(LOW)


def join(mine, received):
    both = jnp.concatenate(received, axis=1).astype(WIDE)
    width = both.shape[1]
    return (mine + jnp.pad(both, ((0, 0), (0, mine.shape[1] - width)))).astype(LOW)


def clip_names(label_ref):
    clips, rank, width = label_ref.shape
    return label_ref[...].reshape(clips * rank, width).astype(WIDE).T


def slot_take(names, slots, rank):
    source = lax.broadcasted_iota(jnp.int32, names.shape, 1)
    target = (source & (rank - 1)) + rank * names.astype(jnp.int32)
    place = lax.broadcasted_iota(jnp.int32, (slots * rank, names.shape[1]), 0)
    return jnp.where(place == target, 1.0, 0.0).astype(LOW)


def slot_copies(unit, count, everyone_ref, arrived, in_sems):
    return [
        pltpu.make_async_copy(
            everyone_ref.at[:, :, pl.ds(unit * number, unit)], arrived.at[number], in_sems.at[number]
        )
        for number in range(count)
    ]


def slot_work(plan, slots, carried, everyone_ref, label_ref, earlier, out_refs, scratch, wait=True):
    names, arrived, totals, in_sems, out_sems = scratch
    clips, rank, unit = arrived.shape[1:]
    incoming = slot_copies(unit, len(plan), everyone_ref, arrived, in_sems)
    names[...] = clip_names(label_ref)
    outgoing = []
    for number, (which, ref) in enumerate(zip(carried, earlier)):
        copy = pltpu.make_async_copy(ref.at[0], out_refs[which].at[0], out_sems.at[len(plan) + number])
        copy.start()
        outgoing.append(copy)
    for number, (column, which, place) in enumerate(plan):
        incoming[number].wait()
        take = slot_take(names[column : column + 1], slots, rank)
        total = mm(take, arrived[number].reshape(clips * rank, unit))
        totals[number] = total.reshape(slots, rank, unit)
        out_ref = out_refs[which]
        target = out_ref.at[place] if len(out_ref.shape) == 4 else out_ref.at[:, :, pl.ds(unit * place, unit)]
        copy = pltpu.make_async_copy(totals.at[number], target, out_sems.at[number])
        copy.start()
        outgoing.append(copy)
    if wait:
        for copy in outgoing:
            copy.wait()


def slot_wait(plan, unit, carried, earlier, out_refs, scratch):
    totals, out_sems = scratch[2], scratch[4]
    for number, (which, ref) in enumerate(zip(carried, earlier)):
        pltpu.make_async_copy(ref.at[0], out_refs[which].at[0], out_sems.at[len(plan) + number]).wait()
    for number, (_, which, place) in enumerate(plan):
        pltpu.make_async_copy(totals.at[number], out_refs[which].at[place], out_sems.at[number]).wait()


def slot_scratch(everyone, plan, slots, unit, carried):
    clips, rank, _ = everyone.shape
    units = len(plan)
    return [
        pltpu.VMEM((2 * HEAD_DIM, clips * rank), WIDE),
        pltpu.VMEM((units, clips, rank, unit), LOW),
        pltpu.VMEM((units, slots, rank, unit), WIDE),
        pltpu.SemaphoreType.DMA((units,)),
        pltpu.SemaphoreType.DMA((units + len(carried),)),
    ]


def slot_specs(labelled, carried):
    clips, rank, total = labelled.shape
    label_width = 2 * HEAD_DIM
    return [IN_PLACE, whole((clips, rank, label_width), (0, 0, total // label_width - 1))] + [
        whole(array.shape) for array in carried.values()
    ]


def slot_shapes(everyone, outs, slots):
    rank = everyone.shape[1]
    return tuple(
        shaped((slots, rank, width) if stack is None else (stack, slots, rank, width), WIDE)
        for stack, width in outs
    )


def slot_sum_body(_, plan, slots, carried, outs, everyone_ref, label_ref, *refs):
    scratch = refs[-5:]
    for copy in slot_copies(scratch[1].shape[3], len(plan), everyone_ref, scratch[1], scratch[3]):
        copy.start()
    slot_work(
        plan, slots, carried, everyone_ref, label_ref, refs[: len(carried)], refs[-5 - outs : -5], scratch
    )


def slot_sums(meta, everyone, plan, outs, slots, unit, carried, name, after):
    return call(
        lambda m, *refs: slot_sum_body(m, plan, slots, tuple(carried), len(outs), *refs),
        (1,),
        slot_specs(everyone, carried) + [IN_PLACE] * len(after),
        (IN_PLACE,) * len(outs),
        slot_shapes(everyone, outs, slots),
        slot_scratch(everyone, plan, slots, unit, carried),
        0,
        2 * everyone.size,
        name,
        (meta, everyone, everyone, *carried.values(), *after),
    )


def causal_keep(rows):
    key_at = lax.broadcasted_iota(jnp.int32, (rows, rows), 0)
    return key_at <= lax.broadcasted_iota(jnp.int32, (rows, rows), 1)


def turned(rows):
    return rows.astype(WIDE).T.astype(LOW)


def forward_block(query, keys, value_turned, diagonal, earlier=None):
    score = mm_nt(keys, query)
    if diagonal:
        score = jnp.where(causal_keep(score.shape[0]), score, -1e30)
    largest = jnp.max(score, axis=0, keepdims=True)
    if earlier is not None:
        largest = jnp.maximum(largest, earlier[0])
    mixed = mm(value_turned, jnp.exp(score - largest).astype(LOW))
    if earlier is not None:
        mixed = mixed + earlier[1] * jnp.exp(earlier[0] - largest)
    return largest, mixed


def values_of(rows_ref):
    values = turned(rows_ref[2])
    ones = jnp.ones((RANK_UNIT, values.shape[1]), LOW)
    return [
        jnp.concatenate([values[HEAD_DIM * which : HEAD_DIM * (which + 1)], ones], axis=0)
        for which in (0, 1)
    ]


def forward_finish(blocks, out_ref, log_ref):
    mixes = []
    totals = []
    for largest, mixed in blocks:
        summed = mixed[HEAD_DIM : HEAD_DIM + 1]
        mixes.append(mixed[:HEAD_DIM] * (1.0 / summed))
        totals.append(jnp.broadcast_to(jnp.log(summed) + largest, (HEAD_DIM, summed.shape[1])))
    out_ref[...] = jnp.concatenate(mixes, axis=0).T.astype(LOW)
    log_ref[...] = jnp.concatenate(totals, axis=0).T


MIXED_ROWS = HEAD_DIM + RANK_UNIT
PART_ROWS = MIXED_ROWS + 8


def self_forward_own_body(_, own_ref, part_ref):
    masks = half_masks()
    query = own_ref[0] * jnp.asarray(HEAD_DIM**-0.5, LOW)
    values = values_of(own_ref)
    for which in (0, 1):
        largest, mixed = forward_block(query * masks[which], own_ref[1], values[which], True)
        part_ref[0, which, :MIXED_ROWS] = mixed
        part_ref[0, which, MIXED_ROWS:] = jnp.broadcast_to(largest, (8, largest.shape[1]))


def self_forward_own(meta, own, after):
    _, half, local = own.shape
    pair = 2 * HEAD_DIM
    shape = (local // pair, 2, PART_ROWS, half)
    return call(
        lambda m, own_ref, after_ref, part_ref: self_forward_own_body(m, own_ref, part_ref),
        (local // pair,),
        [pl.BlockSpec((3, half, pair), lambda p, m: (0, 0, p)), IN_PLACE],
        pl.BlockSpec((1,) + shape[1:], lambda p, m: (p, 0, 0, 0)),
        shaped(shape, WIDE),
        [],
        4 * half * half * local,
        10 * half * local,
        "self_forward_own",
        (meta, own, after),
    )


def self_forward_body(
    meta, part_ref, own_ref, other_ref, out_own_ref, out_other_ref, log_own_ref, log_other_ref, keys, values, queries
):
    side = meta[10]
    masks = half_masks()
    for slot, ref in ((0, own_ref), (1, other_ref)):
        keys[slot] = ref[1]
        queries[slot] = ref[0] * jnp.asarray(HEAD_DIM**-0.5, LOW)
        for which, value in enumerate(values_of(ref)):
            values[slot, which] = value
    blocks = []
    for which in (0, 1):
        own = (part_ref[0, which, MIXED_ROWS : MIXED_ROWS + 1], part_ref[0, which, :MIXED_ROWS])
        other = forward_block(queries[1] * masks[which], keys[1], values[1, which], True)
        earlier = (jnp.where(side == 0, other[0], own[0]), jnp.where(side == 0, other[1], own[1]))
        later = forward_block(
            queries[1 - side] * masks[which], keys[side], values[side, which], False, earlier
        )
        blocks.append(
            (
                (jnp.where(side == 0, own[0], later[0]), jnp.where(side == 0, own[1], later[1])),
                (jnp.where(side == 0, later[0], other[0]), jnp.where(side == 0, later[1], other[1])),
            )
        )
    forward_finish([blocks[0][0], blocks[1][0]], out_own_ref, log_own_ref)
    forward_finish([blocks[0][1], blocks[1][1]], out_other_ref, log_other_ref)


def self_forward(meta, part, own, other):
    _, half, local = own.shape
    pair = 2 * HEAD_DIM
    three = pl.BlockSpec((3, half, pair), lambda p, m: (0, 0, p))
    one = pl.BlockSpec((half, pair), lambda p, m: (0, p))
    rows = shaped((half, local), LOW)
    logs = shaped((half, local), WIDE)
    return call(
        self_forward_body,
        (local // pair,),
        [pl.BlockSpec((1,) + part.shape[1:], lambda p, m: (p, 0, 0, 0)), three, three],
        (one, one, one, one),
        (rows, rows, logs, logs),
        [
            pltpu.VMEM((2, half, pair), LOW),
            pltpu.VMEM((2, 2, MIXED_ROWS, half), LOW),
            pltpu.VMEM((2, half, pair), LOW),
        ],
        12 * half * half * local,
        20 * half * local,
        "self_forward",
        (meta, part, own, other),
    )


def three_parts(column):
    high = column.astype(LOW)
    rest = column - high.astype(WIDE)
    middle = rest.astype(LOW)
    return high, middle, (rest - middle.astype(WIDE)).astype(LOW)


def back_prepare_keys(slot, rows_ref, scratch):
    key_turned, _, _, _, key_wide, _, value_wide = scratch
    lane = lax.broadcasted_iota(jnp.int32, (1, 2 * HEAD_DIM), 1)
    key_turned[slot] = turned(rows_ref[1])
    for which in (0, 1):
        spare = HEAD_DIM * (1 - which)
        marked = jnp.where((lane >= spare) & (lane < spare + 3), 1.0, 0.0).astype(LOW)
        key_wide[slot, which] = rows_ref[1] * (1 - marked) + marked
        value_wide[slot, which] = rows_ref[2] * (1 - marked) + marked


def back_prepare_queries(slot, rows_ref, mixed_ref, logs_ref, grad_refs, scratch):
    _, query_turned, grad_turned, query_wide, _, grad_wide, _ = scratch
    masks = half_masks()
    lane = lax.broadcasted_iota(jnp.int32, (1, 2 * HEAD_DIM), 1)
    grad = jnp.concatenate([ref[...] for ref in grad_refs], axis=0)
    product = grad.astype(WIDE) * mixed_ref[...].astype(WIDE)
    query = rows_ref[0] * jnp.asarray(HEAD_DIM**-0.5, LOW)
    logs = logs_ref[...]
    query_turned[slot] = turned(query)
    grad_turned[slot] = turned(grad)
    for which in (0, 1):
        spare = HEAD_DIM * (1 - which)
        marks = [jnp.where(lane == spare + i, 1.0, 0.0).astype(LOW) for i in range(3)]
        inner = jnp.sum(product * masks[which].astype(WIDE), axis=-1, keepdims=True)
        query_rows = query * masks[which]
        for part, mark in zip(three_parts(logs[:, HEAD_DIM * which : HEAD_DIM * which + 1]), marks):
            query_rows = query_rows - part * mark
        query_wide[slot, which] = query_rows
        grad_rows = grad * masks[which]
        for part, mark in zip(three_parts(inner), marks):
            grad_rows = grad_rows - part * mark
        grad_wide[slot, which] = grad_rows


def back_block(queries, query_slot, keys, key_slot, diagonal, totals):
    _, query_turned, grad_turned, query_wide, _, grad_wide, _ = queries
    key_turned, _, _, _, key_wide, _, value_wide = keys
    half = key_turned.shape[2]
    for which in (0, 1):
        head = slice(HEAD_DIM * which, HEAD_DIM * (which + 1))
        score = mm_nt(key_wide[0, which], query_wide[0, which])
        if diagonal:
            score = jnp.where(causal_keep(half), score, -1e30)
        prob = jnp.exp(score)
        prob_grad = mm_nt(value_wide[0, which], grad_wide[0, which])
        score_grad = (prob * prob_grad).astype(LOW)
        totals[2, key_slot, head] += mm_nt(grad_turned[0, head], prob.astype(LOW))
        totals[1, key_slot, head] += mm_nt(query_turned[0, head], score_grad)
        totals[0, query_slot, head] += mm(key_turned[0, head], score_grad)


def self_back_own_body(_, own_ref, z_ref, log_ref, grad_ref, out_ref, *refs):
    prepared = refs[:-1]
    totals = refs[-1]
    totals[...] = jnp.zeros_like(totals)
    back_prepare_keys(0, own_ref, prepared)
    back_prepare_queries(0, own_ref, z_ref, log_ref, (grad_ref,), prepared)
    back_block(prepared, 0, prepared, 0, True, totals)
    out_ref[...] = totals[:, 0]


def prepared_specs(half):
    pair = 2 * HEAD_DIM
    return (pl.BlockSpec((1, pair, half), lambda p, m: (0, p, 0)),) * 3 + (
        pl.BlockSpec((1, 2, half, pair), lambda p, m: (0, 0, 0, p)),
    ) * 4


def self_back_own(meta, own, z_own, log_own, grad_own):
    _, half, local = own.shape
    pair = 2 * HEAD_DIM
    three = pl.BlockSpec((3, half, pair), lambda p, m: (0, 0, p))
    one = pl.BlockSpec((half, pair), lambda p, m: (0, p))
    return call(
        self_back_own_body,
        (local // pair,),
        [three, one, one, one],
        (pl.BlockSpec((3, pair, half), lambda p, m: (0, p, 0)),) + prepared_specs(half),
        (shaped((3, local, half), WIDE),)
        + (shaped((1, local, half), LOW),) * 3
        + (shaped((1, 2, half, local), LOW),) * 4,
        [pltpu.VMEM((3, 1, pair, half), WIDE)],
        100 * half * half * local,
        50 * half * local,
        "self_back_own",
        (meta, own, z_own, log_own, grad_own),
    )


def self_back_body(
    meta,
    part_ref,
    *refs,
):
    own = refs[:7]
    other_ref, z_ref, log_ref, grad_first_ref, grad_second_ref, _, out_own_ref, out_other_ref = refs[7:15]
    other = refs[15:22]
    totals = refs[22]
    side = meta[10]
    totals[:, 0] = part_ref[...]
    totals[:, 1] = jnp.zeros_like(totals[:, 1])
    back_prepare_keys(0, other_ref, other)
    back_prepare_queries(0, other_ref, z_ref, log_ref, (grad_first_ref, grad_second_ref), other)
    back_block(other, 1, other, 1, True, totals)

    @pl.when(side == 0)
    def _():
        back_block(other, 1, own, 0, False, totals)

    @pl.when(side != 0)
    def _():
        back_block(own, 0, other, 1, False, totals)

    for slot, ref in ((0, out_own_ref), (1, out_other_ref)):
        ref[0] = (totals[0, slot].T * HEAD_DIM**-0.5).astype(LOW)
        ref[1] = totals[1, slot].T.astype(LOW)
        ref[2] = totals[2, slot].T.astype(LOW)


def self_back(meta, part, prepared, other, z_other, log_other, grads_other, after):
    _, half, local = other.shape
    pair = 2 * HEAD_DIM
    three = pl.BlockSpec((3, half, pair), lambda p, m: (0, 0, p))
    one = pl.BlockSpec((half, pair), lambda p, m: (0, p))
    return call(
        self_back_body,
        (local // pair,),
        [pl.BlockSpec((3, pair, half), lambda p, m: (0, p, 0)), *prepared_specs(half), three, one, one]
        + [pl.BlockSpec((half // 2, pair), lambda p, m: (0, p))] * 2
        + [IN_PLACE],
        (three, three),
        (shaped(other.shape, LOW), shaped(other.shape, LOW)),
        [pltpu.VMEM((1, pair, half), LOW)] * 3
        + [pltpu.VMEM((1, 2, half, pair), LOW)] * 4
        + [pltpu.VMEM((3, 2, pair, half), WIDE)],
        200 * half * half * local,
        60 * half * local,
        "self_back",
        (meta, part, *prepared, other, z_other, log_other, *grads_other, after),
    )


def halves_of(ref, local):
    step = ref.shape[1] // 2
    return (
        ref[:, :step, :].reshape(local, ref.shape[2]),
        ref[:, step:, :].reshape(local, ref.shape[2]),
    )


def full_of(ref):
    return ref[...].reshape(ref.shape[0] * ref.shape[1], ref.shape[2])


def fetch_weights(step, order, sources, gathered, held, sems, between=()):
    copies = {}
    for which in order:
        copies[which] = (
            pltpu.make_async_copy(sources[which], held[2 * which], sems.at[2 * which]),
            pltpu.make_async_copy(gathered.at[:, which], held[2 * which + 1], sems.at[2 * which + 1]),
        )

    @pl.when(step == 0)
    def _():
        for place, which in enumerate(order):
            for copy in copies[which]:
                copy.start()
            for copy in between[place] if between else ():
                copy.start()

    def ready(which):
        @pl.when(step == 0)
        def _():
            for copy in copies[which]:
                copy.wait()

        return held[2 * which], held[2 * which + 1]

    return ready


TILE_HEADS = 4


def tile_span(tile):
    return slice(TILE_HEADS * HEAD_DIM * tile, TILE_HEADS * HEAD_DIM * (tile + 1))


def tile_masks():
    lane = lax.broadcasted_iota(jnp.int32, (1, TILE_HEADS * HEAD_DIM), 1)
    return [jnp.where(lane // HEAD_DIM == head, 1.0, 0.0).astype(LOW) for head in range(TILE_HEADS)]


def text_tile(rows, tile, masks):
    part = rows[:, tile_span(tile)]
    return jnp.concatenate([part * mask for mask in masks], axis=0)


def by_head(values, reduce):
    keys, rows = values.shape
    apart = values.reshape(TILE_HEADS, keys // TILE_HEADS, rows)
    reduced = reduce(apart, axis=1, keepdims=True)
    return jnp.broadcast_to(reduced, apart.shape).reshape(keys, rows)


def text_weights(key_tile, query):
    scores = mm_nt(key_tile, query)
    weights = jnp.exp(scores - by_head(scores, jnp.max))
    return weights * (1.0 / by_head(weights, jnp.sum))


def mix_text(query, keys, values):
    masks = tile_masks()
    mixed = []
    for tile in range(query.shape[1] // (TILE_HEADS * HEAD_DIM)):
        one_query = query[:, tile_span(tile)] * jnp.asarray(HEAD_DIM**-0.5, LOW)
        weights = text_weights(text_tile(keys, tile, masks), one_query)
        mixed.append(mm_tn(weights.astype(LOW), text_tile(values, tile, masks)).astype(LOW))
    return jnp.concatenate(mixed, axis=1)


def middle_forward_body(
    _,
    x_ref,
    z_own_ref,
    z_other_ref,
    out_weight_ref,
    query_weight_ref,
    cross_weight_ref,
    gathered_ref,
    down3_ref,
    down3_other_ref,
    up3_ref,
    down4_ref,
    up4_ref,
    up4_other_ref,
    down7_ref,
    down7_other_ref,
    up7_ref,
    text_own_ref,
    text_other_ref,
    gain_two_ref,
    gain_three_ref,
    stream_one_ref,
    stream_two_ref,
    rows_three_ref,
    query_out_own_ref,
    query_out_other_ref,
    z2_own_ref,
    z2_other_ref,
    rank3_ref,
    rank4_ref,
    rank7_ref,
    *scratch,
):
    local = z_own_ref.shape[1]
    ready = fetch_weights(
        pl.program_id(0),
        (0, 1, 2),
        (out_weight_ref, query_weight_ref, cross_weight_ref),
        gathered_ref,
        scratch[:6],
        scratch[6],
    )

    def out_product(own, other, which, down, down_other, up, rank_ref):
        rank = (mm_nt(down, own) + mm_nt(down_other, other)).astype(LOW)
        rank_ref[...] = rank
        weight_own, weight_other_ref = ready(which)
        first, second = halves_of(weight_other_ref, local)
        product = mm(own, weight_own[...]) + mm_tn(rank, up)
        return product + jnp.concatenate([mm(other, first), mm(other, second)], axis=1)

    stream = x_ref[...].astype(WIDE) + out_product(
        z_own_ref[...],
        z_other_ref[...],
        0,
        down3_ref[0, 0],
        down3_other_ref[...],
        up3_ref[0, 0],
        rank3_ref,
    )
    stream_one_ref[...] = stream
    rows_two = norm_rows(stream, gain_two_ref[...])[0].astype(LOW)
    rank = low_rank(down4_ref[0, 0], rows_two)
    rank4_ref[...] = rank
    query_own_ref, query_other_ref = ready(1)
    query_own = (mm(rows_two, query_own_ref[...]) + mm_tn(rank, up4_ref[0, 0])).astype(LOW)
    query_other = (
        mm(rows_two, full_of(query_other_ref)) + mm_tn(rank, up4_other_ref[...])
    ).astype(LOW)
    query_out_own_ref[...] = query_own
    query_out_other_ref[...] = query_other
    z2_own = mix_text(query_own, text_own_ref[0], text_own_ref[1])
    z2_other = mix_text(query_other, text_other_ref[0], text_other_ref[1])
    z2_own_ref[...] = z2_own
    z2_other_ref[...] = z2_other
    stream = stream + out_product(
        z2_own,
        z2_other,
        2,
        down7_ref[0, 0],
        down7_other_ref[...],
        up7_ref[0, 0],
        rank7_ref,
    )
    stream_two_ref[...] = stream
    rows_three_ref[...] = norm_rows(stream, gain_three_ref[...])[0].astype(LOW)


def chosen(table, entry, slot):
    shape = (1, 1) + table.shape[2:]
    return pl.BlockSpec(
        shape, lambda t, m: (entry, m[slot], 0, 0), pipeline_mode=pl.Buffered(1)
    )


def middle_specs(weights, gathered, tables, packed):
    attention_down, attention_up, cross_down, cross_up = tables
    rank = (RANK_UNIT, gathered.shape[3])
    specs = [
        IN_PLACE,
        IN_PLACE,
        IN_PLACE,
        IN_PLACE,
        chosen(attention_down, 0, 3),
        whole(rank, (0, 0)),
        chosen(attention_up, 0, 3),
        chosen(cross_down, 0, 4),
        chosen(cross_up, 0, 4),
        whole(rank, (0, 2)),
        chosen(attention_down, 1, 7),
        whole(rank, (0, 1)),
        chosen(attention_up, 1, 7),
    ]
    args = weights + (
        gathered,
        attention_down,
        packed,
        attention_up,
        cross_down,
        cross_up,
        packed,
        attention_down,
        packed,
        attention_up,
    )
    return specs, args


def middle_scratch(weights, gathered):
    shards, _, depth, local = gathered.shape
    held = []
    for weight in weights:
        held += [pltpu.VMEM(weight.shape, LOW), pltpu.VMEM((shards, depth, local), LOW)]
    return held + [pltpu.SemaphoreType.DMA((2 * len(weights),))]


def middle_forward(meta, x, z_own, z_other, weights, gathered, tables, packed, text_own, text_other, gains):
    frames, width = x.shape
    local = z_own.shape[1]
    block = min(512, frames)
    wide = pl.BlockSpec((block, width), lambda t, m: (t, 0))
    narrow = pl.BlockSpec((block, local), lambda t, m: (t, 0))
    ranks = pl.BlockSpec((RANK_UNIT, block), lambda t, m: (0, t))
    specs, args = middle_specs(weights, gathered, tables, packed)
    return call(
        middle_forward_body,
        (frames // block,),
        [wide, narrow, narrow]
        + specs
        + [whole(text_own.shape), whole(text_other.shape), whole((1, width)), whole((1, width))],
        (wide, wide, wide, narrow, narrow, narrow, narrow) + (ranks,) * 3,
        (
            shaped((frames, width), WIDE),
            shaped((frames, width), WIDE),
            shaped((frames, width), LOW),
            shaped((frames, local), LOW),
            shaped((frames, local), LOW),
            shaped((frames, local), LOW),
            shaped((frames, local), LOW),
        )
        + (shaped((RANK_UNIT, frames), LOW),) * 3,
        middle_scratch(weights, gathered),
        6 * frames * width * width,
        6 * width * width + 20 * frames * width,
        "middle_forward",
        (meta, x, z_own, z_other) + args + (text_own, text_other) + gains,
    )


def middle_back_body(
    meta,
    last,
    grad_ref,
    stream_one_ref,
    z_own_ref,
    z_other_ref,
    query_in_own_ref,
    query_in_other_ref,
    z2_own_ref,
    z2_other_ref,
    out_weight_ref,
    query_weight_ref,
    cross_weight_ref,
    gathered_ref,
    down3_ref,
    down3_other_ref,
    up3_ref,
    down4_ref,
    up4_ref,
    up4_other_ref,
    down7_ref,
    down7_other_ref,
    up7_ref,
    text_own_ref,
    text_other_ref,
    gain_two_ref,
    text_ref,
    down5_ref,
    down6_ref,
    up5_ref,
    up6_ref,
    up5_other_ref,
    up6_other_ref,
    rank3_ref,
    rank4_ref,
    rank7_ref,
    grad_one_ref,
    dz_own_ref,
    dz_first_ref,
    dz_second_ref,
    text_grad_own_ref,
    mine_ref,
    theirs_ref,
    text_mine_ref,
    text_theirs_ref,
    key_total,
    value_total,
    ga3_ref,
    gb3_ref,
    ga4_ref,
    gb4_ref,
    ga7_ref,
    gb7_ref,
    *scratch,
):
    step = pl.program_id(0)
    late = scratch[7:12]
    late_sems = scratch[13]
    late_copies = [
        pltpu.make_async_copy(source, target, late_sems.at[number])
        for number, (source, target) in enumerate(
            zip((query_in_own_ref, query_in_other_ref, stream_one_ref, z_own_ref, z_other_ref), late)
        )
    ]
    query_in_own_ref, query_in_other_ref, stream_one_ref, z_own_ref, z_other_ref = late
    grad_one_copy = pltpu.make_async_copy(scratch[12], grad_one_ref, late_sems.at[5])
    ready = fetch_weights(
        step,
        (2, 1, 0),
        (out_weight_ref, query_weight_ref, cross_weight_ref),
        gathered_ref,
        scratch[:6],
        scratch[6],
        (late_copies[:2], late_copies[2:], ()),
    )
    local = z_own_ref.shape[1]
    tiles = local // (TILE_HEADS * HEAD_DIM)
    masks = tile_masks()
    scale = jnp.asarray(HEAD_DIM**-0.5, LOW)

    @pl.when(step == 0)
    def _():
        key_total[...] = jnp.zeros_like(key_total)
        value_total[...] = jnp.zeros_like(value_total)
        for ref in (ga3_ref, gb3_ref, ga4_ref, gb4_ref, ga7_ref, gb7_ref):
            ref[...] = jnp.zeros_like(ref)

    def out_back(grad, own, other, which, down, down_other, up, ga_ref, gb_ref, rank):
        grad_rank = low_rank(up, grad)
        ga_ref[:, :local] += mm(grad_rank, own)
        ga_ref[:, local:] += mm(grad_rank, other)
        gb_ref[...] += mm(rank, grad)
        weight_own, weight_other_ref = ready(which)
        first, second = halves_of(weight_other_ref, local)
        middle = grad.shape[1] // 2
        grad_own = mm_nt(grad, weight_own[...]) + mm_tn(grad_rank, down)
        grad_other = (
            mm_nt(grad[:, :middle], first)
            + mm_nt(grad[:, middle:], second)
            + mm_tn(grad_rank, down_other)
        )
        return grad_own.astype(LOW), grad_other.astype(LOW)

    grad = grad_ref[...]
    dz2_own, dz2_other = out_back(
        grad.astype(LOW),
        z2_own_ref[...],
        z2_other_ref[...],
        2,
        down7_ref[0, 0],
        down7_other_ref[...],
        up7_ref[0, 0],
        ga7_ref,
        gb7_ref,
        rank7_ref[...],
    )

    def text_back(query, dz2, keys, values, part):
        query_grads = []
        for tile in range(tiles):
            key_tile = text_tile(keys, tile, masks)
            value_tile = text_tile(values, tile, masks)
            one_query = query[:, tile_span(tile)] * scale
            one_grad = dz2[:, tile_span(tile)]
            probs = text_weights(key_tile, one_query)
            prob_grads = mm_nt(value_tile, one_grad)
            inner = by_head(probs * prob_grads, jnp.sum)
            score_grads = (probs * (prob_grads - inner)).astype(LOW)
            query_grads.append((mm_tn(score_grads, key_tile) * HEAD_DIM**-0.5).astype(LOW))
            key_total[part, tile] += mm(score_grads, one_query)
            value_total[part, tile] += mm(probs.astype(LOW), one_grad)
        return jnp.concatenate(query_grads, axis=1)

    for copy in late_copies[:2]:
        copy.wait()
    dq_own = text_back(query_in_own_ref[...], dz2_own, text_own_ref[0], text_own_ref[1], 0)
    dq_other = text_back(query_in_other_ref[...], dz2_other, text_other_ref[0], text_other_ref[1], 1)

    for copy in late_copies[2:]:
        copy.wait()
    rows_two, normed, inverse = norm_rows(stream_one_ref[...], gain_two_ref[...])
    rows_two = rows_two.astype(LOW)
    rank = rank4_ref[...]
    grad_rank = (mm_nt(up4_ref[0, 0], dq_own) + mm_nt(up4_other_ref[...], dq_other)).astype(LOW)
    ga4_ref[...] += mm(grad_rank, rows_two)
    gb4_ref[:, :local] += mm(rank, dq_own)
    gb4_ref[:, local:] += mm(rank, dq_other)
    query_own_ref, query_other_ref = ready(1)
    grad_rows = (
        mm_nt(dq_own, query_own_ref[...])
        + mm_nt(dq_other, full_of(query_other_ref))
        + mm_tn(grad_rank, down4_ref[0, 0])
    )
    grad = grad + norm_back(grad_rows, gain_two_ref[...], normed, inverse)
    scratch[12][...] = grad
    grad_one_copy.start()
    dz_own, dz_other = out_back(
        grad.astype(LOW),
        z_own_ref[...],
        z_other_ref[...],
        0,
        down3_ref[0, 0],
        down3_other_ref[...],
        up3_ref[0, 0],
        ga3_ref,
        gb3_ref,
        rank3_ref[...],
    )
    dz_own_ref[...] = dz_own
    half = dz_first_ref.shape[0]
    dz_first_ref[...] = dz_other[:half]
    dz_second_ref[...] = dz_other[half:]
    grad_one_copy.wait()

    @pl.when(step == last)
    def _():
        split_columns(meta, mine_ref, theirs_ref, 0, ga4_ref)
        own_columns(mine_ref, theirs_ref, local, gb4_ref)
        own_columns(mine_ref, theirs_ref, 2 * local, ga3_ref)
        own_columns(mine_ref, theirs_ref, 3 * local, ga7_ref)
        split_columns(meta, mine_ref, theirs_ref, 4 * local, gb3_ref)
        split_columns(meta, mine_ref, theirs_ref, 5 * local, gb7_ref)
        texts = text_ref.shape[0]
        for slot, total in enumerate((key_total, value_total)):
            for part in (0, 1):
                for tile in range(tiles):
                    stacked = total[part, tile]
                    rows = 0.0
                    for head, mask in enumerate(masks):
                        rows = rows + stacked[HEAD_DIM * head : HEAD_DIM * (head + 1)] * mask.astype(WIDE)
                    if part == 0:
                        text_grad_own_ref[slot, :, tile_span(tile)] = rows
                    else:
                        text_theirs_ref[texts * slot : texts * (slot + 1), tile_span(tile)] = rows.astype(LOW)
        text = text_ref[...]
        factors = ((down5_ref, up5_ref, up5_other_ref), (down6_ref, up6_ref, up6_other_ref))
        for slot, (down_ref, up_ref, up_other_ref) in enumerate(factors):
            grad_own = text_grad_own_ref[slot].astype(LOW)
            grad_other = text_theirs_ref[texts * slot : texts * (slot + 1)]
            rank = low_rank(down_ref[0, 0], text)
            grad_rank = mm_nt(up_ref[0, 0], grad_own) + mm_nt(up_other_ref[...], grad_other)
            ga4_ref[...] = mm(grad_rank.astype(LOW), text)
            first = slice(2 * texts + RANK_UNIT * slot, 2 * texts + RANK_UNIT * (slot + 1))
            second = slice(2 * texts + RANK_UNIT * (2 + slot), 2 * texts + RANK_UNIT * (3 + slot))
            split_columns(meta, text_mine_ref.at[:, pl.ds(slot * local, local)], text_theirs_ref.at[first], 0, ga4_ref)
            text_mine_ref[:, (2 + slot) * local : (3 + slot) * local] = mm(rank, grad_own)
            text_theirs_ref[second] = mm(rank, grad_other).astype(LOW)


def middle_back(
    meta, grad, stream_one, z_own, z_other, q_own, q_other, z2_own, z2_other,
    weights, gathered, tables, packed, text_own, text_other, gain, text, ranks,
):
    frames, width = grad.shape
    local = z_own.shape[1]
    tiles = local // (TILE_HEADS * HEAD_DIM)
    wide = whole((frames, width))
    narrow = whole((frames, local))
    specs, args = middle_specs(weights, gathered, tables, packed)
    rank = (RANK_UNIT, width)
    packs = (RANK_UNIT, 6 * local)
    text_packs = (RANK_UNIT, 4 * local)
    text_rows = (2 * text.shape[0] + 4 * RANK_UNIT, local)
    _, _, cross_down, cross_up = tables
    return call(
        lambda m, *refs: middle_back_body(m, 0, *refs),
        (1,),
        [wide, IN_PLACE]
        + [IN_PLACE] * 4
        + [narrow] * 2
        + specs
        + [whole(text_own.shape), whole(text_other.shape), whole((1, width)), whole(text.shape)]
        + [chosen(cross_down, 1, 5), chosen(cross_down, 2, 6), chosen(cross_up, 1, 5), chosen(cross_up, 2, 6)]
        + [whole((RANK_UNIT, local), (0, 3)), whole((RANK_UNIT, local), (0, 4))]
        + [whole((RANK_UNIT, frames))] * 3,
        (IN_PLACE, narrow, whole((frames // 2, local)), whole((frames // 2, local)), whole(text_own.shape))
        + (whole(packs), whole(packs), whole(text_packs), whole(text_rows)),
        (
            shaped((frames, width), WIDE),
            shaped((frames, local), LOW),
            shaped((frames // 2, local), LOW),
            shaped((frames // 2, local), LOW),
            shaped(text_own.shape, WIDE),
            shaped(packs, WIDE),
            shaped(packs, LOW),
            shaped(text_packs, WIDE),
            shaped(text_rows, LOW),
        ),
        [
            pltpu.VMEM((2, tiles, TILE_HEADS * HEAD_DIM, TILE_HEADS * HEAD_DIM), WIDE),
            pltpu.VMEM((2, tiles, TILE_HEADS * HEAD_DIM, TILE_HEADS * HEAD_DIM), WIDE),
        ]
        + [pltpu.VMEM(rank, WIDE)] * 6
        + middle_scratch(weights, gathered)
        + [pltpu.VMEM((frames, local), LOW)] * 2
        + [pltpu.VMEM((frames, width), WIDE)]
        + [pltpu.VMEM((frames, local), LOW)] * 2
        + [pltpu.VMEM((frames, width), WIDE), pltpu.SemaphoreType.DMA((6,))],
        6 * frames * width * width,
        6 * width * width + 24 * frames * width,
        "middle_back",
        (meta, grad, stream_one, z_own, z_other, q_own, q_other, z2_own, z2_other)
        + args
        + (text_own, text_other, gain, text)
        + (cross_down, cross_down, cross_up, cross_up, packed, packed)
        + tuple(ranks),
    )


def feed_tile(
    rows_ref, cot_ref, up_weight, down_weight, up_rank, down_rank,
    ga9_ref, gb8_ref, branch, grad_rows, rank9, grad_rank8, rank8, grad_rank9,
):
    frames = rows_ref.shape[0]
    block = min(256, frames)
    low_pre = mm_tn(rank8[...], up_rank)
    low_grad = mm_tn(grad_rank9[...], down_rank)
    hidden_blocks = []
    grad_blocks = []
    for first in range(0, frames, block):
        span = slice(first, first + block)
        pre = mm(rows_ref[span], up_weight) + low_pre[span]
        grad_hidden = mm_nt(cot_ref[span], down_weight) + low_grad[span]
        hidden, slope = gelu_parts(pre)
        hidden = hidden.astype(LOW)
        grad_pre = (grad_hidden * slope).astype(LOW)
        branch[span] += mm(hidden, down_weight)
        grad_rows[span] += mm_nt(grad_pre, up_weight)
        hidden_blocks.append(hidden)
        grad_blocks.append(grad_pre)
    hidden = jnp.concatenate(hidden_blocks, axis=0)
    grad_pre = jnp.concatenate(grad_blocks, axis=0)
    rank9[...] += mm_nt(down_rank, hidden)
    grad_rank8[...] += mm_nt(up_rank, grad_pre)
    ga9_ref[...] = mm(grad_rank9[...], hidden).astype(ga9_ref.dtype)
    gb8_ref[...] = mm(rank8[...], grad_pre).astype(gb8_ref.dtype)


def feed_own_body(
    _, rows_ref, cot_ref, up_weight_ref, down_weight_ref, up_rank_ref, down_rank_ref,
    down8_ref, up9_ref,
    branch_ref, grad_rows_ref, rank9_ref, grad_rank8_ref, rank8, grad_rank9, ga9_ref, gb8_ref,
):
    @pl.when(pl.program_id(0) == 0)
    def _():
        rank8[...] = low_rank(down8_ref[0], rows_ref[...])
        grad_rank9[...] = low_rank(up9_ref[0], cot_ref[...])
        for ref in (branch_ref, grad_rows_ref, rank9_ref, grad_rank8_ref):
            ref[...] = jnp.zeros_like(ref)

    feed_tile(
        rows_ref, cot_ref, up_weight_ref[...], down_weight_ref[...], up_rank_ref[0], down_rank_ref[0],
        ga9_ref, gb8_ref, branch_ref, grad_rows_ref, rank9_ref, grad_rank8_ref, rank8, grad_rank9,
    )


def table_tile(tile, slot):
    return pl.BlockSpec((1, RANK_UNIT, tile), lambda t, m: (m[slot], 0, t))


def feed_own(meta, rows, cot, up_weight, down_weight, input_down, input_up, output_down, output_up, tile):
    frames, width = rows.shape
    hidden = up_weight.shape[1]
    grads = pl.BlockSpec((RANK_UNIT, tile), lambda t, m: (0, t))
    picked = pl.BlockSpec((1, RANK_UNIT, width), lambda t, m: (m[8], 0, 0))
    picked_out = pl.BlockSpec((1, RANK_UNIT, width), lambda t, m: (m[9], 0, 0))
    rank = (RANK_UNIT, frames)
    return call(
        feed_own_body,
        (hidden // tile,),
        [
            whole((frames, width)),
            whole((frames, width)),
            pl.BlockSpec((width, tile), lambda t, m: (0, t)),
            pl.BlockSpec((tile, width), lambda t, m: (t, 0)),
            table_tile(tile, 8),
            table_tile(tile, 9),
            picked,
            picked_out,
        ],
        (whole((frames, width)), whole((frames, width))) + (whole(rank),) * 4 + (grads, grads),
        (
            shaped((frames, width), WIDE),
            shaped((frames, width), WIDE),
            shaped(rank, WIDE),
            shaped(rank, WIDE),
            shaped(rank, LOW),
            shaped(rank, LOW),
            shaped((RANK_UNIT, hidden), WIDE),
            shaped((RANK_UNIT, hidden), WIDE),
        ),
        [],
        8 * frames * width * hidden,
        4 * width * hidden + 12 * frames * width,
        "feed_own",
        (meta, rows, cot, up_weight, down_weight, input_up, output_down, input_down, output_up),
    )


def feed_other_body(
    meta, last, rows_ref, cot_ref, up_weight_ref, down_weight_ref, up_rank_ref, down_rank_ref,
    down8_ref, up9_ref, branch_in_ref, grad_rows_in_ref, rank9_in_ref, grad_rank8_in_ref, rank8, grad_rank9,
    stream_ref, gain_ref,
    out_ref, grad_ref, mine_ref, theirs_ref,
    branch, grad_rows, rank9, grad_rank8, ga8_ref, gb9_ref, branch_in, grad_rows_in, stream_in, sems,
    out_held, grad_held, out_sems,
):
    step = pl.program_id(0)
    copies = [
        pltpu.make_async_copy(source, target, sems.at[i])
        for i, (source, target) in enumerate(
            ((branch_in_ref, branch_in), (grad_rows_in_ref, grad_rows_in), (stream_ref, stream_in))
        )
    ]

    @pl.when(step == 0)
    def _():
        for copy in copies:
            copy.start()
        branch[...] = jnp.zeros_like(branch)
        grad_rows[...] = jnp.zeros_like(grad_rows)
        rank9[...] = rank9_in_ref[...]
        grad_rank8[...] = grad_rank8_in_ref[...]

    shards, _, depth, tile = up_weight_ref.shape
    hidden = (last + 1) * tile
    first = pl.multiple_of(step * tile, 128)
    gb8_ref = theirs_ref.at[:, pl.ds(first, tile)]
    ga9_ref = theirs_ref.at[:, pl.ds(pl.multiple_of(hidden + first, 128), tile)]
    up_weight = up_weight_ref[...].reshape(shards * depth, tile)
    down_weight = down_weight_ref[...].reshape(tile, down_weight_ref.shape[3])
    feed_tile(
        rows_ref, cot_ref, up_weight, down_weight, up_rank_ref[...], down_rank_ref[...],
        ga9_ref, gb8_ref, branch, grad_rows, rank9, grad_rank8, rank8, grad_rank9,
    )

    @pl.when(step == last)
    def _():
        for copy in copies:
            copy.wait()
        frames = rows_ref.shape[0]
        block = min(128, frames)
        last8 = grad_rank8[...].astype(LOW)
        last9 = rank9[...].astype(LOW)
        ga8_ref[...] = mm(last8, rows_ref[...])
        gb9_ref[...] = mm(last9, cot_ref[...])
        half = ga8_ref.shape[1] // 2
        split_columns(meta, mine_ref, theirs_ref, 0, ga8_ref, 2 * hidden)
        split_columns(meta, mine_ref, theirs_ref, half, gb9_ref, 2 * hidden)
        flushes = []
        for first in range(0, frames, block):
            span = slice(first, first + block)
            stream = stream_in[span]
            out = stream + (branch[span] + branch_in[span]) + mm_tn(last9[:, span], up9_ref[0])
            out_held[span] = out.astype(LOW)
            flushes.append(pltpu.make_async_copy(out_held.at[span], out_ref.at[span], out_sems.at[len(flushes)]))
            flushes[-1].start()
            _, normed, inverse = norm_rows(stream, gain_ref[...])
            grad = grad_rows[span] + grad_rows_in[span] + mm_tn(last8[:, span], down8_ref[0])
            grad_held[span] = cot_ref[span].astype(WIDE) + norm_back(
                grad, gain_ref[...], normed, inverse
            )
            flushes.append(pltpu.make_async_copy(grad_held.at[span], grad_ref.at[span], out_sems.at[len(flushes)]))
            flushes[-1].start()
        for copy in flushes:
            copy.wait()


def feed_other(
    meta, rows, cot, gathered, packed, first_pack, input_down, output_up, carried, stream, gain, tile
):
    frames, width = rows.shape
    shards, quarters, depth, _ = gathered.shape
    hidden = quarters // 2 * width
    per_half = width // tile
    own_shards = tile // (quarters // 2 * depth)
    down_first = quarters // 2
    picked = pl.BlockSpec((1, RANK_UNIT, width), lambda t, m: (m[8], 0, 0))
    picked_out = pl.BlockSpec((1, RANK_UNIT, width), lambda t, m: (m[9], 0, 0))
    rank = (RANK_UNIT, frames)
    steps = hidden // tile
    full = whole((frames, width))
    wide = pltpu.VMEM((frames, width), WIDE)
    return call(
        lambda m, *refs: feed_other_body(m, steps - 1, *refs),
        (steps,),
        [
            full,
            full,
            pl.BlockSpec(
                (shards, 1, depth, tile),
                lambda t, m: (0, down_first + t // per_half, 0, t % per_half),
            ),
            pl.BlockSpec((own_shards, down_first, depth, width), lambda t, m: (t, 0, 0, 0)),
            pl.BlockSpec((RANK_UNIT, tile), lambda t, m: (0, first_pack // tile + t)),
            pl.BlockSpec((RANK_UNIT, tile), lambda t, m: (0, (first_pack + hidden) // tile + t)),
            picked,
            picked_out,
            IN_PLACE,
            IN_PLACE,
            whole(rank),
            whole(rank),
            whole(rank),
            whole(rank),
            IN_PLACE,
            whole((1, width)),
        ],
        (IN_PLACE, IN_PLACE, whole((RANK_UNIT, width)), whole((RANK_UNIT, 2 * hidden + width))),
        (
            shaped((frames, width), LOW),
            shaped((frames, width), WIDE),
            shaped((RANK_UNIT, width), WIDE),
            shaped((RANK_UNIT, 2 * hidden + width), LOW),
        ),
        [
            wide,
            wide,
            pltpu.VMEM(rank, WIDE),
            pltpu.VMEM(rank, WIDE),
            pltpu.VMEM((RANK_UNIT, width), WIDE),
            pltpu.VMEM((RANK_UNIT, width), WIDE),
            wide,
            wide,
            wide,
            pltpu.SemaphoreType.DMA((3,)),
            pltpu.VMEM((frames, width), LOW),
            wide,
            pltpu.SemaphoreType.DMA((2 * (frames // min(128, frames)),)),
        ],
        8 * frames * width * hidden,
        4 * width * hidden + 24 * frames * width,
        "feed_other",
        (meta, rows, cot, gathered, gathered, packed, packed, input_down, output_up)
        + tuple(carried)
        + (stream, gain),
    )


def last_norm_body(_, half, slot_part, x_ref, own_ref, first_ref, second_ref, grad_ref, gain_ref, *refs):
    plan, slots, carried, outs = slot_part
    step = pl.program_id(0)
    everyone_ref, label_ref = refs[:2]
    earlier = refs[2 : 2 + len(carried)]
    out_ref = refs[-6 - outs]
    scratch = refs[-5:]

    @pl.when(step == 0)
    def _():
        for copy in slot_copies(scratch[1].shape[3], len(plan), everyone_ref, scratch[1], scratch[3]):
            copy.start()

    _, normed, inverse = norm_rows(x_ref[...].astype(WIDE), gain_ref[...])
    other = jnp.where(step < half, first_ref[...].astype(WIDE), second_ref[...].astype(WIDE))
    total = own_ref[...] + other
    out_ref[...] = grad_ref[...] + norm_back(total, gain_ref[...], normed, inverse)

    @pl.when(step == 0)
    def _():
        slot_work(plan, slots, carried, everyone_ref, label_ref, earlier, refs[-5 - outs : -5], scratch, False)

    @pl.when(step == 2 * half - 1)
    def _():
        slot_wait(plan, scratch[1].shape[3], carried, earlier, refs[-5 - outs : -5], scratch)


def last_norm(meta, x, own, received, grad, gain, everyone, labelled, plan, outs, slots, unit, carried, after):
    frames, width = x.shape
    block = min(256, frames // 2)
    half = frames // 2 // block
    rows = pl.BlockSpec((block, width), lambda t, _: (t, 0))
    first = pl.BlockSpec((block, width), lambda t, _: (jnp.minimum(t, half - 1), 0))
    second = pl.BlockSpec((block, width), lambda t, _: (jnp.maximum(t - half, 0), 0))
    slot_part = (plan, slots, tuple(carried), len(outs))
    return call(
        lambda m, *refs: last_norm_body(m, half, slot_part, *refs),
        (2 * half,),
        [rows, rows, first, second, rows, whole((1, width))]
        + slot_specs(labelled, carried)
        + [IN_PLACE] * len(after),
        (rows,) + (IN_PLACE,) * len(outs),
        (shaped(x.shape, WIDE),) + slot_shapes(everyone, outs, slots),
        slot_scratch(everyone, plan, slots, unit, carried),
        20 * x.size,
        16 * x.size,
        "last_norm",
        (meta, x, own, *received, grad, gain, everyone, labelled, *carried.values(), *after),
    )


def on_pair(
    inputs,
    encoder_text_states,
    cotangent,
    clip_adapter_index,
    self_norm_gain,
    cross_norm_gain,
    feed_norm_gain,
    self_query_key_value_weight,
    self_output_weight,
    cross_query_weight,
    cross_key_value_weight,
    cross_output_weight,
    up_weight,
    down_weight,
    self_first_factors,
    self_second_factors,
    cross_first_factors,
    cross_second_factors,
    attention_first_factors,
    attention_second_factors,
    input_first_factors,
    input_second_factors,
    output_first_factors,
    output_second_factors,
):
    x = inputs[0]
    text = encoder_text_states[0]
    cot = cotangent[0]
    width = x.shape[1]
    local = self_output_weight.shape[0]
    hidden = up_weight.shape[1]
    slots = input_first_factors.shape[0]
    group_count = lax.axis_size("dp")
    place = lax.axis_index("dp")
    side = lax.axis_index("tensor")
    picks = clip_adapter_index[0]
    meta = jnp.concatenate([picks, jnp.stack([side, place]).astype(jnp.int32)])
    gain_one, gain_two, gain_three = (
        vec.reshape(1, width) for vec in (self_norm_gain, cross_norm_gain, feed_norm_gain)
    )

    def swap(array):
        return lax.ppermute(array, "tensor", [(0, 1), (1, 0)])

    depth = width // group_count
    step = local // group_count

    def share(weight, size):
        return lax.dynamic_slice_in_dim(weight, place * size, size, axis=0)

    def side_by_side(rows, count):
        return rows.reshape(rows.shape[0], count, -1).transpose(1, 0, 2)

    out_share = side_by_side(share(self_output_weight, step), 2).reshape(depth, local)
    query_share = share(cross_query_weight, depth)
    cross_share = side_by_side(share(cross_output_weight, step), 2).reshape(depth, local)
    share_one = jnp.stack([swap(out_share), swap(query_share), swap(cross_share)])
    rows_one = first_norm(meta, x, gain_one)
    share_one, rows_one = lax.optimization_barrier((share_one, rows_one))
    gathered_one = lax.all_gather(share_one, "dp", axis=0)
    rows_one_other = swap(rows_one)
    factors = picked_factors(
        meta,
        [
            (attention_first_factors, 0, 3),
            (attention_first_factors, 1, 7),
            (cross_second_factors, 0, 4),
            (cross_second_factors, 1, 5),
            (cross_second_factors, 2, 6),
            (input_second_factors, None, 8),
            (output_first_factors, None, 9),
        ],
    )
    packed = swap(factors)
    first_pack = 5 * local

    heads_own, ranks_own = project_heads(
        meta, rows_one, self_query_key_value_weight, self_first_factors, self_second_factors, 0, 0, "own_heads"
    )
    part_own = self_forward_own(meta, heads_own, factors)
    text_own, _ = project_heads(
        meta, text, cross_key_value_weight, cross_first_factors, cross_second_factors, 5, 1, "text_heads"
    )
    text_other = swap(text_own)
    share_two = feed_share(
        meta, down_weight, up_weight, depth, (part_own, text_own, rows_one_other)
    )
    heads_other, ranks_other = project_heads(
        meta, rows_one_other, self_query_key_value_weight, self_first_factors, self_second_factors,
        0, 0, "other_heads", (share_two,),
    )
    z_own_frames, z_other_frames, log_own, log_other = self_forward(meta, part_own, heads_own, heads_other)
    share_two, z_other_frames = lax.optimization_barrier((swap(share_two), z_other_frames))
    gathered_two = lax.all_gather(share_two, "dp", axis=0)
    z_other_heads = swap(z_other_frames)
    weights = (self_output_weight, cross_query_weight, cross_output_weight)
    tables = (attention_first_factors, attention_second_factors, cross_first_factors, cross_second_factors)
    stream_one, stream_two, rows_three, q_own, q_other, z2_own, z2_other, *middle_ranks = middle_forward(
        meta, x, z_own_frames, z_other_heads, weights, gathered_one, tables, packed,
        text_own, text_other, (gain_two, gain_three),
    )
    tile = local
    *carried, ga9_own, gb8_own = feed_own(
        meta, rows_three, cot, up_weight, down_weight, input_first_factors, input_second_factors,
        output_first_factors, output_second_factors, tile,
    )
    output, grad_two, feed_mine, feed_theirs = feed_other(
        meta, rows_three, cot, gathered_two, packed, first_pack, input_first_factors,
        output_second_factors, carried, stream_two, gain_three, tile,
    )

    feed_received = swap(feed_theirs)

    (
        grad_one, dz_own_heads, *dz_other_heads, text_grad_own, middle_mine, middle_theirs,
        text_mine_rank, text_theirs,
    ) = middle_back(
        meta, grad_two, stream_one, z_own_frames, z_other_heads, q_own, q_other, z2_own, z2_other,
        weights, gathered_one, tables, packed, text_own, text_other, gain_two, text, middle_ranks,
    )
    feed_received, middle_theirs, *dz_other_heads = lax.optimization_barrier(
        (feed_received, middle_theirs, *dz_other_heads)
    )
    *dz_other_frames, text_theirs = lax.optimization_barrier(
        (*[swap(half) for half in dz_other_heads], text_theirs)
    )

    unit = local
    hidden_units = hidden // unit
    labels = jnp.zeros((RANK_UNIT, 2 * HEAD_DIM), LOW).at[:, : picks.shape[0]].set(picks.astype(LOW)[None])
    early = jnp.concatenate(
        [
            join(middle_mine, [swap(middle_theirs)]),
            join(feed_mine, [feed_received[:, 2 * hidden :]]),
            join(jnp.concatenate([gb8_own, ga9_own], axis=1), [feed_received[:, : 2 * hidden]]),
            labels,
        ],
        axis=1,
    )
    early_all = lax.all_gather(early, "dp", axis=0)
    grads_part, *prepared = self_back_own(meta, heads_own, z_own_frames, log_own, dz_own_heads)
    grads_own, grads_other = self_back(
        meta, grads_part, prepared, heads_other, z_other_frames, log_other, dz_other_frames, early
    )
    text_received, grads_own = lax.optimization_barrier((swap(text_theirs), grads_own))
    texts = text.shape[0]
    text_grad_other = text_received[: 2 * texts].reshape(text_grad_own.shape)
    text_received_rank = side_by_side(
        text_received[2 * texts :].reshape(4, RANK_UNIT, local).transpose(1, 0, 2).reshape(RANK_UNIT, -1), 1
    )[0]
    text_heads_grad = (text_grad_own + text_grad_other.astype(WIDE)).astype(LOW)
    mine, theirs = first_grads(
        meta, [rows_one, rows_one_other], [grads_own, grads_other], self_second_factors, 0, "self_first"
    )
    seconds = second_grads(meta, [ranks_own, ranks_other], [grads_own, grads_other], "self_second", theirs)
    theirs, seconds = lax.optimization_barrier((swap(theirs), seconds))
    partial_other = [
        project_back_heads(
            meta, grads_other, self_query_key_value_weight, self_first_factors, self_second_factors,
            0, 0, LOW, "other_back", seconds, (part, 2),
        )
        for part in range(2)
    ]
    received = [swap(part) for part in partial_other]
    late = jnp.concatenate(
        [join(mine, [theirs]), seconds, join(text_mine_rank, [text_received_rank])], axis=1
    )
    late, early_all = lax.optimization_barrier((late, early_all))
    late_all = lax.all_gather(late, "dp", axis=0)
    text_rows = project_back_heads(
        meta, text_heads_grad, cross_key_value_weight, cross_first_factors, cross_second_factors,
        5, 1, WIDE, "text_back", partial_other[1],
    )
    text_halves = (text_rows[:, : width // 2], text_rows[:, width // 2 :])
    text_mine = jnp.where(side == 0, text_halves[0], text_halves[1])
    text_theirs = jnp.where(side == 0, text_halves[1], text_halves[0])
    text_received = swap(text_theirs.astype(LOW))
    partial_own = project_back_heads(
        meta, grads_own, self_query_key_value_weight, self_first_factors, self_second_factors,
        0, 0, WIDE, "own_back", late,
    )
    sum_query_a, sum_query_b, sum_out_a, sum_out_b, sum_up_a, sum_down_b, sum_up_b, sum_down_a = slot_sums(
        meta,
        early_all,
        [(4, 0, 0), (4, 1, 0), (3, 2, 0), (7, 2, 1), (3, 3, 0), (7, 3, 1), (8, 4, 0), (9, 5, 0)]
        + [(8, 6, i) for i in range(hidden_units)]
        + [(9, 7, i) for i in range(hidden_units)],
        [(1, unit), (1, unit), (2, unit), (2, unit), (None, unit), (None, unit), (None, hidden), (None, hidden)],
        slots, unit, {}, "early_slots", (partial_own,),
    )
    *received, text_received, sum_up_a = lax.optimization_barrier((*received, text_received, sum_up_a))
    text_grad = text_mine + text_received.astype(WIDE)
    input_grad, sum_self_a, sum_self_b, sum_cross_a, sum_cross_b = last_norm(
        meta, x, partial_own, received, grad_one, gain_one,
        late_all,
        early_all,
        [(0, 0, 0), (1, 0, 1), (2, 0, 2), (0, 1, 0), (1, 1, 1), (2, 1, 2)]
        + [(5, 2, 1), (6, 2, 2), (5, 3, 1), (6, 3, 2)],
        [(3, unit), (3, unit), (3, unit), (3, unit)],
        slots, unit, {2: sum_query_a, 3: sum_query_b}, (sum_up_a,),
    )
    return (
        output[None],
        input_grad[None],
        text_grad[None],
        sum_self_a,
        sum_self_b,
        sum_cross_a,
        sum_cross_b,
        sum_out_a,
        sum_out_b,
        sum_up_a,
        sum_up_b,
        sum_down_a,
        sum_down_b,
    )


def solution(mesh):
    in_specs = (
        P("dp", "tensor", None),
        P("dp", None, None),
        P("dp", "tensor", None),
        P("dp", None),
        P(),
        P(),
        P(),
        P(None, None, "tensor"),
        P("tensor", None),
        P(None, "tensor"),
        P(None, None, "tensor"),
        P("tensor", None),
        P(None, "tensor"),
        P("tensor", None),
        P(),
        P(None, None, None, "tensor"),
        P(),
        P(None, None, None, "tensor"),
        P(None, None, None, "tensor"),
        P(),
        P(),
        P(None, None, "tensor"),
        P(None, None, "tensor"),
        P(),
    )
    out_specs = (
        P("dp", "tensor", None),
        P("dp", "tensor", None),
        P("dp", None, "tensor"),
        P(None, None, None, "tensor"),
        P(None, None, None, "tensor"),
        P(None, None, None, "tensor"),
        P(None, None, None, "tensor"),
        P(None, None, None, "tensor"),
        P(None, None, None, "tensor"),
        P(None, None, "tensor"),
        P(None, None, "tensor"),
        P(None, None, "tensor"),
        P(None, None, "tensor"),
    )
    layer = on_pair if mesh.shape["tensor"] == 2 else on_device
    return jax.shard_map(
        layer, mesh=mesh, in_specs=in_specs, out_specs=out_specs, check_vma=False
    )
```
